32 devices in a mesh: gx: 2 (over y), gz: 4 (over z), gy: 4 (over x, core).
Axes of the slice: x: 2, y: 2, z: 4, core: 2. Of those that a mesh axis runs over, the one named last changes fastest.
Arguments:
- spectral: float32 [2, 128, 32, 2048], P(None, 'gz', 'gy', 'gx'), may hold values from -6 to 6
- shifts: int32 [128, 32], P('gz', 'gy'), may hold values from 0 to 2047
- colour: int32 [32, 2048], P('gy', 'gx'), may hold values 0 or 1
- pressure: float32 [128, 32, 2048], P('gz', 'gy', 'gx'), may hold values from -5 to 7
- source: float32 [128, 32, 2048], P('gz', 'gy', 'gx'), may hold values from -4.5 to 7
Outputs:
- log_perm: float32 [128, 32, 2048], P('gz', 'gy', 'gx')
- smoothed: float32 [128, 32, 2048], P('gz', 'gy', 'gx')
The draws below stay inside these ranges and needn't reach their ends.
All inputs are finite; a program needn't handle non-finite values. No bound on the sum of `colour` on one device may be relied on, other than what follows from the above.
Results may differ from the reference program's by a relative error of at most 0.0038.
Values sent between devices are 32-bit elements; how exact they have to be, the bound alone decides.
No kernel may reach another device: no remote copies, remote signals or barrier semaphores. Data moves between devices by JAX's collectives and lax.ppermute only.
A program may use at most 128 MiB of HBM per device.

```python
import math
import jax
import jax.numpy as jnp
from jax import lax

NX = 2048
NY = 32
NZ = 128
VERT = 4096


def drawn_field(key, level_lo, level_hi):
    level_key, noise_key = jax.random.split(key)
    level = jax.random.uniform(level_key, (1, NY, NX), jnp.float32, level_lo, level_hi)
    rough = jnp.clip(jax.random.normal(noise_key, (NZ, NY, NX), jnp.float32), -5.0, 5.0)
    return (level + rough).astype(jnp.float32)


def draw_pressure(key, part):
    field_key = jax.random.fold_in(key, 11)
    return drawn_field(field_key, 0.0, 2.0)


def draw_source(key, part):
    field_key = jax.random.fold_in(key, 23)
    return drawn_field(field_key, 0.5, 2.0)


def touch_ends(drawn, rng, smallest, largest):
    extent = drawn.shape
    place = [jax.random.randint(jax.random.fold_in(rng, axis), (), 0, extent[axis]) for axis in range(len(extent))]
    drawn = drawn.at[tuple(place)].set(smallest)
    longest = extent.index(max(extent))
    place[longest] = (place[longest] + 1) % extent[longest]
    return drawn.at[tuple(place)].set(largest)


def level_of(own_key, dims, pieces, low, largest):
    def one(axis_at, blocks):
        draws = jax.random.uniform(jax.random.fold_in(jax.random.fold_in(own_key, 6), axis_at), (blocks,), jnp.float32, low / len(pieces), largest / len(pieces))
        return jnp.repeat(jnp.exp(draws), dims[axis_at] // blocks).reshape((-1,) + (1,) * (len(dims) - axis_at - 1))

    factor_of = one(*pieces[0])
    for cut in pieces[1:]:
        factor_of = factor_of * one(*cut)
    return factor_of


def gaussian(rng, extent, spread, bound, shards=(), kind=jnp.bfloat16):
    values = jax.random.normal(rng, extent, jnp.float32) * spread
    if len(shards) > 0:
        values = level_of(rng, extent, shards, -0.22, 0.18) * values
    return jnp.clip(values, min=-bound, max=bound).astype(kind)


def setup_inputs(seed: int = 0) -> dict:
    seeds = jax.random.split(jax.random.key(seed), 6)
    spectral = gaussian(seeds[0], (2, NZ, NY, NX), 1.0, 6.0, ((1, 4), (2, 4), (3, 2)), jnp.float32)
    shifts = touch_ends(jax.random.randint(seeds[1], (NZ, NY), 0, NX), jax.random.fold_in(seeds[1], 1), 0, NX - 1).astype(jnp.int32)
    colour = touch_ends((jax.random.randint(seeds[2], (NY, NX), 0, 2) < 1).astype(jnp.int32), jax.random.fold_in(seeds[2], 1), 0, 1)
    pressure = draw_pressure(jax.random.fold_in(seeds[5], 71), 0)
    source = draw_source(jax.random.fold_in(seeds[5], 71), 0)
    return {"spectral": spectral, "shifts": shifts, "colour": colour, "pressure": pressure, "source": source}


STORE = 1.0

def spectral_slice(packed):
    coeff_slice, shift_row = packed
    wave_index = jnp.arange(NX, dtype=jnp.int32)
    wave_turns = shift_row[:, None] * wave_index[None, :] % NX
    phase_angle = wave_turns.astype(jnp.float32) * (2.0 * math.pi / NX)
    cosine = jnp.cos(phase_angle)
    sine_part = jnp.sin(phase_angle)
    real_part = coeff_slice[0] * cosine - coeff_slice[1] * sine_part
    imag_part = coeff_slice[0] * sine_part + coeff_slice[1] * cosine
    spectrum = lax.complex(real_part, imag_part)
    return jnp.real(jnp.fft.ifft(spectrum, axis=-1)) * math.sqrt(NX)

def harmonic(center, beside):
    return 2.0 * center * beside / (center + beside)

def thomas(lower_diagonal, main_diagonal, upper_diagonal, right_hand_side):

    def forward_scan(carried_state, row_entries):
        previous_ratio, previous_eliminated = carried_state
        column_lower, main_c, sup_c, column_right_hand = row_entries
        present_denominator = main_c - column_lower * previous_ratio
        present_ratio = sup_c / present_denominator
        present_eliminated = (column_right_hand - column_lower * previous_eliminated) / present_denominator
        return ((present_ratio, present_eliminated), (present_ratio, present_eliminated))
    zeroed_layer = jnp.zeros(right_hand_side.shape[1:], right_hand_side.dtype)
    unused_output, (ratio_rows, eliminated_rows) = lax.scan(forward_scan, (zeroed_layer, zeroed_layer), (lower_diagonal, main_diagonal, upper_diagonal, right_hand_side))

    def backward_scan(following_value, row_entries):
        column_ratio, column_eliminated = row_entries
        present_value = column_eliminated - column_ratio * following_value
        return (present_value, present_value)
    unused_output, solved_values = lax.scan(backward_scan, zeroed_layer, (ratio_rows, eliminated_rows), reverse=True)
    return solved_values

def reference(spectral, shifts, colour, pressure, source):
    vert_factor = float(VERT)
    log_perm = lax.map(spectral_slice, (jnp.moveaxis(spectral, 1, 0), shifts))
    perm = jnp.exp(log_perm)
    padded = jnp.pad(perm, 1)
    w_zm = vert_factor * harmonic(perm, padded[:-2, 1:-1, 1:-1])
    w_zp = vert_factor * harmonic(perm, padded[2:, 1:-1, 1:-1])
    w_ym = harmonic(perm, padded[1:-1, :-2, 1:-1])
    w_yp = harmonic(perm, padded[1:-1, 2:, 1:-1])
    w_xm = harmonic(perm, padded[1:-1, 1:-1, :-2])
    w_xp = harmonic(perm, padded[1:-1, 1:-1, 2:])
    main_diagonal = STORE + w_xm + w_xp + w_ym + w_yp + w_zm + w_zp

    def line_solve(current):
        cycle = jnp.pad(current, ((0, 0), (1, 1), (1, 1)))
        right_hand_side = source + w_xm * cycle[:, 1:-1, :-2] + w_xp * cycle[:, 1:-1, 2:]
        right_hand_side = right_hand_side + w_ym * cycle[:, :-2, 1:-1] + w_yp * cycle[:, 2:, 1:-1]
        return thomas(-w_zm, main_diagonal, -w_zp, right_hand_side)
    half = jnp.where((colour == 0)[None], line_solve(pressure), pressure)
    smoothed = jnp.where((colour == 1)[None], line_solve(half), half)
    return (log_perm, smoothed)
```

```python
import functools
import math

import jax
import jax.numpy as jnp
import ml_dtypes
import numpy as np
from jax import lax
from jax.experimental import pallas as pl
from jax.experimental.pallas import tpu as pltpu
from jax.sharding import PartitionSpec as P

NX = 2048


STORE = 1.0


def padded_2(block, sides, width):
    for axis, dim in sides:
        count = lax.axis_size(axis)
        forward = [(i, i + 1) for i in range(count - 1)]
        backward = [(target, source) for source, target in forward]
        low = lax.ppermute(
            lax.slice_in_dim(block, block.shape[dim] - width, None, axis=dim), axis, forward
        )
        high = lax.ppermute(lax.slice_in_dim(block, 0, width, axis=dim), axis, backward)
        block = jnp.concatenate([low, block, high], axis=dim)
    return block


def twisted_coeffs(spectral, shifts, first_wave):
    count = spectral.shape[3]
    wave_index = first_wave + jnp.arange(count, dtype=jnp.int32)
    wave_turns = shifts[:, :, None] * wave_index[None, None, :] % NX
    phase_angle = wave_turns.astype(jnp.float32) * (2.0 * math.pi / NX)
    cosine = jnp.cos(phase_angle)
    sine_part = jnp.sin(phase_angle)
    real_part = spectral[0] * cosine - spectral[1] * sine_part
    imag_part = spectral[0] * sine_part + spectral[1] * cosine
    return jnp.stack([real_part, imag_part])


def basis(count, first_cell, width_cells):
    wave_index = jnp.arange(count, dtype=jnp.int32)
    cell_index = first_cell + jnp.arange(width_cells, dtype=jnp.int32)
    wave_turns = wave_index[:, None] * cell_index[None, :] % NX
    phase_angle = wave_turns.astype(jnp.float32) * (2.0 * math.pi / NX)
    offsets = jnp.concatenate(
        [jnp.zeros((count, 1), jnp.float32), jnp.full((count, 1), 0.5 * math.pi, jnp.float32)],
        axis=0,
    )
    stacked = jnp.concatenate([phase_angle, phase_angle], axis=0) + offsets
    return jnp.cos(stacked) * (1.0 / math.sqrt(NX))


def flatten_pair(piece):
    depth, items, count = (piece.shape[1], piece.shape[2], piece.shape[3])
    return jnp.concatenate(
        [piece[0].reshape(depth * items, count), piece[1].reshape(depth * items, count)], axis=1
    )


def harmonic(center, beside):
    return 2.0 * center * beside / (center + beside)


def thomas(lower_diagonal, main_diagonal, upper_diagonal, right_hand_side):

    def thomas_forward_scan(carried_state, row_entries):
        previous_ratio, previous_eliminated = carried_state
        column_lower, main_c, sup_c, column_right_hand = row_entries
        present_denominator = main_c - column_lower * previous_ratio
        present_ratio = sup_c / present_denominator
        present_eliminated = (
            column_right_hand - column_lower * previous_eliminated
        ) / present_denominator
        return ((present_ratio, present_eliminated), (present_ratio, present_eliminated))

    zeroed_layer = jnp.zeros(right_hand_side.shape[1:], right_hand_side.dtype)
    unused_output, (ratio_rows, eliminated_rows) = lax.scan(
        thomas_forward_scan,
        (zeroed_layer, zeroed_layer),
        (lower_diagonal, main_diagonal, upper_diagonal, right_hand_side),
    )

    def thomas_backward_scan(following_value, row_entries):
        column_ratio, column_eliminated = row_entries
        present_value = column_eliminated - column_ratio * following_value
        return (present_value, present_value)

    unused_output, solved_values = lax.scan(
        thomas_backward_scan, zeroed_layer, (ratio_rows, eliminated_rows), reverse=True
    )
    return solved_values


def factor(lower_diagonal, main_diagonal, upper_diagonal):

    def factor_forward_scan(previous_ratio, row_entries):
        column_lower, main_c, sup_c = row_entries
        present_denominator = main_c - column_lower * previous_ratio
        present_ratio = sup_c / present_denominator
        return (present_ratio, (present_denominator, present_ratio))

    unused_output, (denominator_rows, ratio_rows) = lax.scan(
        factor_forward_scan,
        jnp.zeros_like(main_diagonal[0]),
        (lower_diagonal, main_diagonal, upper_diagonal),
    )
    return (denominator_rows, ratio_rows)


def solve_factored(lower_diagonal, denominator_rows, ratio_rows, right_hand_side):

    def solve_forward_scan(previous_eliminated, row_entries):
        column_lower, column_denominator, column_right_hand = row_entries
        present_eliminated = (
            column_right_hand - column_lower[None] * previous_eliminated
        ) / column_denominator[None]
        return (present_eliminated, present_eliminated)

    unused_output, eliminated_rows = lax.scan(
        solve_forward_scan,
        jnp.zeros_like(right_hand_side[0]),
        (lower_diagonal, denominator_rows, right_hand_side),
    )

    def solve_backward_scan(following_value, row_entries):
        column_ratio, column_eliminated = row_entries
        present_value = column_eliminated - column_ratio[None] * following_value
        return (present_value, present_value)

    unused_output, solved_values = lax.scan(
        solve_backward_scan,
        jnp.zeros_like(right_hand_side[0]),
        (ratio_rows, eliminated_rows),
        reverse=True,
    )
    return solved_values


def generic_body(spectral, shifts, colour, pressure, source):
    total_depth = pressure.shape[0] * lax.axis_size("gz")
    vert_factor = float(total_depth * total_depth // 4)
    width_cells = spectral.shape[3]
    first_cell = lax.axis_index("gx") * width_cells
    twisted = twisted_coeffs(spectral, shifts, first_cell)
    piece = lax.all_to_all(twisted, "gx", split_axis=1, concat_axis=3, tiled=True)
    depth = piece.shape[1]
    items = piece.shape[2]
    length = piece.shape[3]
    flat = flatten_pair(piece)
    block_width = min(512, length)
    blocks = [
        jnp.dot(
            flat,
            basis(length, block * block_width, block_width),
            precision=lax.Precision.HIGHEST,
            preferred_element_type=jnp.float32,
        )
        for block in range(length // block_width)
    ]
    field_rows = jnp.concatenate(blocks, axis=1).reshape(depth, items, length)
    log_perm = lax.all_to_all(field_rows, "gx", split_axis=2, concat_axis=0, tiled=True)
    perm = jnp.exp(log_perm)
    padded = padded_2(perm, (("gx", 2), ("gz", 0), ("gy", 1)), 1)
    w_zm = vert_factor * harmonic(perm, padded[:-2, 1:-1, 1:-1])
    w_zp = vert_factor * harmonic(perm, padded[2:, 1:-1, 1:-1])
    w_ym = harmonic(perm, padded[1:-1, :-2, 1:-1])
    w_yp = harmonic(perm, padded[1:-1, 2:, 1:-1])
    w_xm = harmonic(perm, padded[1:-1, 1:-1, :-2])
    w_xp = harmonic(perm, padded[1:-1, 1:-1, 2:])
    main_diagonal = STORE + w_xm + w_xp + w_ym + w_yp + w_zm + w_zp
    lower_diagonal = -w_zm
    upper_diagonal = -w_zp
    zeroed_layer = jnp.zeros_like(main_diagonal[0])
    inner_sub = jnp.concatenate([zeroed_layer[None], lower_diagonal[2:-1]], axis=0)
    inner_sup = jnp.concatenate([upper_diagonal[1:-2], zeroed_layer[None]], axis=0)
    inner_main = main_diagonal[1:-1]
    denominator_rows, ratio_rows = factor(inner_sub, inner_main, inner_sup)
    unit_rhs = jnp.zeros((inner_main.shape[0], 2) + zeroed_layer.shape, jnp.float32)
    unit_rhs = unit_rhs.at[0, 0].set(-lower_diagonal[1])
    unit_rhs = unit_rhs.at[-1, 1].set(-upper_diagonal[-2])
    coupled = solve_factored(inner_sub, denominator_rows, ratio_rows, unit_rhs)
    left_part = coupled[:, 0]
    right_part = coupled[:, 1]
    sub_first = lower_diagonal[0]
    main_first = main_diagonal[0] + upper_diagonal[0] * left_part[0]
    sup_first = upper_diagonal[0] * right_part[0]
    sub_last = lower_diagonal[-1] * left_part[-1]
    main_last = main_diagonal[-1] + lower_diagonal[-1] * right_part[-1]
    sup_last = upper_diagonal[-1]

    def line_solve(current):
        cycle = padded_2(current, (("gx", 2), ("gy", 1)), 1)
        right_hand_side = source + w_xm * cycle[:, 1:-1, :-2] + w_xp * cycle[:, 1:-1, 2:]
        right_hand_side = right_hand_side + w_ym * cycle[:, :-2, 1:-1] + w_yp * cycle[:, 2:, 1:-1]
        particular = solve_factored(
            inner_sub, denominator_rows, ratio_rows, right_hand_side[1:-1][:, None]
        )[:, 0]
        rhs_first = right_hand_side[0] - upper_diagonal[0] * particular[0]
        rhs_last = right_hand_side[-1] - lower_diagonal[-1] * particular[-1]
        reduced_rows = jnp.stack(
            [sub_first, main_first, sup_first, rhs_first, sub_last, main_last, sup_last, rhs_last]
        )
        gathered = lax.all_gather(reduced_rows, "gz", axis=0, tiled=True)
        segments = gathered.shape[0] // 8
        system = gathered.reshape((2 * segments, 4) + zeroed_layer.shape)
        reduced_sol = thomas(system[:, 0], system[:, 1], system[:, 2], system[:, 3])
        own_pair = lax.dynamic_slice_in_dim(reduced_sol, 2 * lax.axis_index("gz"), 2, 0)
        face_first = own_pair[0]
        face_last = own_pair[1]
        inner = particular + face_first[None] * left_part + face_last[None] * right_part
        return jnp.concatenate([face_first[None], inner, face_last[None]], axis=0)

    half = jnp.where((colour == 0)[None], line_solve(pressure), pressure)
    smoothed = jnp.where((colour == 1)[None], line_solve(half), half)
    return (log_perm, smoothed)


LANES = 128
ROWS = 8
TILE = 256
F32 = jnp.float32
MIB = 1 << 20


def suits(mesh):
    sizes = dict(mesh.shape)
    return sizes["gx"] == 2 and sizes["gz"] == 4 and sizes["gy"] == 4


def params(mib=32):
    return pltpu.CompilerParams(vmem_limit_bytes=mib * MIB)


def wave_tables():
    index = np.arange(NX, dtype=np.int64)
    turns = (index[:, None] * index[None, :]) % NX
    angle = 2.0 * np.pi * np.arange(NX) / NX
    scale = 1.0 / np.sqrt(NX)
    whole = np.stack([(np.cos(angle) * scale)[turns], (-np.sin(angle) * scale)[turns]])
    whole = whole.astype(np.float32)
    high = whole.astype(ml_dtypes.bfloat16)
    low = (whole - high.astype(np.float32)).astype(ml_dtypes.bfloat16)
    return high, low


def cos_sin(turns):
    quarter = (turns + NX // 8) >> 9
    angle = (turns - (quarter << 9)).astype(F32) * (2.0 * math.pi / NX)
    square = angle * angle
    sine = angle * (
        1.0
        + square * (-1.0 / 6 + square * (1.0 / 120 + square * (-1.0 / 5040 + square / 362880)))
    )
    cosine = 1.0 + square * (
        -0.5 + square * (1.0 / 24 + square * (-1.0 / 720 + square * (1.0 / 40320)))
    )
    odd = (quarter & 1) == 1
    first = jnp.where(odd, sine, cosine)
    second = jnp.where(odd, cosine, sine)
    cos_sign = jnp.where(((quarter + 1) & 2) == 2, -1.0, 1.0)
    sin_sign = jnp.where((quarter & 2) == 2, -1.0, 1.0)
    return first * cos_sign, second * sin_sign


def split(values):
    high = values.astype(jnp.bfloat16)
    return high, (values - high.astype(F32)).astype(jnp.bfloat16)


def twist(first_wave, spectral_ref, shifts_ref, high_ref, low_ref, shift_rows):
    depth, items = shifts_ref.shape
    waves = spectral_ref.shape[2]
    eye = (
        lax.broadcasted_iota(jnp.int32, (items, items), 0)
        == lax.broadcasted_iota(jnp.int32, (items, items), 1)
    ).astype(F32)
    for z in range(depth):
        row = jnp.broadcast_to(shifts_ref[z : z + 1, :].astype(F32), (items, items))
        column = jnp.sum(row * eye, axis=1, keepdims=True)
        shift_rows[z * items : (z + 1) * items, :] = jnp.broadcast_to(column, (items, LANES))
    step = 16
    lane = lax.broadcasted_iota(jnp.int32, (step, LANES), 1)

    def rows_of(at, carry):
        rows = pl.ds(pl.multiple_of(at * step, step), step)
        shift = shift_rows[rows, :].astype(jnp.int32)
        cosine, sine = cos_sin((shift * (lane + first_wave)) & (NX - 1))
        turn_cos, turn_sin = cos_sin((shift * LANES) & (NX - 1))
        for part in range(waves // LANES):
            span = slice(part * LANES, (part + 1) * LANES)
            real = spectral_ref[0, rows, span]
            imag = spectral_ref[1, rows, span]
            for place, value in (
                (0, real * cosine - imag * sine),
                (waves, real * sine + imag * cosine),
            ):
                high, low = split(value)
                target = slice(place + part * LANES, place + (part + 1) * LANES)
                high_ref[rows, target] = high
                low_ref[rows, target] = low
            cosine, sine = (
                cosine * turn_cos - sine * turn_sin,
                cosine * turn_sin + sine * turn_cos,
            )
        return carry

    lax.fori_loop(0, depth * items // step, rows_of, 0)


def three_dots(high, low, table_high, table_low):
    table_high = table_high.reshape(-1, table_high.shape[-1])
    table_low = table_low.reshape(-1, table_low.shape[-1])
    dot = functools.partial(jnp.dot, preferred_element_type=F32)
    return dot(high, table_high) + (dot(high, table_low) + dot(low, table_high))


def first_transform_kernel(
    place, spectral_ref, shifts_ref, table_high, table_low, sums, high_ref, low_ref, shift_rows
):
    twist(place[2], spectral_ref, shifts_ref, high_ref, low_ref, shift_rows)
    sums[...] = three_dots(high_ref[...], low_ref[...], table_high[...], table_low[...])


def transform_kernel(place, high_ref, low_ref, table_high, table_low, sums):
    sums[...] = three_dots(high_ref[...], low_ref[...], table_high[...], table_low[...])


def table_specs(waves, column):
    def at(step, place):
        return (0, place[0], place[1] + column + step)

    return [pl.BlockSpec((2, waves, TILE), at)] * 2


def whole(shape):
    return pl.BlockSpec(shape, lambda step, place: (0,) * len(shape))


def first_transform(place, spectral, shifts, tables):
    _, rows, waves = spectral.shape
    half = jax.ShapeDtypeStruct((rows, 2 * waves), jnp.bfloat16)
    return pl.pallas_call(
        first_transform_kernel,
        grid_spec=pltpu.PrefetchScalarGridSpec(
            num_scalar_prefetch=1,
            grid=(1,),
            in_specs=[whole(spectral.shape), whole(shifts.shape)] + table_specs(waves, 0),
            out_specs=[whole((rows, TILE)), whole(half.shape), whole(half.shape)],
            scratch_shapes=[pltpu.VMEM((rows, LANES), F32)],
        ),
        out_shape=[jax.ShapeDtypeStruct((rows, TILE), F32), half, half],
        compiler_params=params(),
        cost_estimate=pl.CostEstimate(
            flops=6 * rows * 2 * waves * TILE, bytes_accessed=8 * MIB, transcendentals=0
        ),
        name="twist_and_first_sums",
    )(place, spectral, shifts, *tables)


def transform(place, high, low, tables, column, tiles, name):
    rows, twice = high.shape
    return pl.pallas_call(
        transform_kernel,
        grid_spec=pltpu.PrefetchScalarGridSpec(
            num_scalar_prefetch=1,
            grid=(tiles,),
            in_specs=[whole(high.shape), whole(low.shape)] + table_specs(twice // 2, column),
            out_specs=pl.BlockSpec((rows, TILE), lambda step, place: (0, step)),
        ),
        out_shape=jax.ShapeDtypeStruct((rows, tiles * TILE), F32),
        compiler_params=params(),
        cost_estimate=pl.CostEstimate(
            flops=6 * rows * twice * tiles * TILE,
            bytes_accessed=(2 + 2 * tiles) * MIB,
            transcendentals=0,
        ),
        name=name,
    )(place, high, low, *tables)


def roll(values, shift, axis):
    return pltpu.roll(values, shift % values.shape[axis], axis)


def column_lane(z, values, target):
    return pltpu.roll(values, (target - z) % LANES, 1)


def pack_edges(z, value, south, north, west, east):
    south[pl.ds(z, 1), :] = value[0:1, :]
    north[pl.ds(z, 1), :] = value[ROWS - 1 : ROWS, :]
    lane = lax.broadcasted_iota(jnp.int32, (ROWS, LANES), 1)
    west[...] = jnp.where(lane == z, jnp.broadcast_to(value[:, :1], (ROWS, LANES)), west[...])
    east[...] = jnp.where(lane == z, jnp.broadcast_to(value[:, -1:], (ROWS, LANES)), east[...])


def edge_shapes(depth, width):
    row = jax.ShapeDtypeStruct((depth, width), F32)
    column = jax.ShapeDtypeStruct((ROWS, LANES), F32)
    return [row, row, column, column]


def field_kernel(depth, own, *refs):
    parts, (log_perm, resist, south, north, west, east) = (refs[:-6], refs[-6:])
    west[...] = jnp.zeros_like(west)
    east[...] = jnp.zeros_like(east)

    def layer(z, carry):
        value = own[z] + jnp.concatenate([part[z] for part in parts], axis=1)
        log_perm[z] = value
        inverse = jnp.exp(-value)
        resist[z] = inverse
        pack_edges(z, inverse, south, north, west, east)
        return carry

    lax.fori_loop(0, depth, layer, 0, unroll=4)


def pressure_edges_kernel(depth, pressure, south, north, west, east):
    west[...] = jnp.zeros_like(west)
    east[...] = jnp.zeros_like(east)

    def layer(z, carry):
        pack_edges(z, pressure[z], south, north, west, east)
        return carry

    lax.fori_loop(0, depth, layer, 0, unroll=4)


def east_of(z, plane, edge):
    lane = lax.broadcasted_iota(jnp.int32, (ROWS, LANES), 1)
    moved = roll(plane, -1, 1)
    last = jnp.where(lane == LANES - 1, column_lane(z, edge, LANES - 1), moved[:, -LANES:])
    return jnp.concatenate([moved[:, :-LANES], last], axis=1)


def west_of(z, plane, edge):
    lane = lax.broadcasted_iota(jnp.int32, (ROWS, LANES), 1)
    moved = roll(plane, 1, 1)
    first = jnp.where(lane == 0, column_lane(z, edge, 0), moved[:, :LANES])
    return jnp.concatenate([first, moved[:, LANES:]], axis=1)


def north_of(z, plane, edge):
    row = lax.broadcasted_iota(jnp.int32, plane.shape, 0)
    return jnp.where(row == ROWS - 1, edge[pl.ds(z, 1), :], roll(plane, -1, 0))


def south_of(z, plane, edge):
    row = lax.broadcasted_iota(jnp.int32, plane.shape, 0)
    return jnp.where(row == 0, edge[pl.ds(z, 1), :], roll(plane, 1, 0))


def inverse_of(values):
    return 1.0 / values


def sides(z, plane, south, north, west, east):
    return (
        south_of(z, plane, south),
        north_of(z, plane, north),
        west_of(z, plane, west[...]),
        east_of(z, plane, east[...]),
    )


def first_sweep_kernel(depth, vert, flags, *refs):
    resist, r_south, r_north, r_west, r_east = refs[:5]
    pressure, p_south, p_north, p_west, p_east = refs[5:10]
    source = refs[10]
    w_south, w_north, w_west, w_east, current, inverse, ratio, lead, reduced = refs[11:]
    shape = resist.shape[1:]
    row = lax.broadcasted_iota(jnp.int32, shape, 0)
    lane = lax.broadcasted_iota(jnp.int32, shape, 1)
    twos = [
        jnp.where(where, 2.0 * flags[at].astype(F32), 2.0)
        for at, where in enumerate(
            (row == 0, row == ROWS - 1, lane == 0, lane == shape[1] - 1)
        )
    ]

    def local(z):
        here = resist[z]
        beside = sides(z, here, r_south, r_north, r_west, r_east)
        weights = [two * inverse_of(here + other) for two, other in zip(twos, beside)]
        for ref, value in zip((w_south, w_north, w_west, w_east), weights):
            ref[z] = value
        around = sides(z, pressure[z], p_south, p_north, p_west, p_east)
        ground = STORE + ((weights[0] + weights[1]) + (weights[2] + weights[3]))
        right = source[z] + (
            (weights[0] * around[0] + weights[1] * around[1])
            + (weights[2] * around[2] + weights[3] * around[3])
        )
        return ground, right

    def layer(z, carry):
        conduct, flow, product, first_first, first_part = carry
        weight = (2.0 * vert) * inverse_of(resist[z - 1] + resist[z])
        reciprocal = inverse_of(conduct + weight)
        quotient = weight * reciprocal
        inverse[z - 1] = reciprocal
        ratio[z - 1] = quotient
        lead[z - 1] = product
        current[z - 1] = flow
        led = product * reciprocal
        first_first = first_first + led * product
        first_part = first_part + led * flow
        ground, right = local(z)
        return (
            ground + conduct * quotient,
            right + flow * quotient,
            product * quotient,
            first_first,
            first_part,
        )

    ground, right = local(0)
    zero = jnp.zeros(shape, F32)
    conduct, flow, product, first_first, first_part = lax.fori_loop(
        1, depth, layer, (ground, right, jnp.ones(shape, F32), zero, zero)
    )
    reciprocal = inverse_of(conduct)
    inverse[depth - 1] = reciprocal
    ratio[depth - 1] = zero
    lead[depth - 1] = product
    current[depth - 1] = flow
    led = product * reciprocal
    reduced[0] = first_first + led * product + resist[0] * (0.5 / vert)
    reduced[1] = led
    reduced[2] = reciprocal + resist[depth - 1] * (0.5 / vert)
    reduced[3] = first_part + led * flow
    reduced[4] = flow * reciprocal


def fluxes(me, first_first, first_last, last_last, first_part, last_part):
    count = len(first_first)
    slopes, parts = [], []
    slope = part = None
    for at in range(1, count):
        main = last_last[at - 1] + first_first[at]
        right = last_part[at - 1] - first_part[at]
        if slope is not None:
            main = main - first_last[at - 1] * slope
            right = right + first_last[at - 1] * part
        reciprocal = inverse_of(main)
        slope = first_last[at] * reciprocal
        part = right * reciprocal
        slopes.append(slope)
        parts.append(part)
    zero = jnp.zeros_like(part)
    values = [zero]
    for slope, part in zip(reversed(slopes), reversed(parts)):
        values.append(part + slope * values[-1])
    values = [zero] + values[::-1]
    enters, leaves = values[0], values[1]
    for at in range(1, count):
        enters = jnp.where(me == at, values[at], enters)
        leaves = jnp.where(me == at, values[at + 1], leaves)
    return enters, leaves


def back_substitute(depth, enters, leaves, current, inverse, ratio, lead, emit):
    def layer(step, following):
        z = depth - 1 - step
        value = inverse[z] * (current[z] + lead[z] * enters) + ratio[z] * following
        emit(z, value)
        return value

    value = inverse[depth - 1] * (current[depth - 1] + lead[depth - 1] * enters - leaves)
    emit(depth - 1, value)
    lax.fori_loop(1, depth, layer, value, unroll=4)


def half_kernel(depth, flags, *refs):
    gathered = refs[:4]
    current, inverse, ratio, lead, pressure, colour = refs[4:10]
    half, south, north, west, east = refs[10:15]
    system = refs[15]
    me = flags[4]
    for step, ref in enumerate(gathered):
        system[me ^ step] = ref[...]
    planes = [[system[segment, at] for segment in range(4)] for at in range(5)]
    enters, leaves = fluxes(me, *planes)
    west[...] = jnp.zeros_like(west)
    east[...] = jnp.zeros_like(east)

    def emit(z, value):
        kept = jnp.where(colour[...] == 0, value, pressure[z])
        half[z] = kept
        pack_edges(z, kept, south, north, west, east)

    back_substitute(depth, enters, leaves, current, inverse, ratio, lead, emit)


def second_sweep_kernel(depth, *refs):
    half, h_south, h_north, h_west, h_east, source = refs[:6]
    w_south, w_north, w_west, w_east, inverse, ratio, lead = refs[6:13]
    current, reduced = refs[13:]

    def local(z):
        around = sides(z, half[z], h_south, h_north, h_west, h_east)
        return source[z] + (
            (w_south[z] * around[0] + w_north[z] * around[1])
            + (w_west[z] * around[2] + w_east[z] * around[3])
        )

    def layer(z, carry):
        flow, first_part = carry
        current[z - 1] = flow
        first_part = first_part + lead[z - 1] * inverse[z - 1] * flow
        return (local(z) + flow * ratio[z - 1], first_part)

    flow, first_part = lax.fori_loop(
        1, depth, layer, (local(0), jnp.zeros(half.shape[1:], F32)), unroll=2
    )
    current[depth - 1] = flow
    reduced[0] = first_part + lead[depth - 1] * inverse[depth - 1] * flow
    reduced[1] = flow * inverse[depth - 1]


def smoothed_kernel(depth, flags, *refs):
    matrices, parts = refs[:4], refs[4:8]
    current, inverse, ratio, lead, half, colour = refs[8:14]
    smoothed, system = refs[14:]
    me = flags[4]
    for step in range(4):
        system[me ^ step, 0:3] = matrices[step][0:3]
        system[me ^ step, 3:5] = parts[step][...]
    planes = [[system[segment, at] for segment in range(4)] for at in range(5)]
    enters, leaves = fluxes(me, *planes)

    def emit(z, value):
        smoothed[z] = jnp.where(colour[...] == 1, value, half[z])

    back_substitute(depth, enters, leaves, current, inverse, ratio, lead, emit)


SCALARS = pl.BlockSpec(memory_space=pltpu.SMEM)
ON_CHIP = pl.BlockSpec(memory_space=pltpu.VMEM)


def call(kernel, name, out_shape, args, flags=None, scratch=(), flops=0):
    specs = [ON_CHIP] * len(args)
    if flags is not None:
        specs = [SCALARS] + specs
        args = [flags] + list(args)
    size = sum(4 * math.prod(leaf.shape) for leaf in jax.tree.leaves((list(args), out_shape)))
    return pl.pallas_call(
        kernel,
        out_shape=out_shape,
        in_specs=specs,
        out_specs=jax.tree.map(lambda _: ON_CHIP, out_shape),
        scratch_shapes=list(scratch),
        compiler_params=params(),
        cost_estimate=pl.CostEstimate(
            flops=flops, bytes_accessed=size, transcendentals=0
        ),
        name=name,
    )(*args)


PAIR = [(0, 1), (1, 0)]
NEAR = [(0, 1), (1, 0), (2, 3), (3, 2)]
MIDDLE = [(1, 2), (2, 1)]
SKIP = [(0, 2), (2, 0), (1, 3), (3, 1)]
CROSS = [(0, 3), (3, 0), (1, 2), (2, 1)]


def exchange_edges(edges):
    south, north, west, east = edges
    gx, gy = lax.axis_index("gx"), lax.axis_index("gy")
    even = gy % 2 == 0
    near = lax.ppermute(jnp.where(even, north, south), "gy", NEAR)
    middle = lax.ppermute(jnp.where(even, south, north), "gy", MIDDLE)
    column = lax.ppermute(jnp.where(gx == 0, east, west), "gx", PAIR)
    return [jnp.where(even, middle, near), jnp.where(even, near, middle), column, column]


def gather_lines(planes):
    return [planes] + [lax.ppermute(planes, "gz", pairs) for pairs in (NEAR, SKIP, CROSS)]


def fast_body(spectral, shifts, colour, pressure, source):
    depth, items, width = pressure.shape
    vert = float((depth * 4) ** 2 // 4)
    waves = spectral.shape[3]
    gx, gz, gy = (lax.axis_index(axis) for axis in ("gx", "gz", "gy"))
    flags = jnp.stack([gy > 0, gy < 3, gx > 0, gx < 1, gz]).astype(jnp.int32)
    tables = [jnp.asarray(table) for table in wave_tables()]
    tiles = width // TILE
    there = jnp.stack([gx, (1 - gx) * tiles, gx * waves]).astype(jnp.int32)
    here = jnp.stack([gx, gx * tiles, gx * waves]).astype(jnp.int32)
    layers = (depth, items, width)

    rows = depth * items
    sums, high, low = first_transform(there, spectral.reshape(2, rows, waves), shifts, tables)
    cube = lambda block: block.reshape(depth, items, block.shape[1])
    parts = [lax.ppermute(sums, "gx", PAIR)]
    for column, count in ((1, 1), (2, 2)):
        sums = transform(there, high, low, tables, column, count, "sums_for_other")
        parts.append(lax.ppermute(sums, "gx", PAIR))
    own = transform(here, high, low, tables, 0, tiles, "own_sums")

    p_edges = exchange_edges(
        call(
            functools.partial(pressure_edges_kernel, depth),
            "pressure_edges",
            edge_shapes(depth, width),
            [pressure],
        )
    )
    block = jax.ShapeDtypeStruct(layers, F32)
    log_perm, resist, *r_edges = call(
        functools.partial(field_kernel, depth),
        "field",
        [block, block] + edge_shapes(depth, width),
        [cube(own)] + [cube(part) for part in parts],
    )
    r_edges = exchange_edges(r_edges)
    *weights, current, inverse, ratio, lead, reduced = call(
        functools.partial(first_sweep_kernel, depth, vert),
        "first_sweep",
        [block] * 8 + [jax.ShapeDtypeStruct((5, items, width), F32)],
        [resist, *r_edges, pressure, *p_edges, source],
        flags,
    )
    gathered = gather_lines(reduced)
    system = [pltpu.VMEM((4, 5, items, width), F32)]
    half, *h_edges = call(
        functools.partial(half_kernel, depth),
        "half",
        [block] + edge_shapes(depth, width),
        [*gathered, current, inverse, ratio, lead, pressure, colour],
        flags,
        system,
    )
    h_edges = exchange_edges(h_edges)
    current, reduced = call(
        functools.partial(second_sweep_kernel, depth),
        "second_sweep",
        [block, jax.ShapeDtypeStruct((2, items, width), F32)],
        [half, *h_edges, source, *weights, inverse, ratio, lead],
    )
    parts = gather_lines(reduced)
    (smoothed,) = call(
        functools.partial(smoothed_kernel, depth),
        "smoothed",
        [block],
        [*gathered, *parts, current, inverse, ratio, lead, half, colour],
        flags,
        system,
    )
    return (log_perm, smoothed)


def solution(mesh):
    body = fast_body if suits(mesh) else generic_body
    in_specs = (
        P(None, "gz", "gy", "gx"),
        P("gz", "gy"),
        P("gy", "gx"),
        P("gz", "gy", "gx"),
        P("gz", "gy", "gx"),
    )
    out_specs = (P("gz", "gy", "gx"), P("gz", "gy", "gx"))
    return jax.shard_map(body, mesh=mesh, in_specs=in_specs, out_specs=out_specs, check_vma=False)
```

```python
import functools
import math

import jax
import jax.numpy as jnp


from jax import lax
from jax.experimental import pallas as pl
from jax.experimental.pallas import tpu as pltpu
from jax.sharding import PartitionSpec as P

NX = 2048


STORE = 1.0


def padded_2(block, sides, width):
    for axis, dim in sides:
        count = lax.axis_size(axis)
        forward = [(i, i + 1) for i in range(count - 1)]
        backward = [(target, source) for source, target in forward]
        low = lax.ppermute(
            lax.slice_in_dim(block, block.shape[dim] - width, None, axis=dim), axis, forward
        )
        high = lax.ppermute(lax.slice_in_dim(block, 0, width, axis=dim), axis, backward)
        block = jnp.concatenate([low, block, high], axis=dim)
    return block


def twisted_coeffs(spectral, shifts, first_wave):
    count = spectral.shape[3]
    wave_index = first_wave + jnp.arange(count, dtype=jnp.int32)
    wave_turns = shifts[:, :, None] * wave_index[None, None, :] % NX
    phase_angle = wave_turns.astype(jnp.float32) * (2.0 * math.pi / NX)
    cosine = jnp.cos(phase_angle)
    sine_part = jnp.sin(phase_angle)
    real_part = spectral[0] * cosine - spectral[1] * sine_part
    imag_part = spectral[0] * sine_part + spectral[1] * cosine
    return jnp.stack([real_part, imag_part])


def basis(count, first_cell, width_cells):
    wave_index = jnp.arange(count, dtype=jnp.int32)
    cell_index = first_cell + jnp.arange(width_cells, dtype=jnp.int32)
    wave_turns = wave_index[:, None] * cell_index[None, :] % NX
    phase_angle = wave_turns.astype(jnp.float32) * (2.0 * math.pi / NX)
    offsets = jnp.concatenate(
        [jnp.zeros((count, 1), jnp.float32), jnp.full((count, 1), 0.5 * math.pi, jnp.float32)],
        axis=0,
    )
    stacked = jnp.concatenate([phase_angle, phase_angle], axis=0) + offsets
    return jnp.cos(stacked) * (1.0 / math.sqrt(NX))


def flatten_pair(piece):
    depth, items, count = (piece.shape[1], piece.shape[2], piece.shape[3])
    return jnp.concatenate(
        [piece[0].reshape(depth * items, count), piece[1].reshape(depth * items, count)], axis=1
    )


def harmonic(center, beside):
    return 2.0 * center * beside / (center + beside)


def thomas(lower_diagonal, main_diagonal, upper_diagonal, right_hand_side):

    def thomas_forward_scan(carried_state, row_entries):
        previous_ratio, previous_eliminated = carried_state
        column_lower, main_c, sup_c, column_right_hand = row_entries
        present_denominator = main_c - column_lower * previous_ratio
        present_ratio = sup_c / present_denominator
        present_eliminated = (
            column_right_hand - column_lower * previous_eliminated
        ) / present_denominator
        return ((present_ratio, present_eliminated), (present_ratio, present_eliminated))

    zeroed_layer = jnp.zeros(right_hand_side.shape[1:], right_hand_side.dtype)
    unused_output, (ratio_rows, eliminated_rows) = lax.scan(
        thomas_forward_scan,
        (zeroed_layer, zeroed_layer),
        (lower_diagonal, main_diagonal, upper_diagonal, right_hand_side),
    )

    def thomas_backward_scan(following_value, row_entries):
        column_ratio, column_eliminated = row_entries
        present_value = column_eliminated - column_ratio * following_value
        return (present_value, present_value)

    unused_output, solved_values = lax.scan(
        thomas_backward_scan, zeroed_layer, (ratio_rows, eliminated_rows), reverse=True
    )
    return solved_values


def factor(lower_diagonal, main_diagonal, upper_diagonal):

    def factor_forward_scan(previous_ratio, row_entries):
        column_lower, main_c, sup_c = row_entries
        present_denominator = main_c - column_lower * previous_ratio
        present_ratio = sup_c / present_denominator
        return (present_ratio, (present_denominator, present_ratio))

    unused_output, (denominator_rows, ratio_rows) = lax.scan(
        factor_forward_scan,
        jnp.zeros_like(main_diagonal[0]),
        (lower_diagonal, main_diagonal, upper_diagonal),
    )
    return (denominator_rows, ratio_rows)


def solve_factored(lower_diagonal, denominator_rows, ratio_rows, right_hand_side):

    def solve_forward_scan(previous_eliminated, row_entries):
        column_lower, column_denominator, column_right_hand = row_entries
        present_eliminated = (
            column_right_hand - column_lower[None] * previous_eliminated
        ) / column_denominator[None]
        return (present_eliminated, present_eliminated)

    unused_output, eliminated_rows = lax.scan(
        solve_forward_scan,
        jnp.zeros_like(right_hand_side[0]),
        (lower_diagonal, denominator_rows, right_hand_side),
    )

    def solve_backward_scan(following_value, row_entries):
        column_ratio, column_eliminated = row_entries
        present_value = column_eliminated - column_ratio[None] * following_value
        return (present_value, present_value)

    unused_output, solved_values = lax.scan(
        solve_backward_scan,
        jnp.zeros_like(right_hand_side[0]),
        (ratio_rows, eliminated_rows),
        reverse=True,
    )
    return solved_values


def generic_body(spectral, shifts, colour, pressure, source):
    total_depth = pressure.shape[0] * lax.axis_size("gz")
    vert_factor = float(total_depth * total_depth // 4)
    width_cells = spectral.shape[3]
    first_cell = lax.axis_index("gx") * width_cells
    twisted = twisted_coeffs(spectral, shifts, first_cell)
    piece = lax.all_to_all(twisted, "gx", split_axis=1, concat_axis=3, tiled=True)
    depth = piece.shape[1]
    items = piece.shape[2]
    length = piece.shape[3]
    flat = flatten_pair(piece)
    block_width = min(512, length)
    blocks = [
        jnp.dot(
            flat,
            basis(length, block * block_width, block_width),
            precision=lax.Precision.HIGHEST,
            preferred_element_type=jnp.float32,
        )
        for block in range(length // block_width)
    ]
    field_rows = jnp.concatenate(blocks, axis=1).reshape(depth, items, length)
    log_perm = lax.all_to_all(field_rows, "gx", split_axis=2, concat_axis=0, tiled=True)
    perm = jnp.exp(log_perm)
    padded = padded_2(perm, (("gx", 2), ("gz", 0), ("gy", 1)), 1)
    w_zm = vert_factor * harmonic(perm, padded[:-2, 1:-1, 1:-1])
    w_zp = vert_factor * harmonic(perm, padded[2:, 1:-1, 1:-1])
    w_ym = harmonic(perm, padded[1:-1, :-2, 1:-1])
    w_yp = harmonic(perm, padded[1:-1, 2:, 1:-1])
    w_xm = harmonic(perm, padded[1:-1, 1:-1, :-2])
    w_xp = harmonic(perm, padded[1:-1, 1:-1, 2:])
    main_diagonal = STORE + w_xm + w_xp + w_ym + w_yp + w_zm + w_zp
    lower_diagonal = -w_zm
    upper_diagonal = -w_zp
    zeroed_layer = jnp.zeros_like(main_diagonal[0])
    inner_sub = jnp.concatenate([zeroed_layer[None], lower_diagonal[2:-1]], axis=0)
    inner_sup = jnp.concatenate([upper_diagonal[1:-2], zeroed_layer[None]], axis=0)
    inner_main = main_diagonal[1:-1]
    denominator_rows, ratio_rows = factor(inner_sub, inner_main, inner_sup)
    unit_rhs = jnp.zeros((inner_main.shape[0], 2) + zeroed_layer.shape, jnp.float32)
    unit_rhs = unit_rhs.at[0, 0].set(-lower_diagonal[1])
    unit_rhs = unit_rhs.at[-1, 1].set(-upper_diagonal[-2])
    coupled = solve_factored(inner_sub, denominator_rows, ratio_rows, unit_rhs)
    left_part = coupled[:, 0]
    right_part = coupled[:, 1]
    sub_first = lower_diagonal[0]
    main_first = main_diagonal[0] + upper_diagonal[0] * left_part[0]
    sup_first = upper_diagonal[0] * right_part[0]
    sub_last = lower_diagonal[-1] * left_part[-1]
    main_last = main_diagonal[-1] + lower_diagonal[-1] * right_part[-1]
    sup_last = upper_diagonal[-1]

    def line_solve(current):
        cycle = padded_2(current, (("gx", 2), ("gy", 1)), 1)
        right_hand_side = source + w_xm * cycle[:, 1:-1, :-2] + w_xp * cycle[:, 1:-1, 2:]
        right_hand_side = right_hand_side + w_ym * cycle[:, :-2, 1:-1] + w_yp * cycle[:, 2:, 1:-1]
        particular = solve_factored(
            inner_sub, denominator_rows, ratio_rows, right_hand_side[1:-1][:, None]
        )[:, 0]
        rhs_first = right_hand_side[0] - upper_diagonal[0] * particular[0]
        rhs_last = right_hand_side[-1] - lower_diagonal[-1] * particular[-1]
        reduced_rows = jnp.stack(
            [sub_first, main_first, sup_first, rhs_first, sub_last, main_last, sup_last, rhs_last]
        )
        gathered = lax.all_gather(reduced_rows, "gz", axis=0, tiled=True)
        segments = gathered.shape[0] // 8
        system = gathered.reshape((2 * segments, 4) + zeroed_layer.shape)
        reduced_sol = thomas(system[:, 0], system[:, 1], system[:, 2], system[:, 3])
        own_pair = lax.dynamic_slice_in_dim(reduced_sol, 2 * lax.axis_index("gz"), 2, 0)
        face_first = own_pair[0]
        face_last = own_pair[1]
        inner = particular + face_first[None] * left_part + face_last[None] * right_part
        return jnp.concatenate([face_first[None], inner, face_last[None]], axis=0)

    half = jnp.where((colour == 0)[None], line_solve(pressure), pressure)
    smoothed = jnp.where((colour == 1)[None], line_solve(half), half)
    return (log_perm, smoothed)


LANES = 128
ROWS = 8
F32 = jnp.float32
MIB = 1 << 20
SUMS_GRANT = 60


def suits(mesh):
    sizes = dict(mesh.shape)
    return sizes["gx"] == 2 and sizes["gz"] == 4 and sizes["gy"] == 4


def params(mib):
    return pltpu.CompilerParams(vmem_limit_bytes=mib * MIB)


def cos_sin(turns):
    quarter = (turns + NX // 8) >> 9
    angle = (turns - (quarter << 9)).astype(F32) * (2.0 * math.pi / NX)
    square = angle * angle
    sine = angle * (
        1.0
        + square * (-1.0 / 6 + square * (1.0 / 120 + square * (-1.0 / 5040 + square / 362880)))
    )
    cosine = 1.0 + square * (
        -0.5 + square * (1.0 / 24 + square * (-1.0 / 720 + square * (1.0 / 40320)))
    )
    odd = (quarter & 1) == 1
    first = jnp.where(odd, sine, cosine)
    second = jnp.where(odd, cosine, sine)
    cos_sign = jnp.where(((quarter + 1) & 2) == 2, -1.0, 1.0)
    sin_sign = jnp.where((quarter & 2) == 2, -1.0, 1.0)
    return first * cos_sign, second * sin_sign


def split(values):
    high = values.astype(jnp.bfloat16)
    return high, (values - high.astype(F32)).astype(jnp.bfloat16)


def times(first, second):
    return (
        first[0] * second[0] - first[1] * second[1],
        first[0] * second[1] + first[1] * second[0],
    )


def plus(first, second):
    return (first[0] + second[0], first[1] + second[1])


def minus(first, second):
    return (first[0] - second[0], first[1] - second[1])


def quarter_turn(value):
    return (-value[1], value[0])


def four_point(first, second, third, fourth):
    even, gap = plus(first, third), minus(first, third)
    odd, turned = plus(second, fourth), quarter_turn(minus(second, fourth))
    return [plus(even, odd), plus(gap, turned), minus(even, odd), minus(gap, turned)]


def eight_point(values):
    even = four_point(*values[0::2])
    odd = four_point(*values[1::2])
    root = math.sqrt(0.5)
    real, imag = odd[1]
    odd[1] = (root * (real - imag), root * (real + imag))
    odd[2] = quarter_turn(odd[2])
    real, imag = odd[3]
    odd[3] = (-root * (real + imag), root * (real - imag))
    return [plus(*pair) for pair in zip(even, odd)] + [minus(*pair) for pair in zip(even, odd)]


def fill_tables(basis, turns):
    groups = NX // LANES
    shape = (LANES, LANES)
    lane = lane_of(shape)
    cells = (lane % groups) * (LANES // groups) + lane // groups
    cosine, sine = cos_sin((row_of(shape) * cells) % LANES * groups)
    for at, value in enumerate((cosine, -sine)):
        rows = slice(at * LANES, (at + 1) * LANES)
        high, low = split(value * (1.0 / math.sqrt(NX)))
        basis[0, rows], basis[1, rows], basis[2, rows] = high, high, low
    shape = (groups, LANES)
    turns[0], turns[1] = cos_sin(row_of(shape) * lane_of(shape))


def diagonal_of(depth):
    square = (depth, depth)
    return row_of(square) == lane_of(square)


def shift_columns(shifts, rows_of, columns):
    depth = shifts.shape[1]
    diagonal = diagonal_of(depth)
    for at, y in enumerate(rows_of):
        spread = jnp.where(diagonal, shifts[y : y + 1, :].astype(F32), 0.0)
        shift = jnp.broadcast_to(jnp.sum(spread, axis=1, keepdims=True), (depth, LANES))
        columns[at * depth : (at + 1) * depth, :] = shift.astype(jnp.int32)


def edge_columns(ys, depth, edges, kept):
    kept[...] = jnp.zeros_like(kept)
    diagonal = diagonal_of(depth)
    for at in range(len(ys)):
        rows = slice(at * depth, (at + 1) * depth)
        for side, lane in enumerate((LANES - 1, 0)):
            column = jnp.broadcast_to(edges[side, rows, lane : lane + 1], (depth, depth))
            row = jnp.sum(jnp.where(diagonal, column, 0.0), axis=0, keepdims=True)
            kept[side, at : at + 1, :depth] = row


def twisted(first_wave, shift, coefficients, rows):
    lane = lane_of(shift.shape)
    phase = cos_sin((shift * (lane + first_wave)) & (NX - 1))
    turn = cos_sin((shift * LANES) & (NX - 1))
    values = []
    for part in range(coefficients.shape[0]):
        values.append(times((coefficients[part, 0, rows], coefficients[part, 1, rows]), phase))
        phase = times(phase, turn)
    return values


def interleave(tiles):
    count = len(tiles)
    lane = lane_of(tiles[0].shape)
    bit = count // 2
    while bit:
        low = (lane & bit) == 0
        moved = list(tiles)
        for at in range(count):
            if not at & bit:
                first, second = tiles[at], tiles[at | bit]
                crossed = jnp.take_along_axis(
                    jnp.where(low, second, first), lane ^ bit, axis=1
                )
                moved[at] = jnp.where(low, first, crossed)
                moved[at | bit] = jnp.where(low, crossed, second)
        tiles = moved
        bit //= 2
    return tiles


def row_sums(g, at, y, depth, items, columns, coefficients, basis, turns, left, right, emit):
    groups = NX // LANES
    sign = 1.0 - 2.0 * g.astype(F32)
    first_wave = g * (coefficients.shape[0] * LANES)
    step = 16
    for part in range(depth // step):
        rows = pl.ds(part * step * items + y, step, stride=items)
        shift = columns[pl.ds(at * depth + part * step, step), :]
        values = twisted(first_wave, shift, coefficients, rows)
        turned = [
            times(value, (sign * math.cos(2 * math.pi * p / groups), sign * math.sin(2 * math.pi * p / groups)))
            if p
            else (sign * value[0], sign * value[1])
            for p, value in enumerate(values)
        ]
        even, odd = eight_point(values), eight_point(turned)
        for group in range(groups):
            value = odd[group // 2] if group % 2 else even[group // 2]
            if group:
                value = times(value, (turns[0, group : group + 1], turns[1, group : group + 1]))
            first = group * depth + part * step
            for place_of, piece in enumerate(value):
                for half, bits in enumerate(split(piece)):
                    target = (2 * half + place_of) * LANES
                    left[first : first + step, target : target + LANES] = bits
    spread = jnp.concatenate([left[...], left[:, : 2 * LANES]], axis=1)
    bases = basis[...].reshape(-1, LANES)
    right[...] = jnp.dot(spread, bases, preferred_element_type=F32)
    for part in range(depth // ROWS):
        tiles = [
            right[group * depth + part * ROWS : group * depth + (part + 1) * ROWS]
            for group in range(groups)
        ]
        emit(pl.ds(at * depth + part * ROWS, ROWS), interleave(tiles))


def load_coefficients(spectral, coefficients, arrivals):
    parts = coefficients.shape[0]
    copies = [
        pltpu.make_async_copy(
            spectral.at[:, :, part * LANES : (part + 1) * LANES],
            coefficients.at[part],
            arrivals.at[part],
        )
        for part in range(parts)
    ]
    for copy in copies:
        copy.start()
    return copies


def keep_edges(rows, tiles, edges):
    half = len(tiles) // 2
    edges[0, rows], edges[1, rows] = tiles[half - 1], tiles[half]


def wide_sums_kernel(ys, shifts, spectral, other, own, kept, *refs):
    columns, edges, coefficients, arrivals, *tables, left, right = refs
    items, depth = shifts.shape
    copies = load_coefficients(spectral, coefficients, arrivals)
    fill_tables(*tables)
    shift_columns(shifts, ys, columns)
    for copy in copies:
        copy.wait()
    g = lax.axis_index("gx")

    def emit(rows, tiles):
        half = len(tiles) // 2
        keep_edges(rows, tiles, edges)
        for tile, (low, high) in enumerate(zip(tiles[:half], tiles[half:])):
            there = slice(tile * LANES, (tile + 1) * LANES)
            other[rows, there] = jnp.where(g == 0, high, low)
            own[rows, there] = jnp.where(g == 0, low, high)

    for at, y in enumerate(ys):
        row_sums(
            *(g, at, y, depth, items, columns, coefficients, *tables),
            *(left.at[at % 2], right.at[at % 2], emit),
        )
    edge_columns(ys, depth, edges, kept)


def last_sums_kernel(ys, shifts, outer_kept, inner_kept, spectral, one, two, own, *refs):
    mine, theirs, kept, columns, edges, coefficients, arrivals, *tables, left, right = refs
    items, depth = shifts.shape
    copies = load_coefficients(spectral, coefficients, arrivals)
    fill_tables(*tables)
    shift_columns(shifts, ys, columns)
    for copy in copies:
        copy.wait()
    g = lax.axis_index("gx")

    def emit(rows, tiles):
        half = len(tiles) // 2
        keep_edges(rows, tiles, edges)
        others = []
        for tile, (low, high) in enumerate(zip(tiles[:half], tiles[half:])):
            own[rows, tile * LANES : (tile + 1) * LANES] = jnp.where(g == 0, low, high)
            others.append(jnp.where(g == 0, high, low))
        start = 0
        for ref in (one, two):
            count = ref.shape[1] // LANES
            for tile in range(count):
                ref[rows, tile * LANES : (tile + 1) * LANES] = jnp.where(
                    g == 0, others[start + tile], others[half - start - count + tile]
                )
            start += count

    for at, y in enumerate(ys):
        row_sums(
            *(g, at, y, depth, items, columns, coefficients, *tables),
            *(left.at[at % 2], right.at[at % 2], emit),
        )
    edge_columns(ys, depth, edges, kept)
    sides_of = [
        jnp.concatenate(
            [outer_kept[side, :1], inner_kept[side], kept[side], outer_kept[side, 1:]], axis=0
        )
        for side in range(2)
    ]
    mine[...] = jnp.where(g == 0, sides_of[0], sides_of[1])
    theirs[...] = jnp.where(g == 0, sides_of[1], sides_of[0])


SCALARS = pl.BlockSpec(memory_space=pltpu.SMEM)
ON_CHIP = pl.BlockSpec(memory_space=pltpu.VMEM)
IN_HBM = pl.BlockSpec(memory_space=pltpu.HBM)


def call(kernel, name, out_shape, args, flags=None, scratch=(), far=(), mib=20, flops=1):
    specs = [ON_CHIP] * len(args) + [IN_HBM] * len(far)
    args = list(args) + list(far)
    if flags is not None:
        specs = [SCALARS] + specs
        args = [flags] + args
    return pl.pallas_call(
        kernel,
        out_shape=out_shape,
        in_specs=specs,
        out_specs=jax.tree.map(lambda _: ON_CHIP, out_shape),
        scratch_shapes=list(scratch),
        compiler_params=params(mib),
        cost_estimate=pl.CostEstimate(flops=flops, bytes_accessed=1, transcendentals=0),
        name=name,
    )(*args)


def roll(values, shift, axis):
    return pltpu.roll(values, shift % values.shape[axis], axis)


def lane_of(shape):
    return lax.broadcasted_iota(jnp.int32, shape, 1)


def row_of(shape):
    return lax.broadcasted_iota(jnp.int32, shape, 0)


def column_to(z, packed, target):
    return pltpu.roll(packed, (target - z) % LANES, 1)


def packed_with(z, packed, plane, lane):
    column = jnp.broadcast_to(plane[:, lane : lane + 1], (ROWS, LANES))
    return jnp.where(lane_of((ROWS, LANES)) == z, column, packed)


def inverse_of(values):
    guess = pl.reciprocal(values, approx=True)
    return guess * (2.0 - values * guess)


def ordered(z, sums, depth):
    spread = pl.ds(z, ROWS, stride=depth)
    return jnp.concatenate([sums[at, spread] for at in range(sums.shape[0])], axis=1)


def place_tiles(sums, rows, first, values):
    for at in range(values.shape[1] // LANES):
        sums[(first >> 7) + at, rows] = values[:, at * LANES : (at + 1) * LANES]


def boundary_plane(g, plane):
    return jnp.where(g == 0, roll(plane[:, -LANES:], 1, 1), plane[:, :LANES])


def outer_field_kernel(depth, flags, own, other, pressure, to_near, to_middle, boundary):
    g, even = flags[0], flags[16] == 0
    low, high = slice(0, depth), slice(depth, 2 * depth)
    south, north = own[low] + other[low], own[high] + other[high]
    to_near[low] = jnp.exp(-jnp.where(even, north, south))
    to_middle[low] = jnp.exp(-jnp.where(even, south, north))

    def layer(z, packed):
        plane = pressure[z]
        keep_rows(depth + z, plane, even, to_near, to_middle, slice(None))
        return packed_with(z, packed, boundary_plane(g, plane), 0)

    boundary[...] = lax.fori_loop(0, depth, layer, jnp.zeros((ROWS, LANES), F32), unroll=8)


def wide_field_kernel(depth, flags, *refs):
    own_outer, outer, own_inner, inner, to_near, to_middle = refs[:6]
    from_near, from_middle, sums_here, sums_there = refs[6:10]
    wide, south_weight, north_weight, south_terms, north_rows, column = refs[10:]
    even = flags[16] == 0
    low, high = slice(0, depth), slice(depth, 2 * depth)
    wide[low] = own_outer[low] + outer[low]
    wide[depth:-depth] = own_inner[...] + inner[...]
    wide[-depth:] = own_outer[high] + outer[high]
    near_weight = 2.0 * inverse_of(to_near[low] + from_near[low])
    middle_weight = (2.0 * flags[15].astype(F32)) * inverse_of(to_middle[low] + from_middle[low])
    south = jnp.where(even, middle_weight, near_weight)
    south_weight[...] = south
    north_weight[...] = jnp.where(even, near_weight, middle_weight)
    south_terms[...] = south * jnp.where(even, from_middle[high], from_near[high])
    north_rows[...] = jnp.where(even, from_near[high], from_middle[high])
    column[...] = jnp.exp(-(sums_here[...] + sums_there[...]))


def lane_slice(start, size):
    return pl.ds(pl.multiple_of(start, LANES), size)


def assemble(sums, depth, wide, own, piece, there):
    inside = wide.shape[0] - depth
    place_tiles(sums, slice(0, inside), 0, wide[:inside, there])
    place_tiles(sums, slice(inside, -depth), 0, own[:, there] + piece[...])
    place_tiles(sums, slice(-depth, None), 0, wide[inside:, there])


def first_field_kernel(depth, flags, *refs):
    wide, own, middle = refs[:3]
    log_perm, resist, low_side, high_side, boundary, sums = refs[3:]
    g, start = flags[0], flags[3]
    assemble(sums, depth, wide, own, middle, lane_slice(start, log_perm.shape[2]))
    edge = lane_slice(own.shape[1] // 2 - LANES - start, 2 * LANES)

    def layer(z, carry):
        low, high, bound = carry
        plane = ordered(z, sums, depth)
        inverse = jnp.exp(-plane)
        log_perm[z] = plane
        resist[z] = inverse
        both = resist[z, :, edge]
        return (
            packed_with(z, low, both, LANES - 1),
            packed_with(z, high, both, LANES),
            packed_with(z, bound, boundary_plane(g, inverse), 0),
        )

    zero = jnp.zeros((ROWS, LANES), F32)
    low_side[...], high_side[...], boundary[...] = lax.fori_loop(
        0, depth, layer, (zero, zero, zero), unroll=8
    )


def second_field_kernel(depth, flags, *refs):
    wide, own, middle, log_near, resist_near = refs[:5]
    log_perm, resist, sums = refs[5:]
    third, known = middle.shape[1], log_near.shape[2]
    there = lane_slice(flags[5], third)
    assemble(sums, depth, wide, own, middle, there)
    extra = resist.shape[2] - third
    target = lane_slice(flags[5] - flags[7], third)
    extra_target = lane_slice(flags[8], extra)
    extra_source = lane_slice(flags[9], extra)

    def layer(z, carry):
        plane = ordered(z, sums, depth)
        log_perm[z, :, lane_slice(flags[3], known)] = log_near[z]
        log_perm[z, :, there] = plane
        resist[z, :, target] = jnp.exp(-plane)
        resist[z, :, extra_target] = resist_near[z, :, extra_source]
        return carry

    lax.fori_loop(0, depth, layer, 0, unroll=8)


def keep_rows(z, value, even, to_near, to_middle, here):
    south, north = value[0:1, :], value[ROWS - 1 : ROWS, :]
    to_near[pl.ds(z, 1), here] = jnp.where(even, north, south)
    to_middle[pl.ds(z, 1), here] = jnp.where(even, south, north)


def with_first(plane, edge):
    first = jnp.where(lane_of((ROWS, LANES)) == 0, edge, plane[:, :LANES])
    return jnp.concatenate([first, plane[:, LANES:]], axis=1)


def with_last(plane, edge):
    last = jnp.where(lane_of((ROWS, LANES)) == LANES - 1, edge, plane[:, -LANES:])
    return jnp.concatenate([plane[:, :-LANES], last], axis=1)


def coupling(z, field, start, size, east_weight, north_weight, south_terms, north_rows, west, column):
    here = lane_slice(start, size)
    plane = field[z, :, here]
    row = row_of(plane.shape)
    at_start = start == 0
    inner = field[z, :, lane_slice(jnp.where(at_start, size, size - LANES), LANES)]
    west_value = jnp.where(at_start, column_to(z, column, 0), roll(inner, 1, 1))
    east_value = jnp.where(at_start, roll(inner, -1, 1), column_to(z, column, LANES - 1))
    to_east, to_north = east_weight * plane, north_weight * plane
    from_west = with_first(roll(to_east, 1, 1), column_to(z, west, 0) * west_value)
    from_east = east_weight * with_last(roll(plane, -1, 1), east_value)
    from_south = jnp.where(row == 0, south_terms[pl.ds(z, 1), here], roll(to_north, 1, 0))
    from_north = north_weight * jnp.where(
        row == ROWS - 1, north_rows[pl.ds(z, 1), here], roll(plane, -1, 0)
    )
    return (from_west + from_east) + (from_south + from_north)


def edge_weights(flags, start, bound, column, low_side, high_side):
    g = flags[0]
    middle = 2.0 * inverse_of(low_side + high_side)
    across = 2.0 * inverse_of(bound + column)
    none = jnp.zeros_like(across)
    west = jnp.where(start == 0, jnp.where(g == 0, none, across), middle)
    east = jnp.where(start == 0, middle, jnp.where(g == 0, across, none))
    return west, east


def first_sweep_kernel(depth, vert, block, flags, *refs):
    resist, low_side, high_side, r_bound, r_column = refs[:5]
    south_weight, north_weight, south_terms, north_rows = refs[5:9]
    pressure, p_column, source = refs[9:12]
    w_east, w_north, west_out, particular, inverse, ratio, lead, reduced = refs[12:20]
    grounds, rights, verticals = refs[20:]
    start, offset = flags[6 + block], flags[10 + block]
    size = inverse.shape[2]
    shape = (ROWS, size)
    here = lane_slice(start, size)
    inside = lane_slice(offset, size)
    west_weight, east_weight = edge_weights(
        flags, start, r_bound[...], r_column[...], low_side[...], high_side[...]
    )
    west_out[...] = west_weight
    column = p_column[...]
    row = row_of(shape)

    def weigh(z, carry):
        plane = resist[z, :, inside]
        east = 2.0 * inverse_of(plane + roll(plane, -1, 1))
        east = with_last(east, column_to(z, east_weight, LANES - 1))
        west = with_first(roll(east, 1, 1), column_to(z, west_weight, 0))
        north = 2.0 * inverse_of(plane + roll(plane, -1, 0))
        north = jnp.where(row == ROWS - 1, north_weight[pl.ds(z, 1), here], north)
        south = jnp.where(row == 0, south_weight[pl.ds(z, 1), here], roll(north, 1, 0))
        w_east[z], w_north[z] = east, north
        grounds[z] = STORE + ((east + west) + (north + south))
        verticals[z] = (2.0 * vert) * inverse_of(
            plane + resist[jnp.minimum(z + 1, depth - 1), :, inside]
        )
        rights[z] = source[z, :, here] + coupling(
            z, pressure, start, size, east, north, south_terms, north_rows, west_weight, column
        )
        return carry

    lax.fori_loop(0, depth, weigh, 0, unroll=4)

    def layer(z, carry):
        conduct, flow, product, first_first, first_part = carry
        weight = verticals[z]
        reciprocal = inverse_of(conduct + weight)
        quotient = weight * reciprocal
        led = product * reciprocal
        inverse[z] = reciprocal
        ratio[z] = quotient
        lead[z] = led
        particular[z] = reciprocal * flow
        return (
            grounds[z + 1] + conduct * quotient,
            rights[z + 1] + flow * quotient,
            product * quotient,
            first_first + led * product,
            first_part + led * flow,
        )

    zero = jnp.zeros(shape, F32)
    conduct, flow, product, first_first, first_part = lax.fori_loop(
        0,
        depth - 1,
        layer,
        (grounds[0], rights[0], jnp.ones(shape, F32), zero, zero),
        unroll=8,
    )
    reciprocal = inverse_of(conduct)
    led = product * reciprocal
    inverse[depth - 1] = reciprocal
    ratio[depth - 1] = zero
    lead[depth - 1] = led
    particular[depth - 1] = flow * reciprocal
    reduced[0] = first_first + led * product + resist[0, :, inside] * (0.5 / vert)
    reduced[1] = led
    reduced[2] = reciprocal + resist[depth - 1, :, inside] * (0.5 / vert)
    reduced[3] = first_part + led * flow
    reduced[4] = flow * reciprocal


def pair_kernel(flags, own_one, own_two, near_one, near_two, across, kept):
    me = flags[14]
    even, lower = me % 2 == 0, me < 2
    for block, (own, near) in enumerate(((own_one, near_one), (own_two, near_two))):
        size = own.shape[2]
        there = slice(block * size, (block + 1) * size)
        first, second = [
            [jnp.where(flip, own[at], near[at]) for at in range(5)]
            for flip in (even, jnp.logical_not(even))
        ]
        reciprocal = inverse_of(first[2] + second[0])
        step = (first[4] - second[3]) * reciprocal
        through = jnp.where(lower, second[1], first[1])
        share = through * reciprocal
        across[0, :, there] = jnp.where(lower, second[2], first[0]) - through * share
        across[1, :, there] = jnp.where(lower, second[4], first[3]) + jnp.where(
            lower, through * step, -through * step
        )
        kept[0, :, there] = share
        kept[1, :, there] = reciprocal
        kept[2, :, there] = step


def ends(me, inner, middle):
    zero = jnp.zeros_like(inner)
    odd = me % 2 == 1
    enters = jnp.where(odd, inner, jnp.where(me == 2, middle, zero))
    leaves = jnp.where(odd, jnp.where(me == 1, middle, zero), inner)
    return enters, leaves


def back_substitute(depth, lines, emit):
    last = depth - 1
    values = tuple(
        (particular[last] + lead[last] * enters) - inverse[last] * leaves
        for enters, leaves, particular, inverse, ratio, lead in lines
    )
    state = emit(last, values, jnp.zeros((ROWS, LANES), F32))

    def layer(step, carry):
        following, state = carry
        z = last - step
        values = tuple(
            (particular[z] + lead[z] * enters) + ratio[z] * beyond
            for (enters, _, particular, _, ratio, lead), beyond in zip(lines, following)
        )
        return values, emit(z, values, state)

    return lax.fori_loop(1, depth, layer, (values, state), unroll=4)[1]


def half_kernel(depth, flags, *refs):
    across, other, kept = refs[:3]
    blocks = (refs[3:7], refs[7:11])
    pressure, colour = refs[11:13]
    half, to_near, to_middle, boundary, joined = refs[13:]
    me, g, even = flags[14], flags[0], flags[16] == 0
    size = blocks[0][0].shape[2]
    spans = [lane_slice(flags[6 + block], size) for block in range(2)]
    lines = []
    for block, state in enumerate(blocks):
        there = slice(block * size, (block + 1) * size)
        sum_of = inverse_of(across[0, :, there] + other[0, :, there])
        joined[:, there] = sum_of
        lead_of = across[1, :, there] - other[1, :, there]
        middle = jnp.where(me < 2, lead_of, -lead_of) * sum_of
        inner = kept[2, :, there] + kept[0, :, there] * middle
        lines.append((*ends(me, inner, middle), *state))
    chosen = [colour[:, here] == 0 for here in spans]

    def emit(z, values, packed):
        for block, (value, here) in enumerate(zip(values, spans)):
            value = jnp.where(chosen[block], value, pressure[z, :, here])
            half[z, :, here] = value
            keep_rows(z, value, even, to_near, to_middle, here)
            if not block:
                packed = packed_with(z, packed, boundary_plane(g, value), 0)
        return packed

    boundary[...] = back_substitute(depth, lines, emit)


def second_sweep_kernel(depth, flags, *refs):
    half, h_near, h_middle, h_column, source, kept, south_weight = refs[:7]
    blocks = (refs[7:13], refs[13:19])
    particulars, near, far = refs[19:21], refs[21], refs[22]
    south_terms, north_rows = refs[23:]
    me, even = flags[14], flags[16] == 0
    size = particulars[0].shape[2]
    starts = [flags[6 + block] for block in range(2)]
    spans = [lane_slice(start, size) for start in starts]
    column = h_column[...]
    south_terms[...] = south_weight[...] * jnp.where(even, h_middle[...], h_near[...])
    north_rows[...] = jnp.where(even, h_near[...], h_middle[...])

    def local(z, block):
        east, north, west = blocks[block][:3]
        return source[z, :, spans[block]] + coupling(
            z,
            half,
            starts[block],
            size,
            east[z],
            north[z],
            south_terms,
            north_rows,
            west[...],
            column,
        )

    def layer(z, carry):
        result = []
        for block, (flow, first_part) in enumerate(carry):
            inverse, ratio, lead = blocks[block][3:6]
            particulars[block][z] = flow * inverse[z]
            first_part = first_part + lead[z] * flow
            result.append((local(z + 1, block) + flow * ratio[z], first_part))
        return tuple(result)

    carry = tuple((local(0, block), jnp.zeros((ROWS, size), F32)) for block in range(2))
    carry = lax.fori_loop(0, depth - 1, layer, carry, unroll=2)
    last = depth - 1
    for block, (flow, first_part) in enumerate(carry):
        inverse, ratio, lead = blocks[block][3:6]
        there = slice(block * size, (block + 1) * size)
        first_part = first_part + lead[last] * flow
        last_part = flow * inverse[last]
        particulars[block][last] = last_part
        asked = jnp.where(me % 2 == 0, last_part, first_part)
        shared = kept[0, :, there] * asked
        outer = jnp.where(me == 1, last_part, jnp.where(me == 2, first_part, 0.0))
        given = outer + jnp.where((me == 0) | (me == 3), shared, -shared)
        near[0, :, there] = asked
        near[1, :, there] = given
        far[:, there] = given


def smoothed_kernel(depth, flags, *refs):
    own, near, skip, cross, kept, joined = refs[:6]
    blocks = (refs[6:10], refs[10:14])
    half, colour, smoothed = refs[14:]
    me = flags[14]
    size = blocks[0][0].shape[2]
    spans = [lane_slice(flags[6 + block], size) for block in range(2)]
    lines = []
    for block, state in enumerate(blocks):
        there = slice(block * size, (block + 1) * size)
        lead_of = (own[1, :, there] + near[1, :, there]) - (skip[:, there] + cross[:, there])
        middle = jnp.where(me < 2, lead_of, -lead_of) * joined[:, there]
        step = own[0, :, there] - near[0, :, there]
        step = jnp.where(me % 2 == 0, step, -step) * kept[1, :, there]
        lines.append((*ends(me, step + kept[0, :, there] * middle, middle), *state))
    chosen = [colour[:, here] == 1 for here in spans]

    def emit(z, values, state):
        for value, here, mine in zip(values, spans, chosen):
            smoothed[z, :, here] = jnp.where(mine, value, half[z, :, here])
        return state

    back_substitute(depth, lines, emit)


PAIR = [(0, 1), (1, 0)]
NEAR = [(0, 1), (1, 0), (2, 3), (3, 2)]
MIDDLE = [(1, 2), (2, 1)]
SKIP = [(0, 2), (2, 0), (1, 3), (3, 1)]
CROSS = [(0, 3), (3, 0), (1, 2), (2, 1)]


def exchange_edges(edges):
    to_near, to_middle, *column = edges
    return [
        lax.ppermute(to_near, "gy", NEAR),
        lax.ppermute(to_middle, "gy", MIDDLE),
        *[lax.ppermute(piece, "gx", PAIR) for piece in column],
    ]


def fast_body(spectral, shifts, colour, pressure, source):
    depth, items, width = pressure.shape
    vert = float((depth * 4) ** 2 // 4)
    waves = spectral.shape[3]
    rows = depth * items
    gx, gz, gy = (lax.axis_index(axis) for axis in ("gx", "gz", "gy"))
    block_size, third = width // 2, 3 * width // 8
    known = width - third

    def placed(start, size):
        return jnp.where(gx == 1, start, width - start - size)

    block_one, block_two = placed(0, block_size), placed(block_size, block_size)
    start_one = placed(0, known)
    extra = known - block_size
    flags = jnp.stack(
        [
            gx,
            placed(0, LANES),
            placed(LANES, known - LANES),
            start_one,
            jnp.zeros_like(gx),
            placed(known, third),
            block_one,
            block_two,
            placed(block_size, extra) - block_two,
            placed(block_size, extra) - start_one,
            block_one - start_one,
            jnp.zeros_like(gx),
            gy > 0,
            gy < 3,
            gz,
            (gy == 1) | (gy == 2),
            gy % 2,
        ]
    ).astype(jnp.int32)

    def shaped(*shape, dtype=F32):
        return jax.ShapeDtypeStruct(shape, dtype)

    groups = NX // LANES
    parts = waves // LANES
    inner_ys, last_ys = (1, 2, 3), tuple(range(4, items - 1))
    last_rows = len(last_ys) * depth
    column_type = shaped(ROWS, LANES)
    coefficients = spectral.reshape(2, rows, waves)

    def scratch(count):
        return [
            pltpu.VMEM((count, LANES), jnp.int32),
            pltpu.VMEM((2, count, LANES), F32),
            pltpu.VMEM((parts, 2, rows, LANES), F32),
            pltpu.SemaphoreType.DMA((parts,)),
            pltpu.VMEM((3, 2 * LANES, LANES), jnp.bfloat16),
            pltpu.VMEM((2, groups, LANES), F32),
            pltpu.VMEM((2, groups * depth, 4 * LANES), jnp.bfloat16),
            pltpu.VMEM((2, groups * depth, LANES), F32),
        ]

    def wide_sums(ys, name, shift_rows, cost):
        return call(
            functools.partial(wide_sums_kernel, ys),
            name,
            [shaped(len(ys) * depth, width)] * 2 + [shaped(2, len(ys), LANES)],
            [shift_rows],
            scratch=scratch(len(ys) * depth),
            far=[coefficients],
            mib=SUMS_GRANT,
            flops=cost,
        )

    shift_rows = shifts.T
    sums, own_outer, outer_kept = wide_sums((0, items - 1), "outer_row_sums", shift_rows, 1)
    outer = lax.ppermute(sums, "gx", PAIR)
    shift_rows, _ = lax.optimization_barrier((shift_rows, own_outer))
    sums, own_inner, inner_kept = wide_sums(inner_ys, "inner_row_sums", shift_rows, 1 << 30)
    inner = lax.ppermute(sums, "gx", PAIR)
    last_one, last_two, own_last, mine, theirs = call(
        functools.partial(last_sums_kernel, last_ys),
        "last_row_sums",
        [shaped(last_rows, size) for size in (known, third, width)] + [column_type] * 2,
        [shift_rows, outer_kept, inner_kept],
        scratch=[pltpu.VMEM((2, len(last_ys), LANES), F32)] + scratch(last_rows),
        far=[coefficients],
        mib=SUMS_GRANT,
        flops=1 << 30,
    )
    column_sums = [theirs, lax.ppermute(mine, "gx", PAIR)]
    last_one, last_two = (lax.ppermute(piece, "gx", PAIR) for piece in (last_one, last_two))
    edge_row, edge_column = shaped(depth, width), shaped(ROWS, LANES)
    edges = [edge_row, edge_row, edge_column]
    to_near, to_middle, p_column = call(
        functools.partial(outer_field_kernel, depth),
        "outer_field",
        [shaped(2 * depth, width)] * 2 + [edge_column],
        [own_outer, outer, pressure],
        flags,
    )
    from_near, from_middle, p_column = exchange_edges([to_near, to_middle, p_column])
    wide, *row_edges, r_column = call(
        functools.partial(wide_field_kernel, depth),
        "wide_field",
        [shaped(rows - last_rows, width)] + [edge_row] * 4 + [edge_column],
        [
            *(own_outer, outer, own_inner, inner, to_near, to_middle),
            *(from_near, from_middle, *column_sums),
        ],
        flags,
    )
    log_near, resist_near, *columns = call(
        functools.partial(first_field_kernel, depth),
        "first_field",
        [shaped(depth, items, known)] * 2 + [edge_column] * 3,
        [wide, own_last, last_one],
        flags,
        [pltpu.VMEM((known // LANES, rows, LANES), F32)],
    )
    block = shaped(depth, items, block_size)

    state_types = [block] * 2 + [edge_column] + [block] * 4

    def first_sweep(at, resist):
        return call(
            functools.partial(first_sweep_kernel, depth, vert, at),
            "first_sweep",
            state_types + [shaped(5, items, block_size)],
            [resist, *columns, r_column, *row_edges, pressure, p_column, source],
            flags,
            [pltpu.VMEM((depth, items, block_size), F32)] * 3,
        )

    *state_one, reduced_one = first_sweep(0, resist_near)
    near_one = lax.ppermute(reduced_one, "gz", NEAR)
    last_two, _ = lax.optimization_barrier((last_two, reduced_one))
    log_perm, resist_far = call(
        functools.partial(second_field_kernel, depth),
        "second_field",
        [shaped(depth, items, width), block],
        [wide, own_last, last_two, log_near, resist_near],
        flags,
        [pltpu.VMEM((third // LANES, rows, LANES), F32)],
    )
    *state_two, reduced_two = first_sweep(1, resist_far)
    near_two = lax.ppermute(reduced_two, "gz", NEAR)
    across, kept = call(
        pair_kernel,
        "join_pair",
        [shaped(2, items, width), shaped(3, items, width)],
        [reduced_one, reduced_two, near_one, near_two],
        flags,
    )
    other = lax.ppermute(across, "gz", SKIP)
    half, *h_edges, joined = call(
        functools.partial(half_kernel, depth),
        "half",
        [shaped(depth, items, width), *edges, shaped(items, width)],
        [across, other, kept, *state_one[3:], *state_two[3:], pressure, colour],
        flags,
    )
    h_edges = exchange_edges(h_edges)
    weights = [[*state[:3], *state[4:]] for state in (state_one, state_two)]
    current_one, current_two, to_near, to_far = call(
        functools.partial(second_sweep_kernel, depth),
        "second_sweep",
        [block, block, shaped(2, items, width), shaped(items, width)],
        [half, *h_edges, source, kept, row_edges[0], *weights[0], *weights[1]],
        flags,
        [pltpu.VMEM((depth, width), F32)] * 2,
    )
    from_near, from_skip, from_cross = (
        lax.ppermute(planes, "gz", pairs)
        for planes, pairs in ((to_near, NEAR), (to_far, SKIP), (to_far, CROSS))
    )
    (smoothed,) = call(
        functools.partial(smoothed_kernel, depth),
        "smoothed",
        [shaped(depth, items, width)],
        [
            *(to_near, from_near, from_skip, from_cross, kept, joined),
            *(current_one, *state_one[4:]),
            *(current_two, *state_two[4:]),
            *(half, colour),
        ],
        flags,
    )
    return (log_perm, smoothed)


def solution(mesh):
    body = fast_body if suits(mesh) else generic_body
    in_specs = (
        P(None, "gz", "gy", "gx"),
        P("gz", "gy"),
        P("gy", "gx"),
        P("gz", "gy", "gx"),
        P("gz", "gy", "gx"),
    )
    out_specs = (P("gz", "gy", "gx"), P("gz", "gy", "gx"))
    return jax.shard_map(body, mesh=mesh, in_specs=in_specs, out_specs=out_specs, check_vma=False)
```

```python
import functools
import math

import jax
import jax.numpy as jnp


from jax import lax
from jax.experimental import pallas as pl
from jax.experimental.pallas import tpu as pltpu
from jax.sharding import PartitionSpec as P

NX = 2048


STORE = 1.0


def padded_2(block, sides, width):
    for axis, dim in sides:
        count = lax.axis_size(axis)
        forward = [(i, i + 1) for i in range(count - 1)]
        backward = [(target, source) for source, target in forward]
        low = lax.ppermute(
            lax.slice_in_dim(block, block.shape[dim] - width, None, axis=dim), axis, forward
        )
        high = lax.ppermute(lax.slice_in_dim(block, 0, width, axis=dim), axis, backward)
        block = jnp.concatenate([low, block, high], axis=dim)
    return block


def twisted_coeffs(spectral, shifts, first_wave):
    count = spectral.shape[3]
    wave_index = first_wave + jnp.arange(count, dtype=jnp.int32)
    wave_turns = shifts[:, :, None] * wave_index[None, None, :] % NX
    phase_angle = wave_turns.astype(jnp.float32) * (2.0 * math.pi / NX)
    cosine = jnp.cos(phase_angle)
    sine_part = jnp.sin(phase_angle)
    real_part = spectral[0] * cosine - spectral[1] * sine_part
    imag_part = spectral[0] * sine_part + spectral[1] * cosine
    return jnp.stack([real_part, imag_part])


def basis(count, first_cell, width_cells):
    wave_index = jnp.arange(count, dtype=jnp.int32)
    cell_index = first_cell + jnp.arange(width_cells, dtype=jnp.int32)
    wave_turns = wave_index[:, None] * cell_index[None, :] % NX
    phase_angle = wave_turns.astype(jnp.float32) * (2.0 * math.pi / NX)
    offsets = jnp.concatenate(
        [jnp.zeros((count, 1), jnp.float32), jnp.full((count, 1), 0.5 * math.pi, jnp.float32)],
        axis=0,
    )
    stacked = jnp.concatenate([phase_angle, phase_angle], axis=0) + offsets
    return jnp.cos(stacked) * (1.0 / math.sqrt(NX))


def flatten_pair(piece):
    depth, items, count = (piece.shape[1], piece.shape[2], piece.shape[3])
    return jnp.concatenate(
        [piece[0].reshape(depth * items, count), piece[1].reshape(depth * items, count)], axis=1
    )


def harmonic(center, beside):
    return 2.0 * center * beside / (center + beside)


def thomas(lower_diagonal, main_diagonal, upper_diagonal, right_hand_side):

    def thomas_forward_scan(carried_state, row_entries):
        previous_ratio, previous_eliminated = carried_state
        column_lower, main_c, sup_c, column_right_hand = row_entries
        present_denominator = main_c - column_lower * previous_ratio
        present_ratio = sup_c / present_denominator
        present_eliminated = (
            column_right_hand - column_lower * previous_eliminated
        ) / present_denominator
        return ((present_ratio, present_eliminated), (present_ratio, present_eliminated))

    zeroed_layer = jnp.zeros(right_hand_side.shape[1:], right_hand_side.dtype)
    unused_output, (ratio_rows, eliminated_rows) = lax.scan(
        thomas_forward_scan,
        (zeroed_layer, zeroed_layer),
        (lower_diagonal, main_diagonal, upper_diagonal, right_hand_side),
    )

    def thomas_backward_scan(following_value, row_entries):
        column_ratio, column_eliminated = row_entries
        present_value = column_eliminated - column_ratio * following_value
        return (present_value, present_value)

    unused_output, solved_values = lax.scan(
        thomas_backward_scan, zeroed_layer, (ratio_rows, eliminated_rows), reverse=True
    )
    return solved_values


def factor(lower_diagonal, main_diagonal, upper_diagonal):

    def factor_forward_scan(previous_ratio, row_entries):
        column_lower, main_c, sup_c = row_entries
        present_denominator = main_c - column_lower * previous_ratio
        present_ratio = sup_c / present_denominator
        return (present_ratio, (present_denominator, present_ratio))

    unused_output, (denominator_rows, ratio_rows) = lax.scan(
        factor_forward_scan,
        jnp.zeros_like(main_diagonal[0]),
        (lower_diagonal, main_diagonal, upper_diagonal),
    )
    return (denominator_rows, ratio_rows)


def solve_factored(lower_diagonal, denominator_rows, ratio_rows, right_hand_side):

    def solve_forward_scan(previous_eliminated, row_entries):
        column_lower, column_denominator, column_right_hand = row_entries
        present_eliminated = (
            column_right_hand - column_lower[None] * previous_eliminated
        ) / column_denominator[None]
        return (present_eliminated, present_eliminated)

    unused_output, eliminated_rows = lax.scan(
        solve_forward_scan,
        jnp.zeros_like(right_hand_side[0]),
        (lower_diagonal, denominator_rows, right_hand_side),
    )

    def solve_backward_scan(following_value, row_entries):
        column_ratio, column_eliminated = row_entries
        present_value = column_eliminated - column_ratio[None] * following_value
        return (present_value, present_value)

    unused_output, solved_values = lax.scan(
        solve_backward_scan,
        jnp.zeros_like(right_hand_side[0]),
        (ratio_rows, eliminated_rows),
        reverse=True,
    )
    return solved_values


def generic_body(spectral, shifts, colour, pressure, source):
    total_depth = pressure.shape[0] * lax.axis_size("gz")
    vert_factor = float(total_depth * total_depth // 4)
    width_cells = spectral.shape[3]
    first_cell = lax.axis_index("gx") * width_cells
    twisted = twisted_coeffs(spectral, shifts, first_cell)
    piece = lax.all_to_all(twisted, "gx", split_axis=1, concat_axis=3, tiled=True)
    depth = piece.shape[1]
    items = piece.shape[2]
    length = piece.shape[3]
    flat = flatten_pair(piece)
    block_width = min(512, length)
    blocks = [
        jnp.dot(
            flat,
            basis(length, block * block_width, block_width),
            precision=lax.Precision.HIGHEST,
            preferred_element_type=jnp.float32,
        )
        for block in range(length // block_width)
    ]
    field_rows = jnp.concatenate(blocks, axis=1).reshape(depth, items, length)
    log_perm = lax.all_to_all(field_rows, "gx", split_axis=2, concat_axis=0, tiled=True)
    perm = jnp.exp(log_perm)
    padded = padded_2(perm, (("gx", 2), ("gz", 0), ("gy", 1)), 1)
    w_zm = vert_factor * harmonic(perm, padded[:-2, 1:-1, 1:-1])
    w_zp = vert_factor * harmonic(perm, padded[2:, 1:-1, 1:-1])
    w_ym = harmonic(perm, padded[1:-1, :-2, 1:-1])
    w_yp = harmonic(perm, padded[1:-1, 2:, 1:-1])
    w_xm = harmonic(perm, padded[1:-1, 1:-1, :-2])
    w_xp = harmonic(perm, padded[1:-1, 1:-1, 2:])
    main_diagonal = STORE + w_xm + w_xp + w_ym + w_yp + w_zm + w_zp
    lower_diagonal = -w_zm
    upper_diagonal = -w_zp
    zeroed_layer = jnp.zeros_like(main_diagonal[0])
    inner_sub = jnp.concatenate([zeroed_layer[None], lower_diagonal[2:-1]], axis=0)
    inner_sup = jnp.concatenate([upper_diagonal[1:-2], zeroed_layer[None]], axis=0)
    inner_main = main_diagonal[1:-1]
    denominator_rows, ratio_rows = factor(inner_sub, inner_main, inner_sup)
    unit_rhs = jnp.zeros((inner_main.shape[0], 2) + zeroed_layer.shape, jnp.float32)
    unit_rhs = unit_rhs.at[0, 0].set(-lower_diagonal[1])
    unit_rhs = unit_rhs.at[-1, 1].set(-upper_diagonal[-2])
    coupled = solve_factored(inner_sub, denominator_rows, ratio_rows, unit_rhs)
    left_part = coupled[:, 0]
    right_part = coupled[:, 1]
    sub_first = lower_diagonal[0]
    main_first = main_diagonal[0] + upper_diagonal[0] * left_part[0]
    sup_first = upper_diagonal[0] * right_part[0]
    sub_last = lower_diagonal[-1] * left_part[-1]
    main_last = main_diagonal[-1] + lower_diagonal[-1] * right_part[-1]
    sup_last = upper_diagonal[-1]

    def line_solve(current):
        cycle = padded_2(current, (("gx", 2), ("gy", 1)), 1)
        right_hand_side = source + w_xm * cycle[:, 1:-1, :-2] + w_xp * cycle[:, 1:-1, 2:]
        right_hand_side = right_hand_side + w_ym * cycle[:, :-2, 1:-1] + w_yp * cycle[:, 2:, 1:-1]
        particular = solve_factored(
            inner_sub, denominator_rows, ratio_rows, right_hand_side[1:-1][:, None]
        )[:, 0]
        rhs_first = right_hand_side[0] - upper_diagonal[0] * particular[0]
        rhs_last = right_hand_side[-1] - lower_diagonal[-1] * particular[-1]
        reduced_rows = jnp.stack(
            [sub_first, main_first, sup_first, rhs_first, sub_last, main_last, sup_last, rhs_last]
        )
        gathered = lax.all_gather(reduced_rows, "gz", axis=0, tiled=True)
        segments = gathered.shape[0] // 8
        system = gathered.reshape((2 * segments, 4) + zeroed_layer.shape)
        reduced_sol = thomas(system[:, 0], system[:, 1], system[:, 2], system[:, 3])
        own_pair = lax.dynamic_slice_in_dim(reduced_sol, 2 * lax.axis_index("gz"), 2, 0)
        face_first = own_pair[0]
        face_last = own_pair[1]
        inner = particular + face_first[None] * left_part + face_last[None] * right_part
        return jnp.concatenate([face_first[None], inner, face_last[None]], axis=0)

    half = jnp.where((colour == 0)[None], line_solve(pressure), pressure)
    smoothed = jnp.where((colour == 1)[None], line_solve(half), half)
    return (log_perm, smoothed)


LANES = 128
ROWS = 8
F32 = jnp.float32
MIB = 1 << 20
SUMS_GRANT = 60


def suits(mesh):
    sizes = dict(mesh.shape)
    return sizes["gx"] == 2 and sizes["gz"] == 4 and sizes["gy"] == 4


def params(mib):
    return pltpu.CompilerParams(vmem_limit_bytes=mib * MIB)


def cos_sin(turns):
    quarter = (turns + NX // 8) >> 9
    angle = (turns - (quarter << 9)).astype(F32) * (2.0 * math.pi / NX)
    square = angle * angle
    sine = angle * (
        1.0
        + square * (-1.0 / 6 + square * (1.0 / 120 + square * (-1.0 / 5040 + square / 362880)))
    )
    cosine = 1.0 + square * (
        -0.5 + square * (1.0 / 24 + square * (-1.0 / 720 + square * (1.0 / 40320)))
    )
    odd = (quarter & 1) == 1
    first = jnp.where(odd, sine, cosine)
    second = jnp.where(odd, cosine, sine)
    cos_sign = jnp.where(((quarter + 1) & 2) == 2, -1.0, 1.0)
    sin_sign = jnp.where((quarter & 2) == 2, -1.0, 1.0)
    return first * cos_sign, second * sin_sign


def split(values):
    high = values.astype(jnp.bfloat16)
    return high, (values - high.astype(F32)).astype(jnp.bfloat16)


def times(first, second):
    return (
        first[0] * second[0] - first[1] * second[1],
        first[0] * second[1] + first[1] * second[0],
    )


def plus(first, second):
    return (first[0] + second[0], first[1] + second[1])


def minus(first, second):
    return (first[0] - second[0], first[1] - second[1])


def quarter_turn(value):
    return (-value[1], value[0])


def four_point(first, second, third, fourth):
    even, gap = plus(first, third), minus(first, third)
    odd, turned = plus(second, fourth), quarter_turn(minus(second, fourth))
    return [plus(even, odd), plus(gap, turned), minus(even, odd), minus(gap, turned)]


def eight_point(values):
    even = four_point(*values[0::2])
    odd = four_point(*values[1::2])
    root = math.sqrt(0.5)
    real, imag = odd[1]
    odd[1] = (root * (real - imag), root * (real + imag))
    odd[2] = quarter_turn(odd[2])
    real, imag = odd[3]
    odd[3] = (-root * (real + imag), root * (real - imag))
    return [plus(*pair) for pair in zip(even, odd)] + [minus(*pair) for pair in zip(even, odd)]


def fill_tables(basis, turns):
    groups = NX // LANES
    shape = (LANES, LANES)
    lane = lane_of(shape)
    cells = (lane % groups) * (LANES // groups) + lane // groups
    cosine, sine = cos_sin((row_of(shape) * cells) % LANES * groups)
    for at, value in enumerate((cosine, -sine)):
        rows = slice(at * LANES, (at + 1) * LANES)
        high, low = split(value * (1.0 / math.sqrt(NX)))
        basis[0, rows], basis[1, rows], basis[2, rows] = high, high, low
    shape = (groups, LANES)
    turns[0], turns[1] = cos_sin(row_of(shape) * lane_of(shape))


def diagonal_of(depth):
    square = (depth, depth)
    return row_of(square) == lane_of(square)


def shift_columns(shifts, rows_of, columns):
    depth = shifts.shape[1]
    diagonal = diagonal_of(depth)
    for at, y in enumerate(rows_of):
        spread = jnp.where(diagonal, shifts[y : y + 1, :].astype(F32), 0.0)
        shift = jnp.broadcast_to(jnp.sum(spread, axis=1, keepdims=True), (depth, LANES))
        columns[at * depth : (at + 1) * depth, :] = shift.astype(jnp.int32)


def edge_columns(ys, depth, edges, kept):
    kept[...] = jnp.zeros_like(kept)
    diagonal = diagonal_of(depth)
    for at in range(len(ys)):
        rows = slice(at * depth, (at + 1) * depth)
        for side in range(edges.shape[0]):
            lane = 0 if side % 2 else LANES - 1
            column = jnp.broadcast_to(edges[side, rows, lane : lane + 1], (depth, depth))
            row = jnp.sum(jnp.where(diagonal, column, 0.0), axis=0, keepdims=True)
            kept[side, at : at + 1, :depth] = row


def twisted(first_wave, shift, coefficients, rows):
    lane = lane_of(shift.shape)
    phase = cos_sin((shift * (lane + first_wave)) & (NX - 1))
    turn = cos_sin((shift * LANES) & (NX - 1))
    values = []
    for part in range(coefficients.shape[0]):
        values.append(times((coefficients[part, 0, rows], coefficients[part, 1, rows]), phase))
        phase = times(phase, turn)
    return values


def interleave(tiles):
    count = len(tiles)
    lane = lane_of(tiles[0].shape)
    bit = count // 2
    while bit:
        low = (lane & bit) == 0
        moved = list(tiles)
        for at in range(count):
            if not at & bit:
                first, second = tiles[at], tiles[at | bit]
                crossed = jnp.take_along_axis(
                    jnp.where(low, second, first), lane ^ bit, axis=1
                )
                moved[at] = jnp.where(low, first, crossed)
                moved[at | bit] = jnp.where(low, crossed, second)
        tiles = moved
        bit //= 2
    return tiles


def row_sums(g, at, y, depth, items, columns, coefficients, basis, turns, left, right, emit):
    groups = NX // LANES
    sign = 1.0 - 2.0 * g.astype(F32)
    first_wave = g * (coefficients.shape[0] * LANES)
    step = 16
    for part in range(depth // step):
        rows = pl.ds(part * step * items + y, step, stride=items)
        shift = columns[pl.ds(at * depth + part * step, step), :]
        values = twisted(first_wave, shift, coefficients, rows)
        turned = [
            times(value, (sign * math.cos(2 * math.pi * p / groups), sign * math.sin(2 * math.pi * p / groups)))
            if p
            else (sign * value[0], sign * value[1])
            for p, value in enumerate(values)
        ]
        even, odd = eight_point(values), eight_point(turned)
        for group in range(groups):
            value = odd[group // 2] if group % 2 else even[group // 2]
            if group:
                value = times(value, (turns[0, group : group + 1], turns[1, group : group + 1]))
            first = group * depth + part * step
            for place_of, piece in enumerate(value):
                for half, bits in enumerate(split(piece)):
                    target = (2 * half + place_of) * LANES
                    left[first : first + step, target : target + LANES] = bits
    spread = jnp.concatenate([left[...], left[:, : 2 * LANES]], axis=1)
    bases = basis[...].reshape(-1, LANES)
    right[...] = jnp.dot(spread, bases, preferred_element_type=F32)
    for part in range(depth // ROWS):
        tiles = [
            right[group * depth + part * ROWS : group * depth + (part + 1) * ROWS]
            for group in range(groups)
        ]
        emit(pl.ds(at * depth + part * ROWS, ROWS), interleave(tiles))


def load_coefficients(spectral, coefficients, arrivals):
    parts = coefficients.shape[0]
    copies = [
        pltpu.make_async_copy(
            spectral.at[:, :, part * LANES : (part + 1) * LANES],
            coefficients.at[part],
            arrivals.at[part],
        )
        for part in range(parts)
    ]
    for copy in copies:
        copy.start()
    return copies


def keep_edges(rows, tiles, edges):
    count = len(tiles) // 4
    for side in range(edges.shape[0]):
        edges[side, rows] = tiles[(side // 2 + 1) * count - 1 + side % 2]


def wide_sums_kernel(ys, shifts, spectral, other, own, kept, *refs):
    columns, edges, coefficients, arrivals, *tables, left, right = refs
    items, depth = shifts.shape
    copies = load_coefficients(spectral, coefficients, arrivals)
    fill_tables(*tables)
    shift_columns(shifts, ys, columns)
    for copy in copies:
        copy.wait()
    g = lax.axis_index("gx")

    def emit(rows, tiles):
        half = len(tiles) // 2
        keep_edges(rows, tiles, edges)
        for tile, (low, high) in enumerate(zip(tiles[:half], tiles[half:])):
            there = slice(tile * LANES, (tile + 1) * LANES)
            other[rows, there] = jnp.where(g == 0, high, low)
            own[rows, there] = jnp.where(g == 0, low, high)

    for at, y in enumerate(ys):
        row_sums(
            *(g, at, y, depth, items, columns, coefficients, *tables),
            *(left.at[at % 2], right.at[at % 2], emit),
        )
    edge_columns(ys, depth, edges, kept)


def last_sums_kernel(ys, shifts, outer_kept, inner_kept, p_column, spectral, one, two, own, *refs):
    columns_own, kept, columns, edges, coefficients, arrivals, *tables, left, right = refs
    items, depth = shifts.shape
    copies = load_coefficients(spectral, coefficients, arrivals)
    fill_tables(*tables)
    shift_columns(shifts, ys, columns)
    for copy in copies:
        copy.wait()
    g = lax.axis_index("gx")

    def emit(rows, tiles):
        half = len(tiles) // 2
        keep_edges(rows, tiles, edges)
        others = []
        for tile, (low, high) in enumerate(zip(tiles[:half], tiles[half:])):
            own[rows, tile * LANES : (tile + 1) * LANES] = jnp.where(g == 0, low, high)
            others.append(jnp.where(g == 0, high, low))
        start = 0
        for ref in (one, two):
            count = ref.shape[1] // LANES
            for tile in range(count):
                ref[rows, tile * LANES : (tile + 1) * LANES] = jnp.where(
                    g == 0, others[start + tile], others[half - start - count + tile]
                )
            start += count

    for at, y in enumerate(ys):
        row_sums(
            *(g, at, y, depth, items, columns, coefficients, *tables),
            *(left.at[at % 2], right.at[at % 2], emit),
        )
    edge_columns(ys, depth, edges, kept)
    sides_of = [
        jnp.concatenate(
            [outer_kept[side, :1], inner_kept[side], kept[side], outer_kept[side, 1:]], axis=0
        )
        for side in range(6)
    ]
    low, high = sides_of[:3], sides_of[3:]
    own_sides = [jnp.where(g == 0, *pair) for pair in ((low[0], high[1]), (low[1], high[2]))]
    own_sides.append(jnp.where(g == 0, low[2], high[0]))
    other_sides = [jnp.where(g == 0, *pair) for pair in ((high[1], low[0]), (high[2], low[1]))]
    other_sides.append(jnp.where(g == 0, high[0], low[2]))
    for at in range(3):
        columns_own[at], columns_own[3 + at] = own_sides[at], other_sides[at]
    extra = slice(one.shape[0] - ROWS, one.shape[0])
    for at, piece in enumerate((*other_sides, own_sides[2], p_column[...])):
        one[extra, at * LANES : (at + 1) * LANES] = piece


SCALARS = pl.BlockSpec(memory_space=pltpu.SMEM)
ON_CHIP = pl.BlockSpec(memory_space=pltpu.VMEM)
IN_HBM = pl.BlockSpec(memory_space=pltpu.HBM)


def call(kernel, name, out_shape, args, flags=None, scratch=(), far=(), mib=20, flops=1):
    specs = [ON_CHIP] * len(args) + [IN_HBM] * len(far)
    args = list(args) + list(far)
    if flags is not None:
        specs = [SCALARS] + specs
        args = [flags] + args
    return pl.pallas_call(
        kernel,
        out_shape=out_shape,
        in_specs=specs,
        out_specs=jax.tree.map(lambda _: ON_CHIP, out_shape),
        scratch_shapes=list(scratch),
        compiler_params=params(mib),
        cost_estimate=pl.CostEstimate(flops=flops, bytes_accessed=1, transcendentals=0),
        name=name,
    )(*args)


def roll(values, shift, axis):
    return pltpu.roll(values, shift % values.shape[axis], axis)


def lane_of(shape):
    return lax.broadcasted_iota(jnp.int32, shape, 1)


def row_of(shape):
    return lax.broadcasted_iota(jnp.int32, shape, 0)


def column_to(z, packed, target):
    return pltpu.roll(packed, (target - z) % LANES, 1)


def packed_with(z, packed, plane, lane):
    column = jnp.broadcast_to(plane[:, lane : lane + 1], (ROWS, LANES))
    return jnp.where(lane_of((ROWS, LANES)) == z, column, packed)


def inverse_of(values):
    guess = pl.reciprocal(values, approx=True)
    return guess * (2.0 - values * guess)


def ordered(z, sums, depth):
    spread = pl.ds(z, ROWS, stride=depth)
    return jnp.concatenate([sums[at, spread] for at in range(sums.shape[0])], axis=1)


def place_tiles(sums, rows, first, values):
    for at in range(values.shape[1] // LANES):
        sums[(first >> 7) + at, rows] = values[:, at * LANES : (at + 1) * LANES]


def boundary_plane(g, plane):
    return jnp.where(g == 0, roll(plane[:, -LANES:], 1, 1), plane[:, :LANES])


def outer_field_kernel(depth, flags, own, other, pressure, to_near, to_middle, boundary):
    g, even = flags[0], flags[16] == 0
    low, high = slice(0, depth), slice(depth, 2 * depth)
    south, north = own[low] + other[low], own[high] + other[high]
    to_near[low] = jnp.exp(-jnp.where(even, north, south))
    to_middle[low] = jnp.exp(-jnp.where(even, south, north))

    def layer(z, packed):
        plane = pressure[z]
        keep_rows(depth + z, plane, even, to_near, to_middle, slice(None))
        return packed_with(z, packed, boundary_plane(g, plane), 0)

    boundary[...] = lax.fori_loop(0, depth, layer, jnp.zeros((ROWS, LANES), F32), unroll=8)


def wide_field_kernel(depth, flags, *refs):
    own_outer, outer, own_inner, inner, to_near, to_middle = refs[:6]
    from_near, from_middle, pressure = refs[6:9]
    wide, south_weight, north_weight, p_south, p_north, p_west, p_east = refs[9:16]
    south_rows, north_rows = refs[16:]
    even = flags[16] == 0
    low, high = slice(0, depth), slice(depth, 2 * depth)
    wide[low] = own_outer[low] + outer[low]
    wide[depth:-depth] = own_inner[...] + inner[...]
    wide[-depth:] = own_outer[high] + outer[high]
    near_weight = 2.0 * inverse_of(to_near[low] + from_near[low])
    middle_weight = (2.0 * flags[15].astype(F32)) * inverse_of(to_middle[low] + from_middle[low])
    south = jnp.where(even, middle_weight, near_weight)
    south_weight[...] = south
    north_weight[...] = jnp.where(even, near_weight, middle_weight)
    south_rows[...] = jnp.where(even, from_middle[high], from_near[high])
    north_rows[...] = jnp.where(even, from_near[high], from_middle[high])
    row = row_of(pressure.shape[1:])

    def layer(z, carry):
        plane = pressure[z]
        p_south[z] = jnp.where(row == 0, south_rows[pl.ds(z, 1), :], roll(plane, 1, 0))
        p_north[z] = jnp.where(row == ROWS - 1, north_rows[pl.ds(z, 1), :], roll(plane, -1, 0))
        p_west[z] = roll(plane, 1, 1)
        p_east[z] = roll(plane, -1, 1)
        return carry

    lax.fori_loop(0, depth, layer, 0, unroll=4)


def lane_slice(start, size):
    return pl.ds(pl.multiple_of(start, LANES), size)


def assemble(sums, depth, wide, own, piece, there):
    inside = wide.shape[0] - depth
    place_tiles(sums, slice(0, inside), 0, wide[:inside, there])
    place_tiles(sums, slice(inside, -depth), 0, own[:, there] + piece[: own.shape[0]])
    place_tiles(sums, slice(-depth, None), 0, wide[inside:, there])


def first_field_kernel(depth, flags, *refs):
    wide, own, middle, columns_own = refs[:4]
    log_perm, resist, low_side, high_side, boundary, column, p_column, sums = refs[4:]
    extra = slice(own.shape[0], own.shape[0] + ROWS)
    came = [middle[extra, at * LANES : (at + 1) * LANES] for at in range(5)]
    for at, ref in enumerate((low_side, high_side, boundary)):
        ref[...] = jnp.exp(-(columns_own[at] + came[at]))
    column[...] = jnp.exp(-(columns_own[5] + came[3]))
    p_column[...] = came[4]
    assemble(sums, depth, wide, own, middle, lane_slice(flags[3], log_perm.shape[2]))

    def layer(z, carry):
        plane = ordered(z, sums, depth)
        log_perm[z] = plane
        resist[z] = jnp.exp(-plane)
        return carry

    lax.fori_loop(0, depth, layer, 0, unroll=8)


def second_field_kernel(depth, flags, *refs):
    wide, own, middle, resist_near = refs[:4]
    log_perm, resist, sums = refs[4:]
    third = middle.shape[1]
    assemble(sums, depth, wide, own, middle, lane_slice(flags[5], third))
    extra = resist.shape[2] - third
    target = lane_slice(flags[5] - flags[7], third)
    extra_target = lane_slice(flags[8], extra)
    extra_source = lane_slice(flags[9], extra)

    def layer(z, carry):
        plane = ordered(z, sums, depth)
        log_perm[z] = plane
        resist[z, :, target] = jnp.exp(-plane)
        resist[z, :, extra_target] = resist_near[z, :, extra_source]
        return carry

    lax.fori_loop(0, depth, layer, 0, unroll=8)


def join_columns_kernel(depth, flags, near, far, _, whole):
    def layer(z, carry):
        whole[z, :, lane_slice(flags[3], near.shape[2])] = near[z]
        whole[z, :, lane_slice(flags[5], far.shape[2])] = far[z]
        return carry

    lax.fori_loop(0, depth, layer, 0, unroll=8)


def keep_rows(z, value, even, to_near, to_middle, here):
    south, north = value[0:1, :], value[ROWS - 1 : ROWS, :]
    to_near[pl.ds(z, 1), here] = jnp.where(even, north, south)
    to_middle[pl.ds(z, 1), here] = jnp.where(even, south, north)


def with_first(plane, edge):
    first = jnp.where(lane_of((ROWS, LANES)) == 0, edge, plane[:, :LANES])
    return jnp.concatenate([first, plane[:, LANES:]], axis=1)


def with_last(plane, edge):
    last = jnp.where(lane_of((ROWS, LANES)) == LANES - 1, edge, plane[:, -LANES:])
    return jnp.concatenate([plane[:, :-LANES], last], axis=1)


def coupling(z, field, start, size, east_weight, north_weight, south_terms, north_rows, west, column):
    here = lane_slice(start, size)
    plane = field[z, :, here]
    row = row_of(plane.shape)
    at_start = start == 0
    inner = field[z, :, lane_slice(jnp.where(at_start, size, size - LANES), LANES)]
    west_value = jnp.where(at_start, column_to(z, column, 0), roll(inner, 1, 1))
    east_value = jnp.where(at_start, roll(inner, -1, 1), column_to(z, column, LANES - 1))
    to_east, to_north = east_weight * plane, north_weight * plane
    from_west = with_first(roll(to_east, 1, 1), column_to(z, west, 0) * west_value)
    from_east = east_weight * with_last(roll(plane, -1, 1), east_value)
    from_south = jnp.where(row == 0, south_terms[pl.ds(z, 1), here], roll(to_north, 1, 0))
    from_north = north_weight * jnp.where(
        row == ROWS - 1, north_rows[pl.ds(z, 1), here], roll(plane, -1, 0)
    )
    return (from_west + from_east) + (from_south + from_north)


def edge_weights(flags, start, bound, column, low_side, high_side):
    g = flags[0]
    middle = 2.0 * inverse_of(low_side + high_side)
    across = 2.0 * inverse_of(bound + column)
    none = jnp.zeros_like(across)
    west = jnp.where(start == 0, jnp.where(g == 0, none, across), middle)
    east = jnp.where(start == 0, middle, jnp.where(g == 0, across, none))
    return west, east


def first_sweep_kernel(depth, vert, block, flags, *refs):
    resist, low_side, high_side, r_bound, r_column, p_column = refs[:6]
    south_weight, north_weight, p_south, p_north, p_west, p_east = refs[6:12]
    source = refs[12]
    w_east, w_north, west_out, particular, inverse, ratio, lead, reduced = refs[13:21]
    grounds, rights, verticals = refs[21:]
    start, offset = flags[6 + block], flags[10 + block]
    size = inverse.shape[2]
    shape = (ROWS, size)
    here = lane_slice(start, size)
    inside = lane_slice(offset, size)
    west_weight, east_weight = edge_weights(
        flags, start, r_bound[...], r_column[...], low_side[...], high_side[...]
    )
    west_out[...] = west_weight
    column = p_column[...]
    row = row_of(shape)

    def weigh(z, carry):
        plane = resist[z, :, inside]
        east = 2.0 * inverse_of(plane + roll(plane, -1, 1))
        east = with_last(east, column_to(z, east_weight, LANES - 1))
        west = with_first(roll(east, 1, 1), column_to(z, west_weight, 0))
        north = 2.0 * inverse_of(plane + roll(plane, -1, 0))
        north = jnp.where(row == ROWS - 1, north_weight[pl.ds(z, 1), here], north)
        south = jnp.where(row == 0, south_weight[pl.ds(z, 1), here], roll(north, 1, 0))
        w_east[z], w_north[z] = east, north
        grounds[z] = STORE + ((east + west) + (north + south))
        verticals[z] = (2.0 * vert) * inverse_of(
            plane + resist[jnp.minimum(z + 1, depth - 1), :, inside]
        )
        p_first, p_last = p_west[z, :, here], p_east[z, :, here]
        p_first = with_first(
            p_first, jnp.where(start == 0, column_to(z, column, 0), p_first[:, :LANES])
        )
        p_last = with_last(
            p_last, jnp.where(start == 0, p_last[:, -LANES:], column_to(z, column, LANES - 1))
        )
        rights[z] = source[z, :, here] + (
            (west * p_first + east * p_last)
            + (south * p_south[z, :, here] + north * p_north[z, :, here])
        )
        return carry

    lax.fori_loop(0, depth, weigh, 0, unroll=4)

    def layer(z, carry):
        conduct, flow, product, first_first, first_part = carry
        weight = verticals[z]
        reciprocal = inverse_of(conduct + weight)
        quotient = weight * reciprocal
        led = product * reciprocal
        inverse[z] = reciprocal
        ratio[z] = quotient
        lead[z] = led
        particular[z] = reciprocal * flow
        return (
            grounds[z + 1] + conduct * quotient,
            rights[z + 1] + flow * quotient,
            product * quotient,
            first_first + led * product,
            first_part + led * flow,
        )

    zero = jnp.zeros(shape, F32)
    conduct, flow, product, first_first, first_part = lax.fori_loop(
        0,
        depth - 1,
        layer,
        (grounds[0], rights[0], jnp.ones(shape, F32), zero, zero),
        unroll=True,
    )
    reciprocal = inverse_of(conduct)
    led = product * reciprocal
    inverse[depth - 1] = reciprocal
    ratio[depth - 1] = zero
    lead[depth - 1] = led
    particular[depth - 1] = flow * reciprocal
    reduced[0] = first_first + led * product + resist[0, :, inside] * (0.5 / vert)
    reduced[1] = led
    reduced[2] = reciprocal + resist[depth - 1, :, inside] * (0.5 / vert)
    reduced[3] = first_part + led * flow
    reduced[4] = flow * reciprocal


def pair_kernel(flags, own_one, own_two, near_one, near_two, across, kept):
    me = flags[14]
    even, lower = me % 2 == 0, me < 2
    for block, (own, near) in enumerate(((own_one, near_one), (own_two, near_two))):
        size = own.shape[2]
        there = slice(block * size, (block + 1) * size)
        first, second = [
            [jnp.where(flip, own[at], near[at]) for at in range(5)]
            for flip in (even, jnp.logical_not(even))
        ]
        reciprocal = inverse_of(first[2] + second[0])
        step = (first[4] - second[3]) * reciprocal
        through = jnp.where(lower, second[1], first[1])
        share = through * reciprocal
        across[0, :, there] = jnp.where(lower, second[2], first[0]) - through * share
        across[1, :, there] = jnp.where(lower, second[4], first[3]) + jnp.where(
            lower, through * step, -through * step
        )
        kept[0, :, there] = share
        kept[1, :, there] = reciprocal
        kept[2, :, there] = step


def ends(me, inner, middle):
    zero = jnp.zeros_like(inner)
    odd = me % 2 == 1
    enters = jnp.where(odd, inner, jnp.where(me == 2, middle, zero))
    leaves = jnp.where(odd, jnp.where(me == 1, middle, zero), inner)
    return enters, leaves


def back_substitute(depth, lines, emit):
    last = depth - 1
    values = tuple(
        (particular[last] + lead[last] * enters) - inverse[last] * leaves
        for enters, leaves, particular, inverse, ratio, lead in lines
    )
    state = emit(last, values, jnp.zeros((ROWS, LANES), F32))

    def layer(step, carry):
        following, state = carry
        z = last - step
        values = tuple(
            (particular[z] + lead[z] * enters) + ratio[z] * beyond
            for (enters, _, particular, _, ratio, lead), beyond in zip(lines, following)
        )
        return values, emit(z, values, state)

    return lax.fori_loop(1, depth, layer, (values, state), unroll=True)[1]


def half_kernel(depth, flags, *refs):
    across, other, kept = refs[:3]
    blocks = (refs[3:7], refs[7:11])
    pressure, colour = refs[11:13]
    half, to_near, to_middle, boundary, joined = refs[13:]
    me, g, even = flags[14], flags[0], flags[16] == 0
    size = blocks[0][0].shape[2]
    spans = [lane_slice(flags[6 + block], size) for block in range(2)]
    lines = []
    for block, state in enumerate(blocks):
        there = slice(block * size, (block + 1) * size)
        sum_of = inverse_of(across[0, :, there] + other[0, :, there])
        joined[:, there] = sum_of
        lead_of = across[1, :, there] - other[1, :, there]
        middle = jnp.where(me < 2, lead_of, -lead_of) * sum_of
        inner = kept[2, :, there] + kept[0, :, there] * middle
        lines.append((*ends(me, inner, middle), *state))
    chosen = [colour[:, here] == 0 for here in spans]

    def emit(z, values, packed):
        for block, (value, here) in enumerate(zip(values, spans)):
            value = jnp.where(chosen[block], value, pressure[z, :, here])
            half[z, :, here] = value
            keep_rows(z, value, even, to_near, to_middle, here)
            if not block:
                packed = packed_with(z, packed, boundary_plane(g, value), 0)
        return packed

    boundary[...] = back_substitute(depth, lines, emit)


def second_sweep_kernel(depth, flags, *refs):
    half, h_near, h_middle, h_column, source, kept, south_weight = refs[:7]
    blocks = (refs[7:13], refs[13:19])
    particulars, near, far = refs[19:21], refs[21], refs[22]
    south_terms, north_rows = refs[23:]
    me, even = flags[14], flags[16] == 0
    size = particulars[0].shape[2]
    starts = [flags[6 + block] for block in range(2)]
    spans = [lane_slice(start, size) for start in starts]
    column = h_column[...]
    south_terms[...] = south_weight[...] * jnp.where(even, h_middle[...], h_near[...])
    north_rows[...] = jnp.where(even, h_near[...], h_middle[...])

    def local(z, block):
        east, north, west = blocks[block][:3]
        return source[z, :, spans[block]] + coupling(
            z,
            half,
            starts[block],
            size,
            east[z],
            north[z],
            south_terms,
            north_rows,
            west[...],
            column,
        )

    def layer(z, carry):
        result = []
        for block, (flow, first_part) in enumerate(carry):
            inverse, ratio, lead = blocks[block][3:6]
            particulars[block][z] = flow * inverse[z]
            first_part = first_part + lead[z] * flow
            result.append((local(z + 1, block) + flow * ratio[z], first_part))
        return tuple(result)

    carry = tuple((local(0, block), jnp.zeros((ROWS, size), F32)) for block in range(2))
    carry = lax.fori_loop(0, depth - 1, layer, carry, unroll=True)
    last = depth - 1
    for block, (flow, first_part) in enumerate(carry):
        inverse, ratio, lead = blocks[block][3:6]
        there = slice(block * size, (block + 1) * size)
        first_part = first_part + lead[last] * flow
        last_part = flow * inverse[last]
        particulars[block][last] = last_part
        asked = jnp.where(me % 2 == 0, last_part, first_part)
        shared = kept[0, :, there] * asked
        outer = jnp.where(me == 1, last_part, jnp.where(me == 2, first_part, 0.0))
        given = outer + jnp.where((me == 0) | (me == 3), shared, -shared)
        near[0, :, there] = asked
        near[1, :, there] = given
        far[:, there] = given


def smoothed_kernel(depth, flags, *refs):
    own, near, skip, cross, kept, joined = refs[:6]
    blocks = (refs[6:10], refs[10:14])
    half, colour, smoothed = refs[14:]
    me = flags[14]
    size = blocks[0][0].shape[2]
    spans = [lane_slice(flags[6 + block], size) for block in range(2)]
    lines = []
    for block, state in enumerate(blocks):
        there = slice(block * size, (block + 1) * size)
        lead_of = (own[1, :, there] + near[1, :, there]) - (skip[:, there] + cross[:, there])
        middle = jnp.where(me < 2, lead_of, -lead_of) * joined[:, there]
        step = own[0, :, there] - near[0, :, there]
        step = jnp.where(me % 2 == 0, step, -step) * kept[1, :, there]
        lines.append((*ends(me, step + kept[0, :, there] * middle, middle), *state))
    chosen = [colour[:, here] == 1 for here in spans]

    def emit(z, values, state):
        for value, here, mine in zip(values, spans, chosen):
            smoothed[z, :, here] = jnp.where(mine, value, half[z, :, here])
        return state

    back_substitute(depth, lines, emit)


PAIR = [(0, 1), (1, 0)]
NEAR = [(0, 1), (1, 0), (2, 3), (3, 2)]
MIDDLE = [(1, 2), (2, 1)]
SKIP = [(0, 2), (2, 0), (1, 3), (3, 1)]
CROSS = [(0, 3), (3, 0), (1, 2), (2, 1)]


def exchange_edges(edges):
    to_near, to_middle, *column = edges
    return [
        lax.ppermute(to_near, "gy", NEAR),
        lax.ppermute(to_middle, "gy", MIDDLE),
        *[lax.ppermute(piece, "gx", PAIR) for piece in column],
    ]


def fast_body(spectral, shifts, colour, pressure, source):
    depth, items, width = pressure.shape
    vert = float((depth * 4) ** 2 // 4)
    waves = spectral.shape[3]
    rows = depth * items
    gx, gz, gy = (lax.axis_index(axis) for axis in ("gx", "gz", "gy"))
    block_size, third = width // 2, 3 * width // 8
    known = width - third

    def placed(start, size):
        return jnp.where(gx == 1, start, width - start - size)

    block_one, block_two = placed(0, block_size), placed(block_size, block_size)
    start_one = placed(0, known)
    extra = known - block_size
    flags = jnp.stack(
        [
            gx,
            placed(0, LANES),
            placed(LANES, known - LANES),
            start_one,
            jnp.zeros_like(gx),
            placed(known, third),
            block_one,
            block_two,
            placed(block_size, extra) - block_two,
            placed(block_size, extra) - start_one,
            block_one - start_one,
            jnp.zeros_like(gx),
            gy > 0,
            gy < 3,
            gz,
            (gy == 1) | (gy == 2),
            gy % 2,
        ]
    ).astype(jnp.int32)

    def shaped(*shape, dtype=F32):
        return jax.ShapeDtypeStruct(shape, dtype)

    groups = NX // LANES
    parts = waves // LANES
    inner_ys, last_ys = (1, 2, 3), tuple(range(4, items - 1))
    last_rows = len(last_ys) * depth
    column_type = shaped(ROWS, LANES)
    coefficients = spectral.reshape(2, rows, waves)

    def scratch(count):
        return [
            pltpu.VMEM((count, LANES), jnp.int32),
            pltpu.VMEM((6, count, LANES), F32),
            pltpu.VMEM((parts, 2, rows, LANES), F32),
            pltpu.SemaphoreType.DMA((parts,)),
            pltpu.VMEM((3, 2 * LANES, LANES), jnp.bfloat16),
            pltpu.VMEM((2, groups, LANES), F32),
            pltpu.VMEM((2, groups * depth, 4 * LANES), jnp.bfloat16),
            pltpu.VMEM((2, groups * depth, LANES), F32),
        ]

    def wide_sums(ys, name, shift_rows, cost):
        return call(
            functools.partial(wide_sums_kernel, ys),
            name,
            [shaped(len(ys) * depth, width)] * 2 + [shaped(6, len(ys), LANES)],
            [shift_rows],
            scratch=scratch(len(ys) * depth),
            far=[coefficients],
            mib=SUMS_GRANT,
            flops=cost,
        )

    shift_rows = shifts.T
    sums, own_outer, outer_kept = wide_sums((0, items - 1), "outer_row_sums", shift_rows, 1)
    outer = lax.ppermute(sums, "gx", PAIR)
    shift_rows, _ = lax.optimization_barrier((shift_rows, own_outer))
    sums, own_inner, inner_kept = wide_sums(inner_ys, "inner_row_sums", shift_rows, 1 << 30)
    inner = lax.ppermute(sums, "gx", PAIR)
    edge_row, edge_column = shaped(depth, width), shaped(ROWS, LANES)
    edges = [edge_row, edge_row, edge_column]
    to_near, to_middle, p_column = call(
        functools.partial(outer_field_kernel, depth),
        "outer_field",
        [shaped(2 * depth, width)] * 2 + [edge_column],
        [own_outer, outer, pressure],
        flags,
    )
    from_near, from_middle = exchange_edges([to_near, to_middle])
    last_one, last_two, own_last, own_columns = call(
        functools.partial(last_sums_kernel, last_ys),
        "last_row_sums",
        [
            shaped(last_rows + ROWS, known),
            shaped(last_rows, third),
            shaped(last_rows, width),
            shaped(6, ROWS, LANES),
        ],
        [shift_rows, outer_kept, inner_kept, p_column],
        scratch=[pltpu.VMEM((6, len(last_ys), LANES), F32)] + scratch(last_rows),
        far=[coefficients],
        mib=SUMS_GRANT,
    )
    last_one, last_two = (lax.ppermute(piece, "gx", PAIR) for piece in (last_one, last_two))
    wide, *around = call(
        functools.partial(wide_field_kernel, depth),
        "wide_field",
        [shaped(rows - last_rows, width)] + [edge_row] * 2 + [shaped(depth, items, width)] * 4,
        [
            *(own_outer, outer, own_inner, inner, to_near, to_middle),
            *(from_near, from_middle, pressure),
        ],
        flags,
        [pltpu.VMEM((depth, width), F32)] * 2,
    )
    log_near, resist_near, *columns = call(
        functools.partial(first_field_kernel, depth),
        "first_field",
        [shaped(depth, items, known)] * 2 + [edge_column] * 5,
        [wide, own_last, last_one, own_columns],
        flags,
        [pltpu.VMEM((known // LANES, rows, LANES), F32)],
    )
    block = shaped(depth, items, block_size)

    state_types = [block] * 2 + [edge_column] + [block] * 4

    def first_sweep(at, resist):
        return call(
            functools.partial(first_sweep_kernel, depth, vert, at),
            "first_sweep",
            state_types + [shaped(5, items, block_size)],
            [resist, *columns, *around, source],
            flags,
            [pltpu.VMEM((depth, items, block_size), F32)] * 3,
        )

    *state_one, reduced_one = first_sweep(0, resist_near)
    near_one = lax.ppermute(reduced_one, "gz", NEAR)
    last_two, _ = lax.optimization_barrier((last_two, reduced_one))
    log_far, resist_far = call(
        functools.partial(second_field_kernel, depth),
        "second_field",
        [shaped(depth, items, third), block],
        [wide, own_last, last_two, resist_near],
        flags,
        [pltpu.VMEM((third // LANES, rows, LANES), F32)],
    )
    *state_two, reduced_two = first_sweep(1, resist_far)
    near_two = lax.ppermute(reduced_two, "gz", NEAR)
    (log_perm,) = call(
        functools.partial(join_columns_kernel, depth),
        "log_perm",
        [shaped(depth, items, width)],
        [log_near, log_far, reduced_two],
        flags,
    )
    across, kept = call(
        pair_kernel,
        "join_pair",
        [shaped(2, items, width), shaped(3, items, width)],
        [reduced_one, reduced_two, near_one, near_two],
        flags,
    )
    other = lax.ppermute(across, "gz", SKIP)
    half, *h_edges, joined = call(
        functools.partial(half_kernel, depth),
        "half",
        [shaped(depth, items, width), *edges, shaped(items, width)],
        [across, other, kept, *state_one[3:], *state_two[3:], pressure, colour],
        flags,
    )
    h_edges = exchange_edges(h_edges)
    weights = [[*state[:3], *state[4:]] for state in (state_one, state_two)]
    current_one, current_two, to_near, to_far = call(
        functools.partial(second_sweep_kernel, depth),
        "second_sweep",
        [block, block, shaped(2, items, width), shaped(items, width)],
        [half, *h_edges, source, kept, around[0], *weights[0], *weights[1]],
        flags,
        [pltpu.VMEM((depth, width), F32)] * 2,
    )
    from_near, from_skip, from_cross = (
        lax.ppermute(planes, "gz", pairs)
        for planes, pairs in ((to_near, NEAR), (to_far, SKIP), (to_far, CROSS))
    )
    (smoothed,) = call(
        functools.partial(smoothed_kernel, depth),
        "smoothed",
        [shaped(depth, items, width)],
        [
            *(to_near, from_near, from_skip, from_cross, kept, joined),
            *(current_one, *state_one[4:]),
            *(current_two, *state_two[4:]),
            *(half, colour),
        ],
        flags,
    )
    return (log_perm, smoothed)


def solution(mesh):
    body = fast_body if suits(mesh) else generic_body
    in_specs = (
        P(None, "gz", "gy", "gx"),
        P("gz", "gy"),
        P("gy", "gx"),
        P("gz", "gy", "gx"),
        P("gz", "gy", "gx"),
    )
    out_specs = (P("gz", "gy", "gx"), P("gz", "gy", "gx"))
    return jax.shard_map(body, mesh=mesh, in_specs=in_specs, out_specs=out_specs, check_vma=False)
```

```python
import functools
import math

import jax
import jax.numpy as jnp


from jax import lax
from jax.experimental import pallas as pl
from jax.experimental.pallas import tpu as pltpu
from jax.sharding import PartitionSpec as P

NX = 2048


STORE = 1.0


def padded_2(block, sides, width):
    for axis, dim in sides:
        count = lax.axis_size(axis)
        forward = [(i, i + 1) for i in range(count - 1)]
        backward = [(target, source) for source, target in forward]
        low = lax.ppermute(
            lax.slice_in_dim(block, block.shape[dim] - width, None, axis=dim), axis, forward
        )
        high = lax.ppermute(lax.slice_in_dim(block, 0, width, axis=dim), axis, backward)
        block = jnp.concatenate([low, block, high], axis=dim)
    return block


def twisted_coeffs(spectral, shifts, first_wave):
    count = spectral.shape[3]
    wave_index = first_wave + jnp.arange(count, dtype=jnp.int32)
    wave_turns = shifts[:, :, None] * wave_index[None, None, :] % NX
    phase_angle = wave_turns.astype(jnp.float32) * (2.0 * math.pi / NX)
    cosine = jnp.cos(phase_angle)
    sine_part = jnp.sin(phase_angle)
    real_part = spectral[0] * cosine - spectral[1] * sine_part
    imag_part = spectral[0] * sine_part + spectral[1] * cosine
    return jnp.stack([real_part, imag_part])


def basis(count, first_cell, width_cells):
    wave_index = jnp.arange(count, dtype=jnp.int32)
    cell_index = first_cell + jnp.arange(width_cells, dtype=jnp.int32)
    wave_turns = wave_index[:, None] * cell_index[None, :] % NX
    phase_angle = wave_turns.astype(jnp.float32) * (2.0 * math.pi / NX)
    offsets = jnp.concatenate(
        [jnp.zeros((count, 1), jnp.float32), jnp.full((count, 1), 0.5 * math.pi, jnp.float32)],
        axis=0,
    )
    stacked = jnp.concatenate([phase_angle, phase_angle], axis=0) + offsets
    return jnp.cos(stacked) * (1.0 / math.sqrt(NX))


def flatten_pair(piece):
    depth, items, count = (piece.shape[1], piece.shape[2], piece.shape[3])
    return jnp.concatenate(
        [piece[0].reshape(depth * items, count), piece[1].reshape(depth * items, count)], axis=1
    )


def harmonic(center, beside):
    return 2.0 * center * beside / (center + beside)


def thomas(lower_diagonal, main_diagonal, upper_diagonal, right_hand_side):

    def thomas_forward_scan(carried_state, row_entries):
        previous_ratio, previous_eliminated = carried_state
        column_lower, main_c, sup_c, column_right_hand = row_entries
        present_denominator = main_c - column_lower * previous_ratio
        present_ratio = sup_c / present_denominator
        present_eliminated = (
            column_right_hand - column_lower * previous_eliminated
        ) / present_denominator
        return ((present_ratio, present_eliminated), (present_ratio, present_eliminated))

    zeroed_layer = jnp.zeros(right_hand_side.shape[1:], right_hand_side.dtype)
    unused_output, (ratio_rows, eliminated_rows) = lax.scan(
        thomas_forward_scan,
        (zeroed_layer, zeroed_layer),
        (lower_diagonal, main_diagonal, upper_diagonal, right_hand_side),
    )

    def thomas_backward_scan(following_value, row_entries):
        column_ratio, column_eliminated = row_entries
        present_value = column_eliminated - column_ratio * following_value
        return (present_value, present_value)

    unused_output, solved_values = lax.scan(
        thomas_backward_scan, zeroed_layer, (ratio_rows, eliminated_rows), reverse=True
    )
    return solved_values


def factor(lower_diagonal, main_diagonal, upper_diagonal):

    def factor_forward_scan(previous_ratio, row_entries):
        column_lower, main_c, sup_c = row_entries
        present_denominator = main_c - column_lower * previous_ratio
        present_ratio = sup_c / present_denominator
        return (present_ratio, (present_denominator, present_ratio))

    unused_output, (denominator_rows, ratio_rows) = lax.scan(
        factor_forward_scan,
        jnp.zeros_like(main_diagonal[0]),
        (lower_diagonal, main_diagonal, upper_diagonal),
    )
    return (denominator_rows, ratio_rows)


def solve_factored(lower_diagonal, denominator_rows, ratio_rows, right_hand_side):

    def solve_forward_scan(previous_eliminated, row_entries):
        column_lower, column_denominator, column_right_hand = row_entries
        present_eliminated = (
            column_right_hand - column_lower[None] * previous_eliminated
        ) / column_denominator[None]
        return (present_eliminated, present_eliminated)

    unused_output, eliminated_rows = lax.scan(
        solve_forward_scan,
        jnp.zeros_like(right_hand_side[0]),
        (lower_diagonal, denominator_rows, right_hand_side),
    )

    def solve_backward_scan(following_value, row_entries):
        column_ratio, column_eliminated = row_entries
        present_value = column_eliminated - column_ratio[None] * following_value
        return (present_value, present_value)

    unused_output, solved_values = lax.scan(
        solve_backward_scan,
        jnp.zeros_like(right_hand_side[0]),
        (ratio_rows, eliminated_rows),
        reverse=True,
    )
    return solved_values


def generic_body(spectral, shifts, colour, pressure, source):
    total_depth = pressure.shape[0] * lax.axis_size("gz")
    vert_factor = float(total_depth * total_depth // 4)
    width_cells = spectral.shape[3]
    first_cell = lax.axis_index("gx") * width_cells
    twisted = twisted_coeffs(spectral, shifts, first_cell)
    piece = lax.all_to_all(twisted, "gx", split_axis=1, concat_axis=3, tiled=True)
    depth = piece.shape[1]
    items = piece.shape[2]
    length = piece.shape[3]
    flat = flatten_pair(piece)
    block_width = min(512, length)
    blocks = [
        jnp.dot(
            flat,
            basis(length, block * block_width, block_width),
            precision=lax.Precision.HIGHEST,
            preferred_element_type=jnp.float32,
        )
        for block in range(length // block_width)
    ]
    field_rows = jnp.concatenate(blocks, axis=1).reshape(depth, items, length)
    log_perm = lax.all_to_all(field_rows, "gx", split_axis=2, concat_axis=0, tiled=True)
    perm = jnp.exp(log_perm)
    padded = padded_2(perm, (("gx", 2), ("gz", 0), ("gy", 1)), 1)
    w_zm = vert_factor * harmonic(perm, padded[:-2, 1:-1, 1:-1])
    w_zp = vert_factor * harmonic(perm, padded[2:, 1:-1, 1:-1])
    w_ym = harmonic(perm, padded[1:-1, :-2, 1:-1])
    w_yp = harmonic(perm, padded[1:-1, 2:, 1:-1])
    w_xm = harmonic(perm, padded[1:-1, 1:-1, :-2])
    w_xp = harmonic(perm, padded[1:-1, 1:-1, 2:])
    main_diagonal = STORE + w_xm + w_xp + w_ym + w_yp + w_zm + w_zp
    lower_diagonal = -w_zm
    upper_diagonal = -w_zp
    zeroed_layer = jnp.zeros_like(main_diagonal[0])
    inner_sub = jnp.concatenate([zeroed_layer[None], lower_diagonal[2:-1]], axis=0)
    inner_sup = jnp.concatenate([upper_diagonal[1:-2], zeroed_layer[None]], axis=0)
    inner_main = main_diagonal[1:-1]
    denominator_rows, ratio_rows = factor(inner_sub, inner_main, inner_sup)
    unit_rhs = jnp.zeros((inner_main.shape[0], 2) + zeroed_layer.shape, jnp.float32)
    unit_rhs = unit_rhs.at[0, 0].set(-lower_diagonal[1])
    unit_rhs = unit_rhs.at[-1, 1].set(-upper_diagonal[-2])
    coupled = solve_factored(inner_sub, denominator_rows, ratio_rows, unit_rhs)
    left_part = coupled[:, 0]
    right_part = coupled[:, 1]
    sub_first = lower_diagonal[0]
    main_first = main_diagonal[0] + upper_diagonal[0] * left_part[0]
    sup_first = upper_diagonal[0] * right_part[0]
    sub_last = lower_diagonal[-1] * left_part[-1]
    main_last = main_diagonal[-1] + lower_diagonal[-1] * right_part[-1]
    sup_last = upper_diagonal[-1]

    def line_solve(current):
        cycle = padded_2(current, (("gx", 2), ("gy", 1)), 1)
        right_hand_side = source + w_xm * cycle[:, 1:-1, :-2] + w_xp * cycle[:, 1:-1, 2:]
        right_hand_side = right_hand_side + w_ym * cycle[:, :-2, 1:-1] + w_yp * cycle[:, 2:, 1:-1]
        particular = solve_factored(
            inner_sub, denominator_rows, ratio_rows, right_hand_side[1:-1][:, None]
        )[:, 0]
        rhs_first = right_hand_side[0] - upper_diagonal[0] * particular[0]
        rhs_last = right_hand_side[-1] - lower_diagonal[-1] * particular[-1]
        reduced_rows = jnp.stack(
            [sub_first, main_first, sup_first, rhs_first, sub_last, main_last, sup_last, rhs_last]
        )
        gathered = lax.all_gather(reduced_rows, "gz", axis=0, tiled=True)
        segments = gathered.shape[0] // 8
        system = gathered.reshape((2 * segments, 4) + zeroed_layer.shape)
        reduced_sol = thomas(system[:, 0], system[:, 1], system[:, 2], system[:, 3])
        own_pair = lax.dynamic_slice_in_dim(reduced_sol, 2 * lax.axis_index("gz"), 2, 0)
        face_first = own_pair[0]
        face_last = own_pair[1]
        inner = particular + face_first[None] * left_part + face_last[None] * right_part
        return jnp.concatenate([face_first[None], inner, face_last[None]], axis=0)

    half = jnp.where((colour == 0)[None], line_solve(pressure), pressure)
    smoothed = jnp.where((colour == 1)[None], line_solve(half), half)
    return (log_perm, smoothed)


LANES = 128
ROWS = 8
F32 = jnp.float32
MIB = 1 << 20
SUMS_GRANT = 60


def suits(mesh):
    sizes = dict(mesh.shape)
    return sizes["gx"] == 2 and sizes["gz"] == 4 and sizes["gy"] == 4


def params(mib):
    return pltpu.CompilerParams(vmem_limit_bytes=mib * MIB)


def cos_sin(turns):
    quarter = (turns + NX // 8) >> 9
    angle = (turns - (quarter << 9)).astype(F32) * (2.0 * math.pi / NX)
    square = angle * angle
    sine = angle * (
        1.0
        + square * (-1.0 / 6 + square * (1.0 / 120 + square * (-1.0 / 5040 + square / 362880)))
    )
    cosine = 1.0 + square * (
        -0.5 + square * (1.0 / 24 + square * (-1.0 / 720 + square * (1.0 / 40320)))
    )
    odd = (quarter & 1) == 1
    first = jnp.where(odd, sine, cosine)
    second = jnp.where(odd, cosine, sine)
    cos_sign = jnp.where(((quarter + 1) & 2) == 2, -1.0, 1.0)
    sin_sign = jnp.where((quarter & 2) == 2, -1.0, 1.0)
    return first * cos_sign, second * sin_sign


def split(values):
    high = values.astype(jnp.bfloat16)
    return high, (values - high.astype(F32)).astype(jnp.bfloat16)


def times(first, second):
    return (
        first[0] * second[0] - first[1] * second[1],
        first[0] * second[1] + first[1] * second[0],
    )


def plus(first, second):
    return (first[0] + second[0], first[1] + second[1])


def minus(first, second):
    return (first[0] - second[0], first[1] - second[1])


def quarter_turn(value):
    return (-value[1], value[0])


def four_point(first, second, third, fourth):
    even, gap = plus(first, third), minus(first, third)
    odd, turned = plus(second, fourth), quarter_turn(minus(second, fourth))
    return [plus(even, odd), plus(gap, turned), minus(even, odd), minus(gap, turned)]


def eight_point(values):
    even = four_point(*values[0::2])
    odd = four_point(*values[1::2])
    root = math.sqrt(0.5)
    real, imag = odd[1]
    odd[1] = (root * (real - imag), root * (real + imag))
    odd[2] = quarter_turn(odd[2])
    real, imag = odd[3]
    odd[3] = (-root * (real + imag), root * (real - imag))
    return [plus(*pair) for pair in zip(even, odd)] + [minus(*pair) for pair in zip(even, odd)]


def fill_tables(basis, turns):
    groups = NX // LANES
    shape = (LANES, LANES)
    lane = lane_of(shape)
    cells = (lane % groups) * (LANES // groups) + lane // groups
    cosine, sine = cos_sin((row_of(shape) * cells) % LANES * groups)
    for at, value in enumerate((cosine, -sine)):
        rows = slice(at * LANES, (at + 1) * LANES)
        high, low = split(value * (1.0 / math.sqrt(NX)))
        basis[0, rows], basis[1, rows], basis[2, rows] = high, high, low
    shape = (groups, LANES)
    turns[0], turns[1] = cos_sin(row_of(shape) * lane_of(shape))


def diagonal_of(depth):
    square = (depth, depth)
    return row_of(square) == lane_of(square)


def shift_columns(shifts, rows_of, columns):
    depth = shifts.shape[1]
    diagonal = diagonal_of(depth)
    for at, y in enumerate(rows_of):
        spread = jnp.where(diagonal, shifts[y : y + 1, :].astype(F32), 0.0)
        shift = jnp.broadcast_to(jnp.sum(spread, axis=1, keepdims=True), (depth, LANES))
        columns[at * depth : (at + 1) * depth, :] = shift.astype(jnp.int32)


def edge_columns(ys, depth, edges, kept):
    kept[...] = jnp.zeros_like(kept)
    diagonal = diagonal_of(depth)
    for at in range(len(ys)):
        rows = slice(at * depth, (at + 1) * depth)
        for side in range(edges.shape[0]):
            lane = 0 if side % 2 else LANES - 1
            column = jnp.broadcast_to(edges[side, rows, lane : lane + 1], (depth, depth))
            row = jnp.sum(jnp.where(diagonal, column, 0.0), axis=0, keepdims=True)
            kept[side, at : at + 1, :depth] = row


def twisted(first_wave, shift, coefficients, rows):
    lane = lane_of(shift.shape)
    phase = cos_sin((shift * (lane + first_wave)) & (NX - 1))
    turn = cos_sin((shift * LANES) & (NX - 1))
    values = []
    for part in range(coefficients.shape[0]):
        values.append(times((coefficients[part, 0, rows], coefficients[part, 1, rows]), phase))
        phase = times(phase, turn)
    return values


def interleave(tiles):
    count = len(tiles)
    lane = lane_of(tiles[0].shape)
    bit = count // 2
    while bit:
        low = (lane & bit) == 0
        moved = list(tiles)
        for at in range(count):
            if not at & bit:
                first, second = tiles[at], tiles[at | bit]
                crossed = jnp.take_along_axis(
                    jnp.where(low, second, first), lane ^ bit, axis=1
                )
                moved[at] = jnp.where(low, first, crossed)
                moved[at | bit] = jnp.where(low, crossed, second)
        tiles = moved
        bit //= 2
    return tiles


def row_sums(g, at, y, depth, items, columns, coefficients, basis, turns, left, right, emit):
    groups = NX // LANES
    sign = 1.0 - 2.0 * g.astype(F32)
    first_wave = g * (coefficients.shape[0] * LANES)
    step = 16
    for part in range(depth // step):
        rows = pl.ds(part * step * items + y, step, stride=items)
        shift = columns[pl.ds(at * depth + part * step, step), :]
        values = twisted(first_wave, shift, coefficients, rows)
        turned = [
            times(value, (sign * math.cos(2 * math.pi * p / groups), sign * math.sin(2 * math.pi * p / groups)))
            if p
            else (sign * value[0], sign * value[1])
            for p, value in enumerate(values)
        ]
        even, odd = eight_point(values), eight_point(turned)
        for group in range(groups):
            value = odd[group // 2] if group % 2 else even[group // 2]
            if group:
                value = times(value, (turns[0, group : group + 1], turns[1, group : group + 1]))
            first = group * depth + part * step
            for place_of, piece in enumerate(value):
                for half, bits in enumerate(split(piece)):
                    target = (2 * half + place_of) * LANES
                    left[first : first + step, target : target + LANES] = bits
    spread = jnp.concatenate([left[...], left[:, : 2 * LANES]], axis=1)
    bases = basis[...].reshape(-1, LANES)
    right[...] = jnp.dot(spread, bases, preferred_element_type=F32)
    for part in range(depth // ROWS):
        tiles = [
            right[group * depth + part * ROWS : group * depth + (part + 1) * ROWS]
            for group in range(groups)
        ]
        emit(pl.ds(at * depth + part * ROWS, ROWS), interleave(tiles))


def load_coefficients(spectral, coefficients, arrivals):
    parts = coefficients.shape[0]
    copies = [
        pltpu.make_async_copy(
            spectral.at[:, :, part * LANES : (part + 1) * LANES],
            coefficients.at[part],
            arrivals.at[part],
        )
        for part in range(parts)
    ]
    for copy in copies:
        copy.start()
    return copies


def keep_edges(rows, tiles, edges):
    count = len(tiles) // 4
    for side in range(edges.shape[0]):
        edges[side, rows] = tiles[(side // 2 + 1) * count - 1 + side % 2]


def inner_sums_kernel(ys, shifts, spectral, pressure, other, own, kept, p_column, *refs):
    tile, sem, *refs = refs
    g = lax.axis_index("gx")
    width = pressure.shape[2]
    there = lane_slice(jnp.where(g == 0, width - LANES, 0), LANES)
    copy = pltpu.make_async_copy(pressure.at[:, :, there], tile, sem)
    copy.start()
    wide_sums_kernel(ys, shifts, spectral, other, own, kept, *refs)
    copy.wait()
    packed = jnp.zeros((ROWS, LANES), F32)
    for z in range(tile.shape[0]):
        packed = packed_with(z, packed, boundary_plane(g, tile[z]), 0)
    p_column[...] = packed


def wide_sums_kernel(ys, shifts, spectral, other, own, kept, *refs):
    columns, edges, coefficients, arrivals, *tables, left, right = refs
    items, depth = shifts.shape
    copies = load_coefficients(spectral, coefficients, arrivals)
    fill_tables(*tables)
    shift_columns(shifts, ys, columns)
    for copy in copies:
        copy.wait()
    g = lax.axis_index("gx")

    def emit(rows, tiles):
        half = len(tiles) // 2
        keep_edges(rows, tiles, edges)
        for tile, (low, high) in enumerate(zip(tiles[:half], tiles[half:])):
            there = slice(tile * LANES, (tile + 1) * LANES)
            other[rows, there] = jnp.where(g == 0, high, low)
            own[rows, there] = jnp.where(g == 0, low, high)

    for at, y in enumerate(ys):
        row_sums(
            *(g, at, y, depth, items, columns, coefficients, *tables),
            *(left.at[at % 2], right.at[at % 2], emit),
        )
    edge_columns(ys, depth, edges, kept)


def last_sums_kernel(ys, shifts, outer_kept, inner_kept, p_column, spectral, one, two, own, *refs):
    columns_own, kept, columns, edges, coefficients, arrivals, *tables, left, right = refs
    items, depth = shifts.shape
    copies = load_coefficients(spectral, coefficients, arrivals)
    fill_tables(*tables)
    shift_columns(shifts, ys, columns)
    for copy in copies:
        copy.wait()
    g = lax.axis_index("gx")

    def emit(rows, tiles):
        half = len(tiles) // 2
        keep_edges(rows, tiles, edges)
        others = []
        for tile, (low, high) in enumerate(zip(tiles[:half], tiles[half:])):
            own[rows, tile * LANES : (tile + 1) * LANES] = jnp.where(g == 0, low, high)
            others.append(jnp.where(g == 0, high, low))
        start = 0
        for ref in (one, two):
            count = ref.shape[1] // LANES
            for tile in range(count):
                ref[rows, tile * LANES : (tile + 1) * LANES] = jnp.where(
                    g == 0, others[start + tile], others[half - start - count + tile]
                )
            start += count

    for at, y in enumerate(ys):
        row_sums(
            *(g, at, y, depth, items, columns, coefficients, *tables),
            *(left.at[at % 2], right.at[at % 2], emit),
        )
    edge_columns(ys, depth, edges, kept)
    sides_of = [
        jnp.concatenate(
            [outer_kept[side, :1], inner_kept[side], kept[side], outer_kept[side, 1:]], axis=0
        )
        for side in range(6)
    ]
    low, high = sides_of[:3], sides_of[3:]
    own_sides = [jnp.where(g == 0, *pair) for pair in ((low[0], high[1]), (low[1], high[2]))]
    own_sides.append(jnp.where(g == 0, low[2], high[0]))
    other_sides = [jnp.where(g == 0, *pair) for pair in ((high[1], low[0]), (high[2], low[1]))]
    other_sides.append(jnp.where(g == 0, high[0], low[2]))
    for at in range(3):
        columns_own[at], columns_own[3 + at] = own_sides[at], other_sides[at]
    extra = slice(one.shape[0] - ROWS, one.shape[0])
    for at, piece in enumerate((*other_sides, own_sides[2], p_column[...])):
        one[extra, at * LANES : (at + 1) * LANES] = piece


SCALARS = pl.BlockSpec(memory_space=pltpu.SMEM)
ON_CHIP = pl.BlockSpec(memory_space=pltpu.VMEM)
IN_HBM = pl.BlockSpec(memory_space=pltpu.HBM)


def call(
    kernel, name, out_shape, args, flags=None, scratch=(), far=(), mib=20, flops=1, out=ON_CHIP
):
    specs = [ON_CHIP] * len(args) + [IN_HBM] * len(far)
    args = list(args) + list(far)
    if flags is not None:
        specs = [SCALARS] + specs
        args = [flags] + args
    return pl.pallas_call(
        kernel,
        out_shape=out_shape,
        in_specs=specs,
        out_specs=jax.tree.map(lambda _: out, out_shape),
        scratch_shapes=list(scratch),
        compiler_params=params(mib),
        cost_estimate=pl.CostEstimate(flops=flops, bytes_accessed=1, transcendentals=0),
        name=name,
    )(*args)


def roll(values, shift, axis):
    return pltpu.roll(values, shift % values.shape[axis], axis)


def lane_of(shape):
    return lax.broadcasted_iota(jnp.int32, shape, 1)


def row_of(shape):
    return lax.broadcasted_iota(jnp.int32, shape, 0)


def column_to(z, packed, target):
    return pltpu.roll(packed, (target - z) % LANES, 1)


def packed_with(z, packed, plane, lane):
    column = jnp.broadcast_to(plane[:, lane : lane + 1], (ROWS, LANES))
    return jnp.where(lane_of((ROWS, LANES)) == z, column, packed)


def inverse_of(values):
    return pl.reciprocal(values, approx=True)


def ordered(z, sums, depth):
    spread = pl.ds(z, ROWS, stride=depth)
    return jnp.concatenate([sums[at, spread] for at in range(sums.shape[0])], axis=1)


def place_tiles(sums, rows, first, values):
    for at in range(values.shape[1] // LANES):
        sums[(first >> 7) + at, rows] = values[:, at * LANES : (at + 1) * LANES]


def boundary_plane(g, plane):
    return jnp.where(g == 0, roll(plane[:, -LANES:], 1, 1), plane[:, :LANES])


def outer_field_kernel(depth, flags, own, other, pressure, to_near, to_middle):
    even = flags[16] == 0
    low, high = slice(0, depth), slice(depth, 2 * depth)
    south, north = own[low] + other[low], own[high] + other[high]
    to_near[low] = jnp.exp(-jnp.where(even, north, south))
    to_middle[low] = jnp.exp(-jnp.where(even, south, north))

    for z in range(depth):
        keep_rows(depth + z, pressure[z], even, to_near, to_middle, slice(None))


def wide_field_kernel(depth, flags, *refs):
    own_outer, outer, own_inner, inner, to_near, to_middle = refs[:6]
    from_near, from_middle, pressure = refs[6:9]
    wide, south_weight, north_weight, p_south, p_north, p_west, p_east = refs[9:16]
    south_rows, north_rows = refs[16:]
    even = flags[16] == 0
    low, high = slice(0, depth), slice(depth, 2 * depth)
    wide[low] = own_outer[low] + outer[low]
    wide[depth:-depth] = own_inner[...] + inner[...]
    wide[-depth:] = own_outer[high] + outer[high]
    near_weight = 2.0 * inverse_of(to_near[low] + from_near[low])
    middle_weight = (2.0 * flags[15].astype(F32)) * inverse_of(to_middle[low] + from_middle[low])
    south = jnp.where(even, middle_weight, near_weight)
    south_weight[...] = south
    north_weight[...] = jnp.where(even, near_weight, middle_weight)
    south_rows[...] = jnp.where(even, from_middle[high], from_near[high])
    north_rows[...] = jnp.where(even, from_near[high], from_middle[high])
    row = row_of(pressure.shape[1:])

    def layer(z, carry):
        plane = pressure[z]
        p_south[z] = jnp.where(row == 0, south_rows[pl.ds(z, 1), :], roll(plane, 1, 0))
        p_north[z] = jnp.where(row == ROWS - 1, north_rows[pl.ds(z, 1), :], roll(plane, -1, 0))
        p_west[z] = roll(plane, 1, 1)
        p_east[z] = roll(plane, -1, 1)
        return carry

    lax.fori_loop(0, depth, layer, 0, unroll=True)


def lane_slice(start, size):
    return pl.ds(pl.multiple_of(start, LANES), size)


def assemble(sums, depth, wide, own, piece, there):
    inside = wide.shape[0] - depth
    place_tiles(sums, slice(0, inside), 0, wide[:inside, there])
    place_tiles(sums, slice(inside, -depth), 0, own[:, there] + piece[: own.shape[0]])
    place_tiles(sums, slice(-depth, None), 0, wide[inside:, there])


def first_field_kernel(depth, flags, *refs):
    wide, own, middle, columns_own = refs[:4]
    log_perm, resist, low_side, high_side, boundary, column, p_column, sums = refs[4:]
    extra = slice(own.shape[0], own.shape[0] + ROWS)
    came = [middle[extra, at * LANES : (at + 1) * LANES] for at in range(5)]
    for at, ref in enumerate((low_side, high_side, boundary)):
        ref[...] = jnp.exp(-(columns_own[at] + came[at]))
    column[...] = jnp.exp(-(columns_own[5] + came[3]))
    p_column[...] = came[4]
    assemble(sums, depth, wide, own, middle, lane_slice(flags[3], log_perm.shape[2]))

    def layer(z, carry):
        plane = ordered(z, sums, depth)
        log_perm[z] = plane
        resist[z] = jnp.exp(-plane)
        return carry

    lax.fori_loop(0, depth, layer, 0, unroll=True)


def second_field_kernel(depth, flags, *refs):
    wide, own, middle, resist_near = refs[:4]
    log_perm, resist, sums = refs[4:]
    third = middle.shape[1]
    assemble(sums, depth, wide, own, middle, lane_slice(flags[5], third))
    extra = resist.shape[2] - third
    target = lane_slice(flags[5] - flags[7], third)
    extra_target = lane_slice(flags[8], extra)
    extra_source = lane_slice(flags[9], extra)

    def layer(z, carry):
        plane = ordered(z, sums, depth)
        log_perm[z] = plane
        resist[z, :, target] = jnp.exp(-plane)
        resist[z, :, extra_target] = resist_near[z, :, extra_source]
        return carry

    lax.fori_loop(0, depth, layer, 0, unroll=True)


def join_columns_kernel(depth, flags, near, far, _, whole):
    def layer(z, carry):
        whole[z, :, lane_slice(flags[3], near.shape[2])] = near[z]
        whole[z, :, lane_slice(flags[5], far.shape[2])] = far[z]
        return carry

    lax.fori_loop(0, depth, layer, 0, unroll=True)


def keep_rows(z, value, even, to_near, to_middle, here):
    south, north = value[0:1, :], value[ROWS - 1 : ROWS, :]
    to_near[pl.ds(z, 1), here] = jnp.where(even, north, south)
    to_middle[pl.ds(z, 1), here] = jnp.where(even, south, north)


def with_first(plane, edge):
    first = jnp.where(lane_of((ROWS, LANES)) == 0, edge, plane[:, :LANES])
    return jnp.concatenate([first, plane[:, LANES:]], axis=1)


def with_last(plane, edge):
    last = jnp.where(lane_of((ROWS, LANES)) == LANES - 1, edge, plane[:, -LANES:])
    return jnp.concatenate([plane[:, :-LANES], last], axis=1)


def coupling(z, field, start, size, east_weight, north_weight, south_terms, north_rows, west, column):
    here = lane_slice(start, size)
    plane = field[z, :, here]
    row = row_of(plane.shape)
    at_start = start == 0
    inner = field[z, :, lane_slice(jnp.where(at_start, size, size - LANES), LANES)]
    west_value = jnp.where(at_start, column_to(z, column, 0), roll(inner, 1, 1))
    east_value = jnp.where(at_start, roll(inner, -1, 1), column_to(z, column, LANES - 1))
    to_east, to_north = east_weight * plane, north_weight * plane
    from_west = with_first(roll(to_east, 1, 1), column_to(z, west, 0) * west_value)
    from_east = east_weight * with_last(roll(plane, -1, 1), east_value)
    from_south = jnp.where(row == 0, south_terms[pl.ds(z, 1), here], roll(to_north, 1, 0))
    from_north = north_weight * jnp.where(
        row == ROWS - 1, north_rows[pl.ds(z, 1), here], roll(plane, -1, 0)
    )
    return (from_west + from_east) + (from_south + from_north)


def edge_weights(flags, start, bound, column, low_side, high_side):
    g = flags[0]
    middle = 2.0 * inverse_of(low_side + high_side)
    across = 2.0 * inverse_of(bound + column)
    none = jnp.zeros_like(across)
    west = jnp.where(start == 0, jnp.where(g == 0, none, across), middle)
    east = jnp.where(start == 0, middle, jnp.where(g == 0, across, none))
    return west, east


def first_sweep_kernel(depth, vert, block, flags, *refs):
    resist, low_side, high_side, r_bound, r_column, p_column = refs[:6]
    south_weight, north_weight, p_south, p_north, p_west, p_east = refs[6:12]
    source = refs[12]
    w_east, w_north, west_out, particular, inverse, ratio, lead, reduced = refs[13:21]
    grounds, rights, verticals = refs[21:]
    start, offset = flags[6 + block], flags[10 + block]
    size = inverse.shape[2]
    shape = (ROWS, size)
    here = lane_slice(start, size)
    inside = lane_slice(offset, size)
    west_weight, east_weight = edge_weights(
        flags, start, r_bound[...], r_column[...], low_side[...], high_side[...]
    )
    west_out[...] = west_weight
    column = p_column[...]
    row = row_of(shape)

    def weigh(z, carry):
        plane = resist[z, :, inside]
        east = 2.0 * inverse_of(plane + roll(plane, -1, 1))
        east = with_last(east, column_to(z, east_weight, LANES - 1))
        west = with_first(roll(east, 1, 1), column_to(z, west_weight, 0))
        north = 2.0 * inverse_of(plane + roll(plane, -1, 0))
        north = jnp.where(row == ROWS - 1, north_weight[pl.ds(z, 1), here], north)
        south = jnp.where(row == 0, south_weight[pl.ds(z, 1), here], roll(north, 1, 0))
        w_east[z], w_north[z] = east, north
        grounds[z] = STORE + ((east + west) + (north + south))
        verticals[z] = (2.0 * vert) * inverse_of(
            plane + resist[jnp.minimum(z + 1, depth - 1), :, inside]
        )
        p_first, p_last = p_west[z, :, here], p_east[z, :, here]
        p_first = with_first(
            p_first, jnp.where(start == 0, column_to(z, column, 0), p_first[:, :LANES])
        )
        p_last = with_last(
            p_last, jnp.where(start == 0, p_last[:, -LANES:], column_to(z, column, LANES - 1))
        )
        rights[z] = source[z, :, here] + (
            (west * p_first + east * p_last)
            + (south * p_south[z, :, here] + north * p_north[z, :, here])
        )
        return carry

    lax.fori_loop(0, depth, weigh, 0, unroll=True)

    def layer(z, carry):
        conduct, flow, product, first_first, first_part = carry
        weight = verticals[z]
        reciprocal = inverse_of(conduct + weight)
        quotient = weight * reciprocal
        led = product * reciprocal
        inverse[z] = reciprocal
        ratio[z] = quotient
        lead[z] = led
        particular[z] = reciprocal * flow
        return (
            grounds[z + 1] + conduct * quotient,
            rights[z + 1] + flow * quotient,
            product * quotient,
            first_first + led * product,
            first_part + led * flow,
        )

    zero = jnp.zeros(shape, F32)
    conduct, flow, product, first_first, first_part = lax.fori_loop(
        0,
        depth - 1,
        layer,
        (grounds[0], rights[0], jnp.ones(shape, F32), zero, zero),
        unroll=True,
    )
    reciprocal = inverse_of(conduct)
    led = product * reciprocal
    inverse[depth - 1] = reciprocal
    ratio[depth - 1] = zero
    lead[depth - 1] = led
    particular[depth - 1] = flow * reciprocal
    reduced[0] = first_first + led * product + resist[0, :, inside] * (0.5 / vert)
    reduced[1] = led
    reduced[2] = reciprocal + resist[depth - 1, :, inside] * (0.5 / vert)
    reduced[3] = first_part + led * flow
    reduced[4] = flow * reciprocal


def pair_kernel(flags, own, near, across, kept):
    me = flags[14]
    even, lower = me % 2 == 0, me < 2
    first, second = [
        [jnp.where(flip, own[at], near[at]) for at in range(5)]
        for flip in (even, jnp.logical_not(even))
    ]
    reciprocal = inverse_of(first[2] + second[0])
    step = (first[4] - second[3]) * reciprocal
    through = jnp.where(lower, second[1], first[1])
    share = through * reciprocal
    across[0] = jnp.where(lower, second[2], first[0]) - through * share
    across[1] = jnp.where(lower, second[4], first[3]) + jnp.where(
        lower, through * step, -through * step
    )
    kept[0], kept[1], kept[2] = share, reciprocal, step


def ends(me, inner, middle):
    zero = jnp.zeros_like(inner)
    odd = me % 2 == 1
    enters = jnp.where(odd, inner, jnp.where(me == 2, middle, zero))
    leaves = jnp.where(odd, jnp.where(me == 1, middle, zero), inner)
    return enters, leaves


def back_substitute(depth, lines, emit):
    last = depth - 1
    values = tuple(
        (particular[last] + lead[last] * enters) - inverse[last] * leaves
        for enters, leaves, particular, inverse, ratio, lead in lines
    )
    state = emit(last, values, jnp.zeros((ROWS, LANES), F32))

    for z in range(last - 1, -1, -1):
        values = tuple(
            (particular[z] + lead[z] * enters) + ratio[z] * beyond
            for (enters, _, particular, _, ratio, lead), beyond in zip(lines, values)
        )
        state = emit(z, values, state)
    return state


def half_kernel(depth, flags, *refs):
    pairs = (refs[0:3], refs[3:6])
    blocks = (refs[6:10], refs[10:14])
    pressure, colour = refs[14:16]
    half, to_near, to_middle, boundary, joined = refs[16:]
    me, g, even = flags[14], flags[0], flags[16] == 0
    size = blocks[0][0].shape[2]
    spans = [lane_slice(flags[6 + block], size) for block in range(2)]
    lines = []
    for block, state in enumerate(blocks):
        across, other, kept = pairs[block]
        sum_of = inverse_of(across[0] + other[0])
        joined[block] = sum_of
        lead_of = across[1] - other[1]
        middle = jnp.where(me < 2, lead_of, -lead_of) * sum_of
        inner = kept[2] + kept[0] * middle
        lines.append((*ends(me, inner, middle), *state))
    chosen = [colour[:, here] == 0 for here in spans]

    def emit(z, values, packed):
        for block, (value, here) in enumerate(zip(values, spans)):
            value = jnp.where(chosen[block], value, pressure[z, :, here])
            half[z, :, here] = value
            keep_rows(z, value, even, to_near, to_middle, here)
            if not block:
                packed = packed_with(z, packed, boundary_plane(g, value), 0)
        return packed

    boundary[...] = back_substitute(depth, lines, emit)


def second_sweep_kernel(depth, flags, *refs):
    half, h_near, h_middle, h_column, source, south_weight = refs[:6]
    shares = refs[6:8]
    blocks = (refs[8:14], refs[14:20])
    particulars, near, far = refs[20:22], refs[22], refs[23]
    south_terms, north_rows = refs[24:]
    me, even = flags[14], flags[16] == 0
    size = particulars[0].shape[2]
    starts = [flags[6 + block] for block in range(2)]
    spans = [lane_slice(start, size) for start in starts]
    column = h_column[...]
    south_terms[...] = south_weight[...] * jnp.where(even, h_middle[...], h_near[...])
    north_rows[...] = jnp.where(even, h_near[...], h_middle[...])

    def local(z, block):
        east, north, west = blocks[block][:3]
        return source[z, :, spans[block]] + coupling(
            z,
            half,
            starts[block],
            size,
            east[z],
            north[z],
            south_terms,
            north_rows,
            west[...],
            column,
        )

    def layer(z, carry):
        result = []
        for block, (flow, first_part) in enumerate(carry):
            inverse, ratio, lead = blocks[block][3:6]
            particulars[block][z] = flow * inverse[z]
            first_part = first_part + lead[z] * flow
            result.append((local(z + 1, block) + flow * ratio[z], first_part))
        return tuple(result)

    carry = tuple((local(0, block), jnp.zeros((ROWS, size), F32)) for block in range(2))
    carry = lax.fori_loop(0, depth - 1, layer, carry, unroll=True)
    last = depth - 1
    for block, (flow, first_part) in enumerate(carry):
        inverse, ratio, lead = blocks[block][3:6]
        there = slice(block * size, (block + 1) * size)
        first_part = first_part + lead[last] * flow
        last_part = flow * inverse[last]
        particulars[block][last] = last_part
        asked = jnp.where(me % 2 == 0, last_part, first_part)
        shared = shares[block][0] * asked
        outer = jnp.where(me == 1, last_part, jnp.where(me == 2, first_part, 0.0))
        given = outer + jnp.where((me == 0) | (me == 3), shared, -shared)
        near[0, :, there] = asked
        near[1, :, there] = given
        far[:, there] = given


def smoothed_kernel(depth, flags, *refs):
    own, near, skip, cross, joined = refs[:5]
    keeps = refs[5:7]
    blocks = (refs[7:11], refs[11:15])
    half, colour, result = refs[15:18]
    smoothed, sems = refs[18:]
    me = flags[14]
    size = blocks[0][0].shape[2]
    spans = [lane_slice(flags[6 + block], size) for block in range(2)]
    lines = []
    for block, state in enumerate(blocks):
        there = slice(block * size, (block + 1) * size)
        kept = keeps[block]
        lead_of = (own[1, :, there] + near[1, :, there]) - (skip[:, there] + cross[:, there])
        middle = jnp.where(me < 2, lead_of, -lead_of) * joined[block]
        step = own[0, :, there] - near[0, :, there]
        step = jnp.where(me % 2 == 0, step, -step) * kept[1]
        lines.append((*ends(me, step + kept[0] * middle, middle), *state))
    chosen = [colour[:, here] == 1 for here in spans]
    count = sems.shape[0]
    layers = depth // count
    copies = [
        pltpu.make_async_copy(
            smoothed.at[pl.ds(at * layers, layers)],
            result.at[pl.ds(at * layers, layers)],
            sems.at[at],
        )
        for at in range(count)
    ]

    def emit(z, values, state):
        for value, here, mine in zip(values, spans, chosen):
            smoothed[z, :, here] = jnp.where(mine, value, half[z, :, here])
        if z % layers == 0:
            copies[z // layers].start()
        return state

    back_substitute(depth, lines, emit)
    for copy in copies:
        copy.wait()


PAIR = [(0, 1), (1, 0)]
NEAR = [(0, 1), (1, 0), (2, 3), (3, 2)]
MIDDLE = [(1, 2), (2, 1)]
SKIP = [(0, 2), (2, 0), (1, 3), (3, 1)]
CROSS = [(0, 3), (3, 0), (1, 2), (2, 1)]


def exchange_edges(edges):
    to_near, to_middle, *column = edges
    return [
        lax.ppermute(to_near, "gy", NEAR),
        lax.ppermute(to_middle, "gy", MIDDLE),
        *[lax.ppermute(piece, "gx", PAIR) for piece in column],
    ]


def fast_body(spectral, shifts, colour, pressure, source):
    depth, items, width = pressure.shape
    vert = float((depth * 4) ** 2 // 4)
    waves = spectral.shape[3]
    rows = depth * items
    gx, gz, gy = (lax.axis_index(axis) for axis in ("gx", "gz", "gy"))
    block_size, third = width // 2, 3 * width // 8
    known = width - third

    def placed(start, size):
        return jnp.where(gx == 1, start, width - start - size)

    block_one, block_two = placed(0, block_size), placed(block_size, block_size)
    start_one = placed(0, known)
    extra = known - block_size
    flags = jnp.stack(
        [
            gx,
            placed(0, LANES),
            placed(LANES, known - LANES),
            start_one,
            jnp.zeros_like(gx),
            placed(known, third),
            block_one,
            block_two,
            placed(block_size, extra) - block_two,
            placed(block_size, extra) - start_one,
            block_one - start_one,
            jnp.zeros_like(gx),
            gy > 0,
            gy < 3,
            gz,
            (gy == 1) | (gy == 2),
            gy % 2,
        ]
    ).astype(jnp.int32)

    def shaped(*shape, dtype=F32):
        return jax.ShapeDtypeStruct(shape, dtype)

    groups = NX // LANES
    parts = waves // LANES
    inner_ys, last_ys = (1, 2, 3), tuple(range(4, items - 1))
    last_rows = len(last_ys) * depth
    column_type = shaped(ROWS, LANES)
    coefficients = spectral.reshape(2, rows, waves)

    def scratch(count):
        return [
            pltpu.VMEM((count, LANES), jnp.int32),
            pltpu.VMEM((6, count, LANES), F32),
            pltpu.VMEM((parts, 2, rows, LANES), F32),
            pltpu.SemaphoreType.DMA((parts,)),
            pltpu.VMEM((3, 2 * LANES, LANES), jnp.bfloat16),
            pltpu.VMEM((2, groups, LANES), F32),
            pltpu.VMEM((2, groups * depth, 4 * LANES), jnp.bfloat16),
            pltpu.VMEM((2, groups * depth, LANES), F32),
        ]

    def wide_types(ys):
        return [shaped(len(ys) * depth, width)] * 2 + [shaped(6, len(ys), LANES)]

    shift_rows = shifts.T
    outer_ys = (0, items - 1)
    sums, own_outer, outer_kept = call(
        functools.partial(wide_sums_kernel, outer_ys),
        "outer_row_sums",
        wide_types(outer_ys),
        [shift_rows],
        scratch=scratch(2 * depth),
        far=[coefficients],
        mib=SUMS_GRANT,
    )
    outer = lax.ppermute(sums, "gx", PAIR)
    shift_rows, _ = lax.optimization_barrier((shift_rows, own_outer))
    sums, own_inner, inner_kept, p_column = call(
        functools.partial(inner_sums_kernel, inner_ys),
        "inner_row_sums",
        wide_types(inner_ys) + [column_type],
        [shift_rows],
        scratch=[pltpu.VMEM((depth, ROWS, LANES), F32), pltpu.SemaphoreType.DMA]
        + scratch(len(inner_ys) * depth),
        far=[coefficients, pressure],
        mib=20,
    )
    inner = lax.ppermute(sums, "gx", PAIR)
    edge_row, edge_column = shaped(depth, width), shaped(ROWS, LANES)
    edges = [edge_row, edge_row, edge_column]
    pressure_rows, _ = lax.optimization_barrier((pressure, own_inner))
    to_near, to_middle = call(
        functools.partial(outer_field_kernel, depth),
        "outer_field",
        [shaped(2 * depth, width)] * 2,
        [own_outer, outer, pressure_rows],
        flags,
    )
    from_near, from_middle = exchange_edges([to_near, to_middle])
    last_one, last_two, own_last, own_columns = call(
        functools.partial(last_sums_kernel, last_ys),
        "last_row_sums",
        [
            shaped(last_rows + ROWS, known),
            shaped(last_rows, third),
            shaped(last_rows, width),
            shaped(6, ROWS, LANES),
        ],
        [shift_rows, outer_kept, inner_kept, p_column],
        scratch=[pltpu.VMEM((6, len(last_ys), LANES), F32)] + scratch(last_rows),
        far=[coefficients],
        mib=20,
    )
    last_one = lax.ppermute(last_one, "gx", PAIR)
    wide, *around = call(
        functools.partial(wide_field_kernel, depth),
        "wide_field",
        [shaped(rows - last_rows, width)] + [edge_row] * 2 + [shaped(depth, items, width)] * 4,
        [
            *(own_outer, outer, own_inner, inner, to_near, to_middle),
            *(from_near, from_middle, pressure),
        ],
        flags,
        [pltpu.VMEM((depth, width), F32)] * 2,
    )
    last_two, _ = lax.optimization_barrier((last_two, wide))
    last_two = lax.ppermute(last_two, "gx", PAIR)
    log_near, resist_near, *columns = call(
        functools.partial(first_field_kernel, depth),
        "first_field",
        [shaped(depth, items, known)] * 2 + [edge_column] * 5,
        [wide, own_last, last_one, own_columns],
        flags,
        [pltpu.VMEM((known // LANES, rows, LANES), F32)],
    )
    block = shaped(depth, items, block_size)

    state_types = [block] * 2 + [edge_column] + [block] * 4

    def first_sweep(at, resist):
        return call(
            functools.partial(first_sweep_kernel, depth, vert, at),
            "first_sweep",
            state_types + [shaped(5, items, block_size)],
            [resist, *columns, *around, source],
            flags,
            [pltpu.VMEM((depth, items, block_size), F32)] * 3,
        )

    *state_one, reduced_one = first_sweep(0, resist_near)
    near_one = lax.ppermute(reduced_one, "gz", NEAR)
    last_two, _ = lax.optimization_barrier((last_two, reduced_one))
    log_far, resist_far = call(
        functools.partial(second_field_kernel, depth),
        "second_field",
        [shaped(depth, items, third), block],
        [wide, own_last, last_two, resist_near],
        flags,
        [pltpu.VMEM((third // LANES, rows, LANES), F32)],
    )
    *state_two, reduced_two = first_sweep(1, resist_far)
    near_two = lax.ppermute(reduced_two, "gz", NEAR)
    (log_perm,) = call(
        functools.partial(join_columns_kernel, depth),
        "log_perm",
        [shaped(depth, items, width)],
        [log_near, log_far, reduced_two],
        flags,
    )
    def join(reduced, near):
        across, kept = call(
            pair_kernel,
            "join_pair",
            [shaped(2, items, block_size), shaped(3, items, block_size)],
            [reduced, near],
            flags,
        )
        return across, lax.ppermute(across, "gz", SKIP), kept

    pair_one, pair_two = join(reduced_one, near_one), join(reduced_two, near_two)
    keeps = [pair_one[2], pair_two[2]]
    half, *h_edges, joined = call(
        functools.partial(half_kernel, depth),
        "half",
        [shaped(depth, items, width), *edges, shaped(2, items, block_size)],
        [*pair_one, *pair_two, *state_one[3:], *state_two[3:], pressure, colour],
        flags,
    )
    h_edges = exchange_edges(h_edges)
    weights = [[*state[:3], *state[4:]] for state in (state_one, state_two)]
    current_one, current_two, to_near, to_far = call(
        functools.partial(second_sweep_kernel, depth),
        "second_sweep",
        [block, block, shaped(2, items, width), shaped(items, width)],
        [half, *h_edges, source, around[0], *keeps, *weights[0], *weights[1]],
        flags,
        [pltpu.VMEM((depth, width), F32)] * 2,
    )
    from_near, from_skip, from_cross = (
        lax.ppermute(planes, "gz", pairs)
        for planes, pairs in ((to_near, NEAR), (to_far, SKIP), (to_far, CROSS))
    )
    (smoothed,) = call(
        functools.partial(smoothed_kernel, depth),
        "smoothed",
        [shaped(depth, items, width)],
        [
            *(to_near, from_near, from_skip, from_cross, joined, *keeps),
            *(current_one, *state_one[4:]),
            *(current_two, *state_two[4:]),
            *(half, colour),
        ],
        flags,
        [pltpu.VMEM((depth, items, width), F32), pltpu.SemaphoreType.DMA((4,))],
        out=IN_HBM,
    )
    return (log_perm, smoothed)


def solution(mesh):
    body = fast_body if suits(mesh) else generic_body
    in_specs = (
        P(None, "gz", "gy", "gx"),
        P("gz", "gy"),
        P("gy", "gx"),
        P("gz", "gy", "gx"),
        P("gz", "gy", "gx"),
    )
    out_specs = (P("gz", "gy", "gx"), P("gz", "gy", "gx"))
    return jax.shard_map(body, mesh=mesh, in_specs=in_specs, out_specs=out_specs, check_vma=False)
```

```python
import functools
import math

import jax
import jax.numpy as jnp


from jax import lax
from jax.experimental import pallas as pl
from jax.experimental.pallas import tpu as pltpu
from jax.sharding import PartitionSpec as P

NX = 2048


STORE = 1.0


def padded_2(block, sides, width):
    for axis, dim in sides:
        count = lax.axis_size(axis)
        forward = [(i, i + 1) for i in range(count - 1)]
        backward = [(target, source) for source, target in forward]
        low = lax.ppermute(
            lax.slice_in_dim(block, block.shape[dim] - width, None, axis=dim), axis, forward
        )
        high = lax.ppermute(lax.slice_in_dim(block, 0, width, axis=dim), axis, backward)
        block = jnp.concatenate([low, block, high], axis=dim)
    return block


def twisted_coeffs(spectral, shifts, first_wave):
    count = spectral.shape[3]
    wave_index = first_wave + jnp.arange(count, dtype=jnp.int32)
    wave_turns = shifts[:, :, None] * wave_index[None, None, :] % NX
    phase_angle = wave_turns.astype(jnp.float32) * (2.0 * math.pi / NX)
    cosine = jnp.cos(phase_angle)
    sine_part = jnp.sin(phase_angle)
    real_part = spectral[0] * cosine - spectral[1] * sine_part
    imag_part = spectral[0] * sine_part + spectral[1] * cosine
    return jnp.stack([real_part, imag_part])


def basis(count, first_cell, width_cells):
    wave_index = jnp.arange(count, dtype=jnp.int32)
    cell_index = first_cell + jnp.arange(width_cells, dtype=jnp.int32)
    wave_turns = wave_index[:, None] * cell_index[None, :] % NX
    phase_angle = wave_turns.astype(jnp.float32) * (2.0 * math.pi / NX)
    offsets = jnp.concatenate(
        [jnp.zeros((count, 1), jnp.float32), jnp.full((count, 1), 0.5 * math.pi, jnp.float32)],
        axis=0,
    )
    stacked = jnp.concatenate([phase_angle, phase_angle], axis=0) + offsets
    return jnp.cos(stacked) * (1.0 / math.sqrt(NX))


def flatten_pair(piece):
    depth, items, count = (piece.shape[1], piece.shape[2], piece.shape[3])
    return jnp.concatenate(
        [piece[0].reshape(depth * items, count), piece[1].reshape(depth * items, count)], axis=1
    )


def harmonic(center, beside):
    return 2.0 * center * beside / (center + beside)


def thomas(lower_diagonal, main_diagonal, upper_diagonal, right_hand_side):

    def thomas_forward_scan(carried_state, row_entries):
        previous_ratio, previous_eliminated = carried_state
        column_lower, main_c, sup_c, column_right_hand = row_entries
        present_denominator = main_c - column_lower * previous_ratio
        present_ratio = sup_c / present_denominator
        present_eliminated = (
            column_right_hand - column_lower * previous_eliminated
        ) / present_denominator
        return ((present_ratio, present_eliminated), (present_ratio, present_eliminated))

    zeroed_layer = jnp.zeros(right_hand_side.shape[1:], right_hand_side.dtype)
    unused_output, (ratio_rows, eliminated_rows) = lax.scan(
        thomas_forward_scan,
        (zeroed_layer, zeroed_layer),
        (lower_diagonal, main_diagonal, upper_diagonal, right_hand_side),
    )

    def thomas_backward_scan(following_value, row_entries):
        column_ratio, column_eliminated = row_entries
        present_value = column_eliminated - column_ratio * following_value
        return (present_value, present_value)

    unused_output, solved_values = lax.scan(
        thomas_backward_scan, zeroed_layer, (ratio_rows, eliminated_rows), reverse=True
    )
    return solved_values


def factor(lower_diagonal, main_diagonal, upper_diagonal):

    def factor_forward_scan(previous_ratio, row_entries):
        column_lower, main_c, sup_c = row_entries
        present_denominator = main_c - column_lower * previous_ratio
        present_ratio = sup_c / present_denominator
        return (present_ratio, (present_denominator, present_ratio))

    unused_output, (denominator_rows, ratio_rows) = lax.scan(
        factor_forward_scan,
        jnp.zeros_like(main_diagonal[0]),
        (lower_diagonal, main_diagonal, upper_diagonal),
    )
    return (denominator_rows, ratio_rows)


def solve_factored(lower_diagonal, denominator_rows, ratio_rows, right_hand_side):

    def solve_forward_scan(previous_eliminated, row_entries):
        column_lower, column_denominator, column_right_hand = row_entries
        present_eliminated = (
            column_right_hand - column_lower[None] * previous_eliminated
        ) / column_denominator[None]
        return (present_eliminated, present_eliminated)

    unused_output, eliminated_rows = lax.scan(
        solve_forward_scan,
        jnp.zeros_like(right_hand_side[0]),
        (lower_diagonal, denominator_rows, right_hand_side),
    )

    def solve_backward_scan(following_value, row_entries):
        column_ratio, column_eliminated = row_entries
        present_value = column_eliminated - column_ratio[None] * following_value
        return (present_value, present_value)

    unused_output, solved_values = lax.scan(
        solve_backward_scan,
        jnp.zeros_like(right_hand_side[0]),
        (ratio_rows, eliminated_rows),
        reverse=True,
    )
    return solved_values


def generic_body(spectral, shifts, colour, pressure, source):
    total_depth = pressure.shape[0] * lax.axis_size("gz")
    vert_factor = float(total_depth * total_depth // 4)
    width_cells = spectral.shape[3]
    first_cell = lax.axis_index("gx") * width_cells
    twisted = twisted_coeffs(spectral, shifts, first_cell)
    piece = lax.all_to_all(twisted, "gx", split_axis=1, concat_axis=3, tiled=True)
    depth = piece.shape[1]
    items = piece.shape[2]
    length = piece.shape[3]
    flat = flatten_pair(piece)
    block_width = min(512, length)
    blocks = [
        jnp.dot(
            flat,
            basis(length, block * block_width, block_width),
            precision=lax.Precision.HIGHEST,
            preferred_element_type=jnp.float32,
        )
        for block in range(length // block_width)
    ]
    field_rows = jnp.concatenate(blocks, axis=1).reshape(depth, items, length)
    log_perm = lax.all_to_all(field_rows, "gx", split_axis=2, concat_axis=0, tiled=True)
    perm = jnp.exp(log_perm)
    padded = padded_2(perm, (("gx", 2), ("gz", 0), ("gy", 1)), 1)
    w_zm = vert_factor * harmonic(perm, padded[:-2, 1:-1, 1:-1])
    w_zp = vert_factor * harmonic(perm, padded[2:, 1:-1, 1:-1])
    w_ym = harmonic(perm, padded[1:-1, :-2, 1:-1])
    w_yp = harmonic(perm, padded[1:-1, 2:, 1:-1])
    w_xm = harmonic(perm, padded[1:-1, 1:-1, :-2])
    w_xp = harmonic(perm, padded[1:-1, 1:-1, 2:])
    main_diagonal = STORE + w_xm + w_xp + w_ym + w_yp + w_zm + w_zp
    lower_diagonal = -w_zm
    upper_diagonal = -w_zp
    zeroed_layer = jnp.zeros_like(main_diagonal[0])
    inner_sub = jnp.concatenate([zeroed_layer[None], lower_diagonal[2:-1]], axis=0)
    inner_sup = jnp.concatenate([upper_diagonal[1:-2], zeroed_layer[None]], axis=0)
    inner_main = main_diagonal[1:-1]
    denominator_rows, ratio_rows = factor(inner_sub, inner_main, inner_sup)
    unit_rhs = jnp.zeros((inner_main.shape[0], 2) + zeroed_layer.shape, jnp.float32)
    unit_rhs = unit_rhs.at[0, 0].set(-lower_diagonal[1])
    unit_rhs = unit_rhs.at[-1, 1].set(-upper_diagonal[-2])
    coupled = solve_factored(inner_sub, denominator_rows, ratio_rows, unit_rhs)
    left_part = coupled[:, 0]
    right_part = coupled[:, 1]
    sub_first = lower_diagonal[0]
    main_first = main_diagonal[0] + upper_diagonal[0] * left_part[0]
    sup_first = upper_diagonal[0] * right_part[0]
    sub_last = lower_diagonal[-1] * left_part[-1]
    main_last = main_diagonal[-1] + lower_diagonal[-1] * right_part[-1]
    sup_last = upper_diagonal[-1]

    def line_solve(current):
        cycle = padded_2(current, (("gx", 2), ("gy", 1)), 1)
        right_hand_side = source + w_xm * cycle[:, 1:-1, :-2] + w_xp * cycle[:, 1:-1, 2:]
        right_hand_side = right_hand_side + w_ym * cycle[:, :-2, 1:-1] + w_yp * cycle[:, 2:, 1:-1]
        particular = solve_factored(
            inner_sub, denominator_rows, ratio_rows, right_hand_side[1:-1][:, None]
        )[:, 0]
        rhs_first = right_hand_side[0] - upper_diagonal[0] * particular[0]
        rhs_last = right_hand_side[-1] - lower_diagonal[-1] * particular[-1]
        reduced_rows = jnp.stack(
            [sub_first, main_first, sup_first, rhs_first, sub_last, main_last, sup_last, rhs_last]
        )
        gathered = lax.all_gather(reduced_rows, "gz", axis=0, tiled=True)
        segments = gathered.shape[0] // 8
        system = gathered.reshape((2 * segments, 4) + zeroed_layer.shape)
        reduced_sol = thomas(system[:, 0], system[:, 1], system[:, 2], system[:, 3])
        own_pair = lax.dynamic_slice_in_dim(reduced_sol, 2 * lax.axis_index("gz"), 2, 0)
        face_first = own_pair[0]
        face_last = own_pair[1]
        inner = particular + face_first[None] * left_part + face_last[None] * right_part
        return jnp.concatenate([face_first[None], inner, face_last[None]], axis=0)

    half = jnp.where((colour == 0)[None], line_solve(pressure), pressure)
    smoothed = jnp.where((colour == 1)[None], line_solve(half), half)
    return (log_perm, smoothed)


LANES = 128
ROWS = 8
F32 = jnp.float32
MIB = 1 << 20
SUMS_GRANT = 60


def suits(mesh):
    sizes = dict(mesh.shape)
    return sizes["gx"] == 2 and sizes["gz"] == 4 and sizes["gy"] == 4


def params(mib):
    return pltpu.CompilerParams(vmem_limit_bytes=mib * MIB)


def cos_sin(turns):
    quarter = (turns + NX // 8) >> 9
    angle = (turns - (quarter << 9)).astype(F32) * (2.0 * math.pi / NX)
    square = angle * angle
    sine = angle * (
        1.0
        + square * (-1.0 / 6 + square * (1.0 / 120 + square * (-1.0 / 5040 + square / 362880)))
    )
    cosine = 1.0 + square * (
        -0.5 + square * (1.0 / 24 + square * (-1.0 / 720 + square * (1.0 / 40320)))
    )
    odd = (quarter & 1) == 1
    first = jnp.where(odd, sine, cosine)
    second = jnp.where(odd, cosine, sine)
    cos_sign = jnp.where(((quarter + 1) & 2) == 2, -1.0, 1.0)
    sin_sign = jnp.where((quarter & 2) == 2, -1.0, 1.0)
    return first * cos_sign, second * sin_sign


def split(values):
    high = values.astype(jnp.bfloat16)
    return high, (values - high.astype(F32)).astype(jnp.bfloat16)


def times(first, second):
    return (
        first[0] * second[0] - first[1] * second[1],
        first[0] * second[1] + first[1] * second[0],
    )


def plus(first, second):
    return (first[0] + second[0], first[1] + second[1])


def minus(first, second):
    return (first[0] - second[0], first[1] - second[1])


def quarter_turn(value):
    return (-value[1], value[0])


def four_point(first, second, third, fourth):
    even, gap = plus(first, third), minus(first, third)
    odd, turned = plus(second, fourth), quarter_turn(minus(second, fourth))
    return [plus(even, odd), plus(gap, turned), minus(even, odd), minus(gap, turned)]


def eight_point(values):
    even = four_point(*values[0::2])
    odd = four_point(*values[1::2])
    root = math.sqrt(0.5)
    real, imag = odd[1]
    odd[1] = (root * (real - imag), root * (real + imag))
    odd[2] = quarter_turn(odd[2])
    real, imag = odd[3]
    odd[3] = (-root * (real + imag), root * (real - imag))
    return [plus(*pair) for pair in zip(even, odd)] + [minus(*pair) for pair in zip(even, odd)]


def fill_tables(basis, turns):
    groups = NX // LANES
    shape = (LANES, LANES)
    lane = lane_of(shape)
    cells = (lane % groups) * (LANES // groups) + lane // groups
    cosine, sine = cos_sin((row_of(shape) * cells) % LANES * groups)
    for at, value in enumerate((cosine, -sine)):
        rows = slice(at * LANES, (at + 1) * LANES)
        high, low = split(value * (1.0 / math.sqrt(NX)))
        basis[0, rows], basis[1, rows], basis[2, rows] = high, high, low
    shape = (groups, LANES)
    turns[0], turns[1] = cos_sin(row_of(shape) * lane_of(shape))


def diagonal_of(depth):
    square = (depth, depth)
    return row_of(square) == lane_of(square)


def shift_columns(shifts, rows_of, columns):
    depth = shifts.shape[1]
    diagonal = diagonal_of(depth)
    for at, y in enumerate(rows_of):
        spread = jnp.where(diagonal, shifts[y : y + 1, :].astype(F32), 0.0)
        shift = jnp.broadcast_to(jnp.sum(spread, axis=1, keepdims=True), (depth, LANES))
        columns[at * depth : (at + 1) * depth, :] = shift.astype(jnp.int32)


def edge_columns(ys, depth, edges, kept):
    kept[...] = jnp.zeros_like(kept)
    diagonal = diagonal_of(depth)
    for at in range(len(ys)):
        rows = slice(at * depth, (at + 1) * depth)
        for side in range(edges.shape[0]):
            lane = 0 if side % 2 else LANES - 1
            column = jnp.broadcast_to(edges[side, rows, lane : lane + 1], (depth, depth))
            row = jnp.sum(jnp.where(diagonal, column, 0.0), axis=0, keepdims=True)
            kept[side, at : at + 1, :depth] = row


def twisted(first_wave, shift, coefficients, rows):
    lane = lane_of(shift.shape)
    phase = cos_sin((shift * (lane + first_wave)) & (NX - 1))
    turn = cos_sin((shift * LANES) & (NX - 1))
    values = []
    for part in range(coefficients.shape[0]):
        values.append(times((coefficients[part, 0, rows], coefficients[part, 1, rows]), phase))
        phase = times(phase, turn)
    return values


def interleave(tiles):
    count = len(tiles)
    lane = lane_of(tiles[0].shape)
    bit = count // 2
    while bit:
        low = (lane & bit) == 0
        moved = list(tiles)
        for at in range(count):
            if not at & bit:
                first, second = tiles[at], tiles[at | bit]
                crossed = jnp.take_along_axis(
                    jnp.where(low, second, first), lane ^ bit, axis=1
                )
                moved[at] = jnp.where(low, first, crossed)
                moved[at | bit] = jnp.where(low, crossed, second)
        tiles = moved
        bit //= 2
    return tiles


def row_sums(g, at, y, depth, items, columns, coefficients, basis, turns, left, right, emit):
    groups = NX // LANES
    sign = 1.0 - 2.0 * g.astype(F32)
    first_wave = g * (coefficients.shape[0] * LANES)
    step = 16
    for part in range(depth // step):
        rows = pl.ds(part * step * items + y, step, stride=items)
        shift = columns[pl.ds(at * depth + part * step, step), :]
        values = twisted(first_wave, shift, coefficients, rows)
        turned = [
            times(value, (sign * math.cos(2 * math.pi * p / groups), sign * math.sin(2 * math.pi * p / groups)))
            if p
            else (sign * value[0], sign * value[1])
            for p, value in enumerate(values)
        ]
        even, odd = eight_point(values), eight_point(turned)
        for group in range(groups):
            value = odd[group // 2] if group % 2 else even[group // 2]
            if group:
                value = times(value, (turns[0, group : group + 1], turns[1, group : group + 1]))
            first = group * depth + part * step
            for place_of, piece in enumerate(value):
                for half, bits in enumerate(split(piece)):
                    target = (2 * half + place_of) * LANES
                    left[first : first + step, target : target + LANES] = bits
    spread = jnp.concatenate([left[...], left[:, : 2 * LANES]], axis=1)
    bases = basis[...].reshape(-1, LANES)
    right[...] = jnp.dot(spread, bases, preferred_element_type=F32)
    for part in range(depth // ROWS):
        tiles = [
            right[group * depth + part * ROWS : group * depth + (part + 1) * ROWS]
            for group in range(groups)
        ]
        emit(pl.ds(at * depth + part * ROWS, ROWS), interleave(tiles))


def load_coefficients(spectral, coefficients, arrivals):
    parts = coefficients.shape[0]
    copies = [
        pltpu.make_async_copy(
            spectral.at[:, :, part * LANES : (part + 1) * LANES],
            coefficients.at[part],
            arrivals.at[part],
        )
        for part in range(parts)
    ]
    for copy in copies:
        copy.start()
    return copies


def keep_edges(rows, tiles, edges):
    count = len(tiles) // 4
    for side in range(edges.shape[0]):
        edges[side, rows] = tiles[(side // 2 + 1) * count - 1 + side % 2]


def inner_sums_kernel(ys, shifts, spectral, pressure, other, own, kept, p_column, *refs):
    tile, sem, *refs = refs
    g = lax.axis_index("gx")
    width = pressure.shape[2]
    there = lane_slice(jnp.where(g == 0, width - LANES, 0), LANES)
    copy = pltpu.make_async_copy(pressure.at[:, :, there], tile, sem)
    copy.start()
    wide_sums_kernel(ys, shifts, spectral, other, own, kept, *refs)
    copy.wait()
    packed = jnp.zeros((ROWS, LANES), F32)
    for z in range(tile.shape[0]):
        packed = packed_with(z, packed, boundary_plane(g, tile[z]), 0)
    p_column[...] = packed


def wide_sums_kernel(ys, shifts, spectral, other, own, kept, *refs):
    columns, edges, coefficients, arrivals, *tables, left, right = refs
    items, depth = shifts.shape
    copies = load_coefficients(spectral, coefficients, arrivals)
    fill_tables(*tables)
    shift_columns(shifts, ys, columns)
    for copy in copies:
        copy.wait()
    g = lax.axis_index("gx")

    def emit(rows, tiles):
        half = len(tiles) // 2
        keep_edges(rows, tiles, edges)
        for tile, (low, high) in enumerate(zip(tiles[:half], tiles[half:])):
            there = slice(tile * LANES, (tile + 1) * LANES)
            other[rows, there] = jnp.where(g == 0, high, low)
            own[rows, there] = jnp.where(g == 0, low, high)

    for at, y in enumerate(ys):
        row_sums(
            *(g, at, y, depth, items, columns, coefficients, *tables),
            *(left.at[at % 2], right.at[at % 2], emit),
        )
    edge_columns(ys, depth, edges, kept)


def last_sums_kernel(ys, shifts, outer_kept, inner_kept, p_column, spectral, one, two, own, *refs):
    columns_own, kept, columns, edges, coefficients, arrivals, *tables, left, right = refs
    items, depth = shifts.shape
    copies = load_coefficients(spectral, coefficients, arrivals)
    fill_tables(*tables)
    shift_columns(shifts, ys, columns)
    for copy in copies:
        copy.wait()
    g = lax.axis_index("gx")

    def emit(rows, tiles):
        half = len(tiles) // 2
        keep_edges(rows, tiles, edges)
        others = []
        for tile, (low, high) in enumerate(zip(tiles[:half], tiles[half:])):
            own[rows, tile * LANES : (tile + 1) * LANES] = jnp.where(g == 0, low, high)
            others.append(jnp.where(g == 0, high, low))
        start = 0
        for ref in (one, two):
            count = ref.shape[1] // LANES
            for tile in range(count):
                ref[rows, tile * LANES : (tile + 1) * LANES] = jnp.where(
                    g == 0, others[start + tile], others[half - start - count + tile]
                )
            start += count

    for at, y in enumerate(ys):
        row_sums(
            *(g, at, y, depth, items, columns, coefficients, *tables),
            *(left.at[at % 2], right.at[at % 2], emit),
        )
    edge_columns(ys, depth, edges, kept)
    sides_of = [
        jnp.concatenate(
            [outer_kept[side, :1], inner_kept[side], kept[side], outer_kept[side, 1:]], axis=0
        )
        for side in range(6)
    ]
    low, high = sides_of[:3], sides_of[3:]
    own_sides = [jnp.where(g == 0, *pair) for pair in ((low[0], high[1]), (low[1], high[2]))]
    own_sides.append(jnp.where(g == 0, low[2], high[0]))
    other_sides = [jnp.where(g == 0, *pair) for pair in ((high[1], low[0]), (high[2], low[1]))]
    other_sides.append(jnp.where(g == 0, high[0], low[2]))
    for at in range(3):
        columns_own[at], columns_own[3 + at] = own_sides[at], other_sides[at]
    extra = slice(one.shape[0] - ROWS, one.shape[0])
    for at, piece in enumerate((*other_sides, own_sides[2], p_column[...])):
        one[extra, at * LANES : (at + 1) * LANES] = piece


ON_CHIP = pl.BlockSpec(memory_space=pltpu.VMEM)
IN_HBM = pl.BlockSpec(memory_space=pltpu.HBM)


def call(
    kernel, name, out_shape, args, flags=None, scratch=(), far=(), mib=20, flops=1, out=ON_CHIP
):
    specs = [ON_CHIP] * len(args) + [IN_HBM] * len(far)
    args = list(args) + list(far)
    body = kernel if flags is None else lambda *refs: kernel(flags(), *refs)
    return pl.pallas_call(
        body,
        out_shape=out_shape,
        in_specs=specs,
        out_specs=jax.tree.map(lambda _: out, out_shape),
        scratch_shapes=list(scratch),
        compiler_params=params(mib),
        cost_estimate=pl.CostEstimate(flops=flops, bytes_accessed=1, transcendentals=0),
        name=name,
    )(*args)


def roll(values, shift, axis):
    return pltpu.roll(values, shift % values.shape[axis], axis)


def lane_of(shape):
    return lax.broadcasted_iota(jnp.int32, shape, 1)


def row_of(shape):
    return lax.broadcasted_iota(jnp.int32, shape, 0)


def column_to(z, packed, target):
    return pltpu.roll(packed, (target - z) % LANES, 1)


def packed_with(z, packed, plane, lane):
    column = jnp.broadcast_to(plane[:, lane : lane + 1], (ROWS, LANES))
    return jnp.where(lane_of((ROWS, LANES)) == z, column, packed)


def inverse_of(values):
    return pl.reciprocal(values, approx=True)


def ordered(z, sums, depth):
    spread = pl.ds(z, ROWS, stride=depth)
    return jnp.concatenate([sums[at, spread] for at in range(sums.shape[0])], axis=1)


def place_tiles(sums, rows, first, values):
    for at in range(values.shape[1] // LANES):
        sums[(first >> 7) + at, rows] = values[:, at * LANES : (at + 1) * LANES]


def boundary_plane(g, plane):
    return jnp.where(g == 0, roll(plane[:, -LANES:], 1, 1), plane[:, :LANES])


def outer_field_kernel(depth, flags, own, other, pressure, to_near, to_middle):
    even = flags[16] == 0
    low, high = slice(0, depth), slice(depth, 2 * depth)
    south, north = own[low] + other[low], own[high] + other[high]
    to_near[low] = jnp.exp(-jnp.where(even, north, south))
    to_middle[low] = jnp.exp(-jnp.where(even, south, north))

    for z in range(depth):
        keep_rows(depth + z, pressure[z], even, to_near, to_middle, slice(None))


def wide_field_kernel(depth, flags, *refs):
    own_outer, outer, own_inner, inner, to_near, to_middle = refs[:6]
    from_near, from_middle, pressure = refs[6:9]
    wide, south_weight, north_weight, p_south, p_north, p_west, p_east = refs[9:16]
    south_rows, north_rows = refs[16:]
    even = flags[16] == 0
    low, high = slice(0, depth), slice(depth, 2 * depth)
    wide[low] = own_outer[low] + outer[low]
    wide[depth:-depth] = own_inner[...] + inner[...]
    wide[-depth:] = own_outer[high] + outer[high]
    near_weight = 2.0 * inverse_of(to_near[low] + from_near[low])
    middle_weight = (2.0 * flags[15].astype(F32)) * inverse_of(to_middle[low] + from_middle[low])
    south = jnp.where(even, middle_weight, near_weight)
    south_weight[...] = south
    north_weight[...] = jnp.where(even, near_weight, middle_weight)
    south_rows[...] = jnp.where(even, from_middle[high], from_near[high])
    north_rows[...] = jnp.where(even, from_near[high], from_middle[high])
    row = row_of(pressure.shape[1:])

    def layer(z, carry):
        plane = pressure[z]
        p_south[z] = jnp.where(row == 0, south_rows[pl.ds(z, 1), :], roll(plane, 1, 0))
        p_north[z] = jnp.where(row == ROWS - 1, north_rows[pl.ds(z, 1), :], roll(plane, -1, 0))
        p_west[z] = roll(plane, 1, 1)
        p_east[z] = roll(plane, -1, 1)
        return carry

    lax.fori_loop(0, depth, layer, 0, unroll=True)


def lane_slice(start, size):
    return pl.ds(pl.multiple_of(start, LANES), size)


def assemble(sums, depth, wide, own, piece, there):
    inside = wide.shape[0] - depth
    place_tiles(sums, slice(0, inside), 0, wide[:inside, there])
    place_tiles(sums, slice(inside, -depth), 0, own[:, there] + piece[: own.shape[0]])
    place_tiles(sums, slice(-depth, None), 0, wide[inside:, there])


def first_field_kernel(depth, flags, *refs):
    wide, own, middle, columns_own = refs[:4]
    log_perm, resist, low_side, high_side, boundary, column, p_column, sums = refs[4:]
    extra = slice(own.shape[0], own.shape[0] + ROWS)
    came = [middle[extra, at * LANES : (at + 1) * LANES] for at in range(5)]
    for at, ref in enumerate((low_side, high_side, boundary)):
        ref[...] = jnp.exp(-(columns_own[at] + came[at]))
    column[...] = jnp.exp(-(columns_own[5] + came[3]))
    p_column[...] = came[4]
    assemble(sums, depth, wide, own, middle, lane_slice(flags[3], log_perm.shape[2]))

    def layer(z, carry):
        plane = ordered(z, sums, depth)
        log_perm[z] = plane
        resist[z] = jnp.exp(-plane)
        return carry

    lax.fori_loop(0, depth, layer, 0, unroll=True)


def second_field_kernel(depth, flags, *refs):
    wide, own, middle, resist_near = refs[:4]
    log_perm, resist, sums = refs[4:]
    third = middle.shape[1]
    assemble(sums, depth, wide, own, middle, lane_slice(flags[5], third))
    extra = resist.shape[2] - third
    target = lane_slice(flags[5] - flags[7], third)
    extra_target = lane_slice(flags[8], extra)
    extra_source = lane_slice(flags[9], extra)

    def layer(z, carry):
        plane = ordered(z, sums, depth)
        log_perm[z] = plane
        resist[z, :, target] = jnp.exp(-plane)
        resist[z, :, extra_target] = resist_near[z, :, extra_source]
        return carry

    lax.fori_loop(0, depth, layer, 0, unroll=True)


def join_columns_kernel(depth, flags, near, far, _, whole):
    def layer(z, carry):
        whole[z, :, lane_slice(flags[3], near.shape[2])] = near[z]
        whole[z, :, lane_slice(flags[5], far.shape[2])] = far[z]
        return carry

    lax.fori_loop(0, depth, layer, 0, unroll=True)


def keep_rows(z, value, even, to_near, to_middle, here):
    south, north = value[0:1, :], value[ROWS - 1 : ROWS, :]
    to_near[pl.ds(z, 1), here] = jnp.where(even, north, south)
    to_middle[pl.ds(z, 1), here] = jnp.where(even, south, north)


def with_first(plane, edge):
    first = jnp.where(lane_of((ROWS, LANES)) == 0, edge, plane[:, :LANES])
    return jnp.concatenate([first, plane[:, LANES:]], axis=1)


def with_last(plane, edge):
    last = jnp.where(lane_of((ROWS, LANES)) == LANES - 1, edge, plane[:, -LANES:])
    return jnp.concatenate([plane[:, :-LANES], last], axis=1)


def coupling(z, field, start, size, east_weight, north_weight, south_terms, north_rows, west, column):
    here = lane_slice(start, size)
    plane = field[z, :, here]
    row = row_of(plane.shape)
    at_start = start == 0
    inner = field[z, :, lane_slice(jnp.where(at_start, size, size - LANES), LANES)]
    west_value = jnp.where(at_start, column_to(z, column, 0), roll(inner, 1, 1))
    east_value = jnp.where(at_start, roll(inner, -1, 1), column_to(z, column, LANES - 1))
    to_east, to_north = east_weight * plane, north_weight * plane
    from_west = with_first(roll(to_east, 1, 1), column_to(z, west, 0) * west_value)
    from_east = east_weight * with_last(roll(plane, -1, 1), east_value)
    from_south = jnp.where(row == 0, south_terms[pl.ds(z, 1), here], roll(to_north, 1, 0))
    from_north = north_weight * jnp.where(
        row == ROWS - 1, north_rows[pl.ds(z, 1), here], roll(plane, -1, 0)
    )
    return (from_west + from_east) + (from_south + from_north)


def edge_weights(flags, start, bound, column, low_side, high_side):
    g = flags[0]
    middle = 2.0 * inverse_of(low_side + high_side)
    across = 2.0 * inverse_of(bound + column)
    none = jnp.zeros_like(across)
    west = jnp.where(start == 0, jnp.where(g == 0, none, across), middle)
    east = jnp.where(start == 0, middle, jnp.where(g == 0, across, none))
    return west, east


def first_sweep_kernel(depth, vert, block, flags, *refs):
    resist, low_side, high_side, r_bound, r_column, p_column = refs[:6]
    south_weight, north_weight, p_south, p_north, p_west, p_east = refs[6:12]
    source = refs[12]
    w_east, w_north, west_out, particular, inverse, ratio, lead, reduced = refs[13:21]
    grounds, rights, verticals = refs[21:]
    start, offset = flags[6 + block], flags[10 + block]
    size = inverse.shape[2]
    shape = (ROWS, size)
    here = lane_slice(start, size)
    inside = lane_slice(offset, size)
    west_weight, east_weight = edge_weights(
        flags, start, r_bound[...], r_column[...], low_side[...], high_side[...]
    )
    west_out[...] = west_weight
    column = p_column[...]
    row = row_of(shape)

    def weigh(z, carry):
        plane = resist[z, :, inside]
        east = 2.0 * inverse_of(plane + roll(plane, -1, 1))
        east = with_last(east, column_to(z, east_weight, LANES - 1))
        west = with_first(roll(east, 1, 1), column_to(z, west_weight, 0))
        north = 2.0 * inverse_of(plane + roll(plane, -1, 0))
        north = jnp.where(row == ROWS - 1, north_weight[pl.ds(z, 1), here], north)
        south = jnp.where(row == 0, south_weight[pl.ds(z, 1), here], roll(north, 1, 0))
        w_east[z], w_north[z] = east, north
        grounds[z] = STORE + ((east + west) + (north + south))
        verticals[z] = (2.0 * vert) * inverse_of(
            plane + resist[jnp.minimum(z + 1, depth - 1), :, inside]
        )
        p_first, p_last = p_west[z, :, here], p_east[z, :, here]
        p_first = with_first(
            p_first, jnp.where(start == 0, column_to(z, column, 0), p_first[:, :LANES])
        )
        p_last = with_last(
            p_last, jnp.where(start == 0, p_last[:, -LANES:], column_to(z, column, LANES - 1))
        )
        rights[z] = source[z, :, here] + (
            (west * p_first + east * p_last)
            + (south * p_south[z, :, here] + north * p_north[z, :, here])
        )
        return carry

    lax.fori_loop(0, depth, weigh, 0, unroll=True)

    def layer(z, carry):
        conduct, flow, product, first_first, first_part = carry
        weight = verticals[z]
        reciprocal = inverse_of(conduct + weight)
        quotient = weight * reciprocal
        led = product * reciprocal
        inverse[z] = reciprocal
        ratio[z] = quotient
        lead[z] = led
        particular[z] = reciprocal * flow
        return (
            grounds[z + 1] + conduct * quotient,
            rights[z + 1] + flow * quotient,
            product * quotient,
            first_first + led * product,
            first_part + led * flow,
        )

    zero = jnp.zeros(shape, F32)
    conduct, flow, product, first_first, first_part = lax.fori_loop(
        0,
        depth - 1,
        layer,
        (grounds[0], rights[0], jnp.ones(shape, F32), zero, zero),
        unroll=True,
    )
    reciprocal = inverse_of(conduct)
    led = product * reciprocal
    inverse[depth - 1] = reciprocal
    ratio[depth - 1] = zero
    lead[depth - 1] = led
    particular[depth - 1] = flow * reciprocal
    reduced[0] = first_first + led * product + resist[0, :, inside] * (0.5 / vert)
    reduced[1] = led
    reduced[2] = reciprocal + resist[depth - 1, :, inside] * (0.5 / vert)
    reduced[3] = first_part + led * flow
    reduced[4] = flow * reciprocal


def pair_kernel(flags, own, near, across, kept):
    me = flags[14]
    even, lower = me % 2 == 0, me < 2
    first, second = [
        [jnp.where(flip, own[at], near[at]) for at in range(5)]
        for flip in (even, jnp.logical_not(even))
    ]
    reciprocal = inverse_of(first[2] + second[0])
    step = (first[4] - second[3]) * reciprocal
    through = jnp.where(lower, second[1], first[1])
    share = through * reciprocal
    across[0] = jnp.where(lower, second[2], first[0]) - through * share
    across[1] = jnp.where(lower, second[4], first[3]) + jnp.where(
        lower, through * step, -through * step
    )
    kept[0], kept[1], kept[2] = share, reciprocal, step


def ends(me, inner, middle):
    zero = jnp.zeros_like(inner)
    odd = me % 2 == 1
    enters = jnp.where(odd, inner, jnp.where(me == 2, middle, zero))
    leaves = jnp.where(odd, jnp.where(me == 1, middle, zero), inner)
    return enters, leaves


def back_substitute(depth, lines, emit):
    last = depth - 1
    values = tuple(
        (particular[last] + lead[last] * enters) - inverse[last] * leaves
        for enters, leaves, particular, inverse, ratio, lead in lines
    )
    state = emit(last, values, jnp.zeros((ROWS, LANES), F32))

    for z in range(last - 1, -1, -1):
        values = tuple(
            (particular[z] + lead[z] * enters) + ratio[z] * beyond
            for (enters, _, particular, _, ratio, lead), beyond in zip(lines, values)
        )
        state = emit(z, values, state)
    return state


def half_kernel(depth, flags, *refs):
    pairs = (refs[0:3], refs[3:6])
    blocks = (refs[6:10], refs[10:14])
    pressure, colour = refs[14:16]
    half, to_near, to_middle, boundary, joined = refs[16:]
    me, g, even = flags[14], flags[0], flags[16] == 0
    size = blocks[0][0].shape[2]
    spans = [lane_slice(flags[6 + block], size) for block in range(2)]
    lines = []
    for block, state in enumerate(blocks):
        across, other, kept = pairs[block]
        sum_of = inverse_of(across[0] + other[0])
        joined[block] = sum_of
        lead_of = across[1] - other[1]
        middle = jnp.where(me < 2, lead_of, -lead_of) * sum_of
        inner = kept[2] + kept[0] * middle
        lines.append((*ends(me, inner, middle), *state))
    chosen = [colour[:, here] == 0 for here in spans]

    def emit(z, values, packed):
        for block, (value, here) in enumerate(zip(values, spans)):
            value = jnp.where(chosen[block], value, pressure[z, :, here])
            half[z, :, here] = value
            keep_rows(z, value, even, to_near, to_middle, here)
            if not block:
                packed = packed_with(z, packed, boundary_plane(g, value), 0)
        return packed

    boundary[...] = back_substitute(depth, lines, emit)


def second_sweep_kernel(depth, flags, *refs):
    half, h_near, h_middle, h_column, source, south_weight = refs[:6]
    shares = refs[6:8]
    blocks = (refs[8:14], refs[14:20])
    particulars, near, far = refs[20:22], refs[22], refs[23]
    south_terms, north_rows = refs[24:]
    me, even = flags[14], flags[16] == 0
    size = particulars[0].shape[2]
    starts = [flags[6 + block] for block in range(2)]
    spans = [lane_slice(start, size) for start in starts]
    column = h_column[...]
    south_terms[...] = south_weight[...] * jnp.where(even, h_middle[...], h_near[...])
    north_rows[...] = jnp.where(even, h_near[...], h_middle[...])

    def local(z, block):
        east, north, west = blocks[block][:3]
        return source[z, :, spans[block]] + coupling(
            z,
            half,
            starts[block],
            size,
            east[z],
            north[z],
            south_terms,
            north_rows,
            west[...],
            column,
        )

    def layer(z, carry):
        result = []
        for block, (flow, first_part) in enumerate(carry):
            inverse, ratio, lead = blocks[block][3:6]
            particulars[block][z] = flow * inverse[z]
            first_part = first_part + lead[z] * flow
            result.append((local(z + 1, block) + flow * ratio[z], first_part))
        return tuple(result)

    carry = tuple((local(0, block), jnp.zeros((ROWS, size), F32)) for block in range(2))
    carry = lax.fori_loop(0, depth - 1, layer, carry, unroll=True)
    last = depth - 1
    for block, (flow, first_part) in enumerate(carry):
        inverse, ratio, lead = blocks[block][3:6]
        there = slice(block * size, (block + 1) * size)
        first_part = first_part + lead[last] * flow
        last_part = flow * inverse[last]
        particulars[block][last] = last_part
        asked = jnp.where(me % 2 == 0, last_part, first_part)
        shared = shares[block][0] * asked
        outer = jnp.where(me == 1, last_part, jnp.where(me == 2, first_part, 0.0))
        given = outer + jnp.where((me == 0) | (me == 3), shared, -shared)
        near[0, :, there] = asked
        near[1, :, there] = given
        far[:, there] = given


def smoothed_kernel(depth, flags, *refs):
    own, near, skip, cross, joined = refs[:5]
    keeps = refs[5:7]
    blocks = (refs[7:11], refs[11:15])
    half, colour, result = refs[15:18]
    smoothed, sems = refs[18:]
    me = flags[14]
    size = blocks[0][0].shape[2]
    spans = [lane_slice(flags[6 + block], size) for block in range(2)]
    lines = []
    for block, state in enumerate(blocks):
        there = slice(block * size, (block + 1) * size)
        kept = keeps[block]
        lead_of = (own[1, :, there] + near[1, :, there]) - (skip[:, there] + cross[:, there])
        middle = jnp.where(me < 2, lead_of, -lead_of) * joined[block]
        step = own[0, :, there] - near[0, :, there]
        step = jnp.where(me % 2 == 0, step, -step) * kept[1]
        lines.append((*ends(me, step + kept[0] * middle, middle), *state))
    chosen = [colour[:, here] == 1 for here in spans]
    count = sems.shape[0]
    layers = depth // count
    copies = [
        pltpu.make_async_copy(
            smoothed.at[pl.ds(at * layers, layers)],
            result.at[pl.ds(at * layers, layers)],
            sems.at[at],
        )
        for at in range(count)
    ]

    def emit(z, values, state):
        for value, here, mine in zip(values, spans, chosen):
            smoothed[z, :, here] = jnp.where(mine, value, half[z, :, here])
        if z % layers == 0:
            copies[z // layers].start()
        return state

    back_substitute(depth, lines, emit)
    for copy in copies:
        copy.wait()


PAIR = [(0, 1), (1, 0)]
NEAR = [(0, 1), (1, 0), (2, 3), (3, 2)]
MIDDLE = [(1, 2), (2, 1)]
SKIP = [(0, 2), (2, 0), (1, 3), (3, 1)]
CROSS = [(0, 3), (3, 0), (1, 2), (2, 1)]


def exchange_edges(edges):
    to_near, to_middle, *column = edges
    return [
        lax.ppermute(to_near, "gy", NEAR),
        lax.ppermute(to_middle, "gy", MIDDLE),
        *[lax.ppermute(piece, "gx", PAIR) for piece in column],
    ]


def fast_body(spectral, shifts, colour, pressure, source):
    depth, items, width = pressure.shape
    vert = float((depth * 4) ** 2 // 4)
    waves = spectral.shape[3]
    rows = depth * items
    block_size, third = width // 2, 3 * width // 8
    known = width - third

    def flags():
        gx, gz, gy = (lax.axis_index(axis) for axis in ("gx", "gz", "gy"))

        def placed(start, size):
            return jnp.where(gx == 1, start, width - start - size)

        block_one, block_two = placed(0, block_size), placed(block_size, block_size)
        start_one = placed(0, known)
        extra = known - block_size
        return [
            gx,
            placed(0, LANES),
            placed(LANES, known - LANES),
            start_one,
            gx,
            placed(known, third),
            block_one,
            block_two,
            placed(block_size, extra) - block_two,
            placed(block_size, extra) - start_one,
            block_one - start_one,
            0,
            gy > 0,
            gy < 3,
            gz,
            ((gy == 1) | (gy == 2)).astype(jnp.int32),
            gy % 2,
        ]

    def shaped(*shape, dtype=F32):
        return jax.ShapeDtypeStruct(shape, dtype)

    groups = NX // LANES
    parts = waves // LANES
    inner_ys, last_ys = (1, 2, 3), tuple(range(4, items - 1))
    last_rows = len(last_ys) * depth
    column_type = shaped(ROWS, LANES)
    coefficients = spectral.reshape(2, rows, waves)

    def scratch(count):
        return [
            pltpu.VMEM((count, LANES), jnp.int32),
            pltpu.VMEM((6, count, LANES), F32),
            pltpu.VMEM((parts, 2, rows, LANES), F32),
            pltpu.SemaphoreType.DMA((parts,)),
            pltpu.VMEM((3, 2 * LANES, LANES), jnp.bfloat16),
            pltpu.VMEM((2, groups, LANES), F32),
            pltpu.VMEM((2, groups * depth, 4 * LANES), jnp.bfloat16),
            pltpu.VMEM((2, groups * depth, LANES), F32),
        ]

    def wide_types(ys):
        return [shaped(len(ys) * depth, width)] * 2 + [shaped(6, len(ys), LANES)]

    shift_rows = shifts.T
    outer_ys = (0, items - 1)
    sums, own_outer, outer_kept = call(
        functools.partial(wide_sums_kernel, outer_ys),
        "outer_row_sums",
        wide_types(outer_ys),
        [shift_rows],
        scratch=scratch(2 * depth),
        far=[coefficients],
        mib=SUMS_GRANT,
    )
    outer = lax.ppermute(sums, "gx", PAIR)
    shift_rows, _ = lax.optimization_barrier((shift_rows, own_outer))
    sums, own_inner, inner_kept, p_column = call(
        functools.partial(inner_sums_kernel, inner_ys),
        "inner_row_sums",
        wide_types(inner_ys) + [column_type],
        [shift_rows],
        scratch=[pltpu.VMEM((depth, ROWS, LANES), F32), pltpu.SemaphoreType.DMA]
        + scratch(len(inner_ys) * depth),
        far=[coefficients, pressure],
        mib=20,
    )
    inner = lax.ppermute(sums, "gx", PAIR)
    edge_row, edge_column = shaped(depth, width), shaped(ROWS, LANES)
    edges = [edge_row, edge_row, edge_column]
    pressure_rows, _ = lax.optimization_barrier((pressure, own_inner))
    to_near, to_middle = call(
        functools.partial(outer_field_kernel, depth),
        "outer_field",
        [shaped(2 * depth, width)] * 2,
        [own_outer, outer, pressure_rows],
        flags,
    )
    from_near, from_middle = exchange_edges([to_near, to_middle])
    last_one, last_two, own_last, own_columns = call(
        functools.partial(last_sums_kernel, last_ys),
        "last_row_sums",
        [
            shaped(last_rows + ROWS, known),
            shaped(last_rows, third),
            shaped(last_rows, width),
            shaped(6, ROWS, LANES),
        ],
        [shift_rows, outer_kept, inner_kept, p_column],
        scratch=[pltpu.VMEM((6, len(last_ys), LANES), F32)] + scratch(last_rows),
        far=[coefficients],
        mib=20,
    )
    last_one = lax.ppermute(last_one, "gx", PAIR)
    wide, *around = call(
        functools.partial(wide_field_kernel, depth),
        "wide_field",
        [shaped(rows - last_rows, width)] + [edge_row] * 2 + [shaped(depth, items, width)] * 4,
        [
            *(own_outer, outer, own_inner, inner, to_near, to_middle),
            *(from_near, from_middle, pressure),
        ],
        flags,
        [pltpu.VMEM((depth, width), F32)] * 2,
    )
    last_two, _ = lax.optimization_barrier((last_two, wide))
    last_two = lax.ppermute(last_two, "gx", PAIR)
    log_near, resist_near, *columns = call(
        functools.partial(first_field_kernel, depth),
        "first_field",
        [shaped(depth, items, known)] * 2 + [edge_column] * 5,
        [wide, own_last, last_one, own_columns],
        flags,
        [pltpu.VMEM((known // LANES, rows, LANES), F32)],
    )
    block = shaped(depth, items, block_size)

    state_types = [block] * 2 + [edge_column] + [block] * 4

    def first_sweep(at, resist):
        return call(
            functools.partial(first_sweep_kernel, depth, vert, at),
            "first_sweep",
            state_types + [shaped(5, items, block_size)],
            [resist, *columns, *around, source],
            flags,
            [pltpu.VMEM((depth, items, block_size), F32)] * 3,
        )

    *state_one, reduced_one = first_sweep(0, resist_near)
    near_one = lax.ppermute(reduced_one, "gz", NEAR)
    last_two, _ = lax.optimization_barrier((last_two, reduced_one))
    log_far, resist_far = call(
        functools.partial(second_field_kernel, depth),
        "second_field",
        [shaped(depth, items, third), block],
        [wide, own_last, last_two, resist_near],
        flags,
        [pltpu.VMEM((third // LANES, rows, LANES), F32)],
    )
    *state_two, reduced_two = first_sweep(1, resist_far)
    near_two = lax.ppermute(reduced_two, "gz", NEAR)
    (log_perm,) = call(
        functools.partial(join_columns_kernel, depth),
        "log_perm",
        [shaped(depth, items, width)],
        [log_near, log_far, reduced_two],
        flags,
    )
    def join(reduced, near):
        across, kept = call(
            pair_kernel,
            "join_pair",
            [shaped(2, items, block_size), shaped(3, items, block_size)],
            [reduced, near],
            flags,
        )
        return across, lax.ppermute(across, "gz", SKIP), kept

    pair_one, pair_two = join(reduced_one, near_one), join(reduced_two, near_two)
    keeps = [pair_one[2], pair_two[2]]
    half, *h_edges, joined = call(
        functools.partial(half_kernel, depth),
        "half",
        [shaped(depth, items, width), *edges, shaped(2, items, block_size)],
        [*pair_one, *pair_two, *state_one[3:], *state_two[3:], pressure, colour],
        flags,
    )
    h_edges = exchange_edges(h_edges)
    weights = [[*state[:3], *state[4:]] for state in (state_one, state_two)]
    current_one, current_two, to_near, to_far = call(
        functools.partial(second_sweep_kernel, depth),
        "second_sweep",
        [block, block, shaped(2, items, width), shaped(items, width)],
        [half, *h_edges, source, around[0], *keeps, *weights[0], *weights[1]],
        flags,
        [pltpu.VMEM((depth, width), F32)] * 2,
    )
    from_near, from_skip, from_cross = (
        lax.ppermute(planes, "gz", pairs)
        for planes, pairs in ((to_near, NEAR), (to_far, SKIP), (to_far, CROSS))
    )
    (smoothed,) = call(
        functools.partial(smoothed_kernel, depth),
        "smoothed",
        [shaped(depth, items, width)],
        [
            *(to_near, from_near, from_skip, from_cross, joined, *keeps),
            *(current_one, *state_one[4:]),
            *(current_two, *state_two[4:]),
            *(half, colour),
        ],
        flags,
        [pltpu.VMEM((depth, items, width), F32), pltpu.SemaphoreType.DMA((4,))],
        out=IN_HBM,
    )
    return (log_perm, smoothed)


def solution(mesh):
    body = fast_body if suits(mesh) else generic_body
    in_specs = (
        P(None, "gz", "gy", "gx"),
        P("gz", "gy"),
        P("gy", "gx"),
        P("gz", "gy", "gx"),
        P("gz", "gy", "gx"),
    )
    out_specs = (P("gz", "gy", "gx"), P("gz", "gy", "gx"))
    return jax.shard_map(body, mesh=mesh, in_specs=in_specs, out_specs=out_specs, check_vma=False)
```

```python
import functools
import math

import jax
import jax.numpy as jnp


from jax import lax
from jax.experimental import pallas as pl
from jax.experimental.pallas import tpu as pltpu
from jax.sharding import PartitionSpec as P

NX = 2048


STORE = 1.0


def padded_2(block, sides, width):
    for axis, dim in sides:
        count = lax.axis_size(axis)
        forward = [(i, i + 1) for i in range(count - 1)]
        backward = [(target, source) for source, target in forward]
        low = lax.ppermute(
            lax.slice_in_dim(block, block.shape[dim] - width, None, axis=dim), axis, forward
        )
        high = lax.ppermute(lax.slice_in_dim(block, 0, width, axis=dim), axis, backward)
        block = jnp.concatenate([low, block, high], axis=dim)
    return block


def twisted_coeffs(spectral, shifts, first_wave):
    count = spectral.shape[3]
    wave_index = first_wave + jnp.arange(count, dtype=jnp.int32)
    wave_turns = shifts[:, :, None] * wave_index[None, None, :] % NX
    phase_angle = wave_turns.astype(jnp.float32) * (2.0 * math.pi / NX)
    cosine = jnp.cos(phase_angle)
    sine_part = jnp.sin(phase_angle)
    real_part = spectral[0] * cosine - spectral[1] * sine_part
    imag_part = spectral[0] * sine_part + spectral[1] * cosine
    return jnp.stack([real_part, imag_part])


def basis(count, first_cell, width_cells):
    wave_index = jnp.arange(count, dtype=jnp.int32)
    cell_index = first_cell + jnp.arange(width_cells, dtype=jnp.int32)
    wave_turns = wave_index[:, None] * cell_index[None, :] % NX
    phase_angle = wave_turns.astype(jnp.float32) * (2.0 * math.pi / NX)
    offsets = jnp.concatenate(
        [jnp.zeros((count, 1), jnp.float32), jnp.full((count, 1), 0.5 * math.pi, jnp.float32)],
        axis=0,
    )
    stacked = jnp.concatenate([phase_angle, phase_angle], axis=0) + offsets
    return jnp.cos(stacked) * (1.0 / math.sqrt(NX))


def flatten_pair(piece):
    depth, items, count = (piece.shape[1], piece.shape[2], piece.shape[3])
    return jnp.concatenate(
        [piece[0].reshape(depth * items, count), piece[1].reshape(depth * items, count)], axis=1
    )


def harmonic(center, beside):
    return 2.0 * center * beside / (center + beside)


def thomas(lower_diagonal, main_diagonal, upper_diagonal, right_hand_side):

    def thomas_forward_scan(carried_state, row_entries):
        previous_ratio, previous_eliminated = carried_state
        column_lower, main_c, sup_c, column_right_hand = row_entries
        present_denominator = main_c - column_lower * previous_ratio
        present_ratio = sup_c / present_denominator
        present_eliminated = (
            column_right_hand - column_lower * previous_eliminated
        ) / present_denominator
        return ((present_ratio, present_eliminated), (present_ratio, present_eliminated))

    zeroed_layer = jnp.zeros(right_hand_side.shape[1:], right_hand_side.dtype)
    unused_output, (ratio_rows, eliminated_rows) = lax.scan(
        thomas_forward_scan,
        (zeroed_layer, zeroed_layer),
        (lower_diagonal, main_diagonal, upper_diagonal, right_hand_side),
    )

    def thomas_backward_scan(following_value, row_entries):
        column_ratio, column_eliminated = row_entries
        present_value = column_eliminated - column_ratio * following_value
        return (present_value, present_value)

    unused_output, solved_values = lax.scan(
        thomas_backward_scan, zeroed_layer, (ratio_rows, eliminated_rows), reverse=True
    )
    return solved_values


def factor(lower_diagonal, main_diagonal, upper_diagonal):

    def factor_forward_scan(previous_ratio, row_entries):
        column_lower, main_c, sup_c = row_entries
        present_denominator = main_c - column_lower * previous_ratio
        present_ratio = sup_c / present_denominator
        return (present_ratio, (present_denominator, present_ratio))

    unused_output, (denominator_rows, ratio_rows) = lax.scan(
        factor_forward_scan,
        jnp.zeros_like(main_diagonal[0]),
        (lower_diagonal, main_diagonal, upper_diagonal),
    )
    return (denominator_rows, ratio_rows)


def solve_factored(lower_diagonal, denominator_rows, ratio_rows, right_hand_side):

    def solve_forward_scan(previous_eliminated, row_entries):
        column_lower, column_denominator, column_right_hand = row_entries
        present_eliminated = (
            column_right_hand - column_lower[None] * previous_eliminated
        ) / column_denominator[None]
        return (present_eliminated, present_eliminated)

    unused_output, eliminated_rows = lax.scan(
        solve_forward_scan,
        jnp.zeros_like(right_hand_side[0]),
        (lower_diagonal, denominator_rows, right_hand_side),
    )

    def solve_backward_scan(following_value, row_entries):
        column_ratio, column_eliminated = row_entries
        present_value = column_eliminated - column_ratio[None] * following_value
        return (present_value, present_value)

    unused_output, solved_values = lax.scan(
        solve_backward_scan,
        jnp.zeros_like(right_hand_side[0]),
        (ratio_rows, eliminated_rows),
        reverse=True,
    )
    return solved_values


def generic_body(spectral, shifts, colour, pressure, source):
    total_depth = pressure.shape[0] * lax.axis_size("gz")
    vert_factor = float(total_depth * total_depth // 4)
    width_cells = spectral.shape[3]
    first_cell = lax.axis_index("gx") * width_cells
    twisted = twisted_coeffs(spectral, shifts, first_cell)
    piece = lax.all_to_all(twisted, "gx", split_axis=1, concat_axis=3, tiled=True)
    depth = piece.shape[1]
    items = piece.shape[2]
    length = piece.shape[3]
    flat = flatten_pair(piece)
    block_width = min(512, length)
    blocks = [
        jnp.dot(
            flat,
            basis(length, block * block_width, block_width),
            precision=lax.Precision.HIGHEST,
            preferred_element_type=jnp.float32,
        )
        for block in range(length // block_width)
    ]
    field_rows = jnp.concatenate(blocks, axis=1).reshape(depth, items, length)
    log_perm = lax.all_to_all(field_rows, "gx", split_axis=2, concat_axis=0, tiled=True)
    perm = jnp.exp(log_perm)
    padded = padded_2(perm, (("gx", 2), ("gz", 0), ("gy", 1)), 1)
    w_zm = vert_factor * harmonic(perm, padded[:-2, 1:-1, 1:-1])
    w_zp = vert_factor * harmonic(perm, padded[2:, 1:-1, 1:-1])
    w_ym = harmonic(perm, padded[1:-1, :-2, 1:-1])
    w_yp = harmonic(perm, padded[1:-1, 2:, 1:-1])
    w_xm = harmonic(perm, padded[1:-1, 1:-1, :-2])
    w_xp = harmonic(perm, padded[1:-1, 1:-1, 2:])
    main_diagonal = STORE + w_xm + w_xp + w_ym + w_yp + w_zm + w_zp
    lower_diagonal = -w_zm
    upper_diagonal = -w_zp
    zeroed_layer = jnp.zeros_like(main_diagonal[0])
    inner_sub = jnp.concatenate([zeroed_layer[None], lower_diagonal[2:-1]], axis=0)
    inner_sup = jnp.concatenate([upper_diagonal[1:-2], zeroed_layer[None]], axis=0)
    inner_main = main_diagonal[1:-1]
    denominator_rows, ratio_rows = factor(inner_sub, inner_main, inner_sup)
    unit_rhs = jnp.zeros((inner_main.shape[0], 2) + zeroed_layer.shape, jnp.float32)
    unit_rhs = unit_rhs.at[0, 0].set(-lower_diagonal[1])
    unit_rhs = unit_rhs.at[-1, 1].set(-upper_diagonal[-2])
    coupled = solve_factored(inner_sub, denominator_rows, ratio_rows, unit_rhs)
    left_part = coupled[:, 0]
    right_part = coupled[:, 1]
    sub_first = lower_diagonal[0]
    main_first = main_diagonal[0] + upper_diagonal[0] * left_part[0]
    sup_first = upper_diagonal[0] * right_part[0]
    sub_last = lower_diagonal[-1] * left_part[-1]
    main_last = main_diagonal[-1] + lower_diagonal[-1] * right_part[-1]
    sup_last = upper_diagonal[-1]

    def line_solve(current):
        cycle = padded_2(current, (("gx", 2), ("gy", 1)), 1)
        right_hand_side = source + w_xm * cycle[:, 1:-1, :-2] + w_xp * cycle[:, 1:-1, 2:]
        right_hand_side = right_hand_side + w_ym * cycle[:, :-2, 1:-1] + w_yp * cycle[:, 2:, 1:-1]
        particular = solve_factored(
            inner_sub, denominator_rows, ratio_rows, right_hand_side[1:-1][:, None]
        )[:, 0]
        rhs_first = right_hand_side[0] - upper_diagonal[0] * particular[0]
        rhs_last = right_hand_side[-1] - lower_diagonal[-1] * particular[-1]
        reduced_rows = jnp.stack(
            [sub_first, main_first, sup_first, rhs_first, sub_last, main_last, sup_last, rhs_last]
        )
        gathered = lax.all_gather(reduced_rows, "gz", axis=0, tiled=True)
        segments = gathered.shape[0] // 8
        system = gathered.reshape((2 * segments, 4) + zeroed_layer.shape)
        reduced_sol = thomas(system[:, 0], system[:, 1], system[:, 2], system[:, 3])
        own_pair = lax.dynamic_slice_in_dim(reduced_sol, 2 * lax.axis_index("gz"), 2, 0)
        face_first = own_pair[0]
        face_last = own_pair[1]
        inner = particular + face_first[None] * left_part + face_last[None] * right_part
        return jnp.concatenate([face_first[None], inner, face_last[None]], axis=0)

    half = jnp.where((colour == 0)[None], line_solve(pressure), pressure)
    smoothed = jnp.where((colour == 1)[None], line_solve(half), half)
    return (log_perm, smoothed)


LANES = 128
ROWS = 8
F32 = jnp.float32
MIB = 1 << 20
SUMS_GRANT = 60


def suits(mesh):
    sizes = dict(mesh.shape)
    return sizes["gx"] == 2 and sizes["gz"] == 4 and sizes["gy"] == 4


def params(mib):
    return pltpu.CompilerParams(vmem_limit_bytes=mib * MIB)


def cos_sin(turns):
    quarter = (turns + NX // 8) >> 9
    angle = (turns - (quarter << 9)).astype(F32) * (2.0 * math.pi / NX)
    square = angle * angle
    sine = angle * (
        1.0
        + square * (-1.0 / 6 + square * (1.0 / 120 + square * (-1.0 / 5040 + square / 362880)))
    )
    cosine = 1.0 + square * (
        -0.5 + square * (1.0 / 24 + square * (-1.0 / 720 + square * (1.0 / 40320)))
    )
    odd = (quarter & 1) == 1
    first = jnp.where(odd, sine, cosine)
    second = jnp.where(odd, cosine, sine)
    cos_sign = jnp.where(((quarter + 1) & 2) == 2, -1.0, 1.0)
    sin_sign = jnp.where((quarter & 2) == 2, -1.0, 1.0)
    return first * cos_sign, second * sin_sign


def split(values):
    high = values.astype(jnp.bfloat16)
    return high, (values - high.astype(F32)).astype(jnp.bfloat16)


def times(first, second):
    return (
        first[0] * second[0] - first[1] * second[1],
        first[0] * second[1] + first[1] * second[0],
    )


def plus(first, second):
    return (first[0] + second[0], first[1] + second[1])


def minus(first, second):
    return (first[0] - second[0], first[1] - second[1])


def quarter_turn(value):
    return (-value[1], value[0])


def four_point(first, second, third, fourth):
    even, gap = plus(first, third), minus(first, third)
    odd, turned = plus(second, fourth), quarter_turn(minus(second, fourth))
    return [plus(even, odd), plus(gap, turned), minus(even, odd), minus(gap, turned)]


def eight_point(values):
    even = four_point(*values[0::2])
    odd = four_point(*values[1::2])
    root = math.sqrt(0.5)
    real, imag = odd[1]
    odd[1] = (root * (real - imag), root * (real + imag))
    odd[2] = quarter_turn(odd[2])
    real, imag = odd[3]
    odd[3] = (-root * (real + imag), root * (real - imag))
    return [plus(*pair) for pair in zip(even, odd)] + [minus(*pair) for pair in zip(even, odd)]


def fill_tables(basis, turns):
    groups = NX // LANES
    shape = (LANES, LANES)
    lane = lane_of(shape)
    cells = (lane % groups) * (LANES // groups) + lane // groups
    cosine, sine = cos_sin((row_of(shape) * cells) % LANES * groups)
    for at, value in enumerate((cosine, -sine)):
        rows = slice(at * LANES, (at + 1) * LANES)
        high, low = split(value * (1.0 / math.sqrt(NX)))
        basis[0, rows], basis[1, rows], basis[2, rows] = high, high, low
    shape = (groups, LANES)
    turns[0], turns[1] = cos_sin(row_of(shape) * lane_of(shape))


def diagonal_of(depth):
    square = (depth, depth)
    return row_of(square) == lane_of(square)


def shift_columns(shifts, rows_of, columns):
    depth = shifts.shape[1]
    diagonal = diagonal_of(depth)
    for at, y in enumerate(rows_of):
        spread = jnp.where(diagonal, shifts[y : y + 1, :].astype(F32), 0.0)
        shift = jnp.broadcast_to(jnp.sum(spread, axis=1, keepdims=True), (depth, LANES))
        columns[at * depth : (at + 1) * depth, :] = shift.astype(jnp.int32)


def edge_columns(ys, depth, edges, kept):
    kept[...] = jnp.zeros_like(kept)
    diagonal = diagonal_of(depth)
    for at in range(len(ys)):
        rows = slice(at * depth, (at + 1) * depth)
        for side in range(edges.shape[0]):
            lane = 0 if side % 2 else LANES - 1
            column = jnp.broadcast_to(edges[side, rows, lane : lane + 1], (depth, depth))
            row = jnp.sum(jnp.where(diagonal, column, 0.0), axis=0, keepdims=True)
            kept[side, at : at + 1, :depth] = row


def twisted(first_wave, shift, coefficients, rows):
    lane = lane_of(shift.shape)
    phase = cos_sin((shift * (lane + first_wave)) & (NX - 1))
    turn = cos_sin((shift * LANES) & (NX - 1))
    values = []
    for part in range(coefficients.shape[0]):
        values.append(times((coefficients[part, 0, rows], coefficients[part, 1, rows]), phase))
        phase = times(phase, turn)
    return values


def interleave(tiles):
    count = len(tiles)
    lane = lane_of(tiles[0].shape)
    bit = count // 2
    while bit:
        low = (lane & bit) == 0
        moved = list(tiles)
        for at in range(count):
            if not at & bit:
                first, second = tiles[at], tiles[at | bit]
                crossed = jnp.take_along_axis(
                    jnp.where(low, second, first), lane ^ bit, axis=1
                )
                moved[at] = jnp.where(low, first, crossed)
                moved[at | bit] = jnp.where(low, crossed, second)
        tiles = moved
        bit //= 2
    return tiles


STEP = 16


def fill_left(g, at, y, depth, items, columns, coefficients, turns, left, part):
    groups = NX // LANES
    sign = 1.0 - 2.0 * g.astype(F32)
    first_wave = g * (coefficients.shape[0] * LANES)
    rows = pl.ds(part * STEP * items + y, STEP, stride=items)
    shift = columns[pl.ds(at * depth + part * STEP, STEP), :]
    values = twisted(first_wave, shift, coefficients, rows)
    angles = [2 * math.pi * p / groups for p in range(len(values))]
    turned = [
        times(value, (sign * math.cos(angle), sign * math.sin(angle)))
        if angle
        else (sign * value[0], sign * value[1])
        for angle, value in zip(angles, values)
    ]
    even, odd = eight_point(values), eight_point(turned)
    for group in range(groups):
        value = odd[group // 2] if group % 2 else even[group // 2]
        if group:
            value = times(value, (turns[0, group : group + 1], turns[1, group : group + 1]))
        first = group * depth + part * STEP
        for place_of, piece in enumerate(value):
            for half, bits in enumerate(split(piece)):
                target = (2 * half + place_of) * LANES
                left[first : first + STEP, target : target + LANES] = bits


def finish_row(at, depth, basis, left, right, emit):
    groups = NX // LANES
    spread = jnp.concatenate([left[...], left[:, : 2 * LANES]], axis=1)
    bases = basis[...].reshape(-1, LANES)
    right[...] = jnp.dot(spread, bases, preferred_element_type=F32)
    for part in range(depth // ROWS):
        tiles = [
            right[group * depth + part * ROWS : group * depth + (part + 1) * ROWS]
            for group in range(groups)
        ]
        emit(pl.ds(at * depth + part * ROWS, ROWS), interleave(tiles))


def load_coefficients(spectral, coefficients, arrivals, items):
    parts, halves = arrivals.shape
    copies = []
    for half in range(halves):
        rows = slice(half * STEP * items, (half + 1) * STEP * items)
        copies.append(
            [
                pltpu.make_async_copy(
                    spectral.at[:, rows, part * LANES : (part + 1) * LANES],
                    coefficients.at[part, :, rows],
                    arrivals.at[part, half],
                )
                for part in range(parts)
            ]
        )
    for half in copies:
        for copy in half:
            copy.start()
    return copies


def all_rows(g, ys, shifts, shift_copy, copies, columns, coefficients, tables, left, right, emit):
    items, depth = shifts.shape
    basis, turns = tables
    fill_tables(basis, turns)
    shift_copy.wait()
    shift_columns(shifts, ys, columns)
    for half, arriving in enumerate(copies):
        for copy in arriving:
            copy.wait()
        for at, y in enumerate(ys):
            fill_left(g, at, y, depth, items, columns, coefficients, turns, left.at[at], half)
    for at in range(len(ys)):
        finish_row(at, depth, basis, left.at[at], right.at[at], emit)


def keep_edges(rows, tiles, edges):
    count = len(tiles) // 4
    for side in range(edges.shape[0]):
        edges[side, rows] = tiles[(side // 2 + 1) * count - 1 + side % 2]


def inner_sums_kernel(ys, shifts, spectral, pressure, other, own, kept, p_column, *refs):
    tile, sem, *refs = refs
    g = lax.axis_index("gx")
    width = pressure.shape[2]
    there = lane_slice(jnp.where(g == 0, width - LANES, 0), LANES)
    copy = pltpu.make_async_copy(pressure.at[:, :, there], tile, sem)
    copy.start()
    wide_sums_kernel(ys, shifts, spectral, other, own, kept, *refs)
    copy.wait()
    packed = jnp.zeros((ROWS, LANES), F32)
    for z in range(tile.shape[0]):
        packed = packed_with(z, packed, boundary_plane(g, tile[z]), 0)
    p_column[...] = packed


def wide_sums_kernel(ys, shifts, spectral, other, own, kept, *refs):
    local, arrived, columns, edges, coefficients, arrivals, *tables, left, right = refs
    items, depth = shifts.shape
    copies = load_coefficients(spectral, coefficients, arrivals, items)
    shift_copy = pltpu.make_async_copy(shifts, local, arrived)
    shift_copy.start()
    g = lax.axis_index("gx")

    def emit(rows, tiles):
        half = len(tiles) // 2
        keep_edges(rows, tiles, edges)
        for tile, (low, high) in enumerate(zip(tiles[:half], tiles[half:])):
            there = slice(tile * LANES, (tile + 1) * LANES)
            other[rows, there] = jnp.where(g == 0, high, low)
            own[rows, there] = jnp.where(g == 0, low, high)

    all_rows(
        *(g, ys, local, shift_copy, copies, columns, coefficients, tables, left, right, emit)
    )
    edge_columns(ys, depth, edges, kept)


def last_sums_kernel(ys, outer_kept, inner_kept, p_column, shifts, spectral, one, two, own, *refs):
    columns_own, kept, local, arrived, columns, edges, coefficients, *refs = refs
    arrivals, *tables, left, right = refs
    items, depth = shifts.shape
    copies = load_coefficients(spectral, coefficients, arrivals, items)
    shift_copy = pltpu.make_async_copy(shifts, local, arrived)
    shift_copy.start()
    g = lax.axis_index("gx")

    def emit(rows, tiles):
        half = len(tiles) // 2
        keep_edges(rows, tiles, edges)
        others = []
        for tile, (low, high) in enumerate(zip(tiles[:half], tiles[half:])):
            own[rows, tile * LANES : (tile + 1) * LANES] = jnp.where(g == 0, low, high)
            others.append(jnp.where(g == 0, high, low))
        start = 0
        for ref in (one, two):
            count = ref.shape[1] // LANES
            for tile in range(count):
                ref[rows, tile * LANES : (tile + 1) * LANES] = jnp.where(
                    g == 0, others[start + tile], others[half - start - count + tile]
                )
            start += count

    all_rows(
        *(g, ys, local, shift_copy, copies, columns, coefficients, tables, left, right, emit)
    )
    edge_columns(ys, depth, edges, kept)
    sides_of = [
        jnp.concatenate(
            [outer_kept[side, :1], inner_kept[side], kept[side], outer_kept[side, 1:]], axis=0
        )
        for side in range(6)
    ]
    low, high = sides_of[:3], sides_of[3:]
    own_sides = [jnp.where(g == 0, *pair) for pair in ((low[0], high[1]), (low[1], high[2]))]
    own_sides.append(jnp.where(g == 0, low[2], high[0]))
    other_sides = [jnp.where(g == 0, *pair) for pair in ((high[1], low[0]), (high[2], low[1]))]
    other_sides.append(jnp.where(g == 0, high[0], low[2]))
    for at in range(3):
        columns_own[at], columns_own[3 + at] = own_sides[at], other_sides[at]
    extra = slice(one.shape[0] - ROWS, one.shape[0])
    for at, piece in enumerate((*other_sides, own_sides[2], p_column[...])):
        one[extra, at * LANES : (at + 1) * LANES] = piece


ON_CHIP = pl.BlockSpec(memory_space=pltpu.VMEM)
IN_HBM = pl.BlockSpec(memory_space=pltpu.HBM)


def call(
    kernel, name, out_shape, args, flags=None, scratch=(), far=(), mib=20, flops=1, out=ON_CHIP
):
    specs = [ON_CHIP] * len(args) + [IN_HBM] * len(far)
    args = list(args) + list(far)
    body = kernel if flags is None else lambda *refs: kernel(flags(), *refs)
    return pl.pallas_call(
        body,
        out_shape=out_shape,
        in_specs=specs,
        out_specs=jax.tree.map(lambda _: out, out_shape),
        scratch_shapes=list(scratch),
        compiler_params=params(mib),
        cost_estimate=pl.CostEstimate(flops=flops, bytes_accessed=1, transcendentals=0),
        name=name,
    )(*args)


def roll(values, shift, axis):
    return pltpu.roll(values, shift % values.shape[axis], axis)


def lane_of(shape):
    return lax.broadcasted_iota(jnp.int32, shape, 1)


def row_of(shape):
    return lax.broadcasted_iota(jnp.int32, shape, 0)


def column_to(z, packed, target):
    return pltpu.roll(packed, (target - z) % LANES, 1)


def packed_with(z, packed, plane, lane):
    column = jnp.broadcast_to(plane[:, lane : lane + 1], (ROWS, LANES))
    return jnp.where(lane_of((ROWS, LANES)) == z, column, packed)


def inverse_of(values):
    return pl.reciprocal(values, approx=True)


def ordered(z, sums, depth):
    spread = pl.ds(z, ROWS, stride=depth)
    return jnp.concatenate([sums[at, spread] for at in range(sums.shape[0])], axis=1)


def place_tiles(sums, rows, first, values):
    for at in range(values.shape[1] // LANES):
        sums[(first >> 7) + at, rows] = values[:, at * LANES : (at + 1) * LANES]


def boundary_plane(g, plane):
    return jnp.where(g == 0, roll(plane[:, -LANES:], 1, 1), plane[:, :LANES])


def outer_field_kernel(depth, flags, own, other, pressure, to_near, to_middle):
    even = flags[16] == 0
    low, high = slice(0, depth), slice(depth, 2 * depth)
    south, north = own[low] + other[low], own[high] + other[high]
    to_near[low] = jnp.exp(-jnp.where(even, north, south))
    to_middle[low] = jnp.exp(-jnp.where(even, south, north))

    for z in range(depth):
        keep_rows(depth + z, pressure[z], even, to_near, to_middle, slice(None))


def wide_field_kernel(depth, flags, *refs):
    own_outer, outer, own_inner, inner, to_near, to_middle = refs[:6]
    from_near, from_middle, pressure = refs[6:9]
    wide, south_weight, north_weight, p_south, p_north, p_west, p_east = refs[9:16]
    south_rows, north_rows = refs[16:]
    even = flags[16] == 0
    low, high = slice(0, depth), slice(depth, 2 * depth)
    wide[low] = own_outer[low] + outer[low]
    wide[depth:-depth] = own_inner[...] + inner[...]
    wide[-depth:] = own_outer[high] + outer[high]
    near_weight = 2.0 * inverse_of(to_near[low] + from_near[low])
    middle_weight = (2.0 * flags[15].astype(F32)) * inverse_of(to_middle[low] + from_middle[low])
    south = jnp.where(even, middle_weight, near_weight)
    south_weight[...] = south
    north_weight[...] = jnp.where(even, near_weight, middle_weight)
    south_rows[...] = jnp.where(even, from_middle[high], from_near[high])
    north_rows[...] = jnp.where(even, from_near[high], from_middle[high])
    row = row_of(pressure.shape[1:])

    def layer(z, carry):
        plane = pressure[z]
        p_south[z] = jnp.where(row == 0, south_rows[pl.ds(z, 1), :], roll(plane, 1, 0))
        p_north[z] = jnp.where(row == ROWS - 1, north_rows[pl.ds(z, 1), :], roll(plane, -1, 0))
        p_west[z] = roll(plane, 1, 1)
        p_east[z] = roll(plane, -1, 1)
        return carry

    lax.fori_loop(0, depth, layer, 0, unroll=True)


def lane_slice(start, size):
    return pl.ds(pl.multiple_of(start, LANES), size)


def assemble(sums, depth, wide, own, piece, there):
    inside = wide.shape[0] - depth
    place_tiles(sums, slice(0, inside), 0, wide[:inside, there])
    place_tiles(sums, slice(inside, -depth), 0, own[:, there] + piece[: own.shape[0]])
    place_tiles(sums, slice(-depth, None), 0, wide[inside:, there])


def first_field_kernel(depth, flags, *refs):
    wide, own, middle, columns_own = refs[:4]
    log_perm, resist, low_side, high_side, boundary, column, p_column, sums = refs[4:]
    extra = slice(own.shape[0], own.shape[0] + ROWS)
    came = [middle[extra, at * LANES : (at + 1) * LANES] for at in range(5)]
    for at, ref in enumerate((low_side, high_side, boundary)):
        ref[...] = jnp.exp(-(columns_own[at] + came[at]))
    column[...] = jnp.exp(-(columns_own[5] + came[3]))
    p_column[...] = came[4]
    assemble(sums, depth, wide, own, middle, lane_slice(flags[3], log_perm.shape[2]))

    def layer(z, carry):
        plane = ordered(z, sums, depth)
        log_perm[z] = plane
        resist[z] = jnp.exp(-plane)
        return carry

    lax.fori_loop(0, depth, layer, 0, unroll=True)


def second_field_kernel(depth, flags, *refs):
    wide, own, middle, resist_near = refs[:4]
    log_perm, resist, sums = refs[4:]
    third = middle.shape[1]
    assemble(sums, depth, wide, own, middle, lane_slice(flags[5], third))
    extra = resist.shape[2] - third
    target = lane_slice(flags[5] - flags[7], third)
    extra_target = lane_slice(flags[8], extra)
    extra_source = lane_slice(flags[9], extra)

    def layer(z, carry):
        plane = ordered(z, sums, depth)
        log_perm[z] = plane
        resist[z, :, target] = jnp.exp(-plane)
        resist[z, :, extra_target] = resist_near[z, :, extra_source]
        return carry

    lax.fori_loop(0, depth, layer, 0, unroll=True)


def join_columns_kernel(depth, flags, near, far, _, whole):
    def layer(z, carry):
        whole[z, :, lane_slice(flags[3], near.shape[2])] = near[z]
        whole[z, :, lane_slice(flags[5], far.shape[2])] = far[z]
        return carry

    lax.fori_loop(0, depth, layer, 0, unroll=True)


def keep_rows(z, value, even, to_near, to_middle, here):
    south, north = value[0:1, :], value[ROWS - 1 : ROWS, :]
    to_near[pl.ds(z, 1), here] = jnp.where(even, north, south)
    to_middle[pl.ds(z, 1), here] = jnp.where(even, south, north)


def with_first(plane, edge):
    first = jnp.where(lane_of((ROWS, LANES)) == 0, edge, plane[:, :LANES])
    return jnp.concatenate([first, plane[:, LANES:]], axis=1)


def with_last(plane, edge):
    last = jnp.where(lane_of((ROWS, LANES)) == LANES - 1, edge, plane[:, -LANES:])
    return jnp.concatenate([plane[:, :-LANES], last], axis=1)


def coupling(z, field, start, size, east_weight, north_weight, south_terms, north_rows, west, column):
    here = lane_slice(start, size)
    plane = field[z, :, here]
    row = row_of(plane.shape)
    at_start = start == 0
    inner = field[z, :, lane_slice(jnp.where(at_start, size, size - LANES), LANES)]
    west_value = jnp.where(at_start, column_to(z, column, 0), roll(inner, 1, 1))
    east_value = jnp.where(at_start, roll(inner, -1, 1), column_to(z, column, LANES - 1))
    to_east, to_north = east_weight * plane, north_weight * plane
    from_west = with_first(roll(to_east, 1, 1), column_to(z, west, 0) * west_value)
    from_east = east_weight * with_last(roll(plane, -1, 1), east_value)
    from_south = jnp.where(row == 0, south_terms[pl.ds(z, 1), here], roll(to_north, 1, 0))
    from_north = north_weight * jnp.where(
        row == ROWS - 1, north_rows[pl.ds(z, 1), here], roll(plane, -1, 0)
    )
    return (from_west + from_east) + (from_south + from_north)


def edge_weights(flags, start, bound, column, low_side, high_side):
    g = flags[0]
    middle = 2.0 * inverse_of(low_side + high_side)
    across = 2.0 * inverse_of(bound + column)
    none = jnp.zeros_like(across)
    west = jnp.where(start == 0, jnp.where(g == 0, none, across), middle)
    east = jnp.where(start == 0, middle, jnp.where(g == 0, across, none))
    return west, east


def first_sweep_kernel(depth, vert, block, flags, *refs):
    resist, low_side, high_side, r_bound, r_column, p_column = refs[:6]
    south_weight, north_weight, p_south, p_north, p_west, p_east = refs[6:12]
    source = refs[12]
    w_east, w_north, west_out, particular, inverse, ratio, lead, reduced = refs[13:21]
    grounds, rights, verticals = refs[21:]
    start, offset = flags[6 + block], flags[10 + block]
    size = inverse.shape[2]
    shape = (ROWS, size)
    here = lane_slice(start, size)
    inside = lane_slice(offset, size)
    west_weight, east_weight = edge_weights(
        flags, start, r_bound[...], r_column[...], low_side[...], high_side[...]
    )
    west_out[...] = west_weight
    column = p_column[...]
    row = row_of(shape)

    def weigh(z, carry):
        plane = resist[z, :, inside]
        east = 2.0 * inverse_of(plane + roll(plane, -1, 1))
        east = with_last(east, column_to(z, east_weight, LANES - 1))
        west = with_first(roll(east, 1, 1), column_to(z, west_weight, 0))
        north = 2.0 * inverse_of(plane + roll(plane, -1, 0))
        north = jnp.where(row == ROWS - 1, north_weight[pl.ds(z, 1), here], north)
        south = jnp.where(row == 0, south_weight[pl.ds(z, 1), here], roll(north, 1, 0))
        w_east[z], w_north[z] = east, north
        grounds[z] = STORE + ((east + west) + (north + south))
        verticals[z] = (2.0 * vert) * inverse_of(
            plane + resist[jnp.minimum(z + 1, depth - 1), :, inside]
        )
        p_first, p_last = p_west[z, :, here], p_east[z, :, here]
        p_first = with_first(
            p_first, jnp.where(start == 0, column_to(z, column, 0), p_first[:, :LANES])
        )
        p_last = with_last(
            p_last, jnp.where(start == 0, p_last[:, -LANES:], column_to(z, column, LANES - 1))
        )
        rights[z] = source[z, :, here] + (
            (west * p_first + east * p_last)
            + (south * p_south[z, :, here] + north * p_north[z, :, here])
        )
        return carry

    lax.fori_loop(0, depth, weigh, 0, unroll=True)

    def layer(z, carry):
        conduct, flow, product, first_first, first_part = carry
        weight = verticals[z]
        reciprocal = inverse_of(conduct + weight)
        quotient = weight * reciprocal
        led = product * reciprocal
        inverse[z] = reciprocal
        ratio[z] = quotient
        lead[z] = led
        particular[z] = reciprocal * flow
        return (
            grounds[z + 1] + conduct * quotient,
            rights[z + 1] + flow * quotient,
            product * quotient,
            first_first + led * product,
            first_part + led * flow,
        )

    zero = jnp.zeros(shape, F32)
    conduct, flow, product, first_first, first_part = lax.fori_loop(
        0,
        depth - 1,
        layer,
        (grounds[0], rights[0], jnp.ones(shape, F32), zero, zero),
        unroll=True,
    )
    reciprocal = inverse_of(conduct)
    led = product * reciprocal
    inverse[depth - 1] = reciprocal
    ratio[depth - 1] = zero
    lead[depth - 1] = led
    particular[depth - 1] = flow * reciprocal
    reduced[0] = first_first + led * product + resist[0, :, inside] * (0.5 / vert)
    reduced[1] = led
    reduced[2] = reciprocal + resist[depth - 1, :, inside] * (0.5 / vert)
    reduced[3] = first_part + led * flow
    reduced[4] = flow * reciprocal


def pair_kernel(flags, own, near, across, kept):
    me = flags[14]
    even, lower = me % 2 == 0, me < 2
    first, second = [
        [jnp.where(flip, own[at], near[at]) for at in range(5)]
        for flip in (even, jnp.logical_not(even))
    ]
    reciprocal = inverse_of(first[2] + second[0])
    step = (first[4] - second[3]) * reciprocal
    through = jnp.where(lower, second[1], first[1])
    share = through * reciprocal
    across[0] = jnp.where(lower, second[2], first[0]) - through * share
    across[1] = jnp.where(lower, second[4], first[3]) + jnp.where(
        lower, through * step, -through * step
    )
    kept[0], kept[1], kept[2] = share, reciprocal, step


def ends(me, inner, middle):
    zero = jnp.zeros_like(inner)
    odd = me % 2 == 1
    enters = jnp.where(odd, inner, jnp.where(me == 2, middle, zero))
    leaves = jnp.where(odd, jnp.where(me == 1, middle, zero), inner)
    return enters, leaves


def back_substitute(depth, lines, emit):
    last = depth - 1
    values = tuple(
        (particular[last] + lead[last] * enters) - inverse[last] * leaves
        for enters, leaves, particular, inverse, ratio, lead in lines
    )
    state = emit(last, values, jnp.zeros((ROWS, LANES), F32))

    for z in range(last - 1, -1, -1):
        values = tuple(
            (particular[z] + lead[z] * enters) + ratio[z] * beyond
            for (enters, _, particular, _, ratio, lead), beyond in zip(lines, values)
        )
        state = emit(z, values, state)
    return state


def half_kernel(depth, flags, *refs):
    pairs = (refs[0:3], refs[3:6])
    blocks = (refs[6:10], refs[10:14])
    pressure, colour = refs[14:16]
    half, to_near, to_middle, boundary, joined = refs[16:]
    me, g, even = flags[14], flags[0], flags[16] == 0
    size = blocks[0][0].shape[2]
    spans = [lane_slice(flags[6 + block], size) for block in range(2)]
    lines = []
    for block, state in enumerate(blocks):
        across, other, kept = pairs[block]
        sum_of = inverse_of(across[0] + other[0])
        joined[block] = sum_of
        lead_of = across[1] - other[1]
        middle = jnp.where(me < 2, lead_of, -lead_of) * sum_of
        inner = kept[2] + kept[0] * middle
        lines.append((*ends(me, inner, middle), *state))
    chosen = [colour[:, here] == 0 for here in spans]

    def emit(z, values, packed):
        for block, (value, here) in enumerate(zip(values, spans)):
            value = jnp.where(chosen[block], value, pressure[z, :, here])
            half[z, :, here] = value
            keep_rows(z, value, even, to_near, to_middle, here)
            if not block:
                packed = packed_with(z, packed, boundary_plane(g, value), 0)
        return packed

    boundary[...] = back_substitute(depth, lines, emit)


def second_sweep_kernel(depth, flags, *refs):
    half, h_near, h_middle, h_column, source, south_weight = refs[:6]
    shares = refs[6:8]
    blocks = (refs[8:14], refs[14:20])
    particulars, near, far = refs[20:22], refs[22], refs[23]
    south_terms, north_rows = refs[24:]
    me, even = flags[14], flags[16] == 0
    size = particulars[0].shape[2]
    starts = [flags[6 + block] for block in range(2)]
    spans = [lane_slice(start, size) for start in starts]
    column = h_column[...]
    south_terms[...] = south_weight[...] * jnp.where(even, h_middle[...], h_near[...])
    north_rows[...] = jnp.where(even, h_near[...], h_middle[...])

    def local(z, block):
        east, north, west = blocks[block][:3]
        return source[z, :, spans[block]] + coupling(
            z,
            half,
            starts[block],
            size,
            east[z],
            north[z],
            south_terms,
            north_rows,
            west[...],
            column,
        )

    def layer(z, carry):
        result = []
        for block, (flow, first_part) in enumerate(carry):
            inverse, ratio, lead = blocks[block][3:6]
            particulars[block][z] = flow * inverse[z]
            first_part = first_part + lead[z] * flow
            result.append((local(z + 1, block) + flow * ratio[z], first_part))
        return tuple(result)

    carry = tuple((local(0, block), jnp.zeros((ROWS, size), F32)) for block in range(2))
    carry = lax.fori_loop(0, depth - 1, layer, carry, unroll=True)
    last = depth - 1
    for block, (flow, first_part) in enumerate(carry):
        inverse, ratio, lead = blocks[block][3:6]
        there = slice(block * size, (block + 1) * size)
        first_part = first_part + lead[last] * flow
        last_part = flow * inverse[last]
        particulars[block][last] = last_part
        asked = jnp.where(me % 2 == 0, last_part, first_part)
        shared = shares[block][0] * asked
        outer = jnp.where(me == 1, last_part, jnp.where(me == 2, first_part, 0.0))
        given = outer + jnp.where((me == 0) | (me == 3), shared, -shared)
        near[0, :, there] = asked
        near[1, :, there] = given
        far[:, there] = given


def smoothed_kernel(depth, flags, *refs):
    own, near, skip, cross, joined = refs[:5]
    keeps = refs[5:7]
    blocks = (refs[7:11], refs[11:15])
    half, colour, result = refs[15:18]
    smoothed, sems = refs[18:]
    me = flags[14]
    size = blocks[0][0].shape[2]
    spans = [lane_slice(flags[6 + block], size) for block in range(2)]
    lines = []
    for block, state in enumerate(blocks):
        there = slice(block * size, (block + 1) * size)
        kept = keeps[block]
        lead_of = (own[1, :, there] + near[1, :, there]) - (skip[:, there] + cross[:, there])
        middle = jnp.where(me < 2, lead_of, -lead_of) * joined[block]
        step = own[0, :, there] - near[0, :, there]
        step = jnp.where(me % 2 == 0, step, -step) * kept[1]
        lines.append((*ends(me, step + kept[0] * middle, middle), *state))
    chosen = [colour[:, here] == 1 for here in spans]
    count = sems.shape[0]
    layers = depth // count
    copies = [
        pltpu.make_async_copy(
            smoothed.at[pl.ds(at * layers, layers)],
            result.at[pl.ds(at * layers, layers)],
            sems.at[at],
        )
        for at in range(count)
    ]

    def emit(z, values, state):
        for value, here, mine in zip(values, spans, chosen):
            smoothed[z, :, here] = jnp.where(mine, value, half[z, :, here])
        if z % layers == 0:
            copies[z // layers].start()
        return state

    back_substitute(depth, lines, emit)
    for copy in copies:
        copy.wait()


PAIR = [(0, 1), (1, 0)]
NEAR = [(0, 1), (1, 0), (2, 3), (3, 2)]
MIDDLE = [(1, 2), (2, 1)]
SKIP = [(0, 2), (2, 0), (1, 3), (3, 1)]
CROSS = [(0, 3), (3, 0), (1, 2), (2, 1)]


def exchange_edges(edges):
    to_near, to_middle, *column = edges
    return [
        lax.ppermute(to_near, "gy", NEAR),
        lax.ppermute(to_middle, "gy", MIDDLE),
        *[lax.ppermute(piece, "gx", PAIR) for piece in column],
    ]


def fast_body(spectral, shifts, colour, pressure, source):
    depth, items, width = pressure.shape
    vert = float((depth * 4) ** 2 // 4)
    waves = spectral.shape[3]
    rows = depth * items
    block_size, third = width // 2, 3 * width // 8
    known = width - third

    def flags():
        gx, gz, gy = (lax.axis_index(axis) for axis in ("gx", "gz", "gy"))

        def placed(start, size):
            return jnp.where(gx == 1, start, width - start - size)

        block_one, block_two = placed(0, block_size), placed(block_size, block_size)
        start_one = placed(0, known)
        extra = known - block_size
        return [
            gx,
            placed(0, LANES),
            placed(LANES, known - LANES),
            start_one,
            gx,
            placed(known, third),
            block_one,
            block_two,
            placed(block_size, extra) - block_two,
            placed(block_size, extra) - start_one,
            block_one - start_one,
            0,
            gy > 0,
            gy < 3,
            gz,
            ((gy == 1) | (gy == 2)).astype(jnp.int32),
            gy % 2,
        ]

    def shaped(*shape, dtype=F32):
        return jax.ShapeDtypeStruct(shape, dtype)

    groups = NX // LANES
    parts = waves // LANES
    inner_ys, last_ys = (1, 2, 3), tuple(range(4, items - 1))
    last_rows = len(last_ys) * depth
    column_type = shaped(ROWS, LANES)
    coefficients = spectral.reshape(2, rows, waves)

    def scratch(count):
        return [
            pltpu.VMEM((items, depth), jnp.int32),
            pltpu.SemaphoreType.DMA,
            pltpu.VMEM((count, LANES), jnp.int32),
            pltpu.VMEM((6, count, LANES), F32),
            pltpu.VMEM((parts, 2, rows, LANES), F32),
            pltpu.SemaphoreType.DMA((parts, depth // STEP)),
            pltpu.VMEM((3, 2 * LANES, LANES), jnp.bfloat16),
            pltpu.VMEM((2, groups, LANES), F32),
            pltpu.VMEM((count // depth, groups * depth, 4 * LANES), jnp.bfloat16),
            pltpu.VMEM((count // depth, groups * depth, LANES), F32),
        ]

    def wide_types(ys):
        return [shaped(len(ys) * depth, width)] * 2 + [shaped(6, len(ys), LANES)]

    shift_rows = shifts.T
    outer_ys = (0, items - 1)
    sums, own_outer, outer_kept = call(
        functools.partial(wide_sums_kernel, outer_ys),
        "outer_row_sums",
        wide_types(outer_ys),
        [],
        scratch=scratch(2 * depth),
        far=[shift_rows, coefficients],
        mib=SUMS_GRANT,
    )
    outer = lax.ppermute(sums, "gx", PAIR)
    shift_rows, _ = lax.optimization_barrier((shift_rows, own_outer))
    sums, own_inner, inner_kept, p_column = call(
        functools.partial(inner_sums_kernel, inner_ys),
        "inner_row_sums",
        wide_types(inner_ys) + [column_type],
        [],
        scratch=[pltpu.VMEM((depth, ROWS, LANES), F32), pltpu.SemaphoreType.DMA]
        + scratch(len(inner_ys) * depth),
        far=[shift_rows, coefficients, pressure],
        mib=20,
    )
    inner = lax.ppermute(sums, "gx", PAIR)
    edge_row, edge_column = shaped(depth, width), shaped(ROWS, LANES)
    edges = [edge_row, edge_row, edge_column]
    last_one, last_two, own_last, own_columns = call(
        functools.partial(last_sums_kernel, last_ys),
        "last_row_sums",
        [
            shaped(last_rows + ROWS, known),
            shaped(last_rows, third),
            shaped(last_rows, width),
            shaped(6, ROWS, LANES),
        ],
        [outer_kept, inner_kept, p_column],
        scratch=[pltpu.VMEM((6, len(last_ys), LANES), F32)] + scratch(last_rows),
        far=[shift_rows, coefficients],
        mib=20,
    )
    pressure_rows, _ = lax.optimization_barrier((pressure, own_last))
    to_near, to_middle = call(
        functools.partial(outer_field_kernel, depth),
        "outer_field",
        [shaped(2 * depth, width)] * 2,
        [own_outer, outer, pressure_rows],
        flags,
    )
    from_near, from_middle = exchange_edges([to_near, to_middle])
    last_one = lax.ppermute(last_one, "gx", PAIR)
    wide, *around = call(
        functools.partial(wide_field_kernel, depth),
        "wide_field",
        [shaped(rows - last_rows, width)] + [edge_row] * 2 + [shaped(depth, items, width)] * 4,
        [
            *(own_outer, outer, own_inner, inner, to_near, to_middle),
            *(from_near, from_middle, pressure),
        ],
        flags,
        [pltpu.VMEM((depth, width), F32)] * 2,
    )
    last_two, _ = lax.optimization_barrier((last_two, wide))
    last_two = lax.ppermute(last_two, "gx", PAIR)
    log_near, resist_near, *columns = call(
        functools.partial(first_field_kernel, depth),
        "first_field",
        [shaped(depth, items, known)] * 2 + [edge_column] * 5,
        [wide, own_last, last_one, own_columns],
        flags,
        [pltpu.VMEM((known // LANES, rows, LANES), F32)],
    )
    block = shaped(depth, items, block_size)

    state_types = [block] * 2 + [edge_column] + [block] * 4

    def first_sweep(at, resist):
        return call(
            functools.partial(first_sweep_kernel, depth, vert, at),
            "first_sweep",
            state_types + [shaped(5, items, block_size)],
            [resist, *columns, *around, source],
            flags,
            [pltpu.VMEM((depth, items, block_size), F32)] * 3,
        )

    *state_one, reduced_one = first_sweep(0, resist_near)
    near_one = lax.ppermute(reduced_one, "gz", NEAR)
    last_two, _ = lax.optimization_barrier((last_two, reduced_one))
    log_far, resist_far = call(
        functools.partial(second_field_kernel, depth),
        "second_field",
        [shaped(depth, items, third), block],
        [wide, own_last, last_two, resist_near],
        flags,
        [pltpu.VMEM((third // LANES, rows, LANES), F32)],
    )
    *state_two, reduced_two = first_sweep(1, resist_far)
    near_two = lax.ppermute(reduced_two, "gz", NEAR)
    (log_perm,) = call(
        functools.partial(join_columns_kernel, depth),
        "log_perm",
        [shaped(depth, items, width)],
        [log_near, log_far, reduced_two],
        flags,
    )
    def join(reduced, near):
        across, kept = call(
            pair_kernel,
            "join_pair",
            [shaped(2, items, block_size), shaped(3, items, block_size)],
            [reduced, near],
            flags,
        )
        return across, lax.ppermute(across, "gz", SKIP), kept

    pair_one, pair_two = join(reduced_one, near_one), join(reduced_two, near_two)
    keeps = [pair_one[2], pair_two[2]]
    half, *h_edges, joined = call(
        functools.partial(half_kernel, depth),
        "half",
        [shaped(depth, items, width), *edges, shaped(2, items, block_size)],
        [*pair_one, *pair_two, *state_one[3:], *state_two[3:], pressure, colour],
        flags,
    )
    h_edges = exchange_edges(h_edges)
    weights = [[*state[:3], *state[4:]] for state in (state_one, state_two)]
    current_one, current_two, to_near, to_far = call(
        functools.partial(second_sweep_kernel, depth),
        "second_sweep",
        [block, block, shaped(2, items, width), shaped(items, width)],
        [half, *h_edges, source, around[0], *keeps, *weights[0], *weights[1]],
        flags,
        [pltpu.VMEM((depth, width), F32)] * 2,
    )
    from_near, from_skip, from_cross = (
        lax.ppermute(planes, "gz", pairs)
        for planes, pairs in ((to_near, NEAR), (to_far, SKIP), (to_far, CROSS))
    )
    (smoothed,) = call(
        functools.partial(smoothed_kernel, depth),
        "smoothed",
        [shaped(depth, items, width)],
        [
            *(to_near, from_near, from_skip, from_cross, joined, *keeps),
            *(current_one, *state_one[4:]),
            *(current_two, *state_two[4:]),
            *(half, colour),
        ],
        flags,
        [pltpu.VMEM((depth, items, width), F32), pltpu.SemaphoreType.DMA((4,))],
        out=IN_HBM,
    )
    return (log_perm, smoothed)


def solution(mesh):
    body = fast_body if suits(mesh) else generic_body
    in_specs = (
        P(None, "gz", "gy", "gx"),
        P("gz", "gy"),
        P("gy", "gx"),
        P("gz", "gy", "gx"),
        P("gz", "gy", "gx"),
    )
    out_specs = (P("gz", "gy", "gx"), P("gz", "gy", "gx"))
    return jax.shard_map(body, mesh=mesh, in_specs=in_specs, out_specs=out_specs, check_vma=False)
```

```python
import functools
import math

import jax
import jax.numpy as jnp


from jax import lax
from jax.experimental import pallas as pl
from jax.experimental.pallas import tpu as pltpu
from jax.sharding import PartitionSpec as P

NX = 2048


STORE = 1.0


def padded_2(block, sides, width):
    for axis, dim in sides:
        count = lax.axis_size(axis)
        forward = [(i, i + 1) for i in range(count - 1)]
        backward = [(target, source) for source, target in forward]
        low = lax.ppermute(
            lax.slice_in_dim(block, block.shape[dim] - width, None, axis=dim), axis, forward
        )
        high = lax.ppermute(lax.slice_in_dim(block, 0, width, axis=dim), axis, backward)
        block = jnp.concatenate([low, block, high], axis=dim)
    return block


def twisted_coeffs(spectral, shifts, first_wave):
    count = spectral.shape[3]
    wave_index = first_wave + jnp.arange(count, dtype=jnp.int32)
    wave_turns = shifts[:, :, None] * wave_index[None, None, :] % NX
    phase_angle = wave_turns.astype(jnp.float32) * (2.0 * math.pi / NX)
    cosine = jnp.cos(phase_angle)
    sine_part = jnp.sin(phase_angle)
    real_part = spectral[0] * cosine - spectral[1] * sine_part
    imag_part = spectral[0] * sine_part + spectral[1] * cosine
    return jnp.stack([real_part, imag_part])


def basis(count, first_cell, width_cells):
    wave_index = jnp.arange(count, dtype=jnp.int32)
    cell_index = first_cell + jnp.arange(width_cells, dtype=jnp.int32)
    wave_turns = wave_index[:, None] * cell_index[None, :] % NX
    phase_angle = wave_turns.astype(jnp.float32) * (2.0 * math.pi / NX)
    offsets = jnp.concatenate(
        [jnp.zeros((count, 1), jnp.float32), jnp.full((count, 1), 0.5 * math.pi, jnp.float32)],
        axis=0,
    )
    stacked = jnp.concatenate([phase_angle, phase_angle], axis=0) + offsets
    return jnp.cos(stacked) * (1.0 / math.sqrt(NX))


def flatten_pair(piece):
    depth, items, count = (piece.shape[1], piece.shape[2], piece.shape[3])
    return jnp.concatenate(
        [piece[0].reshape(depth * items, count), piece[1].reshape(depth * items, count)], axis=1
    )


def harmonic(center, beside):
    return 2.0 * center * beside / (center + beside)


def thomas(lower_diagonal, main_diagonal, upper_diagonal, right_hand_side):

    def thomas_forward_scan(carried_state, row_entries):
        previous_ratio, previous_eliminated = carried_state
        column_lower, main_c, sup_c, column_right_hand = row_entries
        present_denominator = main_c - column_lower * previous_ratio
        present_ratio = sup_c / present_denominator
        present_eliminated = (
            column_right_hand - column_lower * previous_eliminated
        ) / present_denominator
        return ((present_ratio, present_eliminated), (present_ratio, present_eliminated))

    zeroed_layer = jnp.zeros(right_hand_side.shape[1:], right_hand_side.dtype)
    unused_output, (ratio_rows, eliminated_rows) = lax.scan(
        thomas_forward_scan,
        (zeroed_layer, zeroed_layer),
        (lower_diagonal, main_diagonal, upper_diagonal, right_hand_side),
    )

    def thomas_backward_scan(following_value, row_entries):
        column_ratio, column_eliminated = row_entries
        present_value = column_eliminated - column_ratio * following_value
        return (present_value, present_value)

    unused_output, solved_values = lax.scan(
        thomas_backward_scan, zeroed_layer, (ratio_rows, eliminated_rows), reverse=True
    )
    return solved_values


def factor(lower_diagonal, main_diagonal, upper_diagonal):

    def factor_forward_scan(previous_ratio, row_entries):
        column_lower, main_c, sup_c = row_entries
        present_denominator = main_c - column_lower * previous_ratio
        present_ratio = sup_c / present_denominator
        return (present_ratio, (present_denominator, present_ratio))

    unused_output, (denominator_rows, ratio_rows) = lax.scan(
        factor_forward_scan,
        jnp.zeros_like(main_diagonal[0]),
        (lower_diagonal, main_diagonal, upper_diagonal),
    )
    return (denominator_rows, ratio_rows)


def solve_factored(lower_diagonal, denominator_rows, ratio_rows, right_hand_side):

    def solve_forward_scan(previous_eliminated, row_entries):
        column_lower, column_denominator, column_right_hand = row_entries
        present_eliminated = (
            column_right_hand - column_lower[None] * previous_eliminated
        ) / column_denominator[None]
        return (present_eliminated, present_eliminated)

    unused_output, eliminated_rows = lax.scan(
        solve_forward_scan,
        jnp.zeros_like(right_hand_side[0]),
        (lower_diagonal, denominator_rows, right_hand_side),
    )

    def solve_backward_scan(following_value, row_entries):
        column_ratio, column_eliminated = row_entries
        present_value = column_eliminated - column_ratio[None] * following_value
        return (present_value, present_value)

    unused_output, solved_values = lax.scan(
        solve_backward_scan,
        jnp.zeros_like(right_hand_side[0]),
        (ratio_rows, eliminated_rows),
        reverse=True,
    )
    return solved_values


def generic_body(spectral, shifts, colour, pressure, source):
    total_depth = pressure.shape[0] * lax.axis_size("gz")
    vert_factor = float(total_depth * total_depth // 4)
    width_cells = spectral.shape[3]
    first_cell = lax.axis_index("gx") * width_cells
    twisted = twisted_coeffs(spectral, shifts, first_cell)
    piece = lax.all_to_all(twisted, "gx", split_axis=1, concat_axis=3, tiled=True)
    depth = piece.shape[1]
    items = piece.shape[2]
    length = piece.shape[3]
    flat = flatten_pair(piece)
    block_width = min(512, length)
    blocks = [
        jnp.dot(
            flat,
            basis(length, block * block_width, block_width),
            precision=lax.Precision.HIGHEST,
            preferred_element_type=jnp.float32,
        )
        for block in range(length // block_width)
    ]
    field_rows = jnp.concatenate(blocks, axis=1).reshape(depth, items, length)
    log_perm = lax.all_to_all(field_rows, "gx", split_axis=2, concat_axis=0, tiled=True)
    perm = jnp.exp(log_perm)
    padded = padded_2(perm, (("gx", 2), ("gz", 0), ("gy", 1)), 1)
    w_zm = vert_factor * harmonic(perm, padded[:-2, 1:-1, 1:-1])
    w_zp = vert_factor * harmonic(perm, padded[2:, 1:-1, 1:-1])
    w_ym = harmonic(perm, padded[1:-1, :-2, 1:-1])
    w_yp = harmonic(perm, padded[1:-1, 2:, 1:-1])
    w_xm = harmonic(perm, padded[1:-1, 1:-1, :-2])
    w_xp = harmonic(perm, padded[1:-1, 1:-1, 2:])
    main_diagonal = STORE + w_xm + w_xp + w_ym + w_yp + w_zm + w_zp
    lower_diagonal = -w_zm
    upper_diagonal = -w_zp
    zeroed_layer = jnp.zeros_like(main_diagonal[0])
    inner_sub = jnp.concatenate([zeroed_layer[None], lower_diagonal[2:-1]], axis=0)
    inner_sup = jnp.concatenate([upper_diagonal[1:-2], zeroed_layer[None]], axis=0)
    inner_main = main_diagonal[1:-1]
    denominator_rows, ratio_rows = factor(inner_sub, inner_main, inner_sup)
    unit_rhs = jnp.zeros((inner_main.shape[0], 2) + zeroed_layer.shape, jnp.float32)
    unit_rhs = unit_rhs.at[0, 0].set(-lower_diagonal[1])
    unit_rhs = unit_rhs.at[-1, 1].set(-upper_diagonal[-2])
    coupled = solve_factored(inner_sub, denominator_rows, ratio_rows, unit_rhs)
    left_part = coupled[:, 0]
    right_part = coupled[:, 1]
    sub_first = lower_diagonal[0]
    main_first = main_diagonal[0] + upper_diagonal[0] * left_part[0]
    sup_first = upper_diagonal[0] * right_part[0]
    sub_last = lower_diagonal[-1] * left_part[-1]
    main_last = main_diagonal[-1] + lower_diagonal[-1] * right_part[-1]
    sup_last = upper_diagonal[-1]

    def line_solve(current):
        cycle = padded_2(current, (("gx", 2), ("gy", 1)), 1)
        right_hand_side = source + w_xm * cycle[:, 1:-1, :-2] + w_xp * cycle[:, 1:-1, 2:]
        right_hand_side = right_hand_side + w_ym * cycle[:, :-2, 1:-1] + w_yp * cycle[:, 2:, 1:-1]
        particular = solve_factored(
            inner_sub, denominator_rows, ratio_rows, right_hand_side[1:-1][:, None]
        )[:, 0]
        rhs_first = right_hand_side[0] - upper_diagonal[0] * particular[0]
        rhs_last = right_hand_side[-1] - lower_diagonal[-1] * particular[-1]
        reduced_rows = jnp.stack(
            [sub_first, main_first, sup_first, rhs_first, sub_last, main_last, sup_last, rhs_last]
        )
        gathered = lax.all_gather(reduced_rows, "gz", axis=0, tiled=True)
        segments = gathered.shape[0] // 8
        system = gathered.reshape((2 * segments, 4) + zeroed_layer.shape)
        reduced_sol = thomas(system[:, 0], system[:, 1], system[:, 2], system[:, 3])
        own_pair = lax.dynamic_slice_in_dim(reduced_sol, 2 * lax.axis_index("gz"), 2, 0)
        face_first = own_pair[0]
        face_last = own_pair[1]
        inner = particular + face_first[None] * left_part + face_last[None] * right_part
        return jnp.concatenate([face_first[None], inner, face_last[None]], axis=0)

    half = jnp.where((colour == 0)[None], line_solve(pressure), pressure)
    smoothed = jnp.where((colour == 1)[None], line_solve(half), half)
    return (log_perm, smoothed)


LANES = 128
ROWS = 8
F32 = jnp.float32
MIB = 1 << 20
SUMS_GRANT = 60


def suits(mesh):
    sizes = dict(mesh.shape)
    return sizes["gx"] == 2 and sizes["gz"] == 4 and sizes["gy"] == 4


def params(mib):
    return pltpu.CompilerParams(vmem_limit_bytes=mib * MIB)


def cos_sin(turns):
    quarter = (turns + NX // 8) >> 9
    angle = (turns - (quarter << 9)).astype(F32) * (2.0 * math.pi / NX)
    square = angle * angle
    sine = angle * (
        1.0
        + square * (-1.0 / 6 + square * (1.0 / 120 + square * (-1.0 / 5040 + square / 362880)))
    )
    cosine = 1.0 + square * (
        -0.5 + square * (1.0 / 24 + square * (-1.0 / 720 + square * (1.0 / 40320)))
    )
    odd = (quarter & 1) == 1
    first = jnp.where(odd, sine, cosine)
    second = jnp.where(odd, cosine, sine)
    cos_sign = jnp.where(((quarter + 1) & 2) == 2, -1.0, 1.0)
    sin_sign = jnp.where((quarter & 2) == 2, -1.0, 1.0)
    return first * cos_sign, second * sin_sign


def split(values):
    high = values.astype(jnp.bfloat16)
    return high, (values - high.astype(F32)).astype(jnp.bfloat16)


def times(first, second):
    return (
        first[0] * second[0] - first[1] * second[1],
        first[0] * second[1] + first[1] * second[0],
    )


def plus(first, second):
    return (first[0] + second[0], first[1] + second[1])


def minus(first, second):
    return (first[0] - second[0], first[1] - second[1])


def quarter_turn(value):
    return (-value[1], value[0])


def four_point(first, second, third, fourth):
    even, gap = plus(first, third), minus(first, third)
    odd, turned = plus(second, fourth), quarter_turn(minus(second, fourth))
    return [plus(even, odd), plus(gap, turned), minus(even, odd), minus(gap, turned)]


def eight_point(values):
    even = four_point(*values[0::2])
    odd = four_point(*values[1::2])
    root = math.sqrt(0.5)
    real, imag = odd[1]
    odd[1] = (root * (real - imag), root * (real + imag))
    odd[2] = quarter_turn(odd[2])
    real, imag = odd[3]
    odd[3] = (-root * (real + imag), root * (real - imag))
    return [plus(*pair) for pair in zip(even, odd)] + [minus(*pair) for pair in zip(even, odd)]


def fill_tables(basis, turns):
    groups = NX // LANES
    shape = (LANES, LANES)
    lane = lane_of(shape)
    cells = (lane % groups) * (LANES // groups) + lane // groups
    cosine, sine = cos_sin((row_of(shape) * cells) % LANES * groups)
    for at, value in enumerate((cosine, -sine)):
        rows = slice(at * LANES, (at + 1) * LANES)
        high, low = split(value * (1.0 / math.sqrt(NX)))
        basis[0, rows], basis[1, rows], basis[2, rows] = high, high, low
    shape = (groups, LANES)
    turns[0], turns[1] = cos_sin(row_of(shape) * lane_of(shape))


def diagonal_of(depth):
    square = (depth, depth)
    return row_of(square) == lane_of(square)


def shift_columns(shifts, rows_of, columns):
    depth = shifts.shape[1]
    diagonal = diagonal_of(depth)
    for at, y in enumerate(rows_of):
        spread = jnp.where(diagonal, shifts[y : y + 1, :].astype(F32), 0.0)
        shift = jnp.broadcast_to(jnp.sum(spread, axis=1, keepdims=True), (depth, LANES))
        columns[at * depth : (at + 1) * depth, :] = shift.astype(jnp.int32)


def edge_columns(ys, depth, edges, kept):
    kept[...] = jnp.zeros_like(kept)
    diagonal = diagonal_of(depth)
    for at in range(len(ys)):
        rows = slice(at * depth, (at + 1) * depth)
        for side in range(edges.shape[0]):
            lane = 0 if side % 2 else LANES - 1
            column = jnp.broadcast_to(edges[side, rows, lane : lane + 1], (depth, depth))
            row = jnp.sum(jnp.where(diagonal, column, 0.0), axis=0, keepdims=True)
            kept[side, at : at + 1, :depth] = row


def twisted(first_wave, shift, coefficients, rows):
    lane = lane_of(shift.shape)
    phase = cos_sin((shift * (lane + first_wave)) & (NX - 1))
    turn = cos_sin((shift * LANES) & (NX - 1))
    values = []
    for part in range(coefficients.shape[0]):
        values.append(times((coefficients[part, 0, rows], coefficients[part, 1, rows]), phase))
        phase = times(phase, turn)
    return values


def interleave(tiles):
    count = len(tiles)
    lane = lane_of(tiles[0].shape)
    bit = count // 2
    while bit:
        low = (lane & bit) == 0
        moved = list(tiles)
        for at in range(count):
            if not at & bit:
                first, second = tiles[at], tiles[at | bit]
                crossed = jnp.take_along_axis(
                    jnp.where(low, second, first), lane ^ bit, axis=1
                )
                moved[at] = jnp.where(low, first, crossed)
                moved[at | bit] = jnp.where(low, crossed, second)
        tiles = moved
        bit //= 2
    return tiles


STEP = 16


def fill_left(g, at, y, depth, items, columns, coefficients, turns, left, part):
    groups = NX // LANES
    sign = 1.0 - 2.0 * g.astype(F32)
    first_wave = g * (coefficients.shape[0] * LANES)
    rows = pl.ds(part * STEP * items + y, STEP, stride=items)
    shift = columns[pl.ds(at * depth + part * STEP, STEP), :]
    values = twisted(first_wave, shift, coefficients, rows)
    angles = [2 * math.pi * p / groups for p in range(len(values))]
    turned = [
        times(value, (sign * math.cos(angle), sign * math.sin(angle)))
        if angle
        else (sign * value[0], sign * value[1])
        for angle, value in zip(angles, values)
    ]
    even, odd = eight_point(values), eight_point(turned)
    for group in range(groups):
        value = odd[group // 2] if group % 2 else even[group // 2]
        if group:
            value = times(value, (turns[0, group : group + 1], turns[1, group : group + 1]))
        first = group * depth + part * STEP
        for place_of, piece in enumerate(value):
            for half, bits in enumerate(split(piece)):
                target = (2 * half + place_of) * LANES
                left[first : first + STEP, target : target + LANES] = bits


def finish_row(at, depth, basis, left, right, emit):
    groups = NX // LANES
    spread = jnp.concatenate([left[...], left[:, : 2 * LANES]], axis=1)
    bases = basis[...].reshape(-1, LANES)
    right[...] = jnp.dot(spread, bases, preferred_element_type=F32)
    for part in range(depth // ROWS):
        tiles = [
            right[group * depth + part * ROWS : group * depth + (part + 1) * ROWS]
            for group in range(groups)
        ]
        emit(pl.ds(at * depth + part * ROWS, ROWS), interleave(tiles))


def load_coefficients(spectral, coefficients, arrivals, items):
    parts, halves = arrivals.shape
    copies = []
    for half in range(halves):
        rows = slice(half * STEP * items, (half + 1) * STEP * items)
        copies.append(
            [
                pltpu.make_async_copy(
                    spectral.at[:, rows, part * LANES : (part + 1) * LANES],
                    coefficients.at[part, :, rows],
                    arrivals.at[part, half],
                )
                for part in range(parts)
            ]
        )
    for half in copies:
        for copy in half:
            copy.start()
    return copies


def all_rows(g, ys, shifts, shift_copy, copies, columns, coefficients, tables, left, right, emit):
    items, depth = shifts.shape
    basis, turns = tables
    fill_tables(basis, turns)
    shift_copy.wait()
    shift_columns(shifts, ys, columns)
    for half, arriving in enumerate(copies):
        for copy in arriving:
            copy.wait()
        for at, y in enumerate(ys):
            fill_left(g, at, y, depth, items, columns, coefficients, turns, left.at[at], half)
    for at in range(len(ys)):
        finish_row(at, depth, basis, left.at[at], right.at[at], emit)


def keep_edges(rows, tiles, edges):
    count = len(tiles) // 4
    for side in range(edges.shape[0]):
        edges[side, rows] = tiles[(side // 2 + 1) * count - 1 + side % 2]


def inner_sums_kernel(ys, shifts, spectral, pressure, other, own, kept, p_column, *refs):
    tile, sem, *refs = refs
    g = lax.axis_index("gx")
    width = pressure.shape[2]
    there = lane_slice(jnp.where(g == 0, width - LANES, 0), LANES)
    copy = pltpu.make_async_copy(pressure.at[:, :, there], tile, sem)
    copy.start()
    wide_sums_kernel(ys, shifts, spectral, other, own, kept, *refs)
    copy.wait()
    packed = jnp.zeros((ROWS, LANES), F32)
    for z in range(tile.shape[0]):
        packed = packed_with(z, packed, boundary_plane(g, tile[z]), 0)
    p_column[...] = packed


def wide_sums_kernel(ys, shifts, spectral, other, own, kept, *refs):
    local, arrived, columns, edges, coefficients, arrivals, *tables, left, right = refs
    items, depth = shifts.shape
    shift_copy = pltpu.make_async_copy(shifts, local, arrived)
    shift_copy.start()
    copies = load_coefficients(spectral, coefficients, arrivals, items)
    g = lax.axis_index("gx")

    def emit(rows, tiles):
        half = len(tiles) // 2
        keep_edges(rows, tiles, edges)
        for tile, (low, high) in enumerate(zip(tiles[:half], tiles[half:])):
            there = slice(tile * LANES, (tile + 1) * LANES)
            other[rows, there] = jnp.where(g == 0, high, low)
            own[rows, there] = jnp.where(g == 0, low, high)

    all_rows(
        *(g, ys, local, shift_copy, copies, columns, coefficients, tables, left, right, emit)
    )
    edge_columns(ys, depth, edges, kept)


def last_sums_kernel(ys, outer_kept, inner_kept, p_column, shifts, spectral, one, two, own, *refs):
    columns_own, kept, local, arrived, columns, edges, coefficients, *refs = refs
    arrivals, *tables, left, right = refs
    items, depth = shifts.shape
    shift_copy = pltpu.make_async_copy(shifts, local, arrived)
    shift_copy.start()
    copies = load_coefficients(spectral, coefficients, arrivals, items)
    g = lax.axis_index("gx")

    def emit(rows, tiles):
        half = len(tiles) // 2
        keep_edges(rows, tiles, edges)
        others = []
        for tile, (low, high) in enumerate(zip(tiles[:half], tiles[half:])):
            own[rows, tile * LANES : (tile + 1) * LANES] = jnp.where(g == 0, low, high)
            others.append(jnp.where(g == 0, high, low))
        start = 0
        for ref in (one, two):
            count = ref.shape[1] // LANES
            for tile in range(count):
                ref[rows, tile * LANES : (tile + 1) * LANES] = jnp.where(
                    g == 0, others[start + tile], others[half - start - count + tile]
                )
            start += count

    all_rows(
        *(g, ys, local, shift_copy, copies, columns, coefficients, tables, left, right, emit)
    )
    edge_columns(ys, depth, edges, kept)
    sides_of = [
        jnp.concatenate(
            [outer_kept[side, :1], inner_kept[side], kept[side], outer_kept[side, 1:]], axis=0
        )
        for side in range(6)
    ]
    low, high = sides_of[:3], sides_of[3:]
    own_sides = [jnp.where(g == 0, *pair) for pair in ((low[0], high[1]), (low[1], high[2]))]
    own_sides.append(jnp.where(g == 0, low[2], high[0]))
    other_sides = [jnp.where(g == 0, *pair) for pair in ((high[1], low[0]), (high[2], low[1]))]
    other_sides.append(jnp.where(g == 0, high[0], low[2]))
    for at in range(3):
        columns_own[at], columns_own[3 + at] = own_sides[at], other_sides[at]
    extra = slice(one.shape[0] - ROWS, one.shape[0])
    for at, piece in enumerate((*other_sides, own_sides[2], p_column[...])):
        one[extra, at * LANES : (at + 1) * LANES] = piece


ON_CHIP = pl.BlockSpec(memory_space=pltpu.VMEM)
IN_HBM = pl.BlockSpec(memory_space=pltpu.HBM)


def call(
    kernel, name, out_shape, args, flags=None, scratch=(), far=(), mib=20, flops=1, out=ON_CHIP
):
    specs = [ON_CHIP] * len(args) + [IN_HBM] * len(far)
    args = list(args) + list(far)
    body = kernel if flags is None else lambda *refs: kernel(flags(), *refs)
    return pl.pallas_call(
        body,
        out_shape=out_shape,
        in_specs=specs,
        out_specs=jax.tree.map(lambda _: out, out_shape),
        scratch_shapes=list(scratch),
        compiler_params=params(mib),
        cost_estimate=pl.CostEstimate(flops=flops, bytes_accessed=1, transcendentals=0),
        name=name,
    )(*args)


def roll(values, shift, axis):
    return pltpu.roll(values, shift % values.shape[axis], axis)


def lane_of(shape):
    return lax.broadcasted_iota(jnp.int32, shape, 1)


def row_of(shape):
    return lax.broadcasted_iota(jnp.int32, shape, 0)


def column_to(z, packed, target):
    return pltpu.roll(packed, (target - z) % LANES, 1)


def packed_with(z, packed, plane, lane):
    column = jnp.broadcast_to(plane[:, lane : lane + 1], (ROWS, LANES))
    return jnp.where(lane_of((ROWS, LANES)) == z, column, packed)


def inverse_of(values):
    return pl.reciprocal(values, approx=True)


def ordered(z, sums, depth):
    spread = pl.ds(z, ROWS, stride=depth)
    return jnp.concatenate([sums[at, spread] for at in range(sums.shape[0])], axis=1)


def place_tiles(sums, rows, first, values):
    for at in range(values.shape[1] // LANES):
        sums[(first >> 7) + at, rows] = values[:, at * LANES : (at + 1) * LANES]


def boundary_plane(g, plane):
    return jnp.where(g == 0, roll(plane[:, -LANES:], 1, 1), plane[:, :LANES])


def outer_field_kernel(depth, flags, own, other, pressure, to_near, to_middle):
    even = flags[16] == 0
    low, high = slice(0, depth), slice(depth, 2 * depth)
    south, north = own[low] + other[low], own[high] + other[high]
    to_near[low] = jnp.exp(-jnp.where(even, north, south))
    to_middle[low] = jnp.exp(-jnp.where(even, south, north))

    for z in range(depth):
        keep_rows(depth + z, pressure[z], even, to_near, to_middle, slice(None))


def wide_field_kernel(depth, flags, *refs):
    own_outer, outer, own_inner, inner, to_near, to_middle = refs[:6]
    from_near, from_middle, pressure = refs[6:9]
    wide, south_weight, north_weight, p_south, p_north, p_west, p_east = refs[9:16]
    south_rows, north_rows = refs[16:]
    even = flags[16] == 0
    low, high = slice(0, depth), slice(depth, 2 * depth)
    wide[low] = own_outer[low] + outer[low]
    wide[depth:-depth] = own_inner[...] + inner[...]
    wide[-depth:] = own_outer[high] + outer[high]
    near_weight = 2.0 * inverse_of(to_near[low] + from_near[low])
    middle_weight = (2.0 * flags[15].astype(F32)) * inverse_of(to_middle[low] + from_middle[low])
    south = jnp.where(even, middle_weight, near_weight)
    south_weight[...] = south
    north_weight[...] = jnp.where(even, near_weight, middle_weight)
    south_rows[...] = jnp.where(even, from_middle[high], from_near[high])
    north_rows[...] = jnp.where(even, from_near[high], from_middle[high])
    row = row_of(pressure.shape[1:])

    def layer(z, carry):
        plane = pressure[z]
        p_south[z] = jnp.where(row == 0, south_rows[pl.ds(z, 1), :], roll(plane, 1, 0))
        p_north[z] = jnp.where(row == ROWS - 1, north_rows[pl.ds(z, 1), :], roll(plane, -1, 0))
        p_west[z] = roll(plane, 1, 1)
        p_east[z] = roll(plane, -1, 1)
        return carry

    lax.fori_loop(0, depth, layer, 0, unroll=True)


def lane_slice(start, size):
    return pl.ds(pl.multiple_of(start, LANES), size)


def assemble(sums, depth, wide, own, piece, there):
    inside = wide.shape[0] - depth
    place_tiles(sums, slice(0, inside), 0, wide[:inside, there])
    place_tiles(sums, slice(inside, -depth), 0, own[:, there] + piece[: own.shape[0]])
    place_tiles(sums, slice(-depth, None), 0, wide[inside:, there])


def first_field_kernel(depth, flags, *refs):
    wide, own, middle, columns_own = refs[:4]
    log_perm, resist, low_side, high_side, boundary, column, p_column, sums = refs[4:]
    extra = slice(own.shape[0], own.shape[0] + ROWS)
    came = [middle[extra, at * LANES : (at + 1) * LANES] for at in range(5)]
    for at, ref in enumerate((low_side, high_side, boundary)):
        ref[...] = jnp.exp(-(columns_own[at] + came[at]))
    column[...] = jnp.exp(-(columns_own[5] + came[3]))
    p_column[...] = came[4]
    assemble(sums, depth, wide, own, middle, lane_slice(flags[3], log_perm.shape[2]))

    def layer(z, carry):
        plane = ordered(z, sums, depth)
        log_perm[z] = plane
        resist[z] = jnp.exp(-plane)
        return carry

    lax.fori_loop(0, depth, layer, 0, unroll=True)


def second_field_kernel(depth, flags, *refs):
    wide, own, middle, resist_near = refs[:4]
    log_perm, resist, sums = refs[4:]
    third = middle.shape[1]
    assemble(sums, depth, wide, own, middle, lane_slice(flags[5], third))
    extra = resist.shape[2] - third
    target = lane_slice(flags[5] - flags[7], third)
    extra_target = lane_slice(flags[8], extra)
    extra_source = lane_slice(flags[9], extra)

    def layer(z, carry):
        plane = ordered(z, sums, depth)
        log_perm[z] = plane
        resist[z, :, target] = jnp.exp(-plane)
        resist[z, :, extra_target] = resist_near[z, :, extra_source]
        return carry

    lax.fori_loop(0, depth, layer, 0, unroll=True)


def join_columns_kernel(depth, flags, near, far, _, whole):
    def layer(z, carry):
        whole[z, :, lane_slice(flags[3], near.shape[2])] = near[z]
        whole[z, :, lane_slice(flags[5], far.shape[2])] = far[z]
        return carry

    lax.fori_loop(0, depth, layer, 0, unroll=True)


def keep_rows(z, value, even, to_near, to_middle, here):
    south, north = value[0:1, :], value[ROWS - 1 : ROWS, :]
    to_near[pl.ds(z, 1), here] = jnp.where(even, north, south)
    to_middle[pl.ds(z, 1), here] = jnp.where(even, south, north)


def with_first(plane, edge):
    first = jnp.where(lane_of((ROWS, LANES)) == 0, edge, plane[:, :LANES])
    return jnp.concatenate([first, plane[:, LANES:]], axis=1)


def with_last(plane, edge):
    last = jnp.where(lane_of((ROWS, LANES)) == LANES - 1, edge, plane[:, -LANES:])
    return jnp.concatenate([plane[:, :-LANES], last], axis=1)


def coupling(z, field, start, size, east_weight, north_weight, south_terms, north_rows, west, column):
    here = lane_slice(start, size)
    plane = field[z, :, here]
    row = row_of(plane.shape)
    at_start = start == 0
    inner = field[z, :, lane_slice(jnp.where(at_start, size, size - LANES), LANES)]
    west_value = jnp.where(at_start, column_to(z, column, 0), roll(inner, 1, 1))
    east_value = jnp.where(at_start, roll(inner, -1, 1), column_to(z, column, LANES - 1))
    to_east, to_north = east_weight * plane, north_weight * plane
    from_west = with_first(roll(to_east, 1, 1), column_to(z, west, 0) * west_value)
    from_east = east_weight * with_last(roll(plane, -1, 1), east_value)
    from_south = jnp.where(row == 0, south_terms[pl.ds(z, 1), here], roll(to_north, 1, 0))
    from_north = north_weight * jnp.where(
        row == ROWS - 1, north_rows[pl.ds(z, 1), here], roll(plane, -1, 0)
    )
    return (from_west + from_east) + (from_south + from_north)


def edge_weights(flags, start, bound, column, low_side, high_side):
    g = flags[0]
    middle = 2.0 * inverse_of(low_side + high_side)
    across = 2.0 * inverse_of(bound + column)
    none = jnp.zeros_like(across)
    west = jnp.where(start == 0, jnp.where(g == 0, none, across), middle)
    east = jnp.where(start == 0, middle, jnp.where(g == 0, across, none))
    return west, east


def first_sweep_kernel(depth, vert, block, flags, *refs):
    resist, low_side, high_side, r_bound, r_column, p_column = refs[:6]
    south_weight, north_weight, p_south, p_north, p_west, p_east = refs[6:12]
    source = refs[12]
    w_east, w_north, west_out, particular, inverse, ratio, lead, reduced = refs[13:21]
    grounds, rights, verticals = refs[21:]
    start, offset = flags[6 + block], flags[10 + block]
    size = inverse.shape[2]
    shape = (ROWS, size)
    here = lane_slice(start, size)
    inside = lane_slice(offset, size)
    west_weight, east_weight = edge_weights(
        flags, start, r_bound[...], r_column[...], low_side[...], high_side[...]
    )
    west_out[...] = west_weight
    column = p_column[...]
    row = row_of(shape)

    def weigh(z, carry):
        plane = resist[z, :, inside]
        east = 2.0 * inverse_of(plane + roll(plane, -1, 1))
        east = with_last(east, column_to(z, east_weight, LANES - 1))
        west = with_first(roll(east, 1, 1), column_to(z, west_weight, 0))
        north = 2.0 * inverse_of(plane + roll(plane, -1, 0))
        north = jnp.where(row == ROWS - 1, north_weight[pl.ds(z, 1), here], north)
        south = jnp.where(row == 0, south_weight[pl.ds(z, 1), here], roll(north, 1, 0))
        w_east[z], w_north[z] = east, north
        grounds[z] = STORE + ((east + west) + (north + south))
        verticals[z] = (2.0 * vert) * inverse_of(
            plane + resist[jnp.minimum(z + 1, depth - 1), :, inside]
        )
        p_first, p_last = p_west[z, :, here], p_east[z, :, here]
        p_first = with_first(
            p_first, jnp.where(start == 0, column_to(z, column, 0), p_first[:, :LANES])
        )
        p_last = with_last(
            p_last, jnp.where(start == 0, p_last[:, -LANES:], column_to(z, column, LANES - 1))
        )
        rights[z] = source[z, :, here] + (
            (west * p_first + east * p_last)
            + (south * p_south[z, :, here] + north * p_north[z, :, here])
        )
        return carry

    lax.fori_loop(0, depth, weigh, 0, unroll=True)

    def layer(z, carry):
        conduct, flow, product, first_first, first_part = carry
        weight = verticals[z]
        reciprocal = inverse_of(conduct + weight)
        quotient = weight * reciprocal
        led = product * reciprocal
        inverse[z] = reciprocal
        ratio[z] = quotient
        lead[z] = led
        particular[z] = reciprocal * flow
        return (
            grounds[z + 1] + conduct * quotient,
            rights[z + 1] + flow * quotient,
            product * quotient,
            first_first + led * product,
            first_part + led * flow,
        )

    zero = jnp.zeros(shape, F32)
    conduct, flow, product, first_first, first_part = lax.fori_loop(
        0,
        depth - 1,
        layer,
        (grounds[0], rights[0], jnp.ones(shape, F32), zero, zero),
        unroll=True,
    )
    reciprocal = inverse_of(conduct)
    led = product * reciprocal
    inverse[depth - 1] = reciprocal
    ratio[depth - 1] = zero
    lead[depth - 1] = led
    particular[depth - 1] = flow * reciprocal
    reduced[0] = first_first + led * product + resist[0, :, inside] * (0.5 / vert)
    reduced[1] = led
    reduced[2] = reciprocal + resist[depth - 1, :, inside] * (0.5 / vert)
    reduced[3] = first_part + led * flow
    reduced[4] = flow * reciprocal


def pair_kernel(flags, own, near, across, kept):
    me = flags[14]
    even, lower = me % 2 == 0, me < 2
    first, second = [
        [jnp.where(flip, own[at], near[at]) for at in range(5)]
        for flip in (even, jnp.logical_not(even))
    ]
    reciprocal = inverse_of(first[2] + second[0])
    step = (first[4] - second[3]) * reciprocal
    through = jnp.where(lower, second[1], first[1])
    share = through * reciprocal
    across[0] = jnp.where(lower, second[2], first[0]) - through * share
    across[1] = jnp.where(lower, second[4], first[3]) + jnp.where(
        lower, through * step, -through * step
    )
    kept[0], kept[1], kept[2] = share, reciprocal, step


def ends(me, inner, middle):
    zero = jnp.zeros_like(inner)
    odd = me % 2 == 1
    enters = jnp.where(odd, inner, jnp.where(me == 2, middle, zero))
    leaves = jnp.where(odd, jnp.where(me == 1, middle, zero), inner)
    return enters, leaves


def back_substitute(depth, lines, emit):
    last = depth - 1
    values = tuple(
        (particular[last] + lead[last] * enters) - inverse[last] * leaves
        for enters, leaves, particular, inverse, ratio, lead in lines
    )
    state = emit(last, values, jnp.zeros((ROWS, LANES), F32))

    for z in range(last - 1, -1, -1):
        values = tuple(
            (particular[z] + lead[z] * enters) + ratio[z] * beyond
            for (enters, _, particular, _, ratio, lead), beyond in zip(lines, values)
        )
        state = emit(z, values, state)
    return state


def half_kernel(depth, flags, *refs):
    pairs = (refs[0:3], refs[3:6])
    blocks = (refs[6:10], refs[10:14])
    pressure, colour = refs[14:16]
    half, to_near, to_middle, boundary, joined = refs[16:]
    me, g, even = flags[14], flags[0], flags[16] == 0
    size = blocks[0][0].shape[2]
    spans = [lane_slice(flags[6 + block], size) for block in range(2)]
    lines = []
    for block, state in enumerate(blocks):
        across, other, kept = pairs[block]
        sum_of = inverse_of(across[0] + other[0])
        joined[block] = sum_of
        lead_of = across[1] - other[1]
        middle = jnp.where(me < 2, lead_of, -lead_of) * sum_of
        inner = kept[2] + kept[0] * middle
        lines.append((*ends(me, inner, middle), *state))
    chosen = [colour[:, here] == 0 for here in spans]

    def emit(z, values, packed):
        for block, (value, here) in enumerate(zip(values, spans)):
            value = jnp.where(chosen[block], value, pressure[z, :, here])
            half[z, :, here] = value
            keep_rows(z, value, even, to_near, to_middle, here)
            if not block:
                packed = packed_with(z, packed, boundary_plane(g, value), 0)
        return packed

    boundary[...] = back_substitute(depth, lines, emit)


def second_sweep_kernel(depth, flags, *refs):
    half, h_near, h_middle, h_column, source, south_weight = refs[:6]
    shares = refs[6:8]
    blocks = (refs[8:14], refs[14:20])
    particulars, near, far = refs[20:22], refs[22], refs[23]
    south_terms, north_rows = refs[24:]
    me, even = flags[14], flags[16] == 0
    size = particulars[0].shape[2]
    starts = [flags[6 + block] for block in range(2)]
    spans = [lane_slice(start, size) for start in starts]
    column = h_column[...]
    south_terms[...] = south_weight[...] * jnp.where(even, h_middle[...], h_near[...])
    north_rows[...] = jnp.where(even, h_near[...], h_middle[...])

    def local(z, block):
        east, north, west = blocks[block][:3]
        return source[z, :, spans[block]] + coupling(
            z,
            half,
            starts[block],
            size,
            east[z],
            north[z],
            south_terms,
            north_rows,
            west[...],
            column,
        )

    def layer(z, carry):
        result = []
        for block, (flow, first_part) in enumerate(carry):
            inverse, ratio, lead = blocks[block][3:6]
            particulars[block][z] = flow * inverse[z]
            first_part = first_part + lead[z] * flow
            result.append((local(z + 1, block) + flow * ratio[z], first_part))
        return tuple(result)

    carry = tuple((local(0, block), jnp.zeros((ROWS, size), F32)) for block in range(2))
    carry = lax.fori_loop(0, depth - 1, layer, carry, unroll=True)
    last = depth - 1
    for block, (flow, first_part) in enumerate(carry):
        inverse, ratio, lead = blocks[block][3:6]
        there = slice(block * size, (block + 1) * size)
        first_part = first_part + lead[last] * flow
        last_part = flow * inverse[last]
        particulars[block][last] = last_part
        asked = jnp.where(me % 2 == 0, last_part, first_part)
        shared = shares[block][0] * asked
        outer = jnp.where(me == 1, last_part, jnp.where(me == 2, first_part, 0.0))
        given = outer + jnp.where((me == 0) | (me == 3), shared, -shared)
        near[0, :, there] = asked
        near[1, :, there] = given
        far[:, there] = given


def smoothed_kernel(depth, flags, *refs):
    own, near, skip, cross, joined = refs[:5]
    keeps = refs[5:7]
    blocks = (refs[7:11], refs[11:15])
    half, colour, result = refs[15:18]
    smoothed, sems = refs[18:]
    me = flags[14]
    size = blocks[0][0].shape[2]
    spans = [lane_slice(flags[6 + block], size) for block in range(2)]
    lines = []
    for block, state in enumerate(blocks):
        there = slice(block * size, (block + 1) * size)
        kept = keeps[block]
        lead_of = (own[1, :, there] + near[1, :, there]) - (skip[:, there] + cross[:, there])
        middle = jnp.where(me < 2, lead_of, -lead_of) * joined[block]
        step = own[0, :, there] - near[0, :, there]
        step = jnp.where(me % 2 == 0, step, -step) * kept[1]
        lines.append((*ends(me, step + kept[0] * middle, middle), *state))
    chosen = [colour[:, here] == 1 for here in spans]
    count = sems.shape[0]
    layers = depth // count
    copies = [
        pltpu.make_async_copy(
            smoothed.at[pl.ds(at * layers, layers)],
            result.at[pl.ds(at * layers, layers)],
            sems.at[at],
        )
        for at in range(count)
    ]

    def emit(z, values, state):
        for value, here, mine in zip(values, spans, chosen):
            smoothed[z, :, here] = jnp.where(mine, value, half[z, :, here])
        if z % layers == 0:
            copies[z // layers].start()
        return state

    back_substitute(depth, lines, emit)
    for copy in copies:
        copy.wait()


PAIR = [(0, 1), (1, 0)]
NEAR = [(0, 1), (1, 0), (2, 3), (3, 2)]
MIDDLE = [(1, 2), (2, 1), (0, 3), (3, 0)]
SKIP = [(0, 2), (2, 0), (1, 3), (3, 1)]
CROSS = [(0, 3), (3, 0), (1, 2), (2, 1)]


def exchange_edges(edges):
    to_near, to_middle, *column = edges
    return [
        lax.ppermute(to_near, "gy", NEAR),
        lax.ppermute(to_middle, "gy", MIDDLE),
        *[lax.ppermute(piece, "gx", PAIR) for piece in column],
    ]


def fast_body(spectral, shifts, colour, pressure, source):
    depth, items, width = pressure.shape
    vert = float((depth * 4) ** 2 // 4)
    waves = spectral.shape[3]
    rows = depth * items
    block_size, third = width // 2, 3 * width // 8
    known = width - third

    def flags():
        gx, gz, gy = (lax.axis_index(axis) for axis in ("gx", "gz", "gy"))

        def placed(start, size):
            return jnp.where(gx == 1, start, width - start - size)

        block_one, block_two = placed(0, block_size), placed(block_size, block_size)
        start_one = placed(0, known)
        extra = known - block_size
        return [
            gx,
            placed(0, LANES),
            placed(LANES, known - LANES),
            start_one,
            gx,
            placed(known, third),
            block_one,
            block_two,
            placed(block_size, extra) - block_two,
            placed(block_size, extra) - start_one,
            block_one - start_one,
            0,
            gy > 0,
            gy < 3,
            gz,
            ((gy == 1) | (gy == 2)).astype(jnp.int32),
            gy % 2,
        ]

    def shaped(*shape, dtype=F32):
        return jax.ShapeDtypeStruct(shape, dtype)

    groups = NX // LANES
    parts = waves // LANES
    inner_ys, last_ys = (1, 2, 3), tuple(range(4, items - 1))
    last_rows = len(last_ys) * depth
    column_type = shaped(ROWS, LANES)
    coefficients = spectral.reshape(2, rows, waves)

    def scratch(count):
        return [
            pltpu.VMEM((items, depth), jnp.int32),
            pltpu.SemaphoreType.DMA,
            pltpu.VMEM((count, LANES), jnp.int32),
            pltpu.VMEM((6, count, LANES), F32),
            pltpu.VMEM((parts, 2, rows, LANES), F32),
            pltpu.SemaphoreType.DMA((parts, depth // STEP)),
            pltpu.VMEM((3, 2 * LANES, LANES), jnp.bfloat16),
            pltpu.VMEM((2, groups, LANES), F32),
            pltpu.VMEM((count // depth, groups * depth, 4 * LANES), jnp.bfloat16),
            pltpu.VMEM((count // depth, groups * depth, LANES), F32),
        ]

    def wide_types(ys):
        return [shaped(len(ys) * depth, width)] * 2 + [shaped(6, len(ys), LANES)]

    shift_rows = shifts.T
    outer_ys = (0, items - 1)
    sums, own_outer, outer_kept = call(
        functools.partial(wide_sums_kernel, outer_ys),
        "outer_row_sums",
        wide_types(outer_ys),
        [],
        scratch=scratch(2 * depth),
        far=[shift_rows, coefficients],
        mib=SUMS_GRANT,
    )
    outer = lax.ppermute(sums, "gx", PAIR)
    shift_rows, _ = lax.optimization_barrier((shift_rows, own_outer))
    sums, own_inner, inner_kept, p_column = call(
        functools.partial(inner_sums_kernel, inner_ys),
        "inner_row_sums",
        wide_types(inner_ys) + [column_type],
        [],
        scratch=[pltpu.VMEM((depth, ROWS, LANES), F32), pltpu.SemaphoreType.DMA]
        + scratch(len(inner_ys) * depth),
        far=[shift_rows, coefficients, pressure],
        mib=20,
    )
    inner = lax.ppermute(sums, "gx", PAIR)
    edge_row, edge_column = shaped(depth, width), shaped(ROWS, LANES)
    edges = [edge_row, edge_row, edge_column]
    last_one, last_two, own_last, own_columns = call(
        functools.partial(last_sums_kernel, last_ys),
        "last_row_sums",
        [
            shaped(last_rows + ROWS, known),
            shaped(last_rows, third),
            shaped(last_rows, width),
            shaped(6, ROWS, LANES),
        ],
        [outer_kept, inner_kept, p_column],
        scratch=[pltpu.VMEM((6, len(last_ys), LANES), F32)] + scratch(last_rows),
        far=[shift_rows, coefficients],
        mib=20,
    )
    pressure_rows, _ = lax.optimization_barrier((pressure, own_last))
    to_near, to_middle = call(
        functools.partial(outer_field_kernel, depth),
        "outer_field",
        [shaped(2 * depth, width)] * 2,
        [own_outer, outer, pressure_rows],
        flags,
    )
    from_near, from_middle = exchange_edges([to_near, to_middle])
    last_one = lax.ppermute(last_one, "gx", PAIR)
    wide, *around = call(
        functools.partial(wide_field_kernel, depth),
        "wide_field",
        [shaped(rows - last_rows, width)] + [edge_row] * 2 + [shaped(depth, items, width)] * 4,
        [
            *(own_outer, outer, own_inner, inner, to_near, to_middle),
            *(from_near, from_middle, pressure),
        ],
        flags,
        [pltpu.VMEM((depth, width), F32)] * 2,
    )
    last_two, _ = lax.optimization_barrier((last_two, wide))
    last_two = lax.ppermute(last_two, "gx", PAIR)
    log_near, resist_near, *columns = call(
        functools.partial(first_field_kernel, depth),
        "first_field",
        [shaped(depth, items, known)] * 2 + [edge_column] * 5,
        [wide, own_last, last_one, own_columns],
        flags,
        [pltpu.VMEM((known // LANES, rows, LANES), F32)],
    )
    block = shaped(depth, items, block_size)

    state_types = [block] * 2 + [edge_column] + [block] * 4

    def first_sweep(at, resist):
        return call(
            functools.partial(first_sweep_kernel, depth, vert, at),
            "first_sweep",
            state_types + [shaped(5, items, block_size)],
            [resist, *columns, *around, source],
            flags,
            [pltpu.VMEM((depth, items, block_size), F32)] * 3,
        )

    *state_one, reduced_one = first_sweep(0, resist_near)
    near_one = lax.ppermute(reduced_one, "gz", NEAR)
    last_two, _ = lax.optimization_barrier((last_two, reduced_one))
    log_far, resist_far = call(
        functools.partial(second_field_kernel, depth),
        "second_field",
        [shaped(depth, items, third), block],
        [wide, own_last, last_two, resist_near],
        flags,
        [pltpu.VMEM((third // LANES, rows, LANES), F32)],
    )
    *state_two, reduced_two = first_sweep(1, resist_far)
    near_two = lax.ppermute(reduced_two, "gz", NEAR)
    (log_perm,) = call(
        functools.partial(join_columns_kernel, depth),
        "log_perm",
        [shaped(depth, items, width)],
        [log_near, log_far, reduced_two],
        flags,
    )
    def join(reduced, near):
        across, kept = call(
            pair_kernel,
            "join_pair",
            [shaped(2, items, block_size), shaped(3, items, block_size)],
            [reduced, near],
            flags,
        )
        return across, lax.ppermute(across, "gz", SKIP), kept

    pair_one, pair_two = join(reduced_one, near_one), join(reduced_two, near_two)
    keeps = [pair_one[2], pair_two[2]]
    half, *h_edges, joined = call(
        functools.partial(half_kernel, depth),
        "half",
        [shaped(depth, items, width), *edges, shaped(2, items, block_size)],
        [*pair_one, *pair_two, *state_one[3:], *state_two[3:], pressure, colour],
        flags,
    )
    h_edges = exchange_edges(h_edges)
    weights = [[*state[:3], *state[4:]] for state in (state_one, state_two)]
    current_one, current_two, to_near, to_far = call(
        functools.partial(second_sweep_kernel, depth),
        "second_sweep",
        [block, block, shaped(2, items, width), shaped(items, width)],
        [half, *h_edges, source, around[0], *keeps, *weights[0], *weights[1]],
        flags,
        [pltpu.VMEM((depth, width), F32)] * 2,
    )
    from_near, from_skip, from_cross = (
        lax.ppermute(planes, "gz", pairs)
        for planes, pairs in ((to_near, NEAR), (to_far, SKIP), (to_far, CROSS))
    )
    (smoothed,) = call(
        functools.partial(smoothed_kernel, depth),
        "smoothed",
        [shaped(depth, items, width)],
        [
            *(to_near, from_near, from_skip, from_cross, joined, *keeps),
            *(current_one, *state_one[4:]),
            *(current_two, *state_two[4:]),
            *(half, colour),
        ],
        flags,
        [pltpu.VMEM((depth, items, width), F32), pltpu.SemaphoreType.DMA((4,))],
        out=IN_HBM,
    )
    return (log_perm, smoothed)


def solution(mesh):
    body = fast_body if suits(mesh) else generic_body
    in_specs = (
        P(None, "gz", "gy", "gx"),
        P("gz", "gy"),
        P("gy", "gx"),
        P("gz", "gy", "gx"),
        P("gz", "gy", "gx"),
    )
    out_specs = (P("gz", "gy", "gx"), P("gz", "gy", "gx"))
    return jax.shard_map(body, mesh=mesh, in_specs=in_specs, out_specs=out_specs, check_vma=False)
```

```python
import functools
import math

import jax
import jax.numpy as jnp


from jax import lax
from jax.experimental import pallas as pl
from jax.experimental.pallas import tpu as pltpu
from jax.sharding import PartitionSpec as P

NX = 2048


STORE = 1.0


def padded_2(block, sides, width):
    for axis, dim in sides:
        count = lax.axis_size(axis)
        forward = [(i, i + 1) for i in range(count - 1)]
        backward = [(target, source) for source, target in forward]
        low = lax.ppermute(
            lax.slice_in_dim(block, block.shape[dim] - width, None, axis=dim), axis, forward
        )
        high = lax.ppermute(lax.slice_in_dim(block, 0, width, axis=dim), axis, backward)
        block = jnp.concatenate([low, block, high], axis=dim)
    return block


def twisted_coeffs(spectral, shifts, first_wave):
    count = spectral.shape[3]
    wave_index = first_wave + jnp.arange(count, dtype=jnp.int32)
    wave_turns = shifts[:, :, None] * wave_index[None, None, :] % NX
    phase_angle = wave_turns.astype(jnp.float32) * (2.0 * math.pi / NX)
    cosine = jnp.cos(phase_angle)
    sine_part = jnp.sin(phase_angle)
    real_part = spectral[0] * cosine - spectral[1] * sine_part
    imag_part = spectral[0] * sine_part + spectral[1] * cosine
    return jnp.stack([real_part, imag_part])


def basis(count, first_cell, width_cells):
    wave_index = jnp.arange(count, dtype=jnp.int32)
    cell_index = first_cell + jnp.arange(width_cells, dtype=jnp.int32)
    wave_turns = wave_index[:, None] * cell_index[None, :] % NX
    phase_angle = wave_turns.astype(jnp.float32) * (2.0 * math.pi / NX)
    offsets = jnp.concatenate(
        [jnp.zeros((count, 1), jnp.float32), jnp.full((count, 1), 0.5 * math.pi, jnp.float32)],
        axis=0,
    )
    stacked = jnp.concatenate([phase_angle, phase_angle], axis=0) + offsets
    return jnp.cos(stacked) * (1.0 / math.sqrt(NX))


def flatten_pair(piece):
    depth, items, count = (piece.shape[1], piece.shape[2], piece.shape[3])
    return jnp.concatenate(
        [piece[0].reshape(depth * items, count), piece[1].reshape(depth * items, count)], axis=1
    )


def harmonic(center, beside):
    return 2.0 * center * beside / (center + beside)


def thomas(lower_diagonal, main_diagonal, upper_diagonal, right_hand_side):

    def thomas_forward_scan(carried_state, row_entries):
        previous_ratio, previous_eliminated = carried_state
        column_lower, main_c, sup_c, column_right_hand = row_entries
        present_denominator = main_c - column_lower * previous_ratio
        present_ratio = sup_c / present_denominator
        present_eliminated = (
            column_right_hand - column_lower * previous_eliminated
        ) / present_denominator
        return ((present_ratio, present_eliminated), (present_ratio, present_eliminated))

    zeroed_layer = jnp.zeros(right_hand_side.shape[1:], right_hand_side.dtype)
    unused_output, (ratio_rows, eliminated_rows) = lax.scan(
        thomas_forward_scan,
        (zeroed_layer, zeroed_layer),
        (lower_diagonal, main_diagonal, upper_diagonal, right_hand_side),
    )

    def thomas_backward_scan(following_value, row_entries):
        column_ratio, column_eliminated = row_entries
        present_value = column_eliminated - column_ratio * following_value
        return (present_value, present_value)

    unused_output, solved_values = lax.scan(
        thomas_backward_scan, zeroed_layer, (ratio_rows, eliminated_rows), reverse=True
    )
    return solved_values


def factor(lower_diagonal, main_diagonal, upper_diagonal):

    def factor_forward_scan(previous_ratio, row_entries):
        column_lower, main_c, sup_c = row_entries
        present_denominator = main_c - column_lower * previous_ratio
        present_ratio = sup_c / present_denominator
        return (present_ratio, (present_denominator, present_ratio))

    unused_output, (denominator_rows, ratio_rows) = lax.scan(
        factor_forward_scan,
        jnp.zeros_like(main_diagonal[0]),
        (lower_diagonal, main_diagonal, upper_diagonal),
    )
    return (denominator_rows, ratio_rows)


def solve_factored(lower_diagonal, denominator_rows, ratio_rows, right_hand_side):

    def solve_forward_scan(previous_eliminated, row_entries):
        column_lower, column_denominator, column_right_hand = row_entries
        present_eliminated = (
            column_right_hand - column_lower[None] * previous_eliminated
        ) / column_denominator[None]
        return (present_eliminated, present_eliminated)

    unused_output, eliminated_rows = lax.scan(
        solve_forward_scan,
        jnp.zeros_like(right_hand_side[0]),
        (lower_diagonal, denominator_rows, right_hand_side),
    )

    def solve_backward_scan(following_value, row_entries):
        column_ratio, column_eliminated = row_entries
        present_value = column_eliminated - column_ratio[None] * following_value
        return (present_value, present_value)

    unused_output, solved_values = lax.scan(
        solve_backward_scan,
        jnp.zeros_like(right_hand_side[0]),
        (ratio_rows, eliminated_rows),
        reverse=True,
    )
    return solved_values


def generic_body(spectral, shifts, colour, pressure, source):
    total_depth = pressure.shape[0] * lax.axis_size("gz")
    vert_factor = float(total_depth * total_depth // 4)
    width_cells = spectral.shape[3]
    first_cell = lax.axis_index("gx") * width_cells
    twisted = twisted_coeffs(spectral, shifts, first_cell)
    piece = lax.all_to_all(twisted, "gx", split_axis=1, concat_axis=3, tiled=True)
    depth = piece.shape[1]
    items = piece.shape[2]
    length = piece.shape[3]
    flat = flatten_pair(piece)
    block_width = min(512, length)
    blocks = [
        jnp.dot(
            flat,
            basis(length, block * block_width, block_width),
            precision=lax.Precision.HIGHEST,
            preferred_element_type=jnp.float32,
        )
        for block in range(length // block_width)
    ]
    field_rows = jnp.concatenate(blocks, axis=1).reshape(depth, items, length)
    log_perm = lax.all_to_all(field_rows, "gx", split_axis=2, concat_axis=0, tiled=True)
    perm = jnp.exp(log_perm)
    padded = padded_2(perm, (("gx", 2), ("gz", 0), ("gy", 1)), 1)
    w_zm = vert_factor * harmonic(perm, padded[:-2, 1:-1, 1:-1])
    w_zp = vert_factor * harmonic(perm, padded[2:, 1:-1, 1:-1])
    w_ym = harmonic(perm, padded[1:-1, :-2, 1:-1])
    w_yp = harmonic(perm, padded[1:-1, 2:, 1:-1])
    w_xm = harmonic(perm, padded[1:-1, 1:-1, :-2])
    w_xp = harmonic(perm, padded[1:-1, 1:-1, 2:])
    main_diagonal = STORE + w_xm + w_xp + w_ym + w_yp + w_zm + w_zp
    lower_diagonal = -w_zm
    upper_diagonal = -w_zp
    zeroed_layer = jnp.zeros_like(main_diagonal[0])
    inner_sub = jnp.concatenate([zeroed_layer[None], lower_diagonal[2:-1]], axis=0)
    inner_sup = jnp.concatenate([upper_diagonal[1:-2], zeroed_layer[None]], axis=0)
    inner_main = main_diagonal[1:-1]
    denominator_rows, ratio_rows = factor(inner_sub, inner_main, inner_sup)
    unit_rhs = jnp.zeros((inner_main.shape[0], 2) + zeroed_layer.shape, jnp.float32)
    unit_rhs = unit_rhs.at[0, 0].set(-lower_diagonal[1])
    unit_rhs = unit_rhs.at[-1, 1].set(-upper_diagonal[-2])
    coupled = solve_factored(inner_sub, denominator_rows, ratio_rows, unit_rhs)
    left_part = coupled[:, 0]
    right_part = coupled[:, 1]
    sub_first = lower_diagonal[0]
    main_first = main_diagonal[0] + upper_diagonal[0] * left_part[0]
    sup_first = upper_diagonal[0] * right_part[0]
    sub_last = lower_diagonal[-1] * left_part[-1]
    main_last = main_diagonal[-1] + lower_diagonal[-1] * right_part[-1]
    sup_last = upper_diagonal[-1]

    def line_solve(current):
        cycle = padded_2(current, (("gx", 2), ("gy", 1)), 1)
        right_hand_side = source + w_xm * cycle[:, 1:-1, :-2] + w_xp * cycle[:, 1:-1, 2:]
        right_hand_side = right_hand_side + w_ym * cycle[:, :-2, 1:-1] + w_yp * cycle[:, 2:, 1:-1]
        particular = solve_factored(
            inner_sub, denominator_rows, ratio_rows, right_hand_side[1:-1][:, None]
        )[:, 0]
        rhs_first = right_hand_side[0] - upper_diagonal[0] * particular[0]
        rhs_last = right_hand_side[-1] - lower_diagonal[-1] * particular[-1]
        reduced_rows = jnp.stack(
            [sub_first, main_first, sup_first, rhs_first, sub_last, main_last, sup_last, rhs_last]
        )
        gathered = lax.all_gather(reduced_rows, "gz", axis=0, tiled=True)
        segments = gathered.shape[0] // 8
        system = gathered.reshape((2 * segments, 4) + zeroed_layer.shape)
        reduced_sol = thomas(system[:, 0], system[:, 1], system[:, 2], system[:, 3])
        own_pair = lax.dynamic_slice_in_dim(reduced_sol, 2 * lax.axis_index("gz"), 2, 0)
        face_first = own_pair[0]
        face_last = own_pair[1]
        inner = particular + face_first[None] * left_part + face_last[None] * right_part
        return jnp.concatenate([face_first[None], inner, face_last[None]], axis=0)

    half = jnp.where((colour == 0)[None], line_solve(pressure), pressure)
    smoothed = jnp.where((colour == 1)[None], line_solve(half), half)
    return (log_perm, smoothed)


LANES = 128
ROWS = 8
F32 = jnp.float32
MIB = 1 << 20
SUMS_GRANT = 60


def suits(mesh):
    sizes = dict(mesh.shape)
    return sizes["gx"] == 2 and sizes["gz"] == 4 and sizes["gy"] == 4


def params(mib):
    return pltpu.CompilerParams(vmem_limit_bytes=mib * MIB)


def cos_sin(turns):
    quarter = (turns + NX // 8) >> 9
    angle = (turns - (quarter << 9)).astype(F32) * (2.0 * math.pi / NX)
    square = angle * angle
    sine = angle * (
        1.0
        + square * (-1.0 / 6 + square * (1.0 / 120 + square * (-1.0 / 5040 + square / 362880)))
    )
    cosine = 1.0 + square * (
        -0.5 + square * (1.0 / 24 + square * (-1.0 / 720 + square * (1.0 / 40320)))
    )
    odd = (quarter & 1) == 1
    first = jnp.where(odd, sine, cosine)
    second = jnp.where(odd, cosine, sine)
    cos_sign = jnp.where(((quarter + 1) & 2) == 2, -1.0, 1.0)
    sin_sign = jnp.where((quarter & 2) == 2, -1.0, 1.0)
    return first * cos_sign, second * sin_sign


def split(values):
    high = values.astype(jnp.bfloat16)
    return high, (values - high.astype(F32)).astype(jnp.bfloat16)


def times(first, second):
    return (
        first[0] * second[0] - first[1] * second[1],
        first[0] * second[1] + first[1] * second[0],
    )


def plus(first, second):
    return (first[0] + second[0], first[1] + second[1])


def minus(first, second):
    return (first[0] - second[0], first[1] - second[1])


def quarter_turn(value):
    return (-value[1], value[0])


def four_point(first, second, third, fourth):
    even, gap = plus(first, third), minus(first, third)
    odd, turned = plus(second, fourth), quarter_turn(minus(second, fourth))
    return [plus(even, odd), plus(gap, turned), minus(even, odd), minus(gap, turned)]


def eight_point(values):
    even = four_point(*values[0::2])
    odd = four_point(*values[1::2])
    root = math.sqrt(0.5)
    real, imag = odd[1]
    odd[1] = (root * (real - imag), root * (real + imag))
    odd[2] = quarter_turn(odd[2])
    real, imag = odd[3]
    odd[3] = (-root * (real + imag), root * (real - imag))
    return [plus(*pair) for pair in zip(even, odd)] + [minus(*pair) for pair in zip(even, odd)]


def fill_tables(basis, turns):
    groups = NX // LANES
    shape = (LANES, LANES)
    lane = lane_of(shape)
    cells = (lane % groups) * (LANES // groups) + lane // groups
    cosine, sine = cos_sin((row_of(shape) * cells) % LANES * groups)
    for at, value in enumerate((cosine, -sine)):
        rows = slice(at * LANES, (at + 1) * LANES)
        high, low = split(value * (1.0 / math.sqrt(NX)))
        basis[0, rows], basis[1, rows], basis[2, rows] = high, high, low
    shape = (groups, LANES)
    turns[0], turns[1] = cos_sin(row_of(shape) * lane_of(shape))


def diagonal_of(depth):
    square = (depth, depth)
    return row_of(square) == lane_of(square)


def shift_columns(shifts, rows_of, columns):
    depth = shifts.shape[1]
    diagonal = diagonal_of(depth)
    for at, y in enumerate(rows_of):
        spread = jnp.where(diagonal, shifts[y : y + 1, :].astype(F32), 0.0)
        shift = jnp.broadcast_to(jnp.sum(spread, axis=1, keepdims=True), (depth, LANES))
        columns[at * depth : (at + 1) * depth, :] = shift.astype(jnp.int32)


def edge_columns(ys, depth, edges, kept):
    kept[...] = jnp.zeros_like(kept)
    diagonal = diagonal_of(depth)
    for at in range(len(ys)):
        rows = slice(at * depth, (at + 1) * depth)
        for side in range(edges.shape[0]):
            lane = 0 if side % 2 else LANES - 1
            column = jnp.broadcast_to(edges[side, rows, lane : lane + 1], (depth, depth))
            row = jnp.sum(jnp.where(diagonal, column, 0.0), axis=0, keepdims=True)
            kept[side, at : at + 1, :depth] = row


def twisted(first_wave, shift, coefficients, rows):
    lane = lane_of(shift.shape)
    phase = cos_sin((shift * (lane + first_wave)) & (NX - 1))
    turn = cos_sin((shift * LANES) & (NX - 1))
    values = []
    for part in range(coefficients.shape[0]):
        values.append(times((coefficients[part, 0, rows], coefficients[part, 1, rows]), phase))
        phase = times(phase, turn)
    return values


def interleave(tiles):
    count = len(tiles)
    lane = lane_of(tiles[0].shape)
    bit = count // 2
    while bit:
        low = (lane & bit) == 0
        moved = list(tiles)
        for at in range(count):
            if not at & bit:
                first, second = tiles[at], tiles[at | bit]
                crossed = jnp.take_along_axis(
                    jnp.where(low, second, first), lane ^ bit, axis=1
                )
                moved[at] = jnp.where(low, first, crossed)
                moved[at | bit] = jnp.where(low, crossed, second)
        tiles = moved
        bit //= 2
    return tiles


STEP = 16


def fill_left(g, at, y, depth, items, columns, coefficients, turns, left, part):
    groups = NX // LANES
    sign = 1.0 - 2.0 * g.astype(F32)
    first_wave = g * (coefficients.shape[0] * LANES)
    rows = pl.ds(part * STEP * items + y, STEP, stride=items)
    shift = columns[pl.ds(at * depth + part * STEP, STEP), :]
    values = twisted(first_wave, shift, coefficients, rows)
    angles = [2 * math.pi * p / groups for p in range(len(values))]
    turned = [
        times(value, (sign * math.cos(angle), sign * math.sin(angle)))
        if angle
        else (sign * value[0], sign * value[1])
        for angle, value in zip(angles, values)
    ]
    even, odd = eight_point(values), eight_point(turned)
    for group in range(groups):
        value = odd[group // 2] if group % 2 else even[group // 2]
        if group:
            value = times(value, (turns[0, group : group + 1], turns[1, group : group + 1]))
        first = group * depth + part * STEP
        for place_of, piece in enumerate(value):
            for half, bits in enumerate(split(piece)):
                target = (2 * half + place_of) * LANES
                left[first : first + STEP, target : target + LANES] = bits


def finish_row(at, depth, basis, left, right, emit):
    groups = NX // LANES
    spread = jnp.concatenate([left[...], left[:, : 2 * LANES]], axis=1)
    bases = basis[...].reshape(-1, LANES)
    right[...] = jnp.dot(spread, bases, preferred_element_type=F32)
    for part in range(depth // ROWS):
        tiles = [
            right[group * depth + part * ROWS : group * depth + (part + 1) * ROWS]
            for group in range(groups)
        ]
        emit(pl.ds(at * depth + part * ROWS, ROWS), interleave(tiles))


def load_coefficients(spectral, coefficients, arrivals, items):
    parts, halves = arrivals.shape
    copies = []
    for half in range(halves):
        rows = slice(half * STEP * items, (half + 1) * STEP * items)
        copies.append(
            [
                pltpu.make_async_copy(
                    spectral.at[:, rows, part * LANES : (part + 1) * LANES],
                    coefficients.at[part, :, rows],
                    arrivals.at[part, half],
                )
                for part in range(parts)
            ]
        )
    for half in copies:
        for copy in half:
            copy.start()
    return copies


def all_rows(g, ys, shifts, shift_copy, copies, columns, coefficients, tables, left, right, emit):
    items, depth = shifts.shape
    basis, turns = tables
    fill_tables(basis, turns)
    shift_copy.wait()
    shift_columns(shifts, ys, columns)
    for half, arriving in enumerate(copies):
        for copy in arriving:
            copy.wait()
        for at, y in enumerate(ys):
            fill_left(g, at, y, depth, items, columns, coefficients, turns, left.at[at], half)
            if half == len(copies) - 1:
                finish_row(at, depth, basis, left.at[at], right.at[at], emit)


def keep_edges(rows, tiles, edges):
    count = len(tiles) // 4
    for side in range(edges.shape[0]):
        edges[side, rows] = tiles[(side // 2 + 1) * count - 1 + side % 2]


def inner_sums_kernel(ys, shifts, spectral, pressure, other, own, kept, p_column, *refs):
    tile, sem, *refs = refs
    g = lax.axis_index("gx")
    width = pressure.shape[2]
    there = lane_slice(jnp.where(g == 0, width - LANES, 0), LANES)
    copy = pltpu.make_async_copy(pressure.at[:, :, there], tile, sem)
    copy.start()
    wide_sums_kernel(ys, shifts, spectral, other, own, kept, *refs)
    copy.wait()
    packed = jnp.zeros((ROWS, LANES), F32)
    for z in range(tile.shape[0]):
        packed = packed_with(z, packed, boundary_plane(g, tile[z]), 0)
    p_column[...] = packed


def wide_sums_kernel(ys, shifts, spectral, other, own, kept, *refs):
    local, arrived, columns, edges, coefficients, arrivals, *tables, left, right = refs
    items, depth = shifts.shape
    shift_copy = pltpu.make_async_copy(shifts, local, arrived)
    shift_copy.start()
    copies = load_coefficients(spectral, coefficients, arrivals, items)
    g = lax.axis_index("gx")

    def emit(rows, tiles):
        half = len(tiles) // 2
        keep_edges(rows, tiles, edges)
        for tile, (low, high) in enumerate(zip(tiles[:half], tiles[half:])):
            there = slice(tile * LANES, (tile + 1) * LANES)
            other[rows, there] = jnp.where(g == 0, high, low)
            own[rows, there] = jnp.where(g == 0, low, high)

    all_rows(
        *(g, ys, local, shift_copy, copies, columns, coefficients, tables, left, right, emit)
    )
    edge_columns(ys, depth, edges, kept)


def last_sums_kernel(ys, outer_kept, inner_kept, p_column, shifts, spectral, one, two, own, *refs):
    columns_own, kept, local, arrived, columns, edges, coefficients, *refs = refs
    arrivals, *tables, left, right = refs
    items, depth = shifts.shape
    shift_copy = pltpu.make_async_copy(shifts, local, arrived)
    shift_copy.start()
    copies = load_coefficients(spectral, coefficients, arrivals, items)
    g = lax.axis_index("gx")

    def emit(rows, tiles):
        half = len(tiles) // 2
        keep_edges(rows, tiles, edges)
        others = []
        for tile, (low, high) in enumerate(zip(tiles[:half], tiles[half:])):
            own[rows, tile * LANES : (tile + 1) * LANES] = jnp.where(g == 0, low, high)
            others.append(jnp.where(g == 0, high, low))
        start = 0
        for ref in (one, two):
            count = ref.shape[1] // LANES
            for tile in range(count):
                ref[rows, tile * LANES : (tile + 1) * LANES] = jnp.where(
                    g == 0, others[start + tile], others[half - start - count + tile]
                )
            start += count

    all_rows(
        *(g, ys, local, shift_copy, copies, columns, coefficients, tables, left, right, emit)
    )
    edge_columns(ys, depth, edges, kept)
    sides_of = [
        jnp.concatenate(
            [outer_kept[side, :1], inner_kept[side], kept[side], outer_kept[side, 1:]], axis=0
        )
        for side in range(6)
    ]
    low, high = sides_of[:3], sides_of[3:]
    own_sides = [jnp.where(g == 0, *pair) for pair in ((low[0], high[1]), (low[1], high[2]))]
    own_sides.append(jnp.where(g == 0, low[2], high[0]))
    other_sides = [jnp.where(g == 0, *pair) for pair in ((high[1], low[0]), (high[2], low[1]))]
    other_sides.append(jnp.where(g == 0, high[0], low[2]))
    for at in range(3):
        columns_own[at], columns_own[3 + at] = own_sides[at], other_sides[at]
    extra = slice(one.shape[0] - ROWS, one.shape[0])
    for at, piece in enumerate((*other_sides, own_sides[2], p_column[...])):
        one[extra, at * LANES : (at + 1) * LANES] = piece


ON_CHIP = pl.BlockSpec(memory_space=pltpu.VMEM)
IN_HBM = pl.BlockSpec(memory_space=pltpu.HBM)


def call(
    kernel, name, out_shape, args, flags=None, scratch=(), far=(), mib=20, flops=1, out=ON_CHIP
):
    specs = [ON_CHIP] * len(args) + [IN_HBM] * len(far)
    args = list(args) + list(far)
    body = kernel if flags is None else lambda *refs: kernel(flags(), *refs)
    return pl.pallas_call(
        body,
        out_shape=out_shape,
        in_specs=specs,
        out_specs=jax.tree.map(lambda _: out, out_shape),
        scratch_shapes=list(scratch),
        compiler_params=params(mib),
        cost_estimate=pl.CostEstimate(flops=flops, bytes_accessed=1, transcendentals=0),
        name=name,
    )(*args)


def roll(values, shift, axis):
    return pltpu.roll(values, shift % values.shape[axis], axis)


def lane_of(shape):
    return lax.broadcasted_iota(jnp.int32, shape, 1)


def row_of(shape):
    return lax.broadcasted_iota(jnp.int32, shape, 0)


def column_to(z, packed, target):
    return pltpu.roll(packed, (target - z) % LANES, 1)


def packed_with(z, packed, plane, lane):
    column = jnp.broadcast_to(plane[:, lane : lane + 1], (ROWS, LANES))
    return jnp.where(lane_of((ROWS, LANES)) == z, column, packed)


def inverse_of(values):
    return pl.reciprocal(values, approx=True)


def ordered(z, sums, depth):
    spread = pl.ds(z, ROWS, stride=depth)
    return jnp.concatenate([sums[at, spread] for at in range(sums.shape[0])], axis=1)


def place_tiles(sums, rows, first, values):
    for at in range(values.shape[1] // LANES):
        sums[(first >> 7) + at, rows] = values[:, at * LANES : (at + 1) * LANES]


def boundary_plane(g, plane):
    return jnp.where(g == 0, roll(plane[:, -LANES:], 1, 1), plane[:, :LANES])


def outer_field_kernel(depth, flags, own, other, pressure, to_near, to_middle):
    even = flags[16] == 0
    low, high = slice(0, depth), slice(depth, 2 * depth)
    south, north = own[low] + other[low], own[high] + other[high]
    to_near[low] = jnp.exp(-jnp.where(even, north, south))
    to_middle[low] = jnp.exp(-jnp.where(even, south, north))

    for z in range(depth):
        keep_rows(depth + z, pressure[z], even, to_near, to_middle, slice(None))


def wide_field_kernel(depth, flags, *refs):
    own_outer, outer, own_inner, inner, to_near, to_middle = refs[:6]
    from_near, from_middle, pressure = refs[6:9]
    wide, south_weight, north_weight, p_south, p_north, p_west, p_east = refs[9:16]
    south_rows, north_rows = refs[16:]
    even = flags[16] == 0
    low, high = slice(0, depth), slice(depth, 2 * depth)
    wide[low] = own_outer[low] + outer[low]
    wide[depth:-depth] = own_inner[...] + inner[...]
    wide[-depth:] = own_outer[high] + outer[high]
    near_weight = 2.0 * inverse_of(to_near[low] + from_near[low])
    middle_weight = (2.0 * flags[15].astype(F32)) * inverse_of(to_middle[low] + from_middle[low])
    south = jnp.where(even, middle_weight, near_weight)
    south_weight[...] = south
    north_weight[...] = jnp.where(even, near_weight, middle_weight)
    south_rows[...] = jnp.where(even, from_middle[high], from_near[high])
    north_rows[...] = jnp.where(even, from_near[high], from_middle[high])
    row = row_of(pressure.shape[1:])

    def layer(z, carry):
        plane = pressure[z]
        p_south[z] = jnp.where(row == 0, south_rows[pl.ds(z, 1), :], roll(plane, 1, 0))
        p_north[z] = jnp.where(row == ROWS - 1, north_rows[pl.ds(z, 1), :], roll(plane, -1, 0))
        p_west[z] = roll(plane, 1, 1)
        p_east[z] = roll(plane, -1, 1)
        return carry

    lax.fori_loop(0, depth, layer, 0, unroll=True)


def lane_slice(start, size):
    return pl.ds(pl.multiple_of(start, LANES), size)


def assemble(sums, depth, wide, own, piece, there):
    inside = wide.shape[0] - depth
    place_tiles(sums, slice(0, inside), 0, wide[:inside, there])
    place_tiles(sums, slice(inside, -depth), 0, own[:, there] + piece[: own.shape[0]])
    place_tiles(sums, slice(-depth, None), 0, wide[inside:, there])


def first_field_kernel(depth, flags, *refs):
    wide, own, middle, columns_own = refs[:4]
    log_perm, resist, low_side, high_side, boundary, column, p_column, sums = refs[4:]
    extra = slice(own.shape[0], own.shape[0] + ROWS)
    came = [middle[extra, at * LANES : (at + 1) * LANES] for at in range(5)]
    for at, ref in enumerate((low_side, high_side, boundary)):
        ref[...] = jnp.exp(-(columns_own[at] + came[at]))
    column[...] = jnp.exp(-(columns_own[5] + came[3]))
    p_column[...] = came[4]
    assemble(sums, depth, wide, own, middle, lane_slice(flags[3], log_perm.shape[2]))

    def layer(z, carry):
        plane = ordered(z, sums, depth)
        log_perm[z] = plane
        resist[z] = jnp.exp(-plane)
        return carry

    lax.fori_loop(0, depth, layer, 0, unroll=True)


def second_field_kernel(depth, flags, *refs):
    wide, own, middle, resist_near = refs[:4]
    log_perm, resist, sums = refs[4:]
    third = middle.shape[1]
    assemble(sums, depth, wide, own, middle, lane_slice(flags[5], third))
    extra = resist.shape[2] - third
    target = lane_slice(flags[5] - flags[7], third)
    extra_target = lane_slice(flags[8], extra)
    extra_source = lane_slice(flags[9], extra)

    def layer(z, carry):
        plane = ordered(z, sums, depth)
        log_perm[z] = plane
        resist[z, :, target] = jnp.exp(-plane)
        resist[z, :, extra_target] = resist_near[z, :, extra_source]
        return carry

    lax.fori_loop(0, depth, layer, 0, unroll=True)


def join_columns_kernel(depth, flags, near, far, _, whole):
    def layer(z, carry):
        whole[z, :, lane_slice(flags[3], near.shape[2])] = near[z]
        whole[z, :, lane_slice(flags[5], far.shape[2])] = far[z]
        return carry

    lax.fori_loop(0, depth, layer, 0, unroll=True)


def keep_rows(z, value, even, to_near, to_middle, here):
    south, north = value[0:1, :], value[ROWS - 1 : ROWS, :]
    to_near[pl.ds(z, 1), here] = jnp.where(even, north, south)
    to_middle[pl.ds(z, 1), here] = jnp.where(even, south, north)


def with_first(plane, edge):
    first = jnp.where(lane_of((ROWS, LANES)) == 0, edge, plane[:, :LANES])
    return jnp.concatenate([first, plane[:, LANES:]], axis=1)


def with_last(plane, edge):
    last = jnp.where(lane_of((ROWS, LANES)) == LANES - 1, edge, plane[:, -LANES:])
    return jnp.concatenate([plane[:, :-LANES], last], axis=1)


def coupling(z, field, start, size, east_weight, north_weight, south_terms, north_rows, west, column):
    here = lane_slice(start, size)
    plane = field[z, :, here]
    row = row_of(plane.shape)
    at_start = start == 0
    inner = field[z, :, lane_slice(jnp.where(at_start, size, size - LANES), LANES)]
    west_value = jnp.where(at_start, column_to(z, column, 0), roll(inner, 1, 1))
    east_value = jnp.where(at_start, roll(inner, -1, 1), column_to(z, column, LANES - 1))
    to_east, to_north = east_weight * plane, north_weight * plane
    from_west = with_first(roll(to_east, 1, 1), column_to(z, west, 0) * west_value)
    from_east = east_weight * with_last(roll(plane, -1, 1), east_value)
    from_south = jnp.where(row == 0, south_terms[pl.ds(z, 1), here], roll(to_north, 1, 0))
    from_north = north_weight * jnp.where(
        row == ROWS - 1, north_rows[pl.ds(z, 1), here], roll(plane, -1, 0)
    )
    return (from_west + from_east) + (from_south + from_north)


def edge_weights(flags, start, bound, column, low_side, high_side):
    g = flags[0]
    middle = 2.0 * inverse_of(low_side + high_side)
    across = 2.0 * inverse_of(bound + column)
    none = jnp.zeros_like(across)
    west = jnp.where(start == 0, jnp.where(g == 0, none, across), middle)
    east = jnp.where(start == 0, middle, jnp.where(g == 0, across, none))
    return west, east


def first_sweep_kernel(depth, vert, block, flags, *refs):
    resist, low_side, high_side, r_bound, r_column, p_column = refs[:6]
    south_weight, north_weight, p_south, p_north, p_west, p_east = refs[6:12]
    source = refs[12]
    w_east, w_north, west_out, particular, inverse, ratio, lead, reduced = refs[13:21]
    grounds, rights, verticals = refs[21:]
    start, offset = flags[6 + block], flags[10 + block]
    size = inverse.shape[2]
    shape = (ROWS, size)
    here = lane_slice(start, size)
    inside = lane_slice(offset, size)
    west_weight, east_weight = edge_weights(
        flags, start, r_bound[...], r_column[...], low_side[...], high_side[...]
    )
    west_out[...] = west_weight
    column = p_column[...]
    row = row_of(shape)

    def weigh(z, carry):
        plane = resist[z, :, inside]
        east = 2.0 * inverse_of(plane + roll(plane, -1, 1))
        east = with_last(east, column_to(z, east_weight, LANES - 1))
        west = with_first(roll(east, 1, 1), column_to(z, west_weight, 0))
        north = 2.0 * inverse_of(plane + roll(plane, -1, 0))
        north = jnp.where(row == ROWS - 1, north_weight[pl.ds(z, 1), here], north)
        south = jnp.where(row == 0, south_weight[pl.ds(z, 1), here], roll(north, 1, 0))
        w_east[z], w_north[z] = east, north
        grounds[z] = STORE + ((east + west) + (north + south))
        verticals[z] = (2.0 * vert) * inverse_of(
            plane + resist[jnp.minimum(z + 1, depth - 1), :, inside]
        )
        p_first, p_last = p_west[z, :, here], p_east[z, :, here]
        p_first = with_first(
            p_first, jnp.where(start == 0, column_to(z, column, 0), p_first[:, :LANES])
        )
        p_last = with_last(
            p_last, jnp.where(start == 0, p_last[:, -LANES:], column_to(z, column, LANES - 1))
        )
        rights[z] = source[z, :, here] + (
            (west * p_first + east * p_last)
            + (south * p_south[z, :, here] + north * p_north[z, :, here])
        )
        return carry

    lax.fori_loop(0, depth, weigh, 0, unroll=True)

    def layer(z, carry):
        conduct, flow, product, first_first, first_part = carry
        weight = verticals[z]
        reciprocal = inverse_of(conduct + weight)
        quotient = weight * reciprocal
        led = product * reciprocal
        inverse[z] = reciprocal
        ratio[z] = quotient
        lead[z] = led
        particular[z] = reciprocal * flow
        return (
            grounds[z + 1] + conduct * quotient,
            rights[z + 1] + flow * quotient,
            product * quotient,
            first_first + led * product,
            first_part + led * flow,
        )

    zero = jnp.zeros(shape, F32)
    conduct, flow, product, first_first, first_part = lax.fori_loop(
        0,
        depth - 1,
        layer,
        (grounds[0], rights[0], jnp.ones(shape, F32), zero, zero),
        unroll=True,
    )
    reciprocal = inverse_of(conduct)
    led = product * reciprocal
    inverse[depth - 1] = reciprocal
    ratio[depth - 1] = zero
    lead[depth - 1] = led
    particular[depth - 1] = flow * reciprocal
    reduced[0] = first_first + led * product + resist[0, :, inside] * (0.5 / vert)
    reduced[1] = led
    reduced[2] = reciprocal + resist[depth - 1, :, inside] * (0.5 / vert)
    reduced[3] = first_part + led * flow
    reduced[4] = flow * reciprocal


def pair_kernel(flags, own, near, across, kept):
    me = flags[14]
    even, lower = me % 2 == 0, me < 2
    first, second = [
        [jnp.where(flip, own[at], near[at]) for at in range(5)]
        for flip in (even, jnp.logical_not(even))
    ]
    reciprocal = inverse_of(first[2] + second[0])
    step = (first[4] - second[3]) * reciprocal
    through = jnp.where(lower, second[1], first[1])
    share = through * reciprocal
    across[0] = jnp.where(lower, second[2], first[0]) - through * share
    across[1] = jnp.where(lower, second[4], first[3]) + jnp.where(
        lower, through * step, -through * step
    )
    kept[0], kept[1], kept[2] = share, reciprocal, step


def ends(me, inner, middle):
    zero = jnp.zeros_like(inner)
    odd = me % 2 == 1
    enters = jnp.where(odd, inner, jnp.where(me == 2, middle, zero))
    leaves = jnp.where(odd, jnp.where(me == 1, middle, zero), inner)
    return enters, leaves


def back_substitute(depth, lines, emit):
    last = depth - 1
    values = tuple(
        (particular[last] + lead[last] * enters) - inverse[last] * leaves
        for enters, leaves, particular, inverse, ratio, lead in lines
    )
    state = emit(last, values, jnp.zeros((ROWS, LANES), F32))

    for z in range(last - 1, -1, -1):
        values = tuple(
            (particular[z] + lead[z] * enters) + ratio[z] * beyond
            for (enters, _, particular, _, ratio, lead), beyond in zip(lines, values)
        )
        state = emit(z, values, state)
    return state


def half_kernel(depth, flags, *refs):
    pairs = (refs[0:3], refs[3:6])
    blocks = (refs[6:10], refs[10:14])
    pressure, colour = refs[14:16]
    half, to_near, to_middle, boundary, joined = refs[16:]
    me, g, even = flags[14], flags[0], flags[16] == 0
    size = blocks[0][0].shape[2]
    spans = [lane_slice(flags[6 + block], size) for block in range(2)]
    lines = []
    for block, state in enumerate(blocks):
        across, other, kept = pairs[block]
        sum_of = inverse_of(across[0] + other[0])
        joined[block] = sum_of
        lead_of = across[1] - other[1]
        middle = jnp.where(me < 2, lead_of, -lead_of) * sum_of
        inner = kept[2] + kept[0] * middle
        lines.append((*ends(me, inner, middle), *state))
    chosen = [colour[:, here] == 0 for here in spans]

    def emit(z, values, packed):
        for block, (value, here) in enumerate(zip(values, spans)):
            value = jnp.where(chosen[block], value, pressure[z, :, here])
            half[z, :, here] = value
            keep_rows(z, value, even, to_near, to_middle, here)
            if not block:
                packed = packed_with(z, packed, boundary_plane(g, value), 0)
        return packed

    boundary[...] = back_substitute(depth, lines, emit)


def second_sweep_kernel(depth, flags, *refs):
    half, h_near, h_middle, h_column, source, south_weight = refs[:6]
    shares = refs[6:8]
    blocks = (refs[8:14], refs[14:20])
    particulars, near, far = refs[20:22], refs[22], refs[23]
    south_terms, north_rows = refs[24:]
    me, even = flags[14], flags[16] == 0
    size = particulars[0].shape[2]
    starts = [flags[6 + block] for block in range(2)]
    spans = [lane_slice(start, size) for start in starts]
    column = h_column[...]
    south_terms[...] = south_weight[...] * jnp.where(even, h_middle[...], h_near[...])
    north_rows[...] = jnp.where(even, h_near[...], h_middle[...])

    def local(z, block):
        east, north, west = blocks[block][:3]
        return source[z, :, spans[block]] + coupling(
            z,
            half,
            starts[block],
            size,
            east[z],
            north[z],
            south_terms,
            north_rows,
            west[...],
            column,
        )

    def layer(z, carry):
        result = []
        for block, (flow, first_part) in enumerate(carry):
            inverse, ratio, lead = blocks[block][3:6]
            particulars[block][z] = flow * inverse[z]
            first_part = first_part + lead[z] * flow
            result.append((local(z + 1, block) + flow * ratio[z], first_part))
        return tuple(result)

    carry = tuple((local(0, block), jnp.zeros((ROWS, size), F32)) for block in range(2))
    carry = lax.fori_loop(0, depth - 1, layer, carry, unroll=True)
    last = depth - 1
    for block, (flow, first_part) in enumerate(carry):
        inverse, ratio, lead = blocks[block][3:6]
        there = slice(block * size, (block + 1) * size)
        first_part = first_part + lead[last] * flow
        last_part = flow * inverse[last]
        particulars[block][last] = last_part
        asked = jnp.where(me % 2 == 0, last_part, first_part)
        shared = shares[block][0] * asked
        outer = jnp.where(me == 1, last_part, jnp.where(me == 2, first_part, 0.0))
        given = outer + jnp.where((me == 0) | (me == 3), shared, -shared)
        near[0, :, there] = asked
        near[1, :, there] = given
        far[:, there] = given


def smoothed_kernel(depth, flags, *refs):
    own, near, skip, cross, joined = refs[:5]
    keeps = refs[5:7]
    blocks = (refs[7:11], refs[11:15])
    half, colour, result = refs[15:18]
    smoothed, sems = refs[18:]
    me = flags[14]
    size = blocks[0][0].shape[2]
    spans = [lane_slice(flags[6 + block], size) for block in range(2)]
    lines = []
    for block, state in enumerate(blocks):
        there = slice(block * size, (block + 1) * size)
        kept = keeps[block]
        lead_of = (own[1, :, there] + near[1, :, there]) - (skip[:, there] + cross[:, there])
        middle = jnp.where(me < 2, lead_of, -lead_of) * joined[block]
        step = own[0, :, there] - near[0, :, there]
        step = jnp.where(me % 2 == 0, step, -step) * kept[1]
        lines.append((*ends(me, step + kept[0] * middle, middle), *state))
    chosen = [colour[:, here] == 1 for here in spans]
    count = sems.shape[0]
    layers = depth // count
    copies = [
        pltpu.make_async_copy(
            smoothed.at[pl.ds(at * layers, layers)],
            result.at[pl.ds(at * layers, layers)],
            sems.at[at],
        )
        for at in range(count)
    ]

    def emit(z, values, state):
        for value, here, mine in zip(values, spans, chosen):
            smoothed[z, :, here] = jnp.where(mine, value, half[z, :, here])
        if z % layers == 0:
            copies[z // layers].start()
        return state

    back_substitute(depth, lines, emit)
    for copy in copies:
        copy.wait()


PAIR = [(0, 1), (1, 0)]
NEAR = [(0, 1), (1, 0), (2, 3), (3, 2)]
MIDDLE = [(1, 2), (2, 1), (0, 3), (3, 0)]
SKIP = [(0, 2), (2, 0), (1, 3), (3, 1)]
CROSS = [(0, 3), (3, 0), (1, 2), (2, 1)]


def exchange_edges(edges):
    to_near, to_middle, *column = edges
    return [
        lax.ppermute(to_near, "gy", NEAR),
        lax.ppermute(to_middle, "gy", MIDDLE),
        *[lax.ppermute(piece, "gx", PAIR) for piece in column],
    ]


def fast_body(spectral, shifts, colour, pressure, source):
    depth, items, width = pressure.shape
    vert = float((depth * 4) ** 2 // 4)
    waves = spectral.shape[3]
    rows = depth * items
    block_size, third = width // 2, 3 * width // 8
    known = width - third

    def flags():
        gx, gz, gy = (lax.axis_index(axis) for axis in ("gx", "gz", "gy"))

        def placed(start, size):
            return jnp.where(gx == 1, start, width - start - size)

        block_one, block_two = placed(0, block_size), placed(block_size, block_size)
        start_one = placed(0, known)
        extra = known - block_size
        return [
            gx,
            placed(0, LANES),
            placed(LANES, known - LANES),
            start_one,
            gx,
            placed(known, third),
            block_one,
            block_two,
            placed(block_size, extra) - block_two,
            placed(block_size, extra) - start_one,
            block_one - start_one,
            0,
            gy > 0,
            gy < 3,
            gz,
            ((gy == 1) | (gy == 2)).astype(jnp.int32),
            gy % 2,
        ]

    def shaped(*shape, dtype=F32):
        return jax.ShapeDtypeStruct(shape, dtype)

    groups = NX // LANES
    parts = waves // LANES
    inner_ys, last_ys = (1, 2, 3), tuple(range(4, items - 1))
    last_rows = len(last_ys) * depth
    column_type = shaped(ROWS, LANES)
    coefficients = spectral.reshape(2, rows, waves)

    def scratch(count):
        return [
            pltpu.VMEM((items, depth), jnp.int32),
            pltpu.SemaphoreType.DMA,
            pltpu.VMEM((count, LANES), jnp.int32),
            pltpu.VMEM((6, count, LANES), F32),
            pltpu.VMEM((parts, 2, rows, LANES), F32),
            pltpu.SemaphoreType.DMA((parts, depth // STEP)),
            pltpu.VMEM((3, 2 * LANES, LANES), jnp.bfloat16),
            pltpu.VMEM((2, groups, LANES), F32),
            pltpu.VMEM((count // depth, groups * depth, 4 * LANES), jnp.bfloat16),
            pltpu.VMEM((count // depth, groups * depth, LANES), F32),
        ]

    def wide_types(ys):
        return [shaped(len(ys) * depth, width)] * 2 + [shaped(6, len(ys), LANES)]

    shift_rows = shifts.T
    outer_ys = (0, items - 1)
    sums, own_outer, outer_kept = call(
        functools.partial(wide_sums_kernel, outer_ys),
        "outer_row_sums",
        wide_types(outer_ys),
        [],
        scratch=scratch(2 * depth),
        far=[shift_rows, coefficients],
        mib=SUMS_GRANT,
    )
    outer = lax.ppermute(sums, "gx", PAIR)
    shift_rows, _ = lax.optimization_barrier((shift_rows, own_outer))
    sums, own_inner, inner_kept, p_column = call(
        functools.partial(inner_sums_kernel, inner_ys),
        "inner_row_sums",
        wide_types(inner_ys) + [column_type],
        [],
        scratch=[pltpu.VMEM((depth, ROWS, LANES), F32), pltpu.SemaphoreType.DMA]
        + scratch(len(inner_ys) * depth),
        far=[shift_rows, coefficients, pressure],
        mib=20,
    )
    inner = lax.ppermute(sums, "gx", PAIR)
    edge_row, edge_column = shaped(depth, width), shaped(ROWS, LANES)
    edges = [edge_row, edge_row, edge_column]
    last_one, last_two, own_last, own_columns = call(
        functools.partial(last_sums_kernel, last_ys),
        "last_row_sums",
        [
            shaped(last_rows + ROWS, known),
            shaped(last_rows, third),
            shaped(last_rows, width),
            shaped(6, ROWS, LANES),
        ],
        [outer_kept, inner_kept, p_column],
        scratch=[pltpu.VMEM((6, len(last_ys), LANES), F32)] + scratch(last_rows),
        far=[shift_rows, coefficients],
        mib=20,
    )
    pressure_rows, _ = lax.optimization_barrier((pressure, own_last))
    to_near, to_middle = call(
        functools.partial(outer_field_kernel, depth),
        "outer_field",
        [shaped(2 * depth, width)] * 2,
        [own_outer, outer, pressure_rows],
        flags,
    )
    from_near, from_middle = exchange_edges([to_near, to_middle])
    last_one = lax.ppermute(last_one, "gx", PAIR)
    wide, *around = call(
        functools.partial(wide_field_kernel, depth),
        "wide_field",
        [shaped(rows - last_rows, width)] + [edge_row] * 2 + [shaped(depth, items, width)] * 4,
        [
            *(own_outer, outer, own_inner, inner, to_near, to_middle),
            *(from_near, from_middle, pressure),
        ],
        flags,
        [pltpu.VMEM((depth, width), F32)] * 2,
    )
    last_two, _ = lax.optimization_barrier((last_two, wide))
    last_two = lax.ppermute(last_two, "gx", PAIR)
    log_near, resist_near, *columns = call(
        functools.partial(first_field_kernel, depth),
        "first_field",
        [shaped(depth, items, known)] * 2 + [edge_column] * 5,
        [wide, own_last, last_one, own_columns],
        flags,
        [pltpu.VMEM((known // LANES, rows, LANES), F32)],
    )
    block = shaped(depth, items, block_size)

    state_types = [block] * 2 + [edge_column] + [block] * 4

    def first_sweep(at, resist):
        return call(
            functools.partial(first_sweep_kernel, depth, vert, at),
            "first_sweep",
            state_types + [shaped(5, items, block_size)],
            [resist, *columns, *around, source],
            flags,
            [pltpu.VMEM((depth, items, block_size), F32)] * 3,
        )

    *state_one, reduced_one = first_sweep(0, resist_near)
    near_one = lax.ppermute(reduced_one, "gz", NEAR)
    last_two, _ = lax.optimization_barrier((last_two, reduced_one))
    log_far, resist_far = call(
        functools.partial(second_field_kernel, depth),
        "second_field",
        [shaped(depth, items, third), block],
        [wide, own_last, last_two, resist_near],
        flags,
        [pltpu.VMEM((third // LANES, rows, LANES), F32)],
    )
    *state_two, reduced_two = first_sweep(1, resist_far)
    near_two = lax.ppermute(reduced_two, "gz", NEAR)
    (log_perm,) = call(
        functools.partial(join_columns_kernel, depth),
        "log_perm",
        [shaped(depth, items, width)],
        [log_near, log_far, reduced_two],
        flags,
    )
    def join(reduced, near):
        across, kept = call(
            pair_kernel,
            "join_pair",
            [shaped(2, items, block_size), shaped(3, items, block_size)],
            [reduced, near],
            flags,
        )
        return across, lax.ppermute(across, "gz", SKIP), kept

    pair_one, pair_two = join(reduced_one, near_one), join(reduced_two, near_two)
    keeps = [pair_one[2], pair_two[2]]
    half, *h_edges, joined = call(
        functools.partial(half_kernel, depth),
        "half",
        [shaped(depth, items, width), *edges, shaped(2, items, block_size)],
        [*pair_one, *pair_two, *state_one[3:], *state_two[3:], pressure, colour],
        flags,
    )
    h_edges = exchange_edges(h_edges)
    weights = [[*state[:3], *state[4:]] for state in (state_one, state_two)]
    current_one, current_two, to_near, to_far = call(
        functools.partial(second_sweep_kernel, depth),
        "second_sweep",
        [block, block, shaped(2, items, width), shaped(items, width)],
        [half, *h_edges, source, around[0], *keeps, *weights[0], *weights[1]],
        flags,
        [pltpu.VMEM((depth, width), F32)] * 2,
    )
    from_near, from_skip, from_cross = (
        lax.ppermute(planes, "gz", pairs)
        for planes, pairs in ((to_near, NEAR), (to_far, SKIP), (to_far, CROSS))
    )
    (smoothed,) = call(
        functools.partial(smoothed_kernel, depth),
        "smoothed",
        [shaped(depth, items, width)],
        [
            *(to_near, from_near, from_skip, from_cross, joined, *keeps),
            *(current_one, *state_one[4:]),
            *(current_two, *state_two[4:]),
            *(half, colour),
        ],
        flags,
        [pltpu.VMEM((depth, items, width), F32), pltpu.SemaphoreType.DMA((8,))],
        out=IN_HBM,
    )
    return (log_perm, smoothed)


def solution(mesh):
    body = fast_body if suits(mesh) else generic_body
    in_specs = (
        P(None, "gz", "gy", "gx"),
        P("gz", "gy"),
        P("gy", "gx"),
        P("gz", "gy", "gx"),
        P("gz", "gy", "gx"),
    )
    out_specs = (P("gz", "gy", "gx"), P("gz", "gy", "gx"))
    return jax.shard_map(body, mesh=mesh, in_specs=in_specs, out_specs=out_specs, check_vma=False)
```

```python
import functools
import math

import jax
import jax.numpy as jnp


from jax import lax
from jax.experimental import pallas as pl
from jax.experimental.pallas import tpu as pltpu
from jax.sharding import PartitionSpec as P

NX = 2048


STORE = 1.0


def padded_2(block, sides, width):
    for axis, dim in sides:
        count = lax.axis_size(axis)
        forward = [(i, i + 1) for i in range(count - 1)]
        backward = [(target, source) for source, target in forward]
        low = lax.ppermute(
            lax.slice_in_dim(block, block.shape[dim] - width, None, axis=dim), axis, forward
        )
        high = lax.ppermute(lax.slice_in_dim(block, 0, width, axis=dim), axis, backward)
        block = jnp.concatenate([low, block, high], axis=dim)
    return block


def twisted_coeffs(spectral, shifts, first_wave):
    count = spectral.shape[3]
    wave_index = first_wave + jnp.arange(count, dtype=jnp.int32)
    wave_turns = shifts[:, :, None] * wave_index[None, None, :] % NX
    phase_angle = wave_turns.astype(jnp.float32) * (2.0 * math.pi / NX)
    cosine = jnp.cos(phase_angle)
    sine_part = jnp.sin(phase_angle)
    real_part = spectral[0] * cosine - spectral[1] * sine_part
    imag_part = spectral[0] * sine_part + spectral[1] * cosine
    return jnp.stack([real_part, imag_part])


def basis(count, first_cell, width_cells):
    wave_index = jnp.arange(count, dtype=jnp.int32)
    cell_index = first_cell + jnp.arange(width_cells, dtype=jnp.int32)
    wave_turns = wave_index[:, None] * cell_index[None, :] % NX
    phase_angle = wave_turns.astype(jnp.float32) * (2.0 * math.pi / NX)
    offsets = jnp.concatenate(
        [jnp.zeros((count, 1), jnp.float32), jnp.full((count, 1), 0.5 * math.pi, jnp.float32)],
        axis=0,
    )
    stacked = jnp.concatenate([phase_angle, phase_angle], axis=0) + offsets
    return jnp.cos(stacked) * (1.0 / math.sqrt(NX))


def flatten_pair(piece):
    depth, items, count = (piece.shape[1], piece.shape[2], piece.shape[3])
    return jnp.concatenate(
        [piece[0].reshape(depth * items, count), piece[1].reshape(depth * items, count)], axis=1
    )


def harmonic(center, beside):
    return 2.0 * center * beside / (center + beside)


def thomas(lower_diagonal, main_diagonal, upper_diagonal, right_hand_side):

    def thomas_forward_scan(carried_state, row_entries):
        previous_ratio, previous_eliminated = carried_state
        column_lower, main_c, sup_c, column_right_hand = row_entries
        present_denominator = main_c - column_lower * previous_ratio
        present_ratio = sup_c / present_denominator
        present_eliminated = (
            column_right_hand - column_lower * previous_eliminated
        ) / present_denominator
        return ((present_ratio, present_eliminated), (present_ratio, present_eliminated))

    zeroed_layer = jnp.zeros(right_hand_side.shape[1:], right_hand_side.dtype)
    unused_output, (ratio_rows, eliminated_rows) = lax.scan(
        thomas_forward_scan,
        (zeroed_layer, zeroed_layer),
        (lower_diagonal, main_diagonal, upper_diagonal, right_hand_side),
    )

    def thomas_backward_scan(following_value, row_entries):
        column_ratio, column_eliminated = row_entries
        present_value = column_eliminated - column_ratio * following_value
        return (present_value, present_value)

    unused_output, solved_values = lax.scan(
        thomas_backward_scan, zeroed_layer, (ratio_rows, eliminated_rows), reverse=True
    )
    return solved_values


def factor(lower_diagonal, main_diagonal, upper_diagonal):

    def factor_forward_scan(previous_ratio, row_entries):
        column_lower, main_c, sup_c = row_entries
        present_denominator = main_c - column_lower * previous_ratio
        present_ratio = sup_c / present_denominator
        return (present_ratio, (present_denominator, present_ratio))

    unused_output, (denominator_rows, ratio_rows) = lax.scan(
        factor_forward_scan,
        jnp.zeros_like(main_diagonal[0]),
        (lower_diagonal, main_diagonal, upper_diagonal),
    )
    return (denominator_rows, ratio_rows)


def solve_factored(lower_diagonal, denominator_rows, ratio_rows, right_hand_side):

    def solve_forward_scan(previous_eliminated, row_entries):
        column_lower, column_denominator, column_right_hand = row_entries
        present_eliminated = (
            column_right_hand - column_lower[None] * previous_eliminated
        ) / column_denominator[None]
        return (present_eliminated, present_eliminated)

    unused_output, eliminated_rows = lax.scan(
        solve_forward_scan,
        jnp.zeros_like(right_hand_side[0]),
        (lower_diagonal, denominator_rows, right_hand_side),
    )

    def solve_backward_scan(following_value, row_entries):
        column_ratio, column_eliminated = row_entries
        present_value = column_eliminated - column_ratio[None] * following_value
        return (present_value, present_value)

    unused_output, solved_values = lax.scan(
        solve_backward_scan,
        jnp.zeros_like(right_hand_side[0]),
        (ratio_rows, eliminated_rows),
        reverse=True,
    )
    return solved_values


def generic_body(spectral, shifts, colour, pressure, source):
    total_depth = pressure.shape[0] * lax.axis_size("gz")
    vert_factor = float(total_depth * total_depth // 4)
    width_cells = spectral.shape[3]
    first_cell = lax.axis_index("gx") * width_cells
    twisted = twisted_coeffs(spectral, shifts, first_cell)
    piece = lax.all_to_all(twisted, "gx", split_axis=1, concat_axis=3, tiled=True)
    depth = piece.shape[1]
    items = piece.shape[2]
    length = piece.shape[3]
    flat = flatten_pair(piece)
    block_width = min(512, length)
    blocks = [
        jnp.dot(
            flat,
            basis(length, block * block_width, block_width),
            precision=lax.Precision.HIGHEST,
            preferred_element_type=jnp.float32,
        )
        for block in range(length // block_width)
    ]
    field_rows = jnp.concatenate(blocks, axis=1).reshape(depth, items, length)
    log_perm = lax.all_to_all(field_rows, "gx", split_axis=2, concat_axis=0, tiled=True)
    perm = jnp.exp(log_perm)
    padded = padded_2(perm, (("gx", 2), ("gz", 0), ("gy", 1)), 1)
    w_zm = vert_factor * harmonic(perm, padded[:-2, 1:-1, 1:-1])
    w_zp = vert_factor * harmonic(perm, padded[2:, 1:-1, 1:-1])
    w_ym = harmonic(perm, padded[1:-1, :-2, 1:-1])
    w_yp = harmonic(perm, padded[1:-1, 2:, 1:-1])
    w_xm = harmonic(perm, padded[1:-1, 1:-1, :-2])
    w_xp = harmonic(perm, padded[1:-1, 1:-1, 2:])
    main_diagonal = STORE + w_xm + w_xp + w_ym + w_yp + w_zm + w_zp
    lower_diagonal = -w_zm
    upper_diagonal = -w_zp
    zeroed_layer = jnp.zeros_like(main_diagonal[0])
    inner_sub = jnp.concatenate([zeroed_layer[None], lower_diagonal[2:-1]], axis=0)
    inner_sup = jnp.concatenate([upper_diagonal[1:-2], zeroed_layer[None]], axis=0)
    inner_main = main_diagonal[1:-1]
    denominator_rows, ratio_rows = factor(inner_sub, inner_main, inner_sup)
    unit_rhs = jnp.zeros((inner_main.shape[0], 2) + zeroed_layer.shape, jnp.float32)
    unit_rhs = unit_rhs.at[0, 0].set(-lower_diagonal[1])
    unit_rhs = unit_rhs.at[-1, 1].set(-upper_diagonal[-2])
    coupled = solve_factored(inner_sub, denominator_rows, ratio_rows, unit_rhs)
    left_part = coupled[:, 0]
    right_part = coupled[:, 1]
    sub_first = lower_diagonal[0]
    main_first = main_diagonal[0] + upper_diagonal[0] * left_part[0]
    sup_first = upper_diagonal[0] * right_part[0]
    sub_last = lower_diagonal[-1] * left_part[-1]
    main_last = main_diagonal[-1] + lower_diagonal[-1] * right_part[-1]
    sup_last = upper_diagonal[-1]

    def line_solve(current):
        cycle = padded_2(current, (("gx", 2), ("gy", 1)), 1)
        right_hand_side = source + w_xm * cycle[:, 1:-1, :-2] + w_xp * cycle[:, 1:-1, 2:]
        right_hand_side = right_hand_side + w_ym * cycle[:, :-2, 1:-1] + w_yp * cycle[:, 2:, 1:-1]
        particular = solve_factored(
            inner_sub, denominator_rows, ratio_rows, right_hand_side[1:-1][:, None]
        )[:, 0]
        rhs_first = right_hand_side[0] - upper_diagonal[0] * particular[0]
        rhs_last = right_hand_side[-1] - lower_diagonal[-1] * particular[-1]
        reduced_rows = jnp.stack(
            [sub_first, main_first, sup_first, rhs_first, sub_last, main_last, sup_last, rhs_last]
        )
        gathered = lax.all_gather(reduced_rows, "gz", axis=0, tiled=True)
        segments = gathered.shape[0] // 8
        system = gathered.reshape((2 * segments, 4) + zeroed_layer.shape)
        reduced_sol = thomas(system[:, 0], system[:, 1], system[:, 2], system[:, 3])
        own_pair = lax.dynamic_slice_in_dim(reduced_sol, 2 * lax.axis_index("gz"), 2, 0)
        face_first = own_pair[0]
        face_last = own_pair[1]
        inner = particular + face_first[None] * left_part + face_last[None] * right_part
        return jnp.concatenate([face_first[None], inner, face_last[None]], axis=0)

    half = jnp.where((colour == 0)[None], line_solve(pressure), pressure)
    smoothed = jnp.where((colour == 1)[None], line_solve(half), half)
    return (log_perm, smoothed)


LANES = 128
ROWS = 8
F32 = jnp.float32
MIB = 1 << 20
SUMS_GRANT = 60


def suits(mesh):
    sizes = dict(mesh.shape)
    return sizes["gx"] == 2 and sizes["gz"] == 4 and sizes["gy"] == 4


def params(mib):
    return pltpu.CompilerParams(vmem_limit_bytes=mib * MIB)


def cos_sin(turns):
    quarter = (turns + NX // 8) >> 9
    angle = (turns - (quarter << 9)).astype(F32) * (2.0 * math.pi / NX)
    square = angle * angle
    sine = angle * (
        1.0
        + square * (-1.0 / 6 + square * (1.0 / 120 + square * (-1.0 / 5040 + square / 362880)))
    )
    cosine = 1.0 + square * (
        -0.5 + square * (1.0 / 24 + square * (-1.0 / 720 + square * (1.0 / 40320)))
    )
    odd = (quarter & 1) == 1
    first = jnp.where(odd, sine, cosine)
    second = jnp.where(odd, cosine, sine)
    cos_sign = jnp.where(((quarter + 1) & 2) == 2, -1.0, 1.0)
    sin_sign = jnp.where((quarter & 2) == 2, -1.0, 1.0)
    return first * cos_sign, second * sin_sign


def split(values):
    high = values.astype(jnp.bfloat16)
    return high, (values - high.astype(F32)).astype(jnp.bfloat16)


def times(first, second):
    return (
        first[0] * second[0] - first[1] * second[1],
        first[0] * second[1] + first[1] * second[0],
    )


def plus(first, second):
    return (first[0] + second[0], first[1] + second[1])


def minus(first, second):
    return (first[0] - second[0], first[1] - second[1])


def quarter_turn(value):
    return (-value[1], value[0])


def four_point(first, second, third, fourth):
    even, gap = plus(first, third), minus(first, third)
    odd, turned = plus(second, fourth), quarter_turn(minus(second, fourth))
    return [plus(even, odd), plus(gap, turned), minus(even, odd), minus(gap, turned)]


def eight_point(values):
    even = four_point(*values[0::2])
    odd = four_point(*values[1::2])
    root = math.sqrt(0.5)
    real, imag = odd[1]
    odd[1] = (root * (real - imag), root * (real + imag))
    odd[2] = quarter_turn(odd[2])
    real, imag = odd[3]
    odd[3] = (-root * (real + imag), root * (real - imag))
    return [plus(*pair) for pair in zip(even, odd)] + [minus(*pair) for pair in zip(even, odd)]


def fill_tables(basis, turns):
    groups = NX // LANES
    shape = (LANES, LANES)
    lane = lane_of(shape)
    cells = (lane % groups) * (LANES // groups) + lane // groups
    cosine, sine = cos_sin((row_of(shape) * cells) % LANES * groups)
    for at, value in enumerate((cosine, -sine)):
        rows = slice(at * LANES, (at + 1) * LANES)
        high, low = split(value * (1.0 / math.sqrt(NX)))
        basis[0, rows], basis[1, rows], basis[2, rows] = high, high, low
    shape = (groups, LANES)
    turns[0], turns[1] = cos_sin(row_of(shape) * lane_of(shape))


def diagonal_of(depth):
    square = (depth, depth)
    return row_of(square) == lane_of(square)


def shift_columns(shifts, rows_of, columns):
    depth = shifts.shape[1]
    diagonal = diagonal_of(depth)
    for at, y in enumerate(rows_of):
        spread = jnp.where(diagonal, shifts[y : y + 1, :].astype(F32), 0.0)
        shift = jnp.broadcast_to(jnp.sum(spread, axis=1, keepdims=True), (depth, LANES))
        columns[at * depth : (at + 1) * depth, :] = shift.astype(jnp.int32)


def edge_columns(ys, depth, edges, kept):
    kept[...] = jnp.zeros_like(kept)
    diagonal = diagonal_of(depth)
    for at in range(len(ys)):
        rows = slice(at * depth, (at + 1) * depth)
        for side in range(edges.shape[0]):
            lane = 0 if side % 2 else LANES - 1
            column = jnp.broadcast_to(edges[side, rows, lane : lane + 1], (depth, depth))
            row = jnp.sum(jnp.where(diagonal, column, 0.0), axis=0, keepdims=True)
            kept[side, at : at + 1, :depth] = row


def twisted(first_wave, shift, coefficients, rows):
    lane = lane_of(shift.shape)
    phase = cos_sin((shift * (lane + first_wave)) & (NX - 1))
    turn = cos_sin((shift * LANES) & (NX - 1))
    values = []
    for part in range(coefficients.shape[0]):
        values.append(times((coefficients[part, 0, rows], coefficients[part, 1, rows]), phase))
        phase = times(phase, turn)
    return values


def interleave(tiles):
    count = len(tiles)
    lane = lane_of(tiles[0].shape)
    bit = count // 2
    while bit:
        low = (lane & bit) == 0
        moved = list(tiles)
        for at in range(count):
            if not at & bit:
                first, second = tiles[at], tiles[at | bit]
                crossed = jnp.take_along_axis(
                    jnp.where(low, second, first), lane ^ bit, axis=1
                )
                moved[at] = jnp.where(low, first, crossed)
                moved[at | bit] = jnp.where(low, crossed, second)
        tiles = moved
        bit //= 2
    return tiles


STEP = 16


def fill_left(g, at, y, depth, items, columns, coefficients, turns, left, part):
    groups = NX // LANES
    sign = 1.0 - 2.0 * g.astype(F32)
    first_wave = g * (coefficients.shape[0] * LANES)
    rows = pl.ds(part * STEP * items + y, STEP, stride=items)
    shift = columns[pl.ds(at * depth + part * STEP, STEP), :]
    values = twisted(first_wave, shift, coefficients, rows)
    angles = [2 * math.pi * p / groups for p in range(len(values))]
    turned = [
        times(value, (sign * math.cos(angle), sign * math.sin(angle)))
        if angle
        else (sign * value[0], sign * value[1])
        for angle, value in zip(angles, values)
    ]
    even, odd = eight_point(values), eight_point(turned)
    for group in range(groups):
        value = odd[group // 2] if group % 2 else even[group // 2]
        if group:
            value = times(value, (turns[0, group : group + 1], turns[1, group : group + 1]))
        first = group * depth + part * STEP
        for place_of, piece in enumerate(value):
            for half, bits in enumerate(split(piece)):
                target = (2 * half + place_of) * LANES
                left[first : first + STEP, target : target + LANES] = bits


def finish_row(at, depth, basis, left, right, emit):
    groups = NX // LANES
    spread = jnp.concatenate([left[...], left[:, : 2 * LANES]], axis=1)
    bases = basis[...].reshape(-1, LANES)
    right[...] = jnp.dot(spread, bases, preferred_element_type=F32)
    for part in range(depth // ROWS):
        tiles = [
            right[group * depth + part * ROWS : group * depth + (part + 1) * ROWS]
            for group in range(groups)
        ]
        emit(pl.ds(at * depth + part * ROWS, ROWS), interleave(tiles))


def load_coefficients(spectral, coefficients, arrivals, items):
    parts, halves = arrivals.shape
    copies = []
    for half in range(halves):
        rows = slice(half * STEP * items, (half + 1) * STEP * items)
        copies.append(
            [
                pltpu.make_async_copy(
                    spectral.at[:, rows, part * LANES : (part + 1) * LANES],
                    coefficients.at[part, :, rows],
                    arrivals.at[part, half],
                )
                for part in range(parts)
            ]
        )
    for copy in copies[0]:
        copy.start()
    return copies


def all_rows(g, ys, shifts, shift_copy, copies, columns, coefficients, tables, left, right, emit):
    items, depth = shifts.shape
    basis, turns = tables
    fill_tables(basis, turns)
    for half in copies[1:]:
        for copy in half:
            copy.start()
    shift_copy.wait()
    shift_columns(shifts, ys, columns)
    for half, arriving in enumerate(copies):
        for copy in arriving:
            copy.wait()
        for at, y in enumerate(ys):
            fill_left(g, at, y, depth, items, columns, coefficients, turns, left.at[at], half)
            if half == len(copies) - 1:
                finish_row(at, depth, basis, left.at[at], right.at[at], emit)


def keep_edges(rows, tiles, edges):
    count = len(tiles) // 4
    for side in range(edges.shape[0]):
        edges[side, rows] = tiles[(side // 2 + 1) * count - 1 + side % 2]


def inner_sums_kernel(ys, shifts, spectral, pressure, other, own, kept, p_column, *refs):
    tile, sem, *refs = refs
    g = lax.axis_index("gx")
    width = pressure.shape[2]
    there = lane_slice(jnp.where(g == 0, width - LANES, 0), LANES)
    copy = pltpu.make_async_copy(pressure.at[:, :, there], tile, sem)
    copy.start()
    wide_sums_kernel(ys, shifts, spectral, other, own, kept, *refs)
    copy.wait()
    packed = jnp.zeros((ROWS, LANES), F32)
    for z in range(tile.shape[0]):
        packed = packed_with(z, packed, boundary_plane(g, tile[z]), 0)
    p_column[...] = packed


def wide_sums_kernel(ys, shifts, spectral, other, own, kept, *refs):
    local, arrived, columns, edges, coefficients, arrivals, *tables, left, right = refs
    items, depth = shifts.shape
    shift_copy = pltpu.make_async_copy(shifts, local, arrived)
    shift_copy.start()
    copies = load_coefficients(spectral, coefficients, arrivals, items)
    g = lax.axis_index("gx")

    def emit(rows, tiles):
        half = len(tiles) // 2
        keep_edges(rows, tiles, edges)
        for tile, (low, high) in enumerate(zip(tiles[:half], tiles[half:])):
            there = slice(tile * LANES, (tile + 1) * LANES)
            other[rows, there] = jnp.where(g == 0, high, low)
            own[rows, there] = jnp.where(g == 0, low, high)

    all_rows(
        *(g, ys, local, shift_copy, copies, columns, coefficients, tables, left, right, emit)
    )
    edge_columns(ys, depth, edges, kept)


def last_sums_kernel(ys, outer_kept, inner_kept, p_column, shifts, spectral, one, two, own, *refs):
    columns_own, kept, local, arrived, columns, edges, coefficients, *refs = refs
    arrivals, *tables, left, right = refs
    items, depth = shifts.shape
    shift_copy = pltpu.make_async_copy(shifts, local, arrived)
    shift_copy.start()
    copies = load_coefficients(spectral, coefficients, arrivals, items)
    g = lax.axis_index("gx")

    def emit(rows, tiles):
        half = len(tiles) // 2
        keep_edges(rows, tiles, edges)
        others = []
        for tile, (low, high) in enumerate(zip(tiles[:half], tiles[half:])):
            own[rows, tile * LANES : (tile + 1) * LANES] = jnp.where(g == 0, low, high)
            others.append(jnp.where(g == 0, high, low))
        start = 0
        for ref in (one, two):
            count = ref.shape[1] // LANES
            for tile in range(count):
                ref[rows, tile * LANES : (tile + 1) * LANES] = jnp.where(
                    g == 0, others[start + tile], others[half - start - count + tile]
                )
            start += count

    all_rows(
        *(g, ys, local, shift_copy, copies, columns, coefficients, tables, left, right, emit)
    )
    edge_columns(ys, depth, edges, kept)
    sides_of = [
        jnp.concatenate(
            [outer_kept[side, :1], inner_kept[side], kept[side], outer_kept[side, 1:]], axis=0
        )
        for side in range(6)
    ]
    low, high = sides_of[:3], sides_of[3:]
    own_sides = [jnp.where(g == 0, *pair) for pair in ((low[0], high[1]), (low[1], high[2]))]
    own_sides.append(jnp.where(g == 0, low[2], high[0]))
    other_sides = [jnp.where(g == 0, *pair) for pair in ((high[1], low[0]), (high[2], low[1]))]
    other_sides.append(jnp.where(g == 0, high[0], low[2]))
    for at in range(3):
        columns_own[at], columns_own[3 + at] = own_sides[at], other_sides[at]
    extra = slice(one.shape[0] - ROWS, one.shape[0])
    for at, piece in enumerate((*other_sides, own_sides[2], p_column[...])):
        one[extra, at * LANES : (at + 1) * LANES] = piece


ON_CHIP = pl.BlockSpec(memory_space=pltpu.VMEM)
IN_HBM = pl.BlockSpec(memory_space=pltpu.HBM)


def call(
    kernel, name, out_shape, args, flags=None, scratch=(), far=(), mib=20, flops=1, out=ON_CHIP
):
    specs = [ON_CHIP] * len(args) + [IN_HBM] * len(far)
    args = list(args) + list(far)
    body = kernel if flags is None else lambda *refs: kernel(flags(), *refs)
    return pl.pallas_call(
        body,
        out_shape=out_shape,
        in_specs=specs,
        out_specs=jax.tree.map(lambda _: out, out_shape),
        scratch_shapes=list(scratch),
        compiler_params=params(mib),
        cost_estimate=pl.CostEstimate(flops=flops, bytes_accessed=1, transcendentals=0),
        name=name,
    )(*args)


def roll(values, shift, axis):
    return pltpu.roll(values, shift % values.shape[axis], axis)


def lane_of(shape):
    return lax.broadcasted_iota(jnp.int32, shape, 1)


def row_of(shape):
    return lax.broadcasted_iota(jnp.int32, shape, 0)


def column_to(z, packed, target):
    return pltpu.roll(packed, (target - z) % LANES, 1)


def packed_with(z, packed, plane, lane):
    column = jnp.broadcast_to(plane[:, lane : lane + 1], (ROWS, LANES))
    return jnp.where(lane_of((ROWS, LANES)) == z, column, packed)


def inverse_of(values):
    return pl.reciprocal(values, approx=True)


def ordered(z, sums, depth):
    spread = pl.ds(z, ROWS, stride=depth)
    return jnp.concatenate([sums[at, spread] for at in range(sums.shape[0])], axis=1)


def place_tiles(sums, rows, first, values):
    for at in range(values.shape[1] // LANES):
        sums[(first >> 7) + at, rows] = values[:, at * LANES : (at + 1) * LANES]


def boundary_plane(g, plane):
    return jnp.where(g == 0, roll(plane[:, -LANES:], 1, 1), plane[:, :LANES])


def outer_field_kernel(depth, flags, own, other, pressure, to_near, to_middle):
    even = flags[16] == 0
    low, high = slice(0, depth), slice(depth, 2 * depth)
    south, north = own[low] + other[low], own[high] + other[high]
    to_near[low] = jnp.exp(-jnp.where(even, north, south))
    to_middle[low] = jnp.exp(-jnp.where(even, south, north))

    for z in range(depth):
        keep_rows(depth + z, pressure[z], even, to_near, to_middle, slice(None))


def wide_field_kernel(depth, flags, *refs):
    own_outer, outer, own_inner, inner, to_near, to_middle = refs[:6]
    from_near, from_middle, pressure = refs[6:9]
    wide, south_weight, north_weight, p_south, p_north, p_west, p_east = refs[9:16]
    south_rows, north_rows = refs[16:]
    even = flags[16] == 0
    low, high = slice(0, depth), slice(depth, 2 * depth)
    wide[low] = own_outer[low] + outer[low]
    wide[depth:-depth] = own_inner[...] + inner[...]
    wide[-depth:] = own_outer[high] + outer[high]
    near_weight = 2.0 * inverse_of(to_near[low] + from_near[low])
    middle_weight = (2.0 * flags[15].astype(F32)) * inverse_of(to_middle[low] + from_middle[low])
    south = jnp.where(even, middle_weight, near_weight)
    south_weight[...] = south
    north_weight[...] = jnp.where(even, near_weight, middle_weight)
    south_rows[...] = jnp.where(even, from_middle[high], from_near[high])
    north_rows[...] = jnp.where(even, from_near[high], from_middle[high])
    row = row_of(pressure.shape[1:])

    def layer(z, carry):
        plane = pressure[z]
        p_south[z] = jnp.where(row == 0, south_rows[pl.ds(z, 1), :], roll(plane, 1, 0))
        p_north[z] = jnp.where(row == ROWS - 1, north_rows[pl.ds(z, 1), :], roll(plane, -1, 0))
        p_west[z] = roll(plane, 1, 1)
        p_east[z] = roll(plane, -1, 1)
        return carry

    lax.fori_loop(0, depth, layer, 0, unroll=True)


def lane_slice(start, size):
    return pl.ds(pl.multiple_of(start, LANES), size)


def assemble(sums, depth, wide, own, piece, there):
    inside = wide.shape[0] - depth
    place_tiles(sums, slice(0, inside), 0, wide[:inside, there])
    place_tiles(sums, slice(inside, -depth), 0, own[:, there] + piece[: own.shape[0]])
    place_tiles(sums, slice(-depth, None), 0, wide[inside:, there])


def first_field_kernel(depth, flags, *refs):
    wide, own, middle, columns_own = refs[:4]
    log_perm, resist, low_side, high_side, boundary, column, p_column, sums = refs[4:]
    extra = slice(own.shape[0], own.shape[0] + ROWS)
    came = [middle[extra, at * LANES : (at + 1) * LANES] for at in range(5)]
    for at, ref in enumerate((low_side, high_side, boundary)):
        ref[...] = jnp.exp(-(columns_own[at] + came[at]))
    column[...] = jnp.exp(-(columns_own[5] + came[3]))
    p_column[...] = came[4]
    assemble(sums, depth, wide, own, middle, lane_slice(flags[3], log_perm.shape[2]))

    def layer(z, carry):
        plane = ordered(z, sums, depth)
        log_perm[z] = plane
        resist[z] = jnp.exp(-plane)
        return carry

    lax.fori_loop(0, depth, layer, 0, unroll=True)


def second_field_kernel(depth, flags, *refs):
    wide, own, middle, resist_near = refs[:4]
    log_perm, resist, sums = refs[4:]
    third = middle.shape[1]
    assemble(sums, depth, wide, own, middle, lane_slice(flags[5], third))
    extra = resist.shape[2] - third
    target = lane_slice(flags[5] - flags[7], third)
    extra_target = lane_slice(flags[8], extra)
    extra_source = lane_slice(flags[9], extra)

    def layer(z, carry):
        plane = ordered(z, sums, depth)
        log_perm[z] = plane
        resist[z, :, target] = jnp.exp(-plane)
        resist[z, :, extra_target] = resist_near[z, :, extra_source]
        return carry

    lax.fori_loop(0, depth, layer, 0, unroll=True)


def join_columns_kernel(depth, flags, near, far, _, whole):
    def layer(z, carry):
        whole[z, :, lane_slice(flags[3], near.shape[2])] = near[z]
        whole[z, :, lane_slice(flags[5], far.shape[2])] = far[z]
        return carry

    lax.fori_loop(0, depth, layer, 0, unroll=True)


def keep_rows(z, value, even, to_near, to_middle, here):
    south, north = value[0:1, :], value[ROWS - 1 : ROWS, :]
    to_near[pl.ds(z, 1), here] = jnp.where(even, north, south)
    to_middle[pl.ds(z, 1), here] = jnp.where(even, south, north)


def with_first(plane, edge):
    first = jnp.where(lane_of((ROWS, LANES)) == 0, edge, plane[:, :LANES])
    return jnp.concatenate([first, plane[:, LANES:]], axis=1)


def with_last(plane, edge):
    last = jnp.where(lane_of((ROWS, LANES)) == LANES - 1, edge, plane[:, -LANES:])
    return jnp.concatenate([plane[:, :-LANES], last], axis=1)


def coupling(z, field, start, size, east_weight, north_weight, south_terms, north_rows, west, column):
    here = lane_slice(start, size)
    plane = field[z, :, here]
    row = row_of(plane.shape)
    at_start = start == 0
    inner = field[z, :, lane_slice(jnp.where(at_start, size, size - LANES), LANES)]
    west_value = jnp.where(at_start, column_to(z, column, 0), roll(inner, 1, 1))
    east_value = jnp.where(at_start, roll(inner, -1, 1), column_to(z, column, LANES - 1))
    to_east, to_north = east_weight * plane, north_weight * plane
    from_west = with_first(roll(to_east, 1, 1), column_to(z, west, 0) * west_value)
    from_east = east_weight * with_last(roll(plane, -1, 1), east_value)
    from_south = jnp.where(row == 0, south_terms[pl.ds(z, 1), here], roll(to_north, 1, 0))
    from_north = north_weight * jnp.where(
        row == ROWS - 1, north_rows[pl.ds(z, 1), here], roll(plane, -1, 0)
    )
    return (from_west + from_east) + (from_south + from_north)


def edge_weights(flags, start, bound, column, low_side, high_side):
    g = flags[0]
    middle = 2.0 * inverse_of(low_side + high_side)
    across = 2.0 * inverse_of(bound + column)
    none = jnp.zeros_like(across)
    west = jnp.where(start == 0, jnp.where(g == 0, none, across), middle)
    east = jnp.where(start == 0, middle, jnp.where(g == 0, across, none))
    return west, east


def first_sweep_kernel(depth, vert, block, flags, *refs):
    resist, low_side, high_side, r_bound, r_column, p_column = refs[:6]
    south_weight, north_weight, p_south, p_north, p_west, p_east = refs[6:12]
    source = refs[12]
    w_east, w_north, west_out, particular, inverse, ratio, lead, reduced = refs[13:21]
    grounds, rights, verticals = refs[21:]
    start, offset = flags[6 + block], flags[10 + block]
    size = inverse.shape[2]
    shape = (ROWS, size)
    here = lane_slice(start, size)
    inside = lane_slice(offset, size)
    west_weight, east_weight = edge_weights(
        flags, start, r_bound[...], r_column[...], low_side[...], high_side[...]
    )
    west_out[...] = west_weight
    column = p_column[...]
    row = row_of(shape)

    def weigh(z, carry):
        plane = resist[z, :, inside]
        east = 2.0 * inverse_of(plane + roll(plane, -1, 1))
        east = with_last(east, column_to(z, east_weight, LANES - 1))
        west = with_first(roll(east, 1, 1), column_to(z, west_weight, 0))
        north = 2.0 * inverse_of(plane + roll(plane, -1, 0))
        north = jnp.where(row == ROWS - 1, north_weight[pl.ds(z, 1), here], north)
        south = jnp.where(row == 0, south_weight[pl.ds(z, 1), here], roll(north, 1, 0))
        w_east[z], w_north[z] = east, north
        grounds[z] = STORE + ((east + west) + (north + south))
        verticals[z] = (2.0 * vert) * inverse_of(
            plane + resist[jnp.minimum(z + 1, depth - 1), :, inside]
        )
        p_first, p_last = p_west[z, :, here], p_east[z, :, here]
        p_first = with_first(
            p_first, jnp.where(start == 0, column_to(z, column, 0), p_first[:, :LANES])
        )
        p_last = with_last(
            p_last, jnp.where(start == 0, p_last[:, -LANES:], column_to(z, column, LANES - 1))
        )
        rights[z] = source[z, :, here] + (
            (west * p_first + east * p_last)
            + (south * p_south[z, :, here] + north * p_north[z, :, here])
        )
        return carry

    lax.fori_loop(0, depth, weigh, 0, unroll=True)

    def layer(z, carry):
        conduct, flow, product, first_first, first_part = carry
        weight = verticals[z]
        reciprocal = inverse_of(conduct + weight)
        quotient = weight * reciprocal
        led = product * reciprocal
        inverse[z] = reciprocal
        ratio[z] = quotient
        lead[z] = led
        particular[z] = reciprocal * flow
        return (
            grounds[z + 1] + conduct * quotient,
            rights[z + 1] + flow * quotient,
            product * quotient,
            first_first + led * product,
            first_part + led * flow,
        )

    zero = jnp.zeros(shape, F32)
    conduct, flow, product, first_first, first_part = lax.fori_loop(
        0,
        depth - 1,
        layer,
        (grounds[0], rights[0], jnp.ones(shape, F32), zero, zero),
        unroll=True,
    )
    reciprocal = inverse_of(conduct)
    led = product * reciprocal
    inverse[depth - 1] = reciprocal
    ratio[depth - 1] = zero
    lead[depth - 1] = led
    particular[depth - 1] = flow * reciprocal
    reduced[0] = first_first + led * product + resist[0, :, inside] * (0.5 / vert)
    reduced[1] = led
    reduced[2] = reciprocal + resist[depth - 1, :, inside] * (0.5 / vert)
    reduced[3] = first_part + led * flow
    reduced[4] = flow * reciprocal


def pair_kernel(flags, own, near, across, kept):
    me = flags[14]
    even, lower = me % 2 == 0, me < 2
    first, second = [
        [jnp.where(flip, own[at], near[at]) for at in range(5)]
        for flip in (even, jnp.logical_not(even))
    ]
    reciprocal = inverse_of(first[2] + second[0])
    step = (first[4] - second[3]) * reciprocal
    through = jnp.where(lower, second[1], first[1])
    share = through * reciprocal
    across[0] = jnp.where(lower, second[2], first[0]) - through * share
    across[1] = jnp.where(lower, second[4], first[3]) + jnp.where(
        lower, through * step, -through * step
    )
    kept[0], kept[1], kept[2] = share, reciprocal, step


def ends(me, inner, middle):
    zero = jnp.zeros_like(inner)
    odd = me % 2 == 1
    enters = jnp.where(odd, inner, jnp.where(me == 2, middle, zero))
    leaves = jnp.where(odd, jnp.where(me == 1, middle, zero), inner)
    return enters, leaves


def back_substitute(depth, lines, emit):
    last = depth - 1
    values = tuple(
        (particular[last] + lead[last] * enters) - inverse[last] * leaves
        for enters, leaves, particular, inverse, ratio, lead in lines
    )
    state = emit(last, values, jnp.zeros((ROWS, LANES), F32))

    for z in range(last - 1, -1, -1):
        values = tuple(
            (particular[z] + lead[z] * enters) + ratio[z] * beyond
            for (enters, _, particular, _, ratio, lead), beyond in zip(lines, values)
        )
        state = emit(z, values, state)
    return state


def half_kernel(depth, flags, *refs):
    pairs = (refs[0:3], refs[3:6])
    blocks = (refs[6:10], refs[10:14])
    pressure, colour = refs[14:16]
    half, to_near, to_middle, boundary, joined = refs[16:]
    me, g, even = flags[14], flags[0], flags[16] == 0
    size = blocks[0][0].shape[2]
    spans = [lane_slice(flags[6 + block], size) for block in range(2)]
    lines = []
    for block, state in enumerate(blocks):
        across, other, kept = pairs[block]
        sum_of = inverse_of(across[0] + other[0])
        joined[block] = sum_of
        lead_of = across[1] - other[1]
        middle = jnp.where(me < 2, lead_of, -lead_of) * sum_of
        inner = kept[2] + kept[0] * middle
        lines.append((*ends(me, inner, middle), *state))
    chosen = [colour[:, here] == 0 for here in spans]

    def emit(z, values, packed):
        for block, (value, here) in enumerate(zip(values, spans)):
            value = jnp.where(chosen[block], value, pressure[z, :, here])
            half[z, :, here] = value
            keep_rows(z, value, even, to_near, to_middle, here)
            if not block:
                packed = packed_with(z, packed, boundary_plane(g, value), 0)
        return packed

    boundary[...] = back_substitute(depth, lines, emit)


def second_sweep_kernel(depth, flags, *refs):
    half, h_near, h_middle, h_column, source, south_weight = refs[:6]
    shares = refs[6:8]
    blocks = (refs[8:14], refs[14:20])
    particulars, near, far = refs[20:22], refs[22], refs[23]
    south_terms, north_rows = refs[24:]
    me, even = flags[14], flags[16] == 0
    size = particulars[0].shape[2]
    starts = [flags[6 + block] for block in range(2)]
    spans = [lane_slice(start, size) for start in starts]
    column = h_column[...]
    south_terms[...] = south_weight[...] * jnp.where(even, h_middle[...], h_near[...])
    north_rows[...] = jnp.where(even, h_near[...], h_middle[...])

    def local(z, block):
        east, north, west = blocks[block][:3]
        return source[z, :, spans[block]] + coupling(
            z,
            half,
            starts[block],
            size,
            east[z],
            north[z],
            south_terms,
            north_rows,
            west[...],
            column,
        )

    def layer(z, carry):
        result = []
        for block, (flow, first_part) in enumerate(carry):
            inverse, ratio, lead = blocks[block][3:6]
            particulars[block][z] = flow * inverse[z]
            first_part = first_part + lead[z] * flow
            result.append((local(z + 1, block) + flow * ratio[z], first_part))
        return tuple(result)

    carry = tuple((local(0, block), jnp.zeros((ROWS, size), F32)) for block in range(2))
    carry = lax.fori_loop(0, depth - 1, layer, carry, unroll=True)
    last = depth - 1
    for block, (flow, first_part) in enumerate(carry):
        inverse, ratio, lead = blocks[block][3:6]
        there = slice(block * size, (block + 1) * size)
        first_part = first_part + lead[last] * flow
        last_part = flow * inverse[last]
        particulars[block][last] = last_part
        asked = jnp.where(me % 2 == 0, last_part, first_part)
        shared = shares[block][0] * asked
        outer = jnp.where(me == 1, last_part, jnp.where(me == 2, first_part, 0.0))
        given = outer + jnp.where((me == 0) | (me == 3), shared, -shared)
        near[0, :, there] = asked
        near[1, :, there] = given
        far[:, there] = given


def smoothed_kernel(depth, flags, *refs):
    own, near, skip, cross, joined = refs[:5]
    keeps = refs[5:7]
    blocks = (refs[7:11], refs[11:15])
    half, colour, result = refs[15:18]
    smoothed, sems = refs[18:]
    me = flags[14]
    size = blocks[0][0].shape[2]
    spans = [lane_slice(flags[6 + block], size) for block in range(2)]
    lines = []
    for block, state in enumerate(blocks):
        there = slice(block * size, (block + 1) * size)
        kept = keeps[block]
        lead_of = (own[1, :, there] + near[1, :, there]) - (skip[:, there] + cross[:, there])
        middle = jnp.where(me < 2, lead_of, -lead_of) * joined[block]
        step = own[0, :, there] - near[0, :, there]
        step = jnp.where(me % 2 == 0, step, -step) * kept[1]
        lines.append((*ends(me, step + kept[0] * middle, middle), *state))
    chosen = [colour[:, here] == 1 for here in spans]
    count = sems.shape[0]
    layers = depth // count
    copies = [
        pltpu.make_async_copy(
            smoothed.at[pl.ds(at * layers, layers)],
            result.at[pl.ds(at * layers, layers)],
            sems.at[at],
        )
        for at in range(count)
    ]

    def emit(z, values, state):
        for value, here, mine in zip(values, spans, chosen):
            smoothed[z, :, here] = jnp.where(mine, value, half[z, :, here])
        if z % layers == 0:
            copies[z // layers].start()
        return state

    back_substitute(depth, lines, emit)
    for copy in copies:
        copy.wait()


PAIR = [(0, 1), (1, 0)]
NEAR = [(0, 1), (1, 0), (2, 3), (3, 2)]
MIDDLE = [(1, 2), (2, 1), (0, 3), (3, 0)]
SKIP = [(0, 2), (2, 0), (1, 3), (3, 1)]
CROSS = [(0, 3), (3, 0), (1, 2), (2, 1)]


def exchange_edges(edges):
    to_near, to_middle, *column = edges
    return [
        lax.ppermute(to_near, "gy", NEAR),
        lax.ppermute(to_middle, "gy", MIDDLE),
        *[lax.ppermute(piece, "gx", PAIR) for piece in column],
    ]


def fast_body(spectral, shifts, colour, pressure, source):
    depth, items, width = pressure.shape
    vert = float((depth * 4) ** 2 // 4)
    waves = spectral.shape[3]
    rows = depth * items
    block_size, third = width // 2, 3 * width // 8
    known = width - third

    def flags():
        gx, gz, gy = (lax.axis_index(axis) for axis in ("gx", "gz", "gy"))

        def placed(start, size):
            return jnp.where(gx == 1, start, width - start - size)

        block_one, block_two = placed(0, block_size), placed(block_size, block_size)
        start_one = placed(0, known)
        extra = known - block_size
        return [
            gx,
            placed(0, LANES),
            placed(LANES, known - LANES),
            start_one,
            gx,
            placed(known, third),
            block_one,
            block_two,
            placed(block_size, extra) - block_two,
            placed(block_size, extra) - start_one,
            block_one - start_one,
            0,
            gy > 0,
            gy < 3,
            gz,
            ((gy == 1) | (gy == 2)).astype(jnp.int32),
            gy % 2,
        ]

    def shaped(*shape, dtype=F32):
        return jax.ShapeDtypeStruct(shape, dtype)

    groups = NX // LANES
    parts = waves // LANES
    inner_ys, last_ys = (1, 2, 3), tuple(range(4, items - 1))
    last_rows = len(last_ys) * depth
    column_type = shaped(ROWS, LANES)
    coefficients = spectral.reshape(2, rows, waves)

    def scratch(count):
        return [
            pltpu.VMEM((items, depth), jnp.int32),
            pltpu.SemaphoreType.DMA,
            pltpu.VMEM((count, LANES), jnp.int32),
            pltpu.VMEM((6, count, LANES), F32),
            pltpu.VMEM((parts, 2, rows, LANES), F32),
            pltpu.SemaphoreType.DMA((parts, depth // STEP)),
            pltpu.VMEM((3, 2 * LANES, LANES), jnp.bfloat16),
            pltpu.VMEM((2, groups, LANES), F32),
            pltpu.VMEM((count // depth, groups * depth, 4 * LANES), jnp.bfloat16),
            pltpu.VMEM((count // depth, groups * depth, LANES), F32),
        ]

    def wide_types(ys):
        return [shaped(len(ys) * depth, width)] * 2 + [shaped(6, len(ys), LANES)]

    shift_rows = shifts.T
    outer_ys = (0, items - 1)
    sums, own_outer, outer_kept = call(
        functools.partial(wide_sums_kernel, outer_ys),
        "outer_row_sums",
        wide_types(outer_ys),
        [],
        scratch=scratch(2 * depth),
        far=[shift_rows, coefficients],
        mib=SUMS_GRANT,
    )
    outer = lax.ppermute(sums, "gx", PAIR)
    shift_rows, _ = lax.optimization_barrier((shift_rows, own_outer))
    sums, own_inner, inner_kept, p_column = call(
        functools.partial(inner_sums_kernel, inner_ys),
        "inner_row_sums",
        wide_types(inner_ys) + [column_type],
        [],
        scratch=[pltpu.VMEM((depth, ROWS, LANES), F32), pltpu.SemaphoreType.DMA]
        + scratch(len(inner_ys) * depth),
        far=[shift_rows, coefficients, pressure],
        mib=20,
    )
    inner = lax.ppermute(sums, "gx", PAIR)
    edge_row, edge_column = shaped(depth, width), shaped(ROWS, LANES)
    edges = [edge_row, edge_row, edge_column]
    last_one, last_two, own_last, own_columns = call(
        functools.partial(last_sums_kernel, last_ys),
        "last_row_sums",
        [
            shaped(last_rows + ROWS, known),
            shaped(last_rows, third),
            shaped(last_rows, width),
            shaped(6, ROWS, LANES),
        ],
        [outer_kept, inner_kept, p_column],
        scratch=[pltpu.VMEM((6, len(last_ys), LANES), F32)] + scratch(last_rows),
        far=[shift_rows, coefficients],
        mib=20,
    )
    pressure_rows, _ = lax.optimization_barrier((pressure, own_last))
    to_near, to_middle = call(
        functools.partial(outer_field_kernel, depth),
        "outer_field",
        [shaped(2 * depth, width)] * 2,
        [own_outer, outer, pressure_rows],
        flags,
    )
    from_near, from_middle = exchange_edges([to_near, to_middle])
    last_one = lax.ppermute(last_one, "gx", PAIR)
    wide, *around = call(
        functools.partial(wide_field_kernel, depth),
        "wide_field",
        [shaped(rows - last_rows, width)] + [edge_row] * 2 + [shaped(depth, items, width)] * 4,
        [
            *(own_outer, outer, own_inner, inner, to_near, to_middle),
            *(from_near, from_middle, pressure),
        ],
        flags,
        [pltpu.VMEM((depth, width), F32)] * 2,
    )
    last_two, _ = lax.optimization_barrier((last_two, wide))
    last_two = lax.ppermute(last_two, "gx", PAIR)
    log_near, resist_near, *columns = call(
        functools.partial(first_field_kernel, depth),
        "first_field",
        [shaped(depth, items, known)] * 2 + [edge_column] * 5,
        [wide, own_last, last_one, own_columns],
        flags,
        [pltpu.VMEM((known // LANES, rows, LANES), F32)],
    )
    block = shaped(depth, items, block_size)

    state_types = [block] * 2 + [edge_column] + [block] * 4

    def first_sweep(at, resist):
        return call(
            functools.partial(first_sweep_kernel, depth, vert, at),
            "first_sweep",
            state_types + [shaped(5, items, block_size)],
            [resist, *columns, *around, source],
            flags,
            [pltpu.VMEM((depth, items, block_size), F32)] * 3,
        )

    *state_one, reduced_one = first_sweep(0, resist_near)
    near_one = lax.ppermute(reduced_one, "gz", NEAR)
    last_two, _ = lax.optimization_barrier((last_two, reduced_one))
    log_far, resist_far = call(
        functools.partial(second_field_kernel, depth),
        "second_field",
        [shaped(depth, items, third), block],
        [wide, own_last, last_two, resist_near],
        flags,
        [pltpu.VMEM((third // LANES, rows, LANES), F32)],
    )
    *state_two, reduced_two = first_sweep(1, resist_far)
    near_two = lax.ppermute(reduced_two, "gz", NEAR)
    (log_perm,) = call(
        functools.partial(join_columns_kernel, depth),
        "log_perm",
        [shaped(depth, items, width)],
        [log_near, log_far, reduced_two],
        flags,
    )
    def join(reduced, near):
        across, kept = call(
            pair_kernel,
            "join_pair",
            [shaped(2, items, block_size), shaped(3, items, block_size)],
            [reduced, near],
            flags,
        )
        return across, lax.ppermute(across, "gz", SKIP), kept

    pair_one, pair_two = join(reduced_one, near_one), join(reduced_two, near_two)
    keeps = [pair_one[2], pair_two[2]]
    half, *h_edges, joined = call(
        functools.partial(half_kernel, depth),
        "half",
        [shaped(depth, items, width), *edges, shaped(2, items, block_size)],
        [*pair_one, *pair_two, *state_one[3:], *state_two[3:], pressure, colour],
        flags,
    )
    h_edges = exchange_edges(h_edges)
    weights = [[*state[:3], *state[4:]] for state in (state_one, state_two)]
    current_one, current_two, to_near, to_far = call(
        functools.partial(second_sweep_kernel, depth),
        "second_sweep",
        [block, block, shaped(2, items, width), shaped(items, width)],
        [half, *h_edges, source, around[0], *keeps, *weights[0], *weights[1]],
        flags,
        [pltpu.VMEM((depth, width), F32)] * 2,
    )
    from_near, from_skip, from_cross = (
        lax.ppermute(planes, "gz", pairs)
        for planes, pairs in ((to_near, NEAR), (to_far, SKIP), (to_far, CROSS))
    )
    (smoothed,) = call(
        functools.partial(smoothed_kernel, depth),
        "smoothed",
        [shaped(depth, items, width)],
        [
            *(to_near, from_near, from_skip, from_cross, joined, *keeps),
            *(current_one, *state_one[4:]),
            *(current_two, *state_two[4:]),
            *(half, colour),
        ],
        flags,
        [pltpu.VMEM((depth, items, width), F32), pltpu.SemaphoreType.DMA((8,))],
        out=IN_HBM,
    )
    return (log_perm, smoothed)


def solution(mesh):
    body = fast_body if suits(mesh) else generic_body
    in_specs = (
        P(None, "gz", "gy", "gx"),
        P("gz", "gy"),
        P("gy", "gx"),
        P("gz", "gy", "gx"),
        P("gz", "gy", "gx"),
    )
    out_specs = (P("gz", "gy", "gx"), P("gz", "gy", "gx"))
    return jax.shard_map(body, mesh=mesh, in_specs=in_specs, out_specs=out_specs, check_vma=False)
```
